32 devices in a mesh: ctx: 8 (over z, y), wt: 4 (over x, core).
Axes of the slice: x: 2, y: 2, z: 4, core: 2. Of those that a mesh axis runs over, the one named last changes fastest.
Arguments:
- tokens: bfloat16 [4, 8, 320, 1024], P('wt', 'ctx'), may hold values from -6 to 6
- cotangent: bfloat16 [4, 8, 320, 1024], P('wt', 'ctx'), may hold values from -6 to 6
- w_query: bfloat16 [1024, 1024], P('wt', 'ctx'), may hold values from -0.1875 to 0.1875
- w_key: bfloat16 [1024, 1024], P('wt', 'ctx'), may hold values from -0.1875 to 0.1875
- w_value: bfloat16 [1024, 1024], P('wt', 'ctx'), may hold values from -0.1875 to 0.1875
- w_out: bfloat16 [1024, 1024], P('wt', 'ctx'), may hold values from -1 to 1
- gain_attn: bfloat16 [1024], P('wt'), may hold values from 0.5 to 1.5
- gain_ffn: bfloat16 [1024], P('wt'), may hold values from 0.5 to 1.5
- w_router: bfloat16 [1024, 3], P('wt'), may hold values from -0.125 to 0.125
- rel_bias: bfloat16 [32, 16], P(None, 'wt'), may hold values from -4 to 4
- exp_gate: bfloat16 [3, 1024, 2816], P(None, 'wt', 'ctx'), may hold values from -0.1875 to 0.1875
- exp_up: bfloat16 [3, 1024, 2816], P(None, 'wt', 'ctx'), may hold values from -0.1875 to 0.1875
- exp_down: bfloat16 [3, 2816, 1024], P(None, 'ctx', 'wt'), may hold values from -0.3125 to 0.3125
- bucket_table: int32 [768], replicated, may hold values from 0 to 31
- expert_ids: int32 [4, 8, 320, 2], P('wt', 'ctx'), may hold values from 0 to 2, as said below
- priority: int32 [4, 8, 320], P('wt', 'ctx'), may hold values from 0 to 319, each once within a row
Outputs:
- output: bfloat16 [4, 8, 320, 1024], P('wt', 'ctx')
- grad_tokens: bfloat16 [4, 8, 320, 1024], P('wt', 'ctx')
- grad_query: float32 [1024, 1024], P('wt', 'ctx')
- grad_key: float32 [1024, 1024], P('wt', 'ctx')
- grad_value: float32 [1024, 1024], P('wt', 'ctx')
- grad_out: float32 [1024, 1024], P('wt', 'ctx')
- grad_gain_attn: float32 [1024], P('wt')
- grad_gain_ffn: float32 [1024], P('wt')
- grad_router: float32 [1024, 3], P('wt')
- grad_rel_bias: float32 [32, 16], P(None, 'wt')
- grad_exp_gate: float32 [3, 1024, 2816], P(None, 'wt', 'ctx')
- grad_exp_up: float32 [3, 1024, 2816], P(None, 'wt', 'ctx')
- grad_exp_down: float32 [3, 2816, 1024], P(None, 'ctx', 'wt')
The draws below stay inside these ranges and needn't reach their ends.
Inputs may be any that keep to these rules, and one draw needn't show every extreme that they name: `expert_ids`: each token names 2 different experts. `priority`: within each block the 320 ranks are a permutation.
All inputs are finite; a program needn't handle non-finite values.
Results may differ from the reference program's by a relative error of at most 0.018.
Values may be sent and summed in bfloat16 or wider, within the bound.
No kernel may reach another device: no remote copies, remote signals or barrier semaphores. Data moves between devices by JAX's collectives and lax.ppermute only.
A program may use at most 384 MiB of HBM per device.

```python
import jax
import jax.numpy as jnp
from jax import lax

D = 1024
HEADS = 16
HEAD_DIM = 64
FF = 2816
BUCKETS = 32
EXPERTS = 3
TOP = 2
PROMPT_DEV = 64
TOKD = 320
PROMPT = 512
DISTS = 768
GROUPS = 4
BLOCKS = 8
CAP = 267


def draw_expert_ids(key, part):
    key = jax.random.fold_in(key, 7)
    key_fav, key_roll, key_other, key_order = jax.random.split(key, 4)
    favoured = jax.random.randint(key_fav, (GROUPS, BLOCKS, 1), 0, EXPERTS)
    roll = jax.random.randint(key_roll, (GROUPS, BLOCKS, TOKD), 0, 16)
    step_other = jax.random.randint(key_other, (GROUPS, BLOCKS, TOKD), 1, EXPERTS)
    partner = (favoured + step_other) % EXPERTS
    spare = (favoured + EXPERTS - step_other) % EXPERTS
    first = jnp.where(roll < 15, favoured, spare)
    flip = jax.random.randint(key_order, (GROUPS, BLOCKS, TOKD), 0, 2)
    leading = jnp.where(flip == 0, first, partner)
    trailing = jnp.where(flip == 0, partner, first)
    return jnp.stack([leading, trailing], axis=-1).astype(jnp.int32)


def touch_ends(values, key, smallest, largest):
    place = [jax.random.randint(jax.random.fold_in(key, axis), (), 0, length) for axis, length in enumerate(values.shape)]
    longest = values.shape.index(max(values.shape))
    beside = place[:longest] + [(place[longest] + 1) % values.shape[longest]] + place[longest + 1:]
    return values.at[tuple(place)].set(smallest).at[tuple(beside)].set(largest)


def block_levels(own_key, dims, cuts, low, largest):
    gain, own = 1.0, jax.random.fold_in(own_key, 6)
    for axis_at, shards_of in cuts:
        heights = jnp.exp(jax.random.uniform(jax.random.fold_in(own, axis_at), (shards_of,), jnp.float32, low / len(cuts), largest / len(cuts)))
        gain = gain * jnp.repeat(heights, dims[axis_at] // shards_of).reshape([-1 if axis == axis_at else 1 for axis in range(len(dims))])
    return gain


def noise(key, extent, spread, limit, cuts=(), kind=jnp.bfloat16):
    level = block_levels(key, extent, cuts, -0.22, 0.18) if cuts else 1.0
    drawn = jax.random.normal(key, extent, jnp.float32) * spread * level
    return jnp.minimum(jnp.maximum(drawn, -limit), limit).astype(kind)


def setup_inputs(seed: int = 0) -> dict:
    arg_keys = jax.random.split(jax.random.key(seed), 17)
    tokens = noise(arg_keys[0], (GROUPS, BLOCKS, TOKD, D), 1.0, 6.0, ((0, 4), (1, 8)))
    cotangent = noise(arg_keys[1], (GROUPS, BLOCKS, TOKD, D), 1.0, 6.0, ((0, 4), (1, 8)))
    w_query = noise(arg_keys[2], (D, D), D ** -0.5, 0.1875, ((0, 4), (1, 8)))
    w_key = noise(arg_keys[3], (D, D), D ** -0.5, 0.1875, ((0, 4), (1, 8)))
    w_value = noise(arg_keys[4], (D, D), D ** -0.5, 0.1875, ((0, 4), (1, 8)))
    w_out = noise(arg_keys[5], (D, D), (max(1, D * 16 // PROMPT)) ** -0.5, 1.0, ((0, 4), (1, 8)))
    gain_attn = jnp.clip(1.0 + 0.1 * jax.random.normal(arg_keys[6], (D,), jnp.float32), 0.5, 1.5).astype(jnp.bfloat16)
    gain_ffn = jnp.clip(1.0 + 0.1 * jax.random.normal(arg_keys[7], (D,), jnp.float32), 0.5, 1.5).astype(jnp.bfloat16)
    w_router = noise(arg_keys[8], (D, EXPERTS), (2 * D) ** -0.5, 0.125, ((0, 4),))
    rel_bias = noise(arg_keys[9], (BUCKETS, HEADS), 1.0, 4.0, ((1, 4),))
    exp_gate = noise(arg_keys[10], (EXPERTS, D, FF), D ** -0.5, 0.1875, ((1, 4), (2, 8)))
    exp_up = noise(arg_keys[11], (EXPERTS, D, FF), D ** -0.5, 0.1875, ((1, 4), (2, 8)))
    exp_down = noise(arg_keys[12], (EXPERTS, FF, D), (FF // 8) ** -0.5, 0.3125, ((1, 8), (2, 4)))
    bucket_table = touch_ends(jax.random.randint(arg_keys[13], (DISTS,), 0, BUCKETS), jax.random.fold_in(arg_keys[13], 1), 0, BUCKETS - 1).astype(jnp.int32)
    expert_ids = draw_expert_ids(jax.random.fold_in(arg_keys[16], 71), 0)
    priority = jax.vmap(lambda own: jax.random.permutation(own, TOKD))(jax.random.split(arg_keys[15], GROUPS * BLOCKS)).reshape((GROUPS, BLOCKS, TOKD)).astype(jnp.int32)
    return {"tokens": tokens, "cotangent": cotangent, "w_query": w_query, "w_key": w_key, "w_value": w_value, "w_out": w_out, "gain_attn": gain_attn, "gain_ffn": gain_ffn, "w_router": w_router, "rel_bias": rel_bias, "exp_gate": exp_gate, "exp_up": exp_up, "exp_down": exp_down, "bucket_table": bucket_table, "expert_ids": expert_ids, "priority": priority}


@jax.custom_vjp
def low(v):
    return lax.optimization_barrier(v.astype(jnp.bfloat16)).astype(jnp.float32)

@jax.custom_vjp
def low_back(v):
    return v

def low_keep(v):
    return (low(v), None)

def low_pass(kept, grad):
    return (grad,)

def back_keep(v):
    return (v, None)

def back_low(kept, grad):
    return (low(grad),)
low.defvjp(low_keep, low_pass)
low_back.defvjp(back_keep, back_low)
precise = lax.Precision.HIGHEST

def rounded_both(values):
    return low_back(low(values))

def rms_norm(values, gain_vec):
    return values * lax.rsqrt(lax.optimization_barrier(jnp.mean(values * values, axis=-1, keepdims=True)) + 1e-06) * gain_vec

def attend(query_rows, prompt_keys, prompt_values, local_keys, local_values, bias_table, block_index):
    all_keys = jnp.concatenate([prompt_keys, local_keys], axis=0)
    all_values = jnp.concatenate([prompt_values, local_values], axis=0)
    row_count = query_rows.shape[0]
    row_index = jnp.arange(row_count, dtype=jnp.int32)
    query_pos = jnp.where(row_index < PROMPT_DEV, block_index * PROMPT_DEV + row_index, PROMPT + row_index - PROMPT_DEV)
    key_pos = jnp.arange(DISTS, dtype=jnp.int32)
    offset = query_pos[:, None] - key_pos[None, :]
    lookup = jnp.clip(offset, 0, DISTS - 1)
    bias_part = jnp.transpose(jnp.take(bias_table, lookup, axis=0), (2, 0, 1))
    query_heads = query_rows.reshape(row_count, HEADS, HEAD_DIM)
    key_heads = all_keys.reshape(DISTS, HEADS, HEAD_DIM)
    value_heads = all_values.reshape(DISTS, HEADS, HEAD_DIM)
    logit_raw = low_back(jnp.einsum('qhd,khd->hqk', query_heads, key_heads, precision=precise) * HEAD_DIM ** (-0.5))
    scores = jnp.where(offset[None] >= 0, logit_raw + bias_part, -1e+30)
    chances = jax.nn.softmax(scores, axis=-1)
    mixed = jnp.einsum('hqk,khd->qhd', low(chances), value_heads, precision=precise)
    return mixed.reshape(row_count, HEADS * HEAD_DIM)

def routing(expert_ids, priority):
    tok_rows = expert_ids.shape[0]
    expert = expert_ids.T.reshape(-1)
    rank_key = (jnp.arange(TOP, dtype=jnp.int32)[:, None] * tok_rows + priority[None, :]).reshape(-1)
    earlier = (expert[:, None] == expert[None, :]) & (rank_key[None, :] < rank_key[:, None])
    places = lax.optimization_barrier(jnp.sum(earlier.astype(jnp.int32), axis=1))
    keep_mask = places < CAP
    slot_ids = expert * CAP + jnp.minimum(places, CAP - 1)
    return (keep_mask, slot_ids)

def experts_block(normed, expert_ids, priority, w_router, exp_gate, exp_up, exp_down):
    keep_mask, slot_ids = routing(expert_ids, priority)
    tok_rows = normed.shape[0]
    slot_hits = jnp.where((slot_ids[:, None] == jnp.arange(EXPERTS * CAP, dtype=jnp.int32)[None, :]) & keep_mask[:, None], 1.0, 0.0)
    dispatch = lax.optimization_barrier(jnp.sum(slot_hits.reshape(TOP, tok_rows, EXPERTS * CAP), axis=0)).T
    inputs = jnp.dot(dispatch, normed, precision=precise).reshape(EXPERTS, CAP, D)
    gate_pre = low_back(jnp.einsum('ecd,edf->ecf', inputs, exp_gate, precision=precise))
    up_pre = low_back(jnp.einsum('ecd,edf->ecf', inputs, exp_up, precision=precise))
    inner_low = low(jax.nn.gelu(gate_pre, approximate=True) * up_pre)
    expert_out = low_back(jnp.einsum('ecf,efd->ecd', inner_low, exp_down, precision=precise)).reshape(EXPERTS * CAP, D)
    logits = jnp.dot(normed, w_router, precision=precise)
    chances = jax.nn.softmax(logits, axis=-1)
    picked = jnp.take_along_axis(chances, expert_ids, axis=1).T.reshape(-1)
    weight_pair = jnp.where(keep_mask, picked, 0.0)
    picked_rows = jnp.take(expert_out, slot_ids, axis=0) * weight_pair[:, None]
    return lax.optimization_barrier(jnp.sum(picked_rows.reshape(TOP, tok_rows, D), axis=0))

def block_layer(tokens, w_query, w_key, w_value, w_out, gain_attn, gain_ffn, w_router, rel_bias, exp_gate, exp_up, exp_down, bucket_table, expert_ids, priority):
    bias_table = jnp.take(rel_bias, bucket_table, axis=0)
    results = []
    for group_idx in range(GROUPS):
        source = tokens[group_idx].reshape(BLOCKS * TOKD, D)
        normed_attn = low(rms_norm(source, gain_attn))
        query_all = rounded_both(jnp.dot(normed_attn, w_query, precision=precise)).reshape(BLOCKS, TOKD, D)
        key_all = rounded_both(jnp.dot(normed_attn, w_key, precision=precise)).reshape(BLOCKS, TOKD, D)
        value_all = rounded_both(jnp.dot(normed_attn, w_value, precision=precise)).reshape(BLOCKS, TOKD, D)
        prompt_keys = key_all[:, :PROMPT_DEV].reshape(PROMPT, D)
        prompt_values = value_all[:, :PROMPT_DEV].reshape(PROMPT, D)

        def one_block(block_item):
            return attend(block_item[0], prompt_keys, prompt_values, block_item[1], block_item[2], bias_table, block_item[3])
        mixed = lax.map(jax.checkpoint(one_block), (query_all, key_all[:, PROMPT_DEV:], value_all[:, PROMPT_DEV:], jnp.arange(BLOCKS, dtype=jnp.int32)))
        mixed = rounded_both(mixed.reshape(BLOCKS * TOKD, D))
        attn_out = low_back(jnp.dot(mixed, w_out, precision=precise))
        hidden = source + attn_out
        normed_ffn = low(rms_norm(hidden, gain_ffn)).reshape(BLOCKS, TOKD, D)

        def one_moe(normed_rows, ids_rows, rank_rows):
            return experts_block(normed_rows, ids_rows, rank_rows, w_router, exp_gate, exp_up, exp_down)
        combined = jax.vmap(one_moe)(normed_ffn, expert_ids[group_idx], priority[group_idx])
        results.append((hidden + combined.reshape(BLOCKS * TOKD, D)).reshape(BLOCKS, TOKD, D))
    return jnp.stack(results)

def reference(tokens, cotangent, w_query, w_key, w_value, w_out, gain_attn, gain_ffn, w_router, rel_bias, exp_gate, exp_up, exp_down, bucket_table, expert_ids, priority):
    floats = (tokens.astype(jnp.float32), w_query.astype(jnp.float32), w_key.astype(jnp.float32), w_value.astype(jnp.float32), w_out.astype(jnp.float32), gain_attn.astype(jnp.float32), gain_ffn.astype(jnp.float32), w_router.astype(jnp.float32), rel_bias.astype(jnp.float32), exp_gate.astype(jnp.float32), exp_up.astype(jnp.float32), exp_down.astype(jnp.float32))

    def wrapped(*arrays):
        return block_layer(*arrays, bucket_table, expert_ids, priority)
    output, pullback = jax.vjp(wrapped, *floats)
    gradients = pullback(cotangent.astype(jnp.float32))
    return (output.astype(jnp.bfloat16), gradients[0].astype(jnp.bfloat16), gradients[1].astype(jnp.float32), gradients[2].astype(jnp.float32), gradients[3].astype(jnp.float32), gradients[4].astype(jnp.float32), gradients[5].astype(jnp.float32), gradients[6].astype(jnp.float32), gradients[7].astype(jnp.float32), gradients[8].astype(jnp.float32), gradients[9].astype(jnp.float32), gradients[10].astype(jnp.float32), gradients[11].astype(jnp.float32))
```

```python
import functools

import jax
import jax.numpy as jnp
from jax import lax
from jax.experimental import pallas as pl
from jax.experimental.pallas import tpu as pltpu
from jax.sharding import PartitionSpec as P

HEADS = 16
HEAD_DIM = 64
BUCKETS = 32
EXPERTS = 3
TOP = 2
LEN = 256
CAP = 267


epsilon = 1e-06
precise = lax.Precision.HIGHEST


def rms_norm(values, gain_vec):
    return (
        values * lax.rsqrt(jnp.mean(values * values, axis=-1, keepdims=True) + epsilon) * gain_vec
    )


def gelu_product(gate_pre, up_pre):
    return jax.nn.gelu(gate_pre, approximate=True) * up_pre


def routing(expert_ids, priority, capacity, expert_count):
    tok_rows = expert_ids.shape[0]
    top_count = expert_ids.shape[1]
    expert = expert_ids.T.reshape(-1)
    rank_key = (
        jnp.arange(top_count, dtype=jnp.int32)[:, None] * tok_rows + priority[None, :]
    ).reshape(-1)
    earlier = (expert[:, None] == expert[None, :]) & (rank_key[None, :] < rank_key[:, None])
    places = jnp.sum(earlier.astype(jnp.int32), axis=1)
    keep_mask = places < capacity
    slot_ids = expert * capacity + jnp.minimum(places, capacity - 1)
    slot_hits = jnp.where(
        (slot_ids[:, None] == jnp.arange(expert_count * capacity, dtype=jnp.int32)[None, :])
        & keep_mask[:, None],
        1.0,
        0.0,
    )
    dispatch = jnp.sum(slot_hits.reshape(top_count, tok_rows, expert_count * capacity), axis=0).T
    return (keep_mask, slot_ids, slot_hits, dispatch)


def gate_values(logits, expert_ids, keep_mask):
    chances = jax.nn.softmax(logits, axis=-1)
    picked = jnp.take_along_axis(chances, expert_ids, axis=1).T.reshape(-1)
    return jnp.where(keep_mask, picked, 0.0)


def toeplitz(reversed_bias, top_start, row_total, key_total):
    window_len = row_total + key_total
    window = lax.dynamic_slice_in_dim(reversed_bias, top_start, window_len, 1)
    tiled = jnp.tile(window, (1, row_total))[:, : row_total * (window_len - 1)]
    return tiled.reshape(window.shape[0], row_total, window_len - 1)[:, :, row_total - 1 :]


def toeplitz_back(grad_block, row_total, key_total):
    window_len = row_total + key_total
    head_total = grad_block.shape[0]
    placed = jnp.pad(grad_block, ((0, 0), (0, 0), (row_total - 1, 0))).reshape(
        head_total, row_total * (window_len - 1)
    )
    placed = jnp.pad(placed, ((0, 0), (0, row_total)))
    return jnp.sum(placed.reshape(head_total, row_total, window_len), axis=1)


def add_window(table, piece, start):
    current = lax.dynamic_slice_in_dim(table, start, piece.shape[1], 1)
    return lax.dynamic_update_slice_in_dim(table, current + piece, start, 1)


def sweep(step_fn, start_state, prompt_items, local_items):
    state_mid, stacked = lax.scan(step_fn, start_state, prompt_items)
    state_end, last_out = step_fn(state_mid, local_items)
    return (state_end, stacked, last_out)


def local(
    tokens,
    cotangent,
    w_query,
    w_key,
    w_value,
    w_out,
    gain_attn,
    gain_ffn,
    w_router,
    rel_bias,
    exp_gate,
    exp_up,
    exp_down,
    bucket_table,
    expert_ids,
    priority,
):
    tok_rows = tokens.shape[2]
    model_width = tokens.shape[3]
    ctx_count = lax.axis_size("ctx")
    my_block = lax.axis_index("ctx")
    prompt_rows = tok_rows - LEN
    cont_rows = tok_rows - prompt_rows
    prompt_len = prompt_rows * ctx_count
    dist_count = bucket_table.shape[0]
    head_count = HEADS
    head_width = HEAD_DIM
    score_scale = HEAD_DIM ** (-0.5)
    steps_count = max(1, ctx_count // 8)
    block_keys = prompt_len // steps_count
    cols_query, cols_key, cols_value, cols_out, cols_gate, cols_up, cols_down = (
        lax.all_gather(w_query, "ctx", axis=1, tiled=True),
        lax.all_gather(w_key, "ctx", axis=1, tiled=True),
        lax.all_gather(w_value, "ctx", axis=1, tiled=True),
        lax.all_gather(w_out, "ctx", axis=1, tiled=True),
        lax.all_gather(exp_gate, "ctx", axis=2, tiled=True),
        lax.all_gather(exp_up, "ctx", axis=2, tiled=True),
        lax.all_gather(exp_down, "ctx", axis=1, tiled=True),
    )
    gathered = (
        lax.all_gather(cols_query, "wt", axis=0, tiled=True),
        lax.all_gather(cols_key, "wt", axis=0, tiled=True),
        lax.all_gather(cols_value, "wt", axis=0, tiled=True),
        lax.all_gather(cols_out, "wt", axis=0, tiled=True),
        lax.all_gather(cols_gate, "wt", axis=1, tiled=True),
        lax.all_gather(cols_up, "wt", axis=1, tiled=True),
        lax.all_gather(cols_down, "wt", axis=2, tiled=True),
        lax.all_gather(gain_attn, "wt", axis=0, tiled=True),
        lax.all_gather(gain_ffn, "wt", axis=0, tiled=True),
        lax.all_gather(w_router, "wt", axis=0, tiled=True),
        lax.all_gather(rel_bias, "wt", axis=1, tiled=True),
    )
    (
        full_query,
        full_key,
        full_value,
        full_out,
        full_gate,
        full_up,
        full_down,
        full_gain_attn,
        full_gain_ffn,
        full_router,
        full_bias,
    ) = gathered
    gain_attn_f = full_gain_attn.astype(jnp.float32)
    gain_ffn_f = full_gain_ffn.astype(jnp.float32)
    source = tokens[0, 0].astype(jnp.float32)
    normed_attn = rms_norm(source, gain_attn_f)
    normed_attn_low = normed_attn.astype(jnp.bfloat16)
    query_low = jnp.dot(normed_attn_low, full_query, preferred_element_type=jnp.float32).astype(
        jnp.bfloat16
    )
    key_low = jnp.dot(normed_attn_low, full_key, preferred_element_type=jnp.float32).astype(
        jnp.bfloat16
    )
    value_low = jnp.dot(normed_attn_low, full_value, preferred_element_type=jnp.float32).astype(
        jnp.bfloat16
    )
    far_keys, far_values = (
        lax.all_gather(key_low[:prompt_rows], "ctx", axis=0, tiled=True),
        lax.all_gather(value_low[:prompt_rows], "ctx", axis=0, tiled=True),
    )
    row_index = jnp.arange(tok_rows, dtype=jnp.int32)
    query_pos = jnp.where(
        row_index < prompt_rows,
        my_block * prompt_rows + row_index,
        prompt_len + row_index - prompt_rows,
    )
    bucket_onehot = jnp.where(
        bucket_table[:, None] == jnp.arange(BUCKETS, dtype=jnp.int32)[None, :], 1.0, 0.0
    )
    bias_rows = jnp.dot(bucket_onehot, full_bias.astype(jnp.float32), precision=precise).T
    reversed_bias = jnp.concatenate([bias_rows[:, ::-1], jnp.zeros_like(bias_rows)], axis=1)
    prompt_starts = jnp.arange(steps_count, dtype=jnp.int32) * block_keys
    local_start = jnp.asarray(prompt_len, dtype=jnp.int32)
    query_heads = query_low.reshape(tok_rows, head_count, head_width)

    def blocks_of(far_array):
        return far_array.reshape(steps_count, block_keys, model_width)

    def window_starts(key_start):
        prompt_top = dist_count - my_block * prompt_rows + key_start - prompt_rows
        cont_top = dist_count - prompt_len + key_start - cont_rows
        return (prompt_top, cont_top)

    def block_scores(key_block, key_start):
        key_total = key_block.shape[0]
        key_heads = key_block.reshape(key_total, head_count, head_width)
        logit_raw = (
            jnp.einsum("qhd,khd->hqk", query_heads, key_heads, preferred_element_type=jnp.float32)
            * score_scale
        )
        key_pos = key_start + jnp.arange(key_total, dtype=jnp.int32)
        offset = query_pos[:, None] - key_pos[None, :]
        prompt_top, cont_top = window_starts(key_start)
        bias_block = jnp.concatenate(
            [
                toeplitz(reversed_bias, prompt_top, prompt_rows, key_total),
                toeplitz(reversed_bias, cont_top, cont_rows, key_total),
            ],
            axis=1,
        )
        return jnp.where(offset[None] >= 0, logit_raw + bias_block, -1e30)

    def stats_step(state_in, block_item):
        run_max, run_sum = state_in
        scores = block_scores(block_item[0], block_item[1])
        new_max = jnp.maximum(run_max, jnp.max(scores, axis=-1))
        new_sum = run_sum * jnp.exp(run_max - new_max) + jnp.sum(
            jnp.exp(scores - new_max[..., None]), axis=-1
        )
        return ((new_max, new_sum), None)

    start_stats = (
        jnp.full((head_count, tok_rows), -1e30, jnp.float32),
        jnp.zeros((head_count, tok_rows), jnp.float32),
    )
    (row_max, row_sum), unused_a, unused_b = sweep(
        stats_step,
        start_stats,
        (blocks_of(far_keys), prompt_starts),
        (key_low[prompt_rows:], local_start),
    )

    def mix_step(state_in, block_item):
        scores = block_scores(block_item[0], block_item[2])
        weights = (jnp.exp(scores - row_max[..., None]) / row_sum[..., None]).astype(jnp.bfloat16)
        value_heads = block_item[1].reshape(-1, head_count, head_width)
        return (
            state_in
            + jnp.einsum("hqk,khd->qhd", weights, value_heads, preferred_element_type=jnp.float32),
            None,
        )

    mixed_exact, unused_c, unused_d = sweep(
        mix_step,
        jnp.zeros((tok_rows, head_count, head_width), jnp.float32),
        (blocks_of(far_keys), blocks_of(far_values), prompt_starts),
        (key_low[prompt_rows:], value_low[prompt_rows:], local_start),
    )
    mixed_low = mixed_exact.reshape(tok_rows, model_width).astype(jnp.bfloat16)
    hidden = source + jnp.dot(mixed_low, full_out, preferred_element_type=jnp.float32)
    normed_ffn_low = rms_norm(hidden, gain_ffn_f).astype(jnp.bfloat16)
    route_ids = expert_ids[0, 0]
    keep_mask, slot_ids, slot_hits, dispatch = routing(route_ids, priority[0, 0], CAP, EXPERTS)
    inputs = (
        jnp.dot(dispatch.astype(jnp.bfloat16), normed_ffn_low, preferred_element_type=jnp.float32)
        .astype(jnp.bfloat16)
        .reshape(EXPERTS, CAP, model_width)
    )
    gate_pre = jnp.einsum("ecd,edf->ecf", inputs, full_gate, preferred_element_type=jnp.float32)
    up_pre = jnp.einsum("ecd,edf->ecf", inputs, full_up, preferred_element_type=jnp.float32)
    inner_low = gelu_product(gate_pre, up_pre).astype(jnp.bfloat16)
    expert_out = jnp.einsum(
        "ecf,efd->ecd", inner_low, full_down, preferred_element_type=jnp.float32
    ).reshape(EXPERTS * CAP, model_width)
    logits = jnp.dot(normed_ffn_low, full_router, preferred_element_type=jnp.float32)
    weight_pair = gate_values(logits, route_ids, keep_mask)
    picked_rows = jnp.take(expert_out, slot_ids, axis=0)
    combined = jnp.sum(
        (picked_rows * weight_pair[:, None]).reshape(TOP, tok_rows, model_width), axis=0
    )
    output = (hidden + combined).astype(jnp.bfloat16).reshape(1, 1, tok_rows, model_width)
    back_keys, back_values = (far_keys, far_values)
    (
        back_query,
        back_key,
        back_value,
        back_out,
        back_gate,
        back_up,
        back_down,
        back_gain_attn,
        back_gain_ffn,
        back_router,
        back_bias,
    ) = gathered
    grad_final = cotangent[0, 0].astype(jnp.float32)
    grad_pair = jnp.where(
        keep_mask, jnp.sum(jnp.tile(grad_final, (TOP, 1)) * picked_rows, axis=-1), 0.0
    )
    slot_weight = jnp.dot(weight_pair, slot_hits, precision=precise)
    grad_expert_out = (
        (jnp.dot(dispatch, grad_final, precision=precise) * slot_weight[:, None])
        .astype(jnp.bfloat16)
        .reshape(EXPERTS, CAP, model_width)
    )
    grad_inner = jnp.einsum(
        "ecd,efd->ecf", grad_expert_out, back_down, preferred_element_type=jnp.float32
    )
    unused_e, inner_pull = jax.vjp(gelu_product, gate_pre, up_pre)
    grad_gate_pre, grad_up_pre = inner_pull(grad_inner)
    grad_gate_low = grad_gate_pre.astype(jnp.bfloat16)
    grad_up_low = grad_up_pre.astype(jnp.bfloat16)
    grad_gate_w = jnp.einsum(
        "ecd,ecf->edf", inputs, grad_gate_low, preferred_element_type=jnp.float32
    )
    grad_up_w = jnp.einsum("ecd,ecf->edf", inputs, grad_up_low, preferred_element_type=jnp.float32)
    grad_down_w = jnp.einsum(
        "ecf,ecd->efd", inner_low, grad_expert_out, preferred_element_type=jnp.float32
    )
    grad_inputs = jnp.einsum(
        "ecf,edf->ecd", grad_gate_low, back_gate, preferred_element_type=jnp.float32
    ) + jnp.einsum("ecf,edf->ecd", grad_up_low, back_up, preferred_element_type=jnp.float32)

    def gate_of_logits(logit_values):
        return gate_values(logit_values, route_ids, keep_mask)

    unused_f, gate_pull = jax.vjp(gate_of_logits, logits)
    (grad_logits,) = gate_pull(grad_pair)
    grad_router_w = jnp.dot(normed_ffn_low.astype(jnp.float32).T, grad_logits, precision=precise)
    grad_normed_ffn = jnp.dot(grad_logits, back_router.astype(jnp.float32).T, precision=precise)
    grad_normed_ffn = grad_normed_ffn + jnp.dot(
        dispatch.T, grad_inputs.reshape(EXPERTS * CAP, model_width), precision=precise
    )
    unused_g, ffn_norm_pull = jax.vjp(rms_norm, hidden, back_gain_ffn.astype(jnp.float32))
    grad_hidden_part, grad_gain_ffn_w = ffn_norm_pull(grad_normed_ffn)
    grad_hidden = grad_final + grad_hidden_part
    grad_hidden_low = grad_hidden.astype(jnp.bfloat16)
    grad_out_w = jnp.dot(mixed_low.T, grad_hidden_low, preferred_element_type=jnp.float32)
    grad_mixed = jnp.dot(grad_hidden_low, back_out.T, preferred_element_type=jnp.float32).astype(
        jnp.bfloat16
    )
    grad_mixed_heads = grad_mixed.reshape(tok_rows, head_count, head_width)
    row_delta = jnp.sum(grad_mixed_heads.astype(jnp.float32) * mixed_exact, axis=-1).T

    def grad_step(state_in, block_item):
        grad_query_acc, grad_reversed = state_in
        key_block, value_block, key_start = block_item
        key_total = key_block.shape[0]
        scores = block_scores(key_block, key_start)
        chances = jnp.exp(scores - row_max[..., None]) / row_sum[..., None]
        value_heads = value_block.reshape(-1, head_count, head_width)
        key_heads = key_block.reshape(-1, head_count, head_width)
        grad_chance = jnp.einsum(
            "qhd,khd->hqk", grad_mixed_heads, value_heads, preferred_element_type=jnp.float32
        )
        grad_value_block = jnp.einsum(
            "hqk,qhd->khd",
            chances.astype(jnp.bfloat16),
            grad_mixed_heads,
            preferred_element_type=jnp.float32,
        )
        grad_scores = chances * (grad_chance - row_delta[..., None])
        prompt_top, cont_top = window_starts(key_start)
        grad_reversed = add_window(
            grad_reversed,
            toeplitz_back(grad_scores[:, :prompt_rows], prompt_rows, key_total),
            prompt_top,
        )
        grad_reversed = add_window(
            grad_reversed,
            toeplitz_back(grad_scores[:, prompt_rows:], cont_rows, key_total),
            cont_top,
        )
        grad_scores_low = grad_scores.astype(jnp.bfloat16)
        grad_query_acc = grad_query_acc + score_scale * jnp.einsum(
            "hqk,khd->qhd", grad_scores_low, key_heads, preferred_element_type=jnp.float32
        )
        grad_key_block = score_scale * jnp.einsum(
            "hqk,qhd->khd", grad_scores_low, query_heads, preferred_element_type=jnp.float32
        )
        return (
            (grad_query_acc, grad_reversed),
            (grad_key_block.reshape(-1, model_width), grad_value_block.reshape(-1, model_width)),
        )

    start_grads = (
        jnp.zeros((tok_rows, head_count, head_width), jnp.float32),
        jnp.zeros((head_count, 2 * dist_count), jnp.float32),
    )
    (
        (grad_query_exact, grad_reversed),
        (far_grad_keys, far_grad_values),
        (near_grad_keys, near_grad_values),
    ) = sweep(
        grad_step,
        start_grads,
        (blocks_of(back_keys), blocks_of(back_values), prompt_starts),
        (key_low[prompt_rows:], value_low[prompt_rows:], local_start),
    )
    own_grad_keys, own_grad_values = (
        lax.psum_scatter(
            far_grad_keys.reshape(prompt_len, model_width), "ctx", scatter_dimension=0, tiled=True
        ),
        lax.psum_scatter(
            far_grad_values.reshape(prompt_len, model_width), "ctx", scatter_dimension=0, tiled=True
        ),
    )
    grad_key_low = jnp.concatenate([own_grad_keys, near_grad_keys], axis=0).astype(jnp.bfloat16)
    grad_value_low = jnp.concatenate([own_grad_values, near_grad_values], axis=0).astype(
        jnp.bfloat16
    )
    grad_query_low = grad_query_exact.reshape(tok_rows, model_width).astype(jnp.bfloat16)
    grad_query_w = jnp.dot(normed_attn_low.T, grad_query_low, preferred_element_type=jnp.float32)
    grad_key_w = jnp.dot(normed_attn_low.T, grad_key_low, preferred_element_type=jnp.float32)
    grad_value_w = jnp.dot(normed_attn_low.T, grad_value_low, preferred_element_type=jnp.float32)
    grad_normed_attn = jnp.dot(grad_query_low, back_query.T, preferred_element_type=jnp.float32)
    grad_normed_attn = grad_normed_attn + jnp.dot(
        grad_key_low, back_key.T, preferred_element_type=jnp.float32
    )
    grad_normed_attn = grad_normed_attn + jnp.dot(
        grad_value_low, back_value.T, preferred_element_type=jnp.float32
    )
    unused_h, attn_norm_pull = jax.vjp(rms_norm, source, back_gain_attn.astype(jnp.float32))
    grad_source_part, grad_gain_attn_w = attn_norm_pull(grad_normed_attn)
    grad_tokens = (
        (grad_hidden + grad_source_part).astype(jnp.bfloat16).reshape(1, 1, tok_rows, model_width)
    )
    grad_bias_rows = grad_reversed[:, :dist_count][:, ::-1]
    grad_bias_w = jnp.dot(bucket_onehot.T, grad_bias_rows.T, precision=precise)
    small_gain_attn, small_gain_ffn, small_router, small_bias = lax.psum(
        (grad_gain_attn_w, grad_gain_ffn_w, grad_router_w, grad_bias_w), "ctx"
    )
    row_parts = (
        lax.psum_scatter(
            grad_query_w.astype(jnp.bfloat16), "wt", scatter_dimension=0, tiled=True
        ).astype(jnp.float32),
        lax.psum_scatter(
            grad_key_w.astype(jnp.bfloat16), "wt", scatter_dimension=0, tiled=True
        ).astype(jnp.float32),
        lax.psum_scatter(
            grad_value_w.astype(jnp.bfloat16), "wt", scatter_dimension=0, tiled=True
        ).astype(jnp.float32),
        lax.psum_scatter(
            grad_out_w.astype(jnp.bfloat16), "wt", scatter_dimension=0, tiled=True
        ).astype(jnp.float32),
        lax.psum_scatter(
            grad_gate_w.astype(jnp.bfloat16), "wt", scatter_dimension=1, tiled=True
        ).astype(jnp.float32),
        lax.psum_scatter(
            grad_up_w.astype(jnp.bfloat16), "wt", scatter_dimension=1, tiled=True
        ).astype(jnp.float32),
        lax.psum_scatter(
            grad_down_w.astype(jnp.bfloat16), "wt", scatter_dimension=2, tiled=True
        ).astype(jnp.float32),
        lax.psum_scatter(
            small_gain_attn.astype(jnp.bfloat16), "wt", scatter_dimension=0, tiled=True
        ).astype(jnp.float32),
        lax.psum_scatter(
            small_gain_ffn.astype(jnp.bfloat16), "wt", scatter_dimension=0, tiled=True
        ).astype(jnp.float32),
        lax.psum_scatter(
            small_router.astype(jnp.bfloat16), "wt", scatter_dimension=0, tiled=True
        ).astype(jnp.float32),
        lax.psum_scatter(
            small_bias.astype(jnp.bfloat16), "wt", scatter_dimension=1, tiled=True
        ).astype(jnp.float32),
    )
    res_query, res_key, res_value, res_out, res_gate, res_up, res_down = (
        lax.psum_scatter(row_parts[0], "ctx", scatter_dimension=1, tiled=True),
        lax.psum_scatter(row_parts[1], "ctx", scatter_dimension=1, tiled=True),
        lax.psum_scatter(row_parts[2], "ctx", scatter_dimension=1, tiled=True),
        lax.psum_scatter(row_parts[3], "ctx", scatter_dimension=1, tiled=True),
        lax.psum_scatter(row_parts[4], "ctx", scatter_dimension=2, tiled=True),
        lax.psum_scatter(row_parts[5], "ctx", scatter_dimension=2, tiled=True),
        lax.psum_scatter(row_parts[6], "ctx", scatter_dimension=1, tiled=True),
    )
    res_gain_attn, res_gain_ffn, res_router, res_bias = (
        row_parts[7],
        row_parts[8],
        row_parts[9],
        row_parts[10],
    )
    return (
        output,
        grad_tokens,
        res_query,
        res_key,
        res_value,
        res_out,
        res_gain_attn,
        res_gain_ffn,
        res_router,
        res_bias,
        res_gate,
        res_up,
        res_down,
    )


BF = jnp.bfloat16
F32 = jnp.float32
FAST_CTX = 8
FAST_WT = 4
NEG = -1e30

SWAP_Y = [(i, i ^ 1) for i in range(8)]
UP_Z = [(i, i + 2) for i in range(6)]
DOWN_Z = [(i, i - 2) for i in range(2, 8)]
SWAP_C = [(i, i ^ 1) for i in range(4)]
SWAP_X = [(i, i ^ 2) for i in range(4)]


def move_y(v):
    return lax.ppermute(v, "ctx", SWAP_Y)


def move_x(v):
    return lax.ppermute(v, "wt", SWAP_X)


def move_c(v):
    return lax.ppermute(v, "wt", SWAP_C)


def up_z(v):
    return lax.ppermute(v, "ctx", UP_Z)


def down_z(v):
    return lax.ppermute(v, "ctx", DOWN_Z)


def shift_z(v, s):
    return lax.ppermute(v, "ctx", [(i, (i + 2 * s) % 8) for i in range(8)])


def after(v, *deps):
    return lax.optimization_barrier((v,) + deps)[0]


def dot_nt(a, b):
    return lax.dot_general(a, b, (((1,), (1,)), ((), ())), preferred_element_type=F32)


def dot_tn(a, b):
    return lax.dot_general(a, b, (((0,), (0,)), ((), ())), preferred_element_type=F32)


def dot_nn(a, b):
    return jnp.dot(a, b, preferred_element_type=F32)


def params(limit=56 * 2**20):
    return pltpu.CompilerParams(vmem_limit_bytes=limit)


ANY = pl.BlockSpec(memory_space=pl.ANY)
SMEM = pl.BlockSpec(memory_space=pltpu.SMEM)


def spread_all(unit):
    pieces = []
    for s in range(4):
        v = unit if s == 0 else shift_z(unit, s)
        if s % 2 == 0:
            a = move_y(v)
            quad = {(0, 0): v, (1, 0): a, (0, 1): move_x(v), (1, 1): move_x(a)}
        else:
            b = move_x(v)
            quad = {(0, 0): v, (0, 1): b, (1, 0): move_y(v), (1, 1): move_y(b)}
        for ry in range(2):
            for rx in range(2):
                piece = quad[(ry, rx)]
                pieces.append(((s, ry, rx, 0), piece))
                pieces.append(((s, ry, rx, 1), move_c(piece)))
    return pieces


def place_kernel(keys, idx, *refs):
    count = len(keys)
    ins, wkv, wq, wo, sem = refs[:count], refs[count], refs[count + 1], refs[count + 2], refs[count + 3]
    z, y, x, c = idx[0], idx[1], idx[2], idx[3]
    copies = []
    for n, (s, ry, rx, rc) in enumerate(keys):
        row = pl.multiple_of(((x ^ rx) * 2 + (c ^ rc)) * 256, 256)
        col = pl.multiple_of((lax.rem(z + 4 - s, 4) * 2 + (y ^ ry)) * 128, 128)
        rows, cols = pl.ds(row, 256), pl.ds(col, 128)
        copies.append(pltpu.make_async_copy(ins[n].at[0], wq.at[rows, cols], sem.at[n, 0]))
        copies.append(pltpu.make_async_copy(ins[n].at[pl.ds(1, 2)], wkv.at[:, rows, cols], sem.at[n, 1]))
        copies.append(pltpu.make_async_copy(ins[n].at[3], wo.at[rows, cols], sem.at[n, 2]))
    for copy in copies:
        copy.start()
    for copy in copies:
        copy.wait()


def place_weights(idx, pieces):
    keys = [k for k, _ in pieces]
    return pl.pallas_call(
        functools.partial(place_kernel, keys),
        out_shape=(
            jax.ShapeDtypeStruct((2, 1024, 1024), BF),
            jax.ShapeDtypeStruct((1024, 1024), BF),
            jax.ShapeDtypeStruct((1024, 1024), BF),
        ),
        in_specs=[SMEM] + [ANY] * len(keys),
        out_specs=(ANY, ANY, ANY),
        scratch_shapes=[pltpu.SemaphoreType.DMA((len(keys), 3))],
        compiler_params=params(),
    )(idx, *[v for _, v in pieces])


def attend_kernel(w_ref, q_ref, k_ref, v_ref, p_ref, o_ref, bc_ref, bp_ref):
    q, k, v = q_ref[...], k_ref[...], v_ref[...]
    lane = lax.broadcasted_iota(jnp.int32, (1, 128), 1)
    outs = []
    for h in range(2):
        base_c, base_p = w_ref[h, 0], w_ref[h, 1]
        for a in range(32):
            bc_ref[8 * a : 8 * a + 8, :] = pltpu.roll(base_c, 1024 - (248 - 8 * a), 1)[:, :768]
        for a in range(8):
            shift = 56 - 8 * a
            bp_ref[8 * a : 8 * a + 8, :] = (pltpu.roll(base_p, 1024 - shift, 1) if shift else base_p)[:, :512]
        mine = (lane < 64) if h == 0 else (lane >= 64)
        qh = jnp.where(mine, q, jnp.zeros_like(q))
        sc = dot_nt(qh[64:], k) * 0.125 + bc_ref[...]
        sp = dot_nt(qh[:64], k[:512]) * 0.125 + bp_ref[...]

        def soft(s):
            e = jnp.exp(s - jnp.max(s, axis=-1, keepdims=True))
            return (e / jnp.sum(e, axis=-1, keepdims=True)).astype(BF)

        pc, pp = soft(sc), soft(sp)
        p_ref[h, 64:, :] = pc
        p_ref[h, :64, :512] = pp
        p_ref[h, :64, 512:] = jnp.zeros((64, 256), BF)
        outs.append(jnp.concatenate([dot_nn(pp, v[:512]), dot_nn(pc, v)], axis=0))
    o_ref[...] = jnp.where(lane < 64, outs[0], outs[1]).astype(BF)


def attend(bias_rows, q, k, v):
    rows, keys = q.shape[0], k.shape[0]
    return pl.pallas_call(
        attend_kernel,
        grid=(8,),
        out_shape=(
            jax.ShapeDtypeStruct((16, rows, keys), BF),
            jax.ShapeDtypeStruct((rows, 1024), BF),
        ),
        in_specs=[
            pl.BlockSpec((2, 2, 8, 1024), lambda j: (j, 0, 0, 0)),
            pl.BlockSpec((rows, 128), lambda j: (0, j)),
            pl.BlockSpec((keys, 128), lambda j: (0, j)),
            pl.BlockSpec((keys, 128), lambda j: (0, j)),
        ],
        out_specs=(
            pl.BlockSpec((2, rows, keys), lambda j: (j, 0, 0)),
            pl.BlockSpec((rows, 128), lambda j: (0, j)),
        ),
        scratch_shapes=[pltpu.VMEM((256, 768), F32), pltpu.VMEM((64, 512), F32)],
        compiler_params=params(),
        cost_estimate=pl.CostEstimate(flops=8 * 320 * 768 * 512, bytes_accessed=14 * 2**20, transcendentals=2**22),
    )(bias_rows, q, k, v)


def attend_back_kernel(p_ref, q_ref, k_ref, v_ref, g_ref, dq_ref, dk_ref, dv_ref, db_ref):
    q, k, v, g = q_ref[...], k_ref[...], v_ref[...], g_ref[...]
    lane = lax.broadcasted_iota(jnp.int32, (1, 128), 1)
    parts = []
    for h in range(2):
        mine = (lane < 64) if h == 0 else (lane >= 64)
        gh = jnp.where(mine, g, jnp.zeros_like(g))
        p = p_ref[h]
        pf = p.astype(F32)
        dp = dot_nt(gh, v)
        delta = jnp.sum(pf * dp, axis=-1, keepdims=True)
        ds = pf * (dp - delta)
        low = ds.astype(BF)
        acc_c = jnp.zeros((8, 1024), F32)
        for a in range(32):
            part = jnp.concatenate([ds[64 + 8 * a : 72 + 8 * a], jnp.zeros((8, 256), F32)], axis=1)
            acc_c = acc_c + pltpu.roll(part, 248 - 8 * a, 1) if a < 31 else acc_c + part
        acc_p = jnp.zeros((8, 1024), F32)
        for a in range(8):
            part = jnp.concatenate([ds[8 * a : 8 * a + 8, :512], jnp.zeros((8, 512), F32)], axis=1)
            acc_p = acc_p + (pltpu.roll(part, 56 - 8 * a, 1) if a < 7 else part)
        db_ref[h, 0] = acc_c
        db_ref[h, 1] = acc_p
        parts.append((dot_nn(low, k) * 0.125, dot_tn(low, q) * 0.125, dot_tn(p, g)))
    for n, ref in enumerate((dq_ref, dk_ref, dv_ref)):
        ref[...] = jnp.where(lane < 64, parts[0][n], parts[1][n]).astype(BF)


def attend_back(p, q, k, v, g):
    rows, keys = q.shape[0], k.shape[0]
    head = lambda n: pl.BlockSpec((n, 128), lambda j: (0, j))
    return pl.pallas_call(
        attend_back_kernel,
        grid=(8,),
        out_shape=(
            jax.ShapeDtypeStruct((rows, 1024), BF),
            jax.ShapeDtypeStruct((keys, 1024), BF),
            jax.ShapeDtypeStruct((keys, 1024), BF),
            jax.ShapeDtypeStruct((16, 2, 8, 1024), F32),
        ),
        in_specs=[
            pl.BlockSpec((2, rows, keys), lambda j: (j, 0, 0)),
            head(rows),
            head(keys),
            head(keys),
            head(rows),
        ],
        out_specs=(
            head(rows),
            head(keys),
            head(keys),
            pl.BlockSpec((2, 2, 8, 1024), lambda j: (j, 0, 0, 0)),
        ),
        compiler_params=params(),
        cost_estimate=pl.CostEstimate(flops=20 * 320 * 768 * 512, bytes_accessed=14 * 2**20, transcendentals=0),
    )(p, q, k, v, g)


def bias_windows(bias_rows, ctx_index):
    rev = jnp.concatenate([bias_rows[:, ::-1], jnp.full((16, 1152), NEG, F32)], axis=1)
    cont = jnp.stack([rev[:, 7 - s : 7 - s + 1024] for s in range(8)], axis=1)
    tail = lax.dynamic_slice_in_dim(rev, 704 - 64 * ctx_index, 1040, 1)
    prompt = jnp.stack([tail[:, 7 - s : 7 - s + 1024] for s in range(8)], axis=1)
    return jnp.stack([cont, prompt], axis=1)


def bias_windows_back(grad, ctx_index):
    def gather(part):
        total = jnp.zeros((16, 1040), F32)
        for s in range(8):
            total = total + jnp.pad(part[:, s], ((0, 0), (7 - s, 9 + s)))
        return total

    wide = jnp.pad(gather(grad[:, 0]), ((0, 0), (0, 880)))
    prompt = gather(grad[:, 1])
    start = 704 - 64 * ctx_index
    moved = lax.dynamic_update_slice_in_dim(jnp.zeros((16, 1920), F32), prompt, start, 1)
    return (wide + moved)[:, :768][:, ::-1]


ORDER = [(half, rc, ry, rx) for half in range(2) for rc in range(2) for ry in range(2) for rx in range(2)]


def spread_plane(v):
    half = v.shape[0] // 2
    a, b = v[:half], v[half:]
    ay, bx = move_y(a), move_x(b)
    ax, by = move_x(a), move_y(b)
    ayx, bxy = move_x(ay), move_y(bx)
    near = {(0, 0, 0): a, (0, 1, 0): ay, (0, 0, 1): ax, (0, 1, 1): ayx, (1, 0, 0): b, (1, 0, 1): bx, (1, 1, 0): by, (1, 1, 1): bxy}
    return [near[(h, ry, rx)] if rc == 0 else move_c(near[(h, ry, rx)]) for h, rc, ry, rx in ORDER]


def add_low(a, b):
    return (a.astype(F32) + b.astype(F32)).astype(BF)


def collect_plane(v):
    rows = v.shape[0] // 16
    w = v.reshape(2, 2, 4, rows, v.shape[1])
    sums = []
    for h in range(2):
        sums.append(add_low(w[h, 0], move_c(w[h, 1])))
    a, b = sums
    sy = add_low(a[2], move_x(a[3]))
    sx = add_low(b[1], move_y(b[3]))
    ax, by = move_x(a[1]), move_y(b[2])
    ay, bx = move_y(sy), move_x(sx)
    f = lambda t: t.astype(F32)
    return jnp.concatenate([f(a[0]) + f(ax) + f(ay), f(b[0]) + f(by) + f(bx)], axis=0)


def expert_kernel(expert, first, last, *refs):
    refs = list(refs)
    idx, x_ref, g_ref, m_ref = refs[:4]
    srcs = refs[4:11]
    at = 11
    if not first:
        out_prev, dx_prev = refs[at : at + 2]
        at += 2
    if last:
        s0_ref, s1_ref = refs[at : at + 2]
        at += 2
    out_ref, dx_ref, dh_ref, win_ref, s_ref, w_scr, sem = refs[at:]
    z = idx[0]

    @pl.when(pl.program_id(0) == 0)
    def _():
        def copy(n, slot):
            rows = pl.ds(pl.multiple_of(slot * 96, 96), 96)
            return pltpu.make_async_copy(srcs[n], w_scr.at[:, rows, :], sem.at[n])

        plan = [(0, z, None)]
        for s in range(1, 4):
            plan.append((s, z + s, z + s <= 3))
            plan.append((3 + s, z - s, z - s >= 0))
        for act in ("start", "wait"):
            for n, slot, ok in plan:
                if ok is None:
                    getattr(copy(n, slot), act)()
                else:

                    @pl.when(ok)
                    def _(n=n, slot=slot, act=act):
                        getattr(copy(n, slot), act)()

    x, g = x_ref[...], g_ref[...]
    w_gu = w_scr[0:2].reshape(768, 1024)
    w_d = w_scr[2]
    gu = dot_nt(x, w_gu)
    gi = dot_nt(g, w_d)
    gate, up = gu[:, :384], gu[:, 384:]
    l = [gate[:, 88 + n : 89 + n] for n in range(3)]
    top = jnp.maximum(jnp.maximum(l[0], l[1]), l[2])
    ex = [jnp.exp(v - top) for v in l]
    inv = 1.0 / (ex[0] + ex[1] + ex[2])
    p = [v * inv for v in ex]
    m = m_ref[...]
    keep = m[:, expert : expert + 1]
    w = p[expert] * keep
    sq = gate * gate
    th = jnp.tanh(0.7978845608028654 * gate * (1.0 + 0.044715 * sq))
    half1 = 0.5 + 0.5 * th
    act = gate * half1
    dact = half1 + (0.5 * gate) * (1.0 - th * th) * (0.7978845608028654 + 0.10703222440890037 * sq)
    inner = (act * up).astype(BF).astype(F32)
    s = jnp.sum(inner * gi, axis=-1, keepdims=True) * keep
    gin = gi * w
    dg = gin * up * dact
    du = gin * act
    if last:
        ss = [s0_ref[...][:, 0:1], s1_ref[...][:, 0:1], s]
        dot = p[0] * ss[0] + p[1] * ss[1] + p[2] * ss[2]
        lane = lax.broadcasted_iota(jnp.int32, (1, 384), 1)
        for n in range(3):
            dg = jnp.where(lane == 88 + n, p[n] * (ss[n] - dot), dg)
    win = (inner * w).astype(BF)
    dh = jnp.concatenate([dg.astype(BF), du.astype(BF)], axis=1)
    dh_ref[...] = dh
    win_ref[...] = win
    s_ref[...] = jnp.broadcast_to(s, s_ref.shape)
    out = dot_nn(win, w_d)
    dx = dot_nn(dh, w_gu)
    if not first:
        out = out + out_prev[...].astype(F32)
        dx = dx + dx_prev[...].astype(F32)
    out_ref[...] = out.astype(BF)
    dx_ref[...] = dx.astype(BF)


def expert_call(expert, idx, x, g, m, srcs, prev, s_prev, tile=512):
    total = x.shape[0]
    first, last = expert == 0, expert == 2
    row = lambda n: pl.BlockSpec((tile, n), lambda i: (i, 0))
    ins = [idx, x, g, m, *srcs]
    specs = [SMEM, row(1024), row(1024), row(8)] + [ANY] * 7
    if not first:
        ins += list(prev)
        specs += [row(1024), row(1024)]
    if last:
        ins += list(s_prev)
        specs += [row(8), row(8)]
    return pl.pallas_call(
        functools.partial(expert_kernel, expert, first, last),
        grid=(total // tile,),
        out_shape=(
            jax.ShapeDtypeStruct((total, 1024), BF),
            jax.ShapeDtypeStruct((total, 1024), BF),
            jax.ShapeDtypeStruct((total, 768), BF),
            jax.ShapeDtypeStruct((total, 384), BF),
            jax.ShapeDtypeStruct((total, 8), F32),
        ),
        in_specs=specs,
        out_specs=(row(1024), row(1024), row(768), row(384), row(8)),
        scratch_shapes=[pltpu.VMEM((3, 384, 1024), BF), pltpu.SemaphoreType.DMA((7,))],
        compiler_params=params(),
        cost_estimate=pl.CostEstimate(
            flops=2 * total * 1024 * 384 * 6, bytes_accessed=total * 1024 * 16, transcendentals=total * 384
        ),
    )(*ins)


def line_spread(v):
    a1, b1 = down_z(v), up_z(v)
    a2, b2 = down_z(a1), up_z(b1)
    a3, b3 = down_z(a2), up_z(b2)
    return [v, a1, a2, a3, b1, b2, b3]


def line_collect(part_of, z):
    at = lambda n: part_of(jnp.clip(z + n, 0, 3))
    d = down_z(at(-3))
    u = up_z(at(3))
    d = down_z(add_low(at(-2), d))
    u = up_z(add_low(at(2), u))
    d = down_z(add_low(at(-1), d))
    u = up_z(add_low(at(1), u))
    return (at(0).astype(F32) + d.astype(F32) + u.astype(F32)).astype(BF)


def trade_wt(v, wt_index):
    at = lambda r: lax.dynamic_index_in_dim(v, wt_index ^ r, 0, keepdims=False)
    got = [at(0), move_c(at(1)), move_x(at(2)), lax.ppermute(at(3), "wt", [(i, i ^ 3) for i in range(4)])]
    return jnp.take(jnp.stack(got), jnp.arange(4, dtype=jnp.int32) ^ wt_index, axis=0)


def sum_all(v):
    v = v + move_c(v)
    v = v + move_x(v)
    v = v + move_y(v)
    v = v + lax.ppermute(v, "ctx", [(i, i ^ 2) for i in range(8)])
    return v + lax.ppermute(v, "ctx", [(i, i ^ 4) for i in range(8)])


def norm_parts(values):
    return values * lax.rsqrt(jnp.mean(values * values, axis=-1, keepdims=True) + epsilon)


def local_fast(
    tokens, cotangent, w_query, w_key, w_value, w_out, gain_attn, gain_ffn, w_router, rel_bias,
    exp_gate, exp_up, exp_down, bucket_table, expert_ids, priority,
):
    ctx_index = lax.axis_index("ctx").astype(jnp.int32)
    wt_index = lax.axis_index("wt").astype(jnp.int32)
    z, y, x, c = ctx_index // 2, ctx_index % 2, wt_index // 2, wt_index % 2
    idx = jnp.stack([z, y, x, c])
    rows_own = tokens[0, 0]

    packed = jnp.concatenate(
        [gain_attn[None], gain_ffn[None], w_router.T, jnp.pad(rel_bias.reshape(1, 128), ((0, 0), (0, 128))),
         jnp.zeros((2, 256), BF)], axis=0
    )
    small = lax.all_gather(packed, "wt", axis=0, tiled=False)
    gain_attn_f = small[:, 0].reshape(1024).astype(F32)
    gain_ffn_f = small[:, 1].reshape(1024).astype(F32)
    bias_f = small[:, 5, :128].reshape(4, 32, 4).transpose(1, 0, 2).reshape(32, 16).astype(F32)

    unit = jnp.stack([w_query, w_key, w_value, w_out])
    w_kv, w_q, w_o = place_weights(idx, spread_all(unit))

    prompt_own = rows_own[:64]
    group = [prompt_own] + [shift_z(prompt_own, s) for s in (3, 2, 1)]
    stack = jnp.stack([jnp.stack([v, move_y(v)]) for v in group])
    stack = lax.dynamic_slice_in_dim(jnp.concatenate([stack, stack], axis=0), (4 - z) % 4, 4, 0)
    stack = lax.dynamic_slice_in_dim(jnp.concatenate([stack, stack[:, :1]], axis=1), y, 2, 1)
    prompts = stack.reshape(512, 1024)

    ids, rank = expert_ids[0, 0], priority[0, 0]
    expert = ids.T.reshape(-1)
    rank_key = (jnp.arange(TOP, dtype=jnp.int32)[:, None] * 320 + rank[None, :]).reshape(-1)
    earlier = (expert[:, None] == expert[None, :]) & (rank_key[None, :] < rank_key[:, None])
    keep = (jnp.sum(earlier.astype(jnp.int32), axis=1) < CAP).reshape(TOP, 320)
    hold = jnp.sum(
        jnp.where((ids.T[:, :, None] == jnp.arange(EXPERTS, dtype=jnp.int32)) & keep[:, :, None], 1.0, 0.0), axis=0
    )
    marks = jnp.pad(hold.reshape(2, 1, 480), ((0, 0), (0, 15), (0, 544))).astype(BF)
    cot = cotangent[0, 0]
    cot_marked = jnp.concatenate([cot[:160], marks[0], cot[160:], marks[1]], axis=0)

    def pieces(v):
        return jnp.pad(v.reshape(3, 4, 88, 256), ((0, 0), (0, 0), (0, 8), (0, 0)))

    gate_t, up_t = exp_gate.transpose(0, 2, 1), exp_up.transpose(0, 2, 1)
    gate_p = pieces(gate_t)
    router_rows = jnp.broadcast_to(
        jnp.pad(w_router.T, ((0, 5), (0, 0)))[None, None], (3, 4, 8, 256)
    )
    gate_p = jnp.concatenate([gate_p[:, :, :88], router_rows], axis=2)
    share = jnp.stack([gate_p, pieces(up_t), pieces(exp_down)], axis=1).transpose(2, 0, 1, 3, 4)
    share = trade_wt(share, wt_index).transpose(1, 2, 3, 0, 4).reshape(3, 3, 96, 1024)
    spread = [line_spread(share[e]) for e in range(3)]

    source = rows_own.astype(F32)
    own_low = (norm_parts(source) * gain_attn_f).astype(BF)
    source_all = jnp.concatenate([prompts.astype(F32), source[64:]], axis=0)
    unit_all = norm_parts(source_all)
    all_low = (unit_all * gain_attn_f).astype(BF)
    q = dot_nn(own_low, w_q).astype(BF)
    k = dot_nn(all_low, w_kv[0]).astype(BF)
    v = dot_nn(all_low, w_kv[1]).astype(BF)
    onehot = jnp.where(bucket_table[:, None] == jnp.arange(BUCKETS, dtype=jnp.int32)[None, :], 1.0, 0.0)
    bias_by_dist = lax.dot_general(bias_f, onehot, (((0,), (1,)), ((), ())), precision=precise)
    windows = bias_windows(bias_by_dist, ctx_index)
    probs, mixed = attend(windows, q, k, v)
    hidden = source + dot_nn(mixed, w_o)
    normed = (norm_parts(hidden) * gain_ffn_f).astype(BF)

    cot_parts = spread_plane(after(cot_marked, w_q))
    marks_all = jnp.stack([v[160] for v in cot_parts])[:, :480].reshape(2560, 3).astype(F32)
    marks_all = jnp.pad(marks_all, ((0, 0), (0, 5)))
    g_all = jnp.concatenate([v[:160] for v in cot_parts], axis=0)
    x_all = jnp.concatenate(spread_plane(normed), axis=0)
    prev, scores, dh, win = None, [], [], []
    for e in range(3):
        out, dx, dh_e, win_e, s_e = expert_call(e, idx, x_all, g_all, marks_all, spread[e], prev, scores)
        prev = (out, dx)
        scores.append(s_e)
        dh.append(dh_e)
        win.append(win_e)
    out, dx = prev

    grad_normed_ffn = collect_plane(dx)
    bulk = []
    for e in range(3):
        gw = dot_tn(dh[e], x_all).astype(BF).reshape(2, 4, 96, 1024)
        dw = dot_tn(win[e], g_all).astype(BF).reshape(1, 4, 96, 1024)
        both = jnp.concatenate([gw, dw], axis=0)
        if e == 2:
            router_part = both[0, 0, 88:91].astype(F32)
        bulk.append(line_collect(lambda n: lax.dynamic_index_in_dim(both, n, 1, keepdims=False), z))
    combined = collect_plane(after(out, grad_normed_ffn))
    output = (hidden + combined).astype(BF).reshape(1, 1, 320, 1024)

    back = jnp.stack(bulk).reshape(3, 3, 96, 4, 256).transpose(3, 0, 1, 2, 4)
    back = trade_wt(back, wt_index)[:, :, :, :88].transpose(1, 2, 0, 3, 4).reshape(3, 3, 352, 256).astype(F32)
    res_gate, res_up, res_down = back[:, 0].transpose(0, 2, 1), back[:, 1].transpose(0, 2, 1), back[:, 2]

    grad_final = cot.astype(F32)
    unused, pull = jax.vjp(rms_norm, hidden, gain_ffn_f)
    grad_part, gain_ffn_part = pull(grad_normed_ffn)
    grad_hidden = grad_final + grad_part
    grad_hidden_low = grad_hidden.astype(BF)
    grad_mixed = dot_nt(grad_hidden_low, w_o).astype(BF)
    dq, dk, dv, dbias = attend_back(probs, q, k, v, grad_mixed)

    gn_all = dot_nt(dk, w_kv[0]) + dot_nt(dv, w_kv[1])
    gn_q = dot_nt(dq, w_q)
    gp = gn_all[:512].astype(BF).reshape(4, 2, 64, 1024)
    gp_keep = lax.dynamic_index_in_dim(gp, y, 1, keepdims=False)
    gp_sum = add_low(gp_keep, move_y(lax.dynamic_index_in_dim(gp, 1 - y, 1, keepdims=False)))
    gp_at = lambda n: lax.dynamic_index_in_dim(gp_sum, (z + n) % 4, 0, keepdims=False)
    gp_own = gp_at(0).astype(F32)
    for s in (1, 2, 3):
        gp_own = gp_own + shift_z(gp_at(s), s).astype(F32)
    gn_own = gn_q + jnp.concatenate([gp_own, gn_all[512:]], axis=0)
    unused, pull = jax.vjp(rms_norm, source, gain_attn_f)
    grad_source, unused = pull(gn_own)
    grad_tokens = (grad_hidden + grad_source).astype(BF).reshape(1, 1, 320, 1024)
    gain_attn_part = jnp.sum(gn_all * unit_all, axis=0) + jnp.sum(gn_q * norm_parts(source), axis=0)

    bias_rows = bias_windows_back(dbias, ctx_index)
    bias_part = jnp.dot(bias_rows, onehot, precision=precise)
    smalls = jnp.concatenate(
        [gain_attn_part[None], gain_ffn_part[None], router_part, jnp.pad(bias_part.reshape(1, 512), ((0, 0), (0, 512))),
         jnp.zeros((2, 1024), F32)], axis=0
    )
    smalls = sum_all(smalls)
    mine = lax.dynamic_slice_in_dim(smalls, wt_index * 256, 256, 1)
    res_gain_attn, res_gain_ffn, res_router = mine[0], mine[1], mine[2:5].T
    res_bias = lax.dynamic_slice_in_dim(smalls[5, :512].reshape(16, 32), wt_index * 4, 4, 0).T

    grads = jnp.stack(
        [dot_tn(own_low, dq).astype(BF), dot_tn(all_low, dk).astype(BF), dot_tn(all_low, dv).astype(BF),
         dot_tn(mixed, grad_hidden_low).astype(BF)]
    ).reshape(4, 2, 2, 256, 1024)
    pick = lambda v, n, d: lax.dynamic_index_in_dim(v, n, d, keepdims=False)
    t = add_low(pick(grads, c, 2), move_c(pick(grads, 1 - c, 2)))
    ta, tb = t[:2].reshape(2, 2, 256, 4, 2, 128), t[2:].reshape(2, 2, 256, 4, 2, 128)
    ta = add_low(pick(ta, x, 1), move_x(pick(ta, 1 - x, 1)))
    tb = add_low(pick(tb, y, 4), move_y(pick(tb, 1 - y, 4)))
    ta = add_low(pick(ta, y, 3), move_y(pick(ta, 1 - y, 3)))
    tb = add_low(pick(tb, x, 1), move_x(pick(tb, 1 - x, 1)))
    tz = jnp.concatenate([ta, tb], axis=0)
    tot = pick(tz, z, 2).astype(F32)
    for s in (1, 2, 3):
        tot = tot + shift_z(pick(tz, (z + s) % 4, 2), s).astype(F32)
    return (
        output, grad_tokens, tot[0], tot[1], tot[2], tot[3], res_gain_attn, res_gain_ffn, res_router, res_bias,
        res_gate, res_up, res_down,
    )


def solution(mesh):
    fast = mesh.shape["ctx"] == FAST_CTX and mesh.shape["wt"] == FAST_WT
    return jax.shard_map(
        local_fast if fast else local,
        mesh=mesh,
        in_specs=(
            P("wt", "ctx", None, None),
            P("wt", "ctx", None, None),
            P("wt", "ctx"),
            P("wt", "ctx"),
            P("wt", "ctx"),
            P("wt", "ctx"),
            P("wt"),
            P("wt"),
            P("wt", None),
            P(None, "wt"),
            P(None, "wt", "ctx"),
            P(None, "wt", "ctx"),
            P(None, "ctx", "wt"),
            P(),
            P("wt", "ctx", None, None),
            P("wt", "ctx", None),
        ),
        out_specs=(
            P("wt", "ctx", None, None),
            P("wt", "ctx", None, None),
            P("wt", "ctx"),
            P("wt", "ctx"),
            P("wt", "ctx"),
            P("wt", "ctx"),
            P("wt"),
            P("wt"),
            P("wt", None),
            P(None, "wt"),
            P(None, "wt", "ctx"),
            P(None, "wt", "ctx"),
            P(None, "ctx", "wt"),
        ),
        check_vma=False,
    )
```

```python
import functools

import jax
import jax.numpy as jnp
from jax import lax
from jax.experimental import pallas as pl
from jax.experimental.pallas import tpu as pltpu
from jax.sharding import PartitionSpec as P

HEADS = 16
HEAD_DIM = 64
BUCKETS = 32
EXPERTS = 3
TOP = 2
LEN = 256
CAP = 267


epsilon = 1e-06
precise = lax.Precision.HIGHEST


def rms_norm(values, gain_vec):
    return (
        values * lax.rsqrt(jnp.mean(values * values, axis=-1, keepdims=True) + epsilon) * gain_vec
    )


def gelu_product(gate_pre, up_pre):
    return jax.nn.gelu(gate_pre, approximate=True) * up_pre


def routing(expert_ids, priority, capacity, expert_count):
    tok_rows = expert_ids.shape[0]
    top_count = expert_ids.shape[1]
    expert = expert_ids.T.reshape(-1)
    rank_key = (
        jnp.arange(top_count, dtype=jnp.int32)[:, None] * tok_rows + priority[None, :]
    ).reshape(-1)
    earlier = (expert[:, None] == expert[None, :]) & (rank_key[None, :] < rank_key[:, None])
    places = jnp.sum(earlier.astype(jnp.int32), axis=1)
    keep_mask = places < capacity
    slot_ids = expert * capacity + jnp.minimum(places, capacity - 1)
    slot_hits = jnp.where(
        (slot_ids[:, None] == jnp.arange(expert_count * capacity, dtype=jnp.int32)[None, :])
        & keep_mask[:, None],
        1.0,
        0.0,
    )
    dispatch = jnp.sum(slot_hits.reshape(top_count, tok_rows, expert_count * capacity), axis=0).T
    return (keep_mask, slot_ids, slot_hits, dispatch)


def gate_values(logits, expert_ids, keep_mask):
    chances = jax.nn.softmax(logits, axis=-1)
    picked = jnp.take_along_axis(chances, expert_ids, axis=1).T.reshape(-1)
    return jnp.where(keep_mask, picked, 0.0)


def toeplitz(reversed_bias, top_start, row_total, key_total):
    window_len = row_total + key_total
    window = lax.dynamic_slice_in_dim(reversed_bias, top_start, window_len, 1)
    tiled = jnp.tile(window, (1, row_total))[:, : row_total * (window_len - 1)]
    return tiled.reshape(window.shape[0], row_total, window_len - 1)[:, :, row_total - 1 :]


def toeplitz_back(grad_block, row_total, key_total):
    window_len = row_total + key_total
    head_total = grad_block.shape[0]
    placed = jnp.pad(grad_block, ((0, 0), (0, 0), (row_total - 1, 0))).reshape(
        head_total, row_total * (window_len - 1)
    )
    placed = jnp.pad(placed, ((0, 0), (0, row_total)))
    return jnp.sum(placed.reshape(head_total, row_total, window_len), axis=1)


def add_window(table, piece, start):
    current = lax.dynamic_slice_in_dim(table, start, piece.shape[1], 1)
    return lax.dynamic_update_slice_in_dim(table, current + piece, start, 1)


def sweep(step_fn, start_state, prompt_items, local_items):
    state_mid, stacked = lax.scan(step_fn, start_state, prompt_items)
    state_end, last_out = step_fn(state_mid, local_items)
    return (state_end, stacked, last_out)


def local(
    tokens,
    cotangent,
    w_query,
    w_key,
    w_value,
    w_out,
    gain_attn,
    gain_ffn,
    w_router,
    rel_bias,
    exp_gate,
    exp_up,
    exp_down,
    bucket_table,
    expert_ids,
    priority,
):
    tok_rows = tokens.shape[2]
    model_width = tokens.shape[3]
    ctx_count = lax.axis_size("ctx")
    my_block = lax.axis_index("ctx")
    prompt_rows = tok_rows - LEN
    cont_rows = tok_rows - prompt_rows
    prompt_len = prompt_rows * ctx_count
    dist_count = bucket_table.shape[0]
    head_count = HEADS
    head_width = HEAD_DIM
    score_scale = HEAD_DIM ** (-0.5)
    steps_count = max(1, ctx_count // 8)
    block_keys = prompt_len // steps_count
    cols_query, cols_key, cols_value, cols_out, cols_gate, cols_up, cols_down = (
        lax.all_gather(w_query, "ctx", axis=1, tiled=True),
        lax.all_gather(w_key, "ctx", axis=1, tiled=True),
        lax.all_gather(w_value, "ctx", axis=1, tiled=True),
        lax.all_gather(w_out, "ctx", axis=1, tiled=True),
        lax.all_gather(exp_gate, "ctx", axis=2, tiled=True),
        lax.all_gather(exp_up, "ctx", axis=2, tiled=True),
        lax.all_gather(exp_down, "ctx", axis=1, tiled=True),
    )
    gathered = (
        lax.all_gather(cols_query, "wt", axis=0, tiled=True),
        lax.all_gather(cols_key, "wt", axis=0, tiled=True),
        lax.all_gather(cols_value, "wt", axis=0, tiled=True),
        lax.all_gather(cols_out, "wt", axis=0, tiled=True),
        lax.all_gather(cols_gate, "wt", axis=1, tiled=True),
        lax.all_gather(cols_up, "wt", axis=1, tiled=True),
        lax.all_gather(cols_down, "wt", axis=2, tiled=True),
        lax.all_gather(gain_attn, "wt", axis=0, tiled=True),
        lax.all_gather(gain_ffn, "wt", axis=0, tiled=True),
        lax.all_gather(w_router, "wt", axis=0, tiled=True),
        lax.all_gather(rel_bias, "wt", axis=1, tiled=True),
    )
    (
        full_query,
        full_key,
        full_value,
        full_out,
        full_gate,
        full_up,
        full_down,
        full_gain_attn,
        full_gain_ffn,
        full_router,
        full_bias,
    ) = gathered
    gain_attn_f = full_gain_attn.astype(jnp.float32)
    gain_ffn_f = full_gain_ffn.astype(jnp.float32)
    source = tokens[0, 0].astype(jnp.float32)
    normed_attn = rms_norm(source, gain_attn_f)
    normed_attn_low = normed_attn.astype(jnp.bfloat16)
    query_low = jnp.dot(normed_attn_low, full_query, preferred_element_type=jnp.float32).astype(
        jnp.bfloat16
    )
    key_low = jnp.dot(normed_attn_low, full_key, preferred_element_type=jnp.float32).astype(
        jnp.bfloat16
    )
    value_low = jnp.dot(normed_attn_low, full_value, preferred_element_type=jnp.float32).astype(
        jnp.bfloat16
    )
    far_keys, far_values = (
        lax.all_gather(key_low[:prompt_rows], "ctx", axis=0, tiled=True),
        lax.all_gather(value_low[:prompt_rows], "ctx", axis=0, tiled=True),
    )
    row_index = jnp.arange(tok_rows, dtype=jnp.int32)
    query_pos = jnp.where(
        row_index < prompt_rows,
        my_block * prompt_rows + row_index,
        prompt_len + row_index - prompt_rows,
    )
    bucket_onehot = jnp.where(
        bucket_table[:, None] == jnp.arange(BUCKETS, dtype=jnp.int32)[None, :], 1.0, 0.0
    )
    bias_rows = jnp.dot(bucket_onehot, full_bias.astype(jnp.float32), precision=precise).T
    reversed_bias = jnp.concatenate([bias_rows[:, ::-1], jnp.zeros_like(bias_rows)], axis=1)
    prompt_starts = jnp.arange(steps_count, dtype=jnp.int32) * block_keys
    local_start = jnp.asarray(prompt_len, dtype=jnp.int32)
    query_heads = query_low.reshape(tok_rows, head_count, head_width)

    def blocks_of(far_array):
        return far_array.reshape(steps_count, block_keys, model_width)

    def window_starts(key_start):
        prompt_top = dist_count - my_block * prompt_rows + key_start - prompt_rows
        cont_top = dist_count - prompt_len + key_start - cont_rows
        return (prompt_top, cont_top)

    def block_scores(key_block, key_start):
        key_total = key_block.shape[0]
        key_heads = key_block.reshape(key_total, head_count, head_width)
        logit_raw = (
            jnp.einsum("qhd,khd->hqk", query_heads, key_heads, preferred_element_type=jnp.float32)
            * score_scale
        )
        key_pos = key_start + jnp.arange(key_total, dtype=jnp.int32)
        offset = query_pos[:, None] - key_pos[None, :]
        prompt_top, cont_top = window_starts(key_start)
        bias_block = jnp.concatenate(
            [
                toeplitz(reversed_bias, prompt_top, prompt_rows, key_total),
                toeplitz(reversed_bias, cont_top, cont_rows, key_total),
            ],
            axis=1,
        )
        return jnp.where(offset[None] >= 0, logit_raw + bias_block, -1e30)

    def stats_step(state_in, block_item):
        run_max, run_sum = state_in
        scores = block_scores(block_item[0], block_item[1])
        new_max = jnp.maximum(run_max, jnp.max(scores, axis=-1))
        new_sum = run_sum * jnp.exp(run_max - new_max) + jnp.sum(
            jnp.exp(scores - new_max[..., None]), axis=-1
        )
        return ((new_max, new_sum), None)

    start_stats = (
        jnp.full((head_count, tok_rows), -1e30, jnp.float32),
        jnp.zeros((head_count, tok_rows), jnp.float32),
    )
    (row_max, row_sum), unused_a, unused_b = sweep(
        stats_step,
        start_stats,
        (blocks_of(far_keys), prompt_starts),
        (key_low[prompt_rows:], local_start),
    )

    def mix_step(state_in, block_item):
        scores = block_scores(block_item[0], block_item[2])
        weights = (jnp.exp(scores - row_max[..., None]) / row_sum[..., None]).astype(jnp.bfloat16)
        value_heads = block_item[1].reshape(-1, head_count, head_width)
        return (
            state_in
            + jnp.einsum("hqk,khd->qhd", weights, value_heads, preferred_element_type=jnp.float32),
            None,
        )

    mixed_exact, unused_c, unused_d = sweep(
        mix_step,
        jnp.zeros((tok_rows, head_count, head_width), jnp.float32),
        (blocks_of(far_keys), blocks_of(far_values), prompt_starts),
        (key_low[prompt_rows:], value_low[prompt_rows:], local_start),
    )
    mixed_low = mixed_exact.reshape(tok_rows, model_width).astype(jnp.bfloat16)
    hidden = source + jnp.dot(mixed_low, full_out, preferred_element_type=jnp.float32)
    normed_ffn_low = rms_norm(hidden, gain_ffn_f).astype(jnp.bfloat16)
    route_ids = expert_ids[0, 0]
    keep_mask, slot_ids, slot_hits, dispatch = routing(route_ids, priority[0, 0], CAP, EXPERTS)
    inputs = (
        jnp.dot(dispatch.astype(jnp.bfloat16), normed_ffn_low, preferred_element_type=jnp.float32)
        .astype(jnp.bfloat16)
        .reshape(EXPERTS, CAP, model_width)
    )
    gate_pre = jnp.einsum("ecd,edf->ecf", inputs, full_gate, preferred_element_type=jnp.float32)
    up_pre = jnp.einsum("ecd,edf->ecf", inputs, full_up, preferred_element_type=jnp.float32)
    inner_low = gelu_product(gate_pre, up_pre).astype(jnp.bfloat16)
    expert_out = jnp.einsum(
        "ecf,efd->ecd", inner_low, full_down, preferred_element_type=jnp.float32
    ).reshape(EXPERTS * CAP, model_width)
    logits = jnp.dot(normed_ffn_low, full_router, preferred_element_type=jnp.float32)
    weight_pair = gate_values(logits, route_ids, keep_mask)
    picked_rows = jnp.take(expert_out, slot_ids, axis=0)
    combined = jnp.sum(
        (picked_rows * weight_pair[:, None]).reshape(TOP, tok_rows, model_width), axis=0
    )
    output = (hidden + combined).astype(jnp.bfloat16).reshape(1, 1, tok_rows, model_width)
    back_keys, back_values = (far_keys, far_values)
    (
        back_query,
        back_key,
        back_value,
        back_out,
        back_gate,
        back_up,
        back_down,
        back_gain_attn,
        back_gain_ffn,
        back_router,
        back_bias,
    ) = gathered
    grad_final = cotangent[0, 0].astype(jnp.float32)
    grad_pair = jnp.where(
        keep_mask, jnp.sum(jnp.tile(grad_final, (TOP, 1)) * picked_rows, axis=-1), 0.0
    )
    slot_weight = jnp.dot(weight_pair, slot_hits, precision=precise)
    grad_expert_out = (
        (jnp.dot(dispatch, grad_final, precision=precise) * slot_weight[:, None])
        .astype(jnp.bfloat16)
        .reshape(EXPERTS, CAP, model_width)
    )
    grad_inner = jnp.einsum(
        "ecd,efd->ecf", grad_expert_out, back_down, preferred_element_type=jnp.float32
    )
    unused_e, inner_pull = jax.vjp(gelu_product, gate_pre, up_pre)
    grad_gate_pre, grad_up_pre = inner_pull(grad_inner)
    grad_gate_low = grad_gate_pre.astype(jnp.bfloat16)
    grad_up_low = grad_up_pre.astype(jnp.bfloat16)
    grad_gate_w = jnp.einsum(
        "ecd,ecf->edf", inputs, grad_gate_low, preferred_element_type=jnp.float32
    )
    grad_up_w = jnp.einsum("ecd,ecf->edf", inputs, grad_up_low, preferred_element_type=jnp.float32)
    grad_down_w = jnp.einsum(
        "ecf,ecd->efd", inner_low, grad_expert_out, preferred_element_type=jnp.float32
    )
    grad_inputs = jnp.einsum(
        "ecf,edf->ecd", grad_gate_low, back_gate, preferred_element_type=jnp.float32
    ) + jnp.einsum("ecf,edf->ecd", grad_up_low, back_up, preferred_element_type=jnp.float32)

    def gate_of_logits(logit_values):
        return gate_values(logit_values, route_ids, keep_mask)

    unused_f, gate_pull = jax.vjp(gate_of_logits, logits)
    (grad_logits,) = gate_pull(grad_pair)
    grad_router_w = jnp.dot(normed_ffn_low.astype(jnp.float32).T, grad_logits, precision=precise)
    grad_normed_ffn = jnp.dot(grad_logits, back_router.astype(jnp.float32).T, precision=precise)
    grad_normed_ffn = grad_normed_ffn + jnp.dot(
        dispatch.T, grad_inputs.reshape(EXPERTS * CAP, model_width), precision=precise
    )
    unused_g, ffn_norm_pull = jax.vjp(rms_norm, hidden, back_gain_ffn.astype(jnp.float32))
    grad_hidden_part, grad_gain_ffn_w = ffn_norm_pull(grad_normed_ffn)
    grad_hidden = grad_final + grad_hidden_part
    grad_hidden_low = grad_hidden.astype(jnp.bfloat16)
    grad_out_w = jnp.dot(mixed_low.T, grad_hidden_low, preferred_element_type=jnp.float32)
    grad_mixed = jnp.dot(grad_hidden_low, back_out.T, preferred_element_type=jnp.float32).astype(
        jnp.bfloat16
    )
    grad_mixed_heads = grad_mixed.reshape(tok_rows, head_count, head_width)
    row_delta = jnp.sum(grad_mixed_heads.astype(jnp.float32) * mixed_exact, axis=-1).T

    def grad_step(state_in, block_item):
        grad_query_acc, grad_reversed = state_in
        key_block, value_block, key_start = block_item
        key_total = key_block.shape[0]
        scores = block_scores(key_block, key_start)
        chances = jnp.exp(scores - row_max[..., None]) / row_sum[..., None]
        value_heads = value_block.reshape(-1, head_count, head_width)
        key_heads = key_block.reshape(-1, head_count, head_width)
        grad_chance = jnp.einsum(
            "qhd,khd->hqk", grad_mixed_heads, value_heads, preferred_element_type=jnp.float32
        )
        grad_value_block = jnp.einsum(
            "hqk,qhd->khd",
            chances.astype(jnp.bfloat16),
            grad_mixed_heads,
            preferred_element_type=jnp.float32,
        )
        grad_scores = chances * (grad_chance - row_delta[..., None])
        prompt_top, cont_top = window_starts(key_start)
        grad_reversed = add_window(
            grad_reversed,
            toeplitz_back(grad_scores[:, :prompt_rows], prompt_rows, key_total),
            prompt_top,
        )
        grad_reversed = add_window(
            grad_reversed,
            toeplitz_back(grad_scores[:, prompt_rows:], cont_rows, key_total),
            cont_top,
        )
        grad_scores_low = grad_scores.astype(jnp.bfloat16)
        grad_query_acc = grad_query_acc + score_scale * jnp.einsum(
            "hqk,khd->qhd", grad_scores_low, key_heads, preferred_element_type=jnp.float32
        )
        grad_key_block = score_scale * jnp.einsum(
            "hqk,qhd->khd", grad_scores_low, query_heads, preferred_element_type=jnp.float32
        )
        return (
            (grad_query_acc, grad_reversed),
            (grad_key_block.reshape(-1, model_width), grad_value_block.reshape(-1, model_width)),
        )

    start_grads = (
        jnp.zeros((tok_rows, head_count, head_width), jnp.float32),
        jnp.zeros((head_count, 2 * dist_count), jnp.float32),
    )
    (
        (grad_query_exact, grad_reversed),
        (far_grad_keys, far_grad_values),
        (near_grad_keys, near_grad_values),
    ) = sweep(
        grad_step,
        start_grads,
        (blocks_of(back_keys), blocks_of(back_values), prompt_starts),
        (key_low[prompt_rows:], value_low[prompt_rows:], local_start),
    )
    own_grad_keys, own_grad_values = (
        lax.psum_scatter(
            far_grad_keys.reshape(prompt_len, model_width), "ctx", scatter_dimension=0, tiled=True
        ),
        lax.psum_scatter(
            far_grad_values.reshape(prompt_len, model_width), "ctx", scatter_dimension=0, tiled=True
        ),
    )
    grad_key_low = jnp.concatenate([own_grad_keys, near_grad_keys], axis=0).astype(jnp.bfloat16)
    grad_value_low = jnp.concatenate([own_grad_values, near_grad_values], axis=0).astype(
        jnp.bfloat16
    )
    grad_query_low = grad_query_exact.reshape(tok_rows, model_width).astype(jnp.bfloat16)
    grad_query_w = jnp.dot(normed_attn_low.T, grad_query_low, preferred_element_type=jnp.float32)
    grad_key_w = jnp.dot(normed_attn_low.T, grad_key_low, preferred_element_type=jnp.float32)
    grad_value_w = jnp.dot(normed_attn_low.T, grad_value_low, preferred_element_type=jnp.float32)
    grad_normed_attn = jnp.dot(grad_query_low, back_query.T, preferred_element_type=jnp.float32)
    grad_normed_attn = grad_normed_attn + jnp.dot(
        grad_key_low, back_key.T, preferred_element_type=jnp.float32
    )
    grad_normed_attn = grad_normed_attn + jnp.dot(
        grad_value_low, back_value.T, preferred_element_type=jnp.float32
    )
    unused_h, attn_norm_pull = jax.vjp(rms_norm, source, back_gain_attn.astype(jnp.float32))
    grad_source_part, grad_gain_attn_w = attn_norm_pull(grad_normed_attn)
    grad_tokens = (
        (grad_hidden + grad_source_part).astype(jnp.bfloat16).reshape(1, 1, tok_rows, model_width)
    )
    grad_bias_rows = grad_reversed[:, :dist_count][:, ::-1]
    grad_bias_w = jnp.dot(bucket_onehot.T, grad_bias_rows.T, precision=precise)
    small_gain_attn, small_gain_ffn, small_router, small_bias = lax.psum(
        (grad_gain_attn_w, grad_gain_ffn_w, grad_router_w, grad_bias_w), "ctx"
    )
    row_parts = (
        lax.psum_scatter(
            grad_query_w.astype(jnp.bfloat16), "wt", scatter_dimension=0, tiled=True
        ).astype(jnp.float32),
        lax.psum_scatter(
            grad_key_w.astype(jnp.bfloat16), "wt", scatter_dimension=0, tiled=True
        ).astype(jnp.float32),
        lax.psum_scatter(
            grad_value_w.astype(jnp.bfloat16), "wt", scatter_dimension=0, tiled=True
        ).astype(jnp.float32),
        lax.psum_scatter(
            grad_out_w.astype(jnp.bfloat16), "wt", scatter_dimension=0, tiled=True
        ).astype(jnp.float32),
        lax.psum_scatter(
            grad_gate_w.astype(jnp.bfloat16), "wt", scatter_dimension=1, tiled=True
        ).astype(jnp.float32),
        lax.psum_scatter(
            grad_up_w.astype(jnp.bfloat16), "wt", scatter_dimension=1, tiled=True
        ).astype(jnp.float32),
        lax.psum_scatter(
            grad_down_w.astype(jnp.bfloat16), "wt", scatter_dimension=2, tiled=True
        ).astype(jnp.float32),
        lax.psum_scatter(
            small_gain_attn.astype(jnp.bfloat16), "wt", scatter_dimension=0, tiled=True
        ).astype(jnp.float32),
        lax.psum_scatter(
            small_gain_ffn.astype(jnp.bfloat16), "wt", scatter_dimension=0, tiled=True
        ).astype(jnp.float32),
        lax.psum_scatter(
            small_router.astype(jnp.bfloat16), "wt", scatter_dimension=0, tiled=True
        ).astype(jnp.float32),
        lax.psum_scatter(
            small_bias.astype(jnp.bfloat16), "wt", scatter_dimension=1, tiled=True
        ).astype(jnp.float32),
    )
    res_query, res_key, res_value, res_out, res_gate, res_up, res_down = (
        lax.psum_scatter(row_parts[0], "ctx", scatter_dimension=1, tiled=True),
        lax.psum_scatter(row_parts[1], "ctx", scatter_dimension=1, tiled=True),
        lax.psum_scatter(row_parts[2], "ctx", scatter_dimension=1, tiled=True),
        lax.psum_scatter(row_parts[3], "ctx", scatter_dimension=1, tiled=True),
        lax.psum_scatter(row_parts[4], "ctx", scatter_dimension=2, tiled=True),
        lax.psum_scatter(row_parts[5], "ctx", scatter_dimension=2, tiled=True),
        lax.psum_scatter(row_parts[6], "ctx", scatter_dimension=1, tiled=True),
    )
    res_gain_attn, res_gain_ffn, res_router, res_bias = (
        row_parts[7],
        row_parts[8],
        row_parts[9],
        row_parts[10],
    )
    return (
        output,
        grad_tokens,
        res_query,
        res_key,
        res_value,
        res_out,
        res_gain_attn,
        res_gain_ffn,
        res_router,
        res_bias,
        res_gate,
        res_up,
        res_down,
    )


BF = jnp.bfloat16
F32 = jnp.float32
FAST_CTX = 8
FAST_WT = 4
NEG = -1e30

SWAP_Y = [(i, i ^ 1) for i in range(8)]
PAIR_Z = [(i, i ^ 2) for i in range(8)]
MID_Z = [(0, 0), (1, 1), (2, 4), (3, 5), (4, 2), (5, 3), (6, 6), (7, 7)]
SWAP_C = [(i, i ^ 1) for i in range(4)]
SWAP_X = [(i, i ^ 2) for i in range(4)]


def move_y(v):
    return lax.ppermute(v, "ctx", SWAP_Y)


def move_x(v):
    return lax.ppermute(v, "wt", SWAP_X)


def move_c(v):
    return lax.ppermute(v, "wt", SWAP_C)


def pair_z(v):
    return lax.ppermute(v, "ctx", PAIR_Z)


def mid_z(v):
    return lax.ppermute(v, "ctx", MID_Z)


def shift_z(v, s):
    return lax.ppermute(v, "ctx", [(i, (i + 2 * s) % 8) for i in range(8)])


def after(v, *deps):
    return lax.optimization_barrier((v,) + deps)[0]


def dot_nt(a, b):
    return lax.dot_general(a, b, (((1,), (1,)), ((), ())), preferred_element_type=F32)


def dot_tn(a, b):
    return lax.dot_general(a, b, (((0,), (0,)), ((), ())), preferred_element_type=F32)


def dot_nn(a, b):
    return jnp.dot(a, b, preferred_element_type=F32)


def params(limit=56 * 2**20):
    return pltpu.CompilerParams(vmem_limit_bytes=limit)


ANY = pl.BlockSpec(memory_space=pl.ANY)
SMEM = pl.BlockSpec(memory_space=pltpu.SMEM)


def spread_all(unit):
    pieces = []
    for s in range(4):
        v = unit if s == 0 else shift_z(unit, s)
        if s % 2 == 0:
            a = move_y(v)
            quad = {(0, 0): v, (1, 0): a, (0, 1): move_x(v), (1, 1): move_x(a)}
        else:
            b = move_x(v)
            quad = {(0, 0): v, (0, 1): b, (1, 0): move_y(v), (1, 1): move_y(b)}
        for ry in range(2):
            for rx in range(2):
                piece = quad[(ry, rx)]
                pieces.append(((s, ry, rx, 0), piece))
                pieces.append(((s, ry, rx, 1), move_c(piece)))
    return pieces


def place_kernel(keys, idx, *refs):
    count = len(keys)
    ins, wkv, wq, wo = refs[:count], refs[count], refs[count + 1], refs[count + 2]
    z, y, x, c = idx[0], idx[1], idx[2], idx[3]
    for n, (s, ry, rx, rc) in enumerate(keys):
        row = pl.multiple_of(((x ^ rx) * 2 + (c ^ rc)) * 256, 256)
        col = pl.multiple_of((lax.rem(z + 4 - s, 4) * 2 + (y ^ ry)) * 128, 128)
        rows, cols = pl.ds(row, 256), pl.ds(col, 128)
        wq[rows, cols] = ins[n][0]
        wkv[0, rows, cols] = ins[n][1]
        wkv[1, rows, cols] = ins[n][2]
        wo[rows, cols] = ins[n][3]


def place_weights(idx, pieces):
    keys = [k for k, _ in pieces]
    whole = pl.BlockSpec(memory_space=pltpu.VMEM)
    return pl.pallas_call(
        functools.partial(place_kernel, keys),
        out_shape=(
            jax.ShapeDtypeStruct((2, 1024, 1024), BF),
            jax.ShapeDtypeStruct((1024, 1024), BF),
            jax.ShapeDtypeStruct((1024, 1024), BF),
        ),
        in_specs=[SMEM] + [whole] * len(keys),
        out_specs=(whole, whole, whole),
        compiler_params=params(),
    )(idx, *[v for _, v in pieces])


def attend_kernel(w_ref, q_ref, k_ref, v_ref, p_ref, o_ref, bc_ref, bp_ref):
    q, k, v = q_ref[...], k_ref[...], v_ref[...]
    lane = lax.broadcasted_iota(jnp.int32, (1, 128), 1)
    outs = []
    for h in range(2):
        base_c, base_p = w_ref[h, 0], w_ref[h, 1]
        for a in range(32):
            bc_ref[8 * a : 8 * a + 8, :] = pltpu.roll(base_c, 1024 - (248 - 8 * a), 1)[:, :768]
        for a in range(8):
            shift = 56 - 8 * a
            bp_ref[8 * a : 8 * a + 8, :] = (pltpu.roll(base_p, 1024 - shift, 1) if shift else base_p)[:, :512]
        mine = (lane < 64) if h == 0 else (lane >= 64)
        qh = jnp.where(mine, q, jnp.zeros_like(q))
        sc = dot_nt(qh[64:], k) * 0.125 + bc_ref[...]
        sp = dot_nt(qh[:64], k[:512]) * 0.125 + bp_ref[...]

        def soft(s):
            e = jnp.exp(s - jnp.max(s, axis=-1, keepdims=True))
            return (e / jnp.sum(e, axis=-1, keepdims=True)).astype(BF)

        pc, pp = soft(sc), soft(sp)
        p_ref[h, 64:, :] = pc
        p_ref[h, :64, :512] = pp
        p_ref[h, :64, 512:] = jnp.zeros((64, 256), BF)
        outs.append(jnp.concatenate([dot_nn(pp, v[:512]), dot_nn(pc, v)], axis=0))
    o_ref[...] = jnp.where(lane < 64, outs[0], outs[1]).astype(BF)


def attend(bias_rows, q, k, v):
    rows, keys = q.shape[0], k.shape[0]
    return pl.pallas_call(
        attend_kernel,
        grid=(8,),
        out_shape=(
            jax.ShapeDtypeStruct((16, rows, keys), BF),
            jax.ShapeDtypeStruct((rows, 1024), BF),
        ),
        in_specs=[
            pl.BlockSpec((2, 2, 8, 1024), lambda j: (j, 0, 0, 0)),
            pl.BlockSpec((rows, 128), lambda j: (0, j)),
            pl.BlockSpec((keys, 128), lambda j: (0, j)),
            pl.BlockSpec((keys, 128), lambda j: (0, j)),
        ],
        out_specs=(
            pl.BlockSpec((2, rows, keys), lambda j: (j, 0, 0)),
            pl.BlockSpec((rows, 128), lambda j: (0, j)),
        ),
        scratch_shapes=[pltpu.VMEM((256, 768), F32), pltpu.VMEM((64, 512), F32)],
        compiler_params=params(),
        cost_estimate=pl.CostEstimate(flops=8 * 320 * 768 * 512, bytes_accessed=14 * 2**20, transcendentals=2**22),
    )(bias_rows, q, k, v)


def attend_back_kernel(p_ref, q_ref, k_ref, v_ref, g_ref, dq_ref, dk_ref, dv_ref, db_ref):
    q, k, v, g = q_ref[...], k_ref[...], v_ref[...], g_ref[...]
    lane = lax.broadcasted_iota(jnp.int32, (1, 128), 1)
    parts = []
    for h in range(2):
        mine = (lane < 64) if h == 0 else (lane >= 64)
        gh = jnp.where(mine, g, jnp.zeros_like(g))
        p = p_ref[h]
        pf = p.astype(F32)
        dp = dot_nt(gh, v)
        delta = jnp.sum(pf * dp, axis=-1, keepdims=True)
        ds = pf * (dp - delta)
        low = ds.astype(BF)
        acc_c = jnp.zeros((8, 1024), F32)
        for a in range(32):
            part = jnp.concatenate([ds[64 + 8 * a : 72 + 8 * a], jnp.zeros((8, 256), F32)], axis=1)
            acc_c = acc_c + pltpu.roll(part, 248 - 8 * a, 1) if a < 31 else acc_c + part
        acc_p = jnp.zeros((8, 1024), F32)
        for a in range(8):
            part = jnp.concatenate([ds[8 * a : 8 * a + 8, :512], jnp.zeros((8, 512), F32)], axis=1)
            acc_p = acc_p + (pltpu.roll(part, 56 - 8 * a, 1) if a < 7 else part)
        db_ref[h, 0] = acc_c
        db_ref[h, 1] = acc_p
        parts.append((dot_nn(low, k) * 0.125, dot_tn(low, q) * 0.125, dot_tn(p, g)))
    for n, ref in enumerate((dq_ref, dk_ref, dv_ref)):
        ref[...] = jnp.where(lane < 64, parts[0][n], parts[1][n]).astype(BF)


def attend_back(p, q, k, v, g):
    rows, keys = q.shape[0], k.shape[0]
    head = lambda n: pl.BlockSpec((n, 128), lambda j: (0, j))
    return pl.pallas_call(
        attend_back_kernel,
        grid=(8,),
        out_shape=(
            jax.ShapeDtypeStruct((rows, 1024), BF),
            jax.ShapeDtypeStruct((keys, 1024), BF),
            jax.ShapeDtypeStruct((keys, 1024), BF),
            jax.ShapeDtypeStruct((16, 2, 8, 1024), F32),
        ),
        in_specs=[
            pl.BlockSpec((2, rows, keys), lambda j: (j, 0, 0)),
            head(rows),
            head(keys),
            head(keys),
            head(rows),
        ],
        out_specs=(
            head(rows),
            head(keys),
            head(keys),
            pl.BlockSpec((2, 2, 8, 1024), lambda j: (j, 0, 0, 0)),
        ),
        compiler_params=params(),
        cost_estimate=pl.CostEstimate(flops=20 * 320 * 768 * 512, bytes_accessed=14 * 2**20, transcendentals=0),
    )(p, q, k, v, g)


def bias_windows(bias_rows, ctx_index):
    rev = jnp.concatenate([bias_rows[:, ::-1], jnp.full((16, 1152), NEG, F32)], axis=1)
    cont = jnp.stack([rev[:, 7 - s : 7 - s + 1024] for s in range(8)], axis=1)
    tail = lax.dynamic_slice_in_dim(rev, 704 - 64 * ctx_index, 1040, 1)
    prompt = jnp.stack([tail[:, 7 - s : 7 - s + 1024] for s in range(8)], axis=1)
    return jnp.stack([cont, prompt], axis=1)


def bias_windows_back(grad, ctx_index):
    def gather(part):
        total = jnp.zeros((16, 1040), F32)
        for s in range(8):
            total = total + jnp.pad(part[:, s], ((0, 0), (7 - s, 9 + s)))
        return total

    wide = jnp.pad(gather(grad[:, 0]), ((0, 0), (0, 880)))
    prompt = gather(grad[:, 1])
    start = 704 - 64 * ctx_index
    moved = lax.dynamic_update_slice_in_dim(jnp.zeros((16, 1920), F32), prompt, start, 1)
    return (wide + moved)[:, :768][:, ::-1]


ORDER = [(half, rc, ry, rx) for half in range(2) for rc in range(2) for ry in range(2) for rx in range(2)]


def spread_plane(v):
    half = v.shape[0] // 2
    a, b = v[:half], v[half:]
    ay, bx = move_y(a), move_x(b)
    ax, by = move_x(a), move_y(b)
    ayx, bxy = move_x(ay), move_y(bx)
    near = {(0, 0, 0): a, (0, 1, 0): ay, (0, 0, 1): ax, (0, 1, 1): ayx, (1, 0, 0): b, (1, 0, 1): bx, (1, 1, 0): by, (1, 1, 1): bxy}
    return [near[(h, ry, rx)] if rc == 0 else move_c(near[(h, ry, rx)]) for h, rc, ry, rx in ORDER]


def add_low(a, b):
    return (a.astype(F32) + b.astype(F32)).astype(BF)


def collect_plane(v):
    rows = v.shape[0] // 16
    w = v.reshape(2, 2, 4, rows, v.shape[1])
    sums = []
    for h in range(2):
        sums.append(add_low(w[h, 0], move_c(w[h, 1])))
    a, b = sums
    sy = add_low(a[2], move_x(a[3]))
    sx = add_low(b[1], move_y(b[3]))
    ax, by = move_x(a[1]), move_y(b[2])
    ay, bx = move_y(sy), move_x(sx)
    f = lambda t: t.astype(F32)
    return jnp.concatenate([f(a[0]) + f(ax) + f(ay), f(b[0]) + f(by) + f(bx)], axis=0)


def expert_kernel(expert, first, last, *refs):
    refs = list(refs)
    idx, x_ref, g_ref, m_ref = refs[:4]
    srcs = refs[4:10]
    at = 10
    if not first:
        out_prev, dx_prev = refs[at : at + 2]
        at += 2
    if last:
        s0_ref, s1_ref = refs[at : at + 2]
        at += 2
    out_ref, dx_ref, dh_ref, win_ref, s_ref, w_scr, sem = refs[at:]
    z = idx[0]

    @pl.when(pl.program_id(0) == 0)
    def _():
        def copy(n, slot):
            rows = pl.ds(pl.multiple_of(slot * 96, 96), 96)
            return pltpu.make_async_copy(srcs[n], w_scr.at[:, rows, :], sem.at[n])

        middle = (z == 1) | (z == 2)
        other, far = jnp.where(z < 2, 2, 1), jnp.where(z < 2, 3, 0)
        plan = [(0, z, None), (1, z ^ 1, None)]
        for n, slot in ((2, other), (3, far)):
            plan += [(n, slot, middle), (n + 2, slot, jnp.logical_not(middle))]
        for act in ("start", "wait"):
            for n, slot, ok in plan:
                if ok is None:
                    getattr(copy(n, slot), act)()
                else:

                    @pl.when(ok)
                    def _(n=n, slot=slot, act=act):
                        getattr(copy(n, slot), act)()

    x, g = x_ref[...], g_ref[...]
    w_gu = w_scr[0:2].reshape(768, 1024)
    w_d = w_scr[2]
    gu = dot_nt(x, w_gu)
    gi = dot_nt(g, w_d)
    gate, up = gu[:, :384], gu[:, 384:]
    l = [gate[:, 88 + n : 89 + n] for n in range(3)]
    top = jnp.maximum(jnp.maximum(l[0], l[1]), l[2])
    ex = [jnp.exp(v - top) for v in l]
    inv = 1.0 / (ex[0] + ex[1] + ex[2])
    p = [v * inv for v in ex]
    m = m_ref[...]
    keep = m[:, expert : expert + 1]
    w = p[expert] * keep
    sq = gate * gate
    th = jnp.tanh(0.7978845608028654 * gate * (1.0 + 0.044715 * sq))
    half1 = 0.5 + 0.5 * th
    act = gate * half1
    dact = half1 + (0.5 * gate) * (1.0 - th * th) * (0.7978845608028654 + 0.10703222440890037 * sq)
    inner = (act * up).astype(BF).astype(F32)
    s = jnp.sum(inner * gi, axis=-1, keepdims=True) * keep
    gin = gi * w
    dg = gin * up * dact
    du = gin * act
    if last:
        ss = [s0_ref[...][:, 0:1], s1_ref[...][:, 0:1], s]
        dot = p[0] * ss[0] + p[1] * ss[1] + p[2] * ss[2]
        lane = lax.broadcasted_iota(jnp.int32, (1, 384), 1)
        for n in range(3):
            dg = jnp.where(lane == 88 + n, p[n] * (ss[n] - dot), dg)
    win = (inner * w).astype(BF)
    dh = jnp.concatenate([dg.astype(BF), du.astype(BF)], axis=1)
    dh_ref[...] = dh
    win_ref[...] = win
    s_ref[...] = jnp.broadcast_to(s, s_ref.shape)
    out = dot_nn(win, w_d)
    dx = dot_nn(dh, w_gu)
    if not first:
        out = out + out_prev[...].astype(F32)
        dx = dx + dx_prev[...].astype(F32)
    out_ref[...] = out.astype(BF)
    dx_ref[...] = dx.astype(BF)


def expert_call(expert, idx, x, g, m, srcs, prev, s_prev, tile=512):
    total = x.shape[0]
    first, last = expert == 0, expert == 2
    row = lambda n: pl.BlockSpec((tile, n), lambda i: (i, 0))
    ins = [idx, x, g, m, *srcs]
    specs = [SMEM, row(1024), row(1024), row(8)] + [ANY] * 6
    if not first:
        ins += list(prev)
        specs += [row(1024), row(1024)]
    if last:
        ins += list(s_prev)
        specs += [row(8), row(8)]
    return pl.pallas_call(
        functools.partial(expert_kernel, expert, first, last),
        grid=(total // tile,),
        out_shape=(
            jax.ShapeDtypeStruct((total, 1024), BF),
            jax.ShapeDtypeStruct((total, 1024), BF),
            jax.ShapeDtypeStruct((total, 768), BF),
            jax.ShapeDtypeStruct((total, 384), BF),
            jax.ShapeDtypeStruct((total, 8), F32),
        ),
        in_specs=specs,
        out_specs=(row(1024), row(1024), row(768), row(384), row(8)),
        scratch_shapes=[pltpu.VMEM((3, 384, 1024), BF), pltpu.SemaphoreType.DMA((6,))],
        compiler_params=params(),
        cost_estimate=pl.CostEstimate(
            flops=2 * total * 1024 * 384 * 6, bytes_accessed=total * 1024 * 16, transcendentals=total * 384
        ),
    )(*ins)


def line_spread(v):
    near = pair_z(v)
    mid_own, mid_far = mid_z(v), mid_z(near)
    return [v, near, mid_own, mid_far, pair_z(mid_own), pair_z(mid_far)]


def line_collect(part_of, z):
    low_half = z < 2
    middle = (z == 1) | (z == 2)
    far, other = part_of(jnp.where(low_half, 3, 0)), part_of(jnp.where(low_half, 2, 1))
    from_far, from_other = pair_z(far), pair_z(other)
    cross_far, cross_own = mid_z(add_low(far, from_far)), mid_z(add_low(other, from_other))
    at_mid = lambda v: jnp.where(middle, v.astype(F32), 0.0)
    near = (part_of(z ^ 1).astype(F32) + at_mid(cross_far)).astype(BF)
    return (part_of(z).astype(F32) + pair_z(near).astype(F32) + at_mid(cross_own)).astype(BF)


def trade_wt(v, wt_index):
    at = lambda r: lax.dynamic_index_in_dim(v, wt_index ^ r, 0, keepdims=False)
    got = [at(0), move_c(at(1)), move_x(at(2)), lax.ppermute(at(3), "wt", [(i, i ^ 3) for i in range(4)])]
    return jnp.take(jnp.stack(got), jnp.arange(4, dtype=jnp.int32) ^ wt_index, axis=0)


def sum_all(v):
    v = v + move_c(v)
    v = v + move_x(v)
    v = v + move_y(v)
    v = v + lax.ppermute(v, "ctx", [(i, i ^ 2) for i in range(8)])
    return v + lax.ppermute(v, "ctx", [(i, i ^ 4) for i in range(8)])


def norm_parts(values):
    return values * lax.rsqrt(jnp.mean(values * values, axis=-1, keepdims=True) + epsilon)


def local_fast(
    tokens, cotangent, w_query, w_key, w_value, w_out, gain_attn, gain_ffn, w_router, rel_bias,
    exp_gate, exp_up, exp_down, bucket_table, expert_ids, priority,
):
    ctx_index = lax.axis_index("ctx").astype(jnp.int32)
    wt_index = lax.axis_index("wt").astype(jnp.int32)
    z, y, x, c = ctx_index // 2, ctx_index % 2, wt_index // 2, wt_index % 2
    idx = jnp.stack([z, y, x, c])
    rows_own = tokens[0, 0]

    packed = jnp.concatenate(
        [gain_attn[None], gain_ffn[None], w_router.T, jnp.pad(rel_bias.reshape(1, 128), ((0, 0), (0, 128))),
         jnp.zeros((2, 256), BF)], axis=0
    )
    small = lax.all_gather(packed, "wt", axis=0, tiled=False)
    gain_attn_f = small[:, 0].reshape(1024).astype(F32)
    gain_ffn_f = small[:, 1].reshape(1024).astype(F32)
    bias_f = small[:, 5, :128].reshape(4, 32, 4).transpose(1, 0, 2).reshape(32, 16).astype(F32)

    unit = jnp.stack([w_query, w_key, w_value, w_out])
    w_kv, w_q, w_o = place_weights(idx, spread_all(unit))

    prompt_own = rows_own[:64]
    group = [prompt_own] + [shift_z(prompt_own, s) for s in (3, 2, 1)]
    stack = jnp.stack([jnp.stack([v, move_y(v)]) for v in group])
    stack = lax.dynamic_slice_in_dim(jnp.concatenate([stack, stack], axis=0), (4 - z) % 4, 4, 0)
    stack = lax.dynamic_slice_in_dim(jnp.concatenate([stack, stack[:, :1]], axis=1), y, 2, 1)
    prompts = stack.reshape(512, 1024)

    ids, rank = expert_ids[0, 0], priority[0, 0]
    expert = ids.T.reshape(-1)
    rank_key = (jnp.arange(TOP, dtype=jnp.int32)[:, None] * 320 + rank[None, :]).reshape(-1)
    earlier = (expert[:, None] == expert[None, :]) & (rank_key[None, :] < rank_key[:, None])
    keep = (jnp.sum(earlier.astype(jnp.int32), axis=1) < CAP).reshape(TOP, 320)
    hold = jnp.sum(
        jnp.where((ids.T[:, :, None] == jnp.arange(EXPERTS, dtype=jnp.int32)) & keep[:, :, None], 1.0, 0.0), axis=0
    )
    marks = jnp.pad(hold.reshape(2, 1, 480), ((0, 0), (0, 15), (0, 544))).astype(BF)
    cot = cotangent[0, 0]
    cot_marked = jnp.concatenate([cot[:160], marks[0], cot[160:], marks[1]], axis=0)

    def pieces(v):
        return jnp.pad(v.reshape(3, 4, 88, 256), ((0, 0), (0, 0), (0, 8), (0, 0)))

    gate_t, up_t = exp_gate.transpose(0, 2, 1), exp_up.transpose(0, 2, 1)
    gate_p = pieces(gate_t)
    router_rows = jnp.broadcast_to(
        jnp.pad(w_router.T, ((0, 5), (0, 0)))[None, None], (3, 4, 8, 256)
    )
    gate_p = jnp.concatenate([gate_p[:, :, :88], router_rows], axis=2)
    share = jnp.stack([gate_p, pieces(up_t), pieces(exp_down)], axis=1).transpose(2, 0, 1, 3, 4)
    share = trade_wt(share, wt_index).transpose(1, 2, 3, 0, 4).reshape(3, 3, 96, 1024)
    spread = [line_spread(share[e]) for e in range(3)]

    source = rows_own.astype(F32)
    own_low = (norm_parts(source) * gain_attn_f).astype(BF)
    source_all = jnp.concatenate([prompts.astype(F32), source[64:]], axis=0)
    unit_all = norm_parts(source_all)
    all_low = (unit_all * gain_attn_f).astype(BF)
    q = dot_nn(own_low, w_q).astype(BF)
    k = dot_nn(all_low, w_kv[0]).astype(BF)
    v = dot_nn(all_low, w_kv[1]).astype(BF)
    onehot = jnp.where(bucket_table[:, None] == jnp.arange(BUCKETS, dtype=jnp.int32)[None, :], 1.0, 0.0)
    bias_by_dist = lax.dot_general(bias_f, onehot, (((0,), (1,)), ((), ())), precision=precise)
    windows = bias_windows(bias_by_dist, ctx_index)
    probs, mixed = attend(windows, q, k, v)
    hidden = source + dot_nn(mixed, w_o)
    normed = (norm_parts(hidden) * gain_ffn_f).astype(BF)

    cot_parts = spread_plane(after(cot_marked, w_q))
    marks_all = jnp.stack([v[160] for v in cot_parts])[:, :480].reshape(2560, 3).astype(F32)
    marks_all = jnp.pad(marks_all, ((0, 0), (0, 5)))
    g_all = jnp.concatenate([v[:160] for v in cot_parts], axis=0)
    x_all = jnp.concatenate(spread_plane(normed), axis=0)
    prev, scores, dh, win = None, [], [], []
    for e in range(3):
        out, dx, dh_e, win_e, s_e = expert_call(e, idx, x_all, g_all, marks_all, spread[e], prev, scores)
        prev = (out, dx)
        scores.append(s_e)
        dh.append(dh_e)
        win.append(win_e)
    out, dx = prev

    grad_normed_ffn = collect_plane(dx)
    bulk = []
    for e in range(3):
        gw = dot_tn(dh[e], x_all).astype(BF).reshape(2, 4, 96, 1024)
        dw = dot_tn(win[e], g_all).astype(BF).reshape(1, 4, 96, 1024)
        both = jnp.concatenate([gw, dw], axis=0)
        if e == 2:
            router_part = both[0, 0, 88:91].astype(F32)
        bulk.append(line_collect(lambda n: lax.dynamic_index_in_dim(both, n, 1, keepdims=False), z))
    combined = collect_plane(after(out, grad_normed_ffn))
    output = (hidden + combined).astype(BF).reshape(1, 1, 320, 1024)

    back = jnp.stack(bulk).reshape(3, 3, 96, 4, 256).transpose(3, 0, 1, 2, 4)
    back = trade_wt(back, wt_index)[:, :, :, :88].transpose(1, 2, 0, 3, 4).reshape(3, 3, 352, 256).astype(F32)
    res_gate, res_up, res_down = back[:, 0].transpose(0, 2, 1), back[:, 1].transpose(0, 2, 1), back[:, 2]

    grad_final = cot.astype(F32)
    unused, pull = jax.vjp(rms_norm, hidden, gain_ffn_f)
    grad_part, gain_ffn_part = pull(grad_normed_ffn)
    grad_hidden = grad_final + grad_part
    grad_hidden_low = grad_hidden.astype(BF)
    grad_mixed = dot_nt(grad_hidden_low, w_o).astype(BF)
    dq, dk, dv, dbias = attend_back(probs, q, k, v, grad_mixed)

    gn_all = dot_nt(dk, w_kv[0]) + dot_nt(dv, w_kv[1])
    gn_q = dot_nt(dq, w_q)
    gp = gn_all[:512].astype(BF).reshape(4, 2, 64, 1024)
    gp_keep = lax.dynamic_index_in_dim(gp, y, 1, keepdims=False)
    gp_sum = add_low(gp_keep, move_y(lax.dynamic_index_in_dim(gp, 1 - y, 1, keepdims=False)))
    gp_at = lambda n: lax.dynamic_index_in_dim(gp_sum, (z + n) % 4, 0, keepdims=False)
    gp_own = gp_at(0).astype(F32)
    for s in (1, 2, 3):
        gp_own = gp_own + shift_z(gp_at(s), s).astype(F32)
    gn_own = gn_q + jnp.concatenate([gp_own, gn_all[512:]], axis=0)
    unused, pull = jax.vjp(rms_norm, source, gain_attn_f)
    grad_source, unused = pull(gn_own)
    grad_tokens = (grad_hidden + grad_source).astype(BF).reshape(1, 1, 320, 1024)
    gain_attn_part = jnp.sum(gn_all * unit_all, axis=0) + jnp.sum(gn_q * norm_parts(source), axis=0)

    bias_rows = bias_windows_back(dbias, ctx_index)
    bias_part = jnp.dot(bias_rows, onehot, precision=precise)
    smalls = jnp.concatenate(
        [gain_attn_part[None], gain_ffn_part[None], router_part, jnp.pad(bias_part.reshape(1, 512), ((0, 0), (0, 512))),
         jnp.zeros((2, 1024), F32)], axis=0
    )
    smalls = sum_all(smalls)
    mine = lax.dynamic_slice_in_dim(smalls, wt_index * 256, 256, 1)
    res_gain_attn, res_gain_ffn, res_router = mine[0], mine[1], mine[2:5].T
    res_bias = lax.dynamic_slice_in_dim(smalls[5, :512].reshape(16, 32), wt_index * 4, 4, 0).T

    grads = jnp.stack(
        [dot_tn(own_low, dq).astype(BF), dot_tn(all_low, dk).astype(BF), dot_tn(all_low, dv).astype(BF),
         dot_tn(mixed, grad_hidden_low).astype(BF)]
    ).reshape(4, 2, 2, 256, 1024)
    pick = lambda v, n, d: lax.dynamic_index_in_dim(v, n, d, keepdims=False)
    t = add_low(pick(grads, c, 2), move_c(pick(grads, 1 - c, 2)))
    ta, tb = t[:2].reshape(2, 2, 256, 4, 2, 128), t[2:].reshape(2, 2, 256, 4, 2, 128)
    ta = add_low(pick(ta, x, 1), move_x(pick(ta, 1 - x, 1)))
    tb = add_low(pick(tb, y, 4), move_y(pick(tb, 1 - y, 4)))
    ta = add_low(pick(ta, y, 3), move_y(pick(ta, 1 - y, 3)))
    tb = add_low(pick(tb, x, 1), move_x(pick(tb, 1 - x, 1)))
    tz = jnp.concatenate([ta, tb], axis=0)
    tot = pick(tz, z, 2).astype(F32)
    for s in (1, 2, 3):
        tot = tot + shift_z(pick(tz, (z + s) % 4, 2), s).astype(F32)
    return (
        output, grad_tokens, tot[0], tot[1], tot[2], tot[3], res_gain_attn, res_gain_ffn, res_router, res_bias,
        res_gate, res_up, res_down,
    )


def solution(mesh):
    fast = mesh.shape["ctx"] == FAST_CTX and mesh.shape["wt"] == FAST_WT
    return jax.shard_map(
        local_fast if fast else local,
        mesh=mesh,
        in_specs=(
            P("wt", "ctx", None, None),
            P("wt", "ctx", None, None),
            P("wt", "ctx"),
            P("wt", "ctx"),
            P("wt", "ctx"),
            P("wt", "ctx"),
            P("wt"),
            P("wt"),
            P("wt", None),
            P(None, "wt"),
            P(None, "wt", "ctx"),
            P(None, "wt", "ctx"),
            P(None, "ctx", "wt"),
            P(),
            P("wt", "ctx", None, None),
            P("wt", "ctx", None),
        ),
        out_specs=(
            P("wt", "ctx", None, None),
            P("wt", "ctx", None, None),
            P("wt", "ctx"),
            P("wt", "ctx"),
            P("wt", "ctx"),
            P("wt", "ctx"),
            P("wt"),
            P("wt"),
            P("wt", None),
            P(None, "wt"),
            P(None, "wt", "ctx"),
            P(None, "wt", "ctx"),
            P(None, "ctx", "wt"),
        ),
        check_vma=False,
    )
```

```python
import functools

import jax
import jax.numpy as jnp
from jax import lax
from jax.experimental import pallas as pl
from jax.experimental.pallas import tpu as pltpu
from jax.sharding import PartitionSpec as P

HEADS = 16
HEAD_DIM = 64
BUCKETS = 32
EXPERTS = 3
TOP = 2
LEN = 256
CAP = 267


epsilon = 1e-06
precise = lax.Precision.HIGHEST


def rms_norm(values, gain_vec):
    return (
        values * lax.rsqrt(jnp.mean(values * values, axis=-1, keepdims=True) + epsilon) * gain_vec
    )


def gelu_product(gate_pre, up_pre):
    return jax.nn.gelu(gate_pre, approximate=True) * up_pre


def routing(expert_ids, priority, capacity, expert_count):
    tok_rows = expert_ids.shape[0]
    top_count = expert_ids.shape[1]
    expert = expert_ids.T.reshape(-1)
    rank_key = (
        jnp.arange(top_count, dtype=jnp.int32)[:, None] * tok_rows + priority[None, :]
    ).reshape(-1)
    earlier = (expert[:, None] == expert[None, :]) & (rank_key[None, :] < rank_key[:, None])
    places = jnp.sum(earlier.astype(jnp.int32), axis=1)
    keep_mask = places < capacity
    slot_ids = expert * capacity + jnp.minimum(places, capacity - 1)
    slot_hits = jnp.where(
        (slot_ids[:, None] == jnp.arange(expert_count * capacity, dtype=jnp.int32)[None, :])
        & keep_mask[:, None],
        1.0,
        0.0,
    )
    dispatch = jnp.sum(slot_hits.reshape(top_count, tok_rows, expert_count * capacity), axis=0).T
    return (keep_mask, slot_ids, slot_hits, dispatch)


def gate_values(logits, expert_ids, keep_mask):
    chances = jax.nn.softmax(logits, axis=-1)
    picked = jnp.take_along_axis(chances, expert_ids, axis=1).T.reshape(-1)
    return jnp.where(keep_mask, picked, 0.0)


def toeplitz(reversed_bias, top_start, row_total, key_total):
    window_len = row_total + key_total
    window = lax.dynamic_slice_in_dim(reversed_bias, top_start, window_len, 1)
    tiled = jnp.tile(window, (1, row_total))[:, : row_total * (window_len - 1)]
    return tiled.reshape(window.shape[0], row_total, window_len - 1)[:, :, row_total - 1 :]


def toeplitz_back(grad_block, row_total, key_total):
    window_len = row_total + key_total
    head_total = grad_block.shape[0]
    placed = jnp.pad(grad_block, ((0, 0), (0, 0), (row_total - 1, 0))).reshape(
        head_total, row_total * (window_len - 1)
    )
    placed = jnp.pad(placed, ((0, 0), (0, row_total)))
    return jnp.sum(placed.reshape(head_total, row_total, window_len), axis=1)


def add_window(table, piece, start):
    current = lax.dynamic_slice_in_dim(table, start, piece.shape[1], 1)
    return lax.dynamic_update_slice_in_dim(table, current + piece, start, 1)


def sweep(step_fn, start_state, prompt_items, local_items):
    state_mid, stacked = lax.scan(step_fn, start_state, prompt_items)
    state_end, last_out = step_fn(state_mid, local_items)
    return (state_end, stacked, last_out)


def local(
    tokens,
    cotangent,
    w_query,
    w_key,
    w_value,
    w_out,
    gain_attn,
    gain_ffn,
    w_router,
    rel_bias,
    exp_gate,
    exp_up,
    exp_down,
    bucket_table,
    expert_ids,
    priority,
):
    tok_rows = tokens.shape[2]
    model_width = tokens.shape[3]
    ctx_count = lax.axis_size("ctx")
    my_block = lax.axis_index("ctx")
    prompt_rows = tok_rows - LEN
    cont_rows = tok_rows - prompt_rows
    prompt_len = prompt_rows * ctx_count
    dist_count = bucket_table.shape[0]
    head_count = HEADS
    head_width = HEAD_DIM
    score_scale = HEAD_DIM ** (-0.5)
    steps_count = max(1, ctx_count // 8)
    block_keys = prompt_len // steps_count
    cols_query, cols_key, cols_value, cols_out, cols_gate, cols_up, cols_down = (
        lax.all_gather(w_query, "ctx", axis=1, tiled=True),
        lax.all_gather(w_key, "ctx", axis=1, tiled=True),
        lax.all_gather(w_value, "ctx", axis=1, tiled=True),
        lax.all_gather(w_out, "ctx", axis=1, tiled=True),
        lax.all_gather(exp_gate, "ctx", axis=2, tiled=True),
        lax.all_gather(exp_up, "ctx", axis=2, tiled=True),
        lax.all_gather(exp_down, "ctx", axis=1, tiled=True),
    )
    gathered = (
        lax.all_gather(cols_query, "wt", axis=0, tiled=True),
        lax.all_gather(cols_key, "wt", axis=0, tiled=True),
        lax.all_gather(cols_value, "wt", axis=0, tiled=True),
        lax.all_gather(cols_out, "wt", axis=0, tiled=True),
        lax.all_gather(cols_gate, "wt", axis=1, tiled=True),
        lax.all_gather(cols_up, "wt", axis=1, tiled=True),
        lax.all_gather(cols_down, "wt", axis=2, tiled=True),
        lax.all_gather(gain_attn, "wt", axis=0, tiled=True),
        lax.all_gather(gain_ffn, "wt", axis=0, tiled=True),
        lax.all_gather(w_router, "wt", axis=0, tiled=True),
        lax.all_gather(rel_bias, "wt", axis=1, tiled=True),
    )
    (
        full_query,
        full_key,
        full_value,
        full_out,
        full_gate,
        full_up,
        full_down,
        full_gain_attn,
        full_gain_ffn,
        full_router,
        full_bias,
    ) = gathered
    gain_attn_f = full_gain_attn.astype(jnp.float32)
    gain_ffn_f = full_gain_ffn.astype(jnp.float32)
    source = tokens[0, 0].astype(jnp.float32)
    normed_attn = rms_norm(source, gain_attn_f)
    normed_attn_low = normed_attn.astype(jnp.bfloat16)
    query_low = jnp.dot(normed_attn_low, full_query, preferred_element_type=jnp.float32).astype(
        jnp.bfloat16
    )
    key_low = jnp.dot(normed_attn_low, full_key, preferred_element_type=jnp.float32).astype(
        jnp.bfloat16
    )
    value_low = jnp.dot(normed_attn_low, full_value, preferred_element_type=jnp.float32).astype(
        jnp.bfloat16
    )
    far_keys, far_values = (
        lax.all_gather(key_low[:prompt_rows], "ctx", axis=0, tiled=True),
        lax.all_gather(value_low[:prompt_rows], "ctx", axis=0, tiled=True),
    )
    row_index = jnp.arange(tok_rows, dtype=jnp.int32)
    query_pos = jnp.where(
        row_index < prompt_rows,
        my_block * prompt_rows + row_index,
        prompt_len + row_index - prompt_rows,
    )
    bucket_onehot = jnp.where(
        bucket_table[:, None] == jnp.arange(BUCKETS, dtype=jnp.int32)[None, :], 1.0, 0.0
    )
    bias_rows = jnp.dot(bucket_onehot, full_bias.astype(jnp.float32), precision=precise).T
    reversed_bias = jnp.concatenate([bias_rows[:, ::-1], jnp.zeros_like(bias_rows)], axis=1)
    prompt_starts = jnp.arange(steps_count, dtype=jnp.int32) * block_keys
    local_start = jnp.asarray(prompt_len, dtype=jnp.int32)
    query_heads = query_low.reshape(tok_rows, head_count, head_width)

    def blocks_of(far_array):
        return far_array.reshape(steps_count, block_keys, model_width)

    def window_starts(key_start):
        prompt_top = dist_count - my_block * prompt_rows + key_start - prompt_rows
        cont_top = dist_count - prompt_len + key_start - cont_rows
        return (prompt_top, cont_top)

    def block_scores(key_block, key_start):
        key_total = key_block.shape[0]
        key_heads = key_block.reshape(key_total, head_count, head_width)
        logit_raw = (
            jnp.einsum("qhd,khd->hqk", query_heads, key_heads, preferred_element_type=jnp.float32)
            * score_scale
        )
        key_pos = key_start + jnp.arange(key_total, dtype=jnp.int32)
        offset = query_pos[:, None] - key_pos[None, :]
        prompt_top, cont_top = window_starts(key_start)
        bias_block = jnp.concatenate(
            [
                toeplitz(reversed_bias, prompt_top, prompt_rows, key_total),
                toeplitz(reversed_bias, cont_top, cont_rows, key_total),
            ],
            axis=1,
        )
        return jnp.where(offset[None] >= 0, logit_raw + bias_block, -1e30)

    def stats_step(state_in, block_item):
        run_max, run_sum = state_in
        scores = block_scores(block_item[0], block_item[1])
        new_max = jnp.maximum(run_max, jnp.max(scores, axis=-1))
        new_sum = run_sum * jnp.exp(run_max - new_max) + jnp.sum(
            jnp.exp(scores - new_max[..., None]), axis=-1
        )
        return ((new_max, new_sum), None)

    start_stats = (
        jnp.full((head_count, tok_rows), -1e30, jnp.float32),
        jnp.zeros((head_count, tok_rows), jnp.float32),
    )
    (row_max, row_sum), unused_a, unused_b = sweep(
        stats_step,
        start_stats,
        (blocks_of(far_keys), prompt_starts),
        (key_low[prompt_rows:], local_start),
    )

    def mix_step(state_in, block_item):
        scores = block_scores(block_item[0], block_item[2])
        weights = (jnp.exp(scores - row_max[..., None]) / row_sum[..., None]).astype(jnp.bfloat16)
        value_heads = block_item[1].reshape(-1, head_count, head_width)
        return (
            state_in
            + jnp.einsum("hqk,khd->qhd", weights, value_heads, preferred_element_type=jnp.float32),
            None,
        )

    mixed_exact, unused_c, unused_d = sweep(
        mix_step,
        jnp.zeros((tok_rows, head_count, head_width), jnp.float32),
        (blocks_of(far_keys), blocks_of(far_values), prompt_starts),
        (key_low[prompt_rows:], value_low[prompt_rows:], local_start),
    )
    mixed_low = mixed_exact.reshape(tok_rows, model_width).astype(jnp.bfloat16)
    hidden = source + jnp.dot(mixed_low, full_out, preferred_element_type=jnp.float32)
    normed_ffn_low = rms_norm(hidden, gain_ffn_f).astype(jnp.bfloat16)
    route_ids = expert_ids[0, 0]
    keep_mask, slot_ids, slot_hits, dispatch = routing(route_ids, priority[0, 0], CAP, EXPERTS)
    inputs = (
        jnp.dot(dispatch.astype(jnp.bfloat16), normed_ffn_low, preferred_element_type=jnp.float32)
        .astype(jnp.bfloat16)
        .reshape(EXPERTS, CAP, model_width)
    )
    gate_pre = jnp.einsum("ecd,edf->ecf", inputs, full_gate, preferred_element_type=jnp.float32)
    up_pre = jnp.einsum("ecd,edf->ecf", inputs, full_up, preferred_element_type=jnp.float32)
    inner_low = gelu_product(gate_pre, up_pre).astype(jnp.bfloat16)
    expert_out = jnp.einsum(
        "ecf,efd->ecd", inner_low, full_down, preferred_element_type=jnp.float32
    ).reshape(EXPERTS * CAP, model_width)
    logits = jnp.dot(normed_ffn_low, full_router, preferred_element_type=jnp.float32)
    weight_pair = gate_values(logits, route_ids, keep_mask)
    picked_rows = jnp.take(expert_out, slot_ids, axis=0)
    combined = jnp.sum(
        (picked_rows * weight_pair[:, None]).reshape(TOP, tok_rows, model_width), axis=0
    )
    output = (hidden + combined).astype(jnp.bfloat16).reshape(1, 1, tok_rows, model_width)
    back_keys, back_values = (far_keys, far_values)
    (
        back_query,
        back_key,
        back_value,
        back_out,
        back_gate,
        back_up,
        back_down,
        back_gain_attn,
        back_gain_ffn,
        back_router,
        back_bias,
    ) = gathered
    grad_final = cotangent[0, 0].astype(jnp.float32)
    grad_pair = jnp.where(
        keep_mask, jnp.sum(jnp.tile(grad_final, (TOP, 1)) * picked_rows, axis=-1), 0.0
    )
    slot_weight = jnp.dot(weight_pair, slot_hits, precision=precise)
    grad_expert_out = (
        (jnp.dot(dispatch, grad_final, precision=precise) * slot_weight[:, None])
        .astype(jnp.bfloat16)
        .reshape(EXPERTS, CAP, model_width)
    )
    grad_inner = jnp.einsum(
        "ecd,efd->ecf", grad_expert_out, back_down, preferred_element_type=jnp.float32
    )
    unused_e, inner_pull = jax.vjp(gelu_product, gate_pre, up_pre)
    grad_gate_pre, grad_up_pre = inner_pull(grad_inner)
    grad_gate_low = grad_gate_pre.astype(jnp.bfloat16)
    grad_up_low = grad_up_pre.astype(jnp.bfloat16)
    grad_gate_w = jnp.einsum(
        "ecd,ecf->edf", inputs, grad_gate_low, preferred_element_type=jnp.float32
    )
    grad_up_w = jnp.einsum("ecd,ecf->edf", inputs, grad_up_low, preferred_element_type=jnp.float32)
    grad_down_w = jnp.einsum(
        "ecf,ecd->efd", inner_low, grad_expert_out, preferred_element_type=jnp.float32
    )
    grad_inputs = jnp.einsum(
        "ecf,edf->ecd", grad_gate_low, back_gate, preferred_element_type=jnp.float32
    ) + jnp.einsum("ecf,edf->ecd", grad_up_low, back_up, preferred_element_type=jnp.float32)

    def gate_of_logits(logit_values):
        return gate_values(logit_values, route_ids, keep_mask)

    unused_f, gate_pull = jax.vjp(gate_of_logits, logits)
    (grad_logits,) = gate_pull(grad_pair)
    grad_router_w = jnp.dot(normed_ffn_low.astype(jnp.float32).T, grad_logits, precision=precise)
    grad_normed_ffn = jnp.dot(grad_logits, back_router.astype(jnp.float32).T, precision=precise)
    grad_normed_ffn = grad_normed_ffn + jnp.dot(
        dispatch.T, grad_inputs.reshape(EXPERTS * CAP, model_width), precision=precise
    )
    unused_g, ffn_norm_pull = jax.vjp(rms_norm, hidden, back_gain_ffn.astype(jnp.float32))
    grad_hidden_part, grad_gain_ffn_w = ffn_norm_pull(grad_normed_ffn)
    grad_hidden = grad_final + grad_hidden_part
    grad_hidden_low = grad_hidden.astype(jnp.bfloat16)
    grad_out_w = jnp.dot(mixed_low.T, grad_hidden_low, preferred_element_type=jnp.float32)
    grad_mixed = jnp.dot(grad_hidden_low, back_out.T, preferred_element_type=jnp.float32).astype(
        jnp.bfloat16
    )
    grad_mixed_heads = grad_mixed.reshape(tok_rows, head_count, head_width)
    row_delta = jnp.sum(grad_mixed_heads.astype(jnp.float32) * mixed_exact, axis=-1).T

    def grad_step(state_in, block_item):
        grad_query_acc, grad_reversed = state_in
        key_block, value_block, key_start = block_item
        key_total = key_block.shape[0]
        scores = block_scores(key_block, key_start)
        chances = jnp.exp(scores - row_max[..., None]) / row_sum[..., None]
        value_heads = value_block.reshape(-1, head_count, head_width)
        key_heads = key_block.reshape(-1, head_count, head_width)
        grad_chance = jnp.einsum(
            "qhd,khd->hqk", grad_mixed_heads, value_heads, preferred_element_type=jnp.float32
        )
        grad_value_block = jnp.einsum(
            "hqk,qhd->khd",
            chances.astype(jnp.bfloat16),
            grad_mixed_heads,
            preferred_element_type=jnp.float32,
        )
        grad_scores = chances * (grad_chance - row_delta[..., None])
        prompt_top, cont_top = window_starts(key_start)
        grad_reversed = add_window(
            grad_reversed,
            toeplitz_back(grad_scores[:, :prompt_rows], prompt_rows, key_total),
            prompt_top,
        )
        grad_reversed = add_window(
            grad_reversed,
            toeplitz_back(grad_scores[:, prompt_rows:], cont_rows, key_total),
            cont_top,
        )
        grad_scores_low = grad_scores.astype(jnp.bfloat16)
        grad_query_acc = grad_query_acc + score_scale * jnp.einsum(
            "hqk,khd->qhd", grad_scores_low, key_heads, preferred_element_type=jnp.float32
        )
        grad_key_block = score_scale * jnp.einsum(
            "hqk,qhd->khd", grad_scores_low, query_heads, preferred_element_type=jnp.float32
        )
        return (
            (grad_query_acc, grad_reversed),
            (grad_key_block.reshape(-1, model_width), grad_value_block.reshape(-1, model_width)),
        )

    start_grads = (
        jnp.zeros((tok_rows, head_count, head_width), jnp.float32),
        jnp.zeros((head_count, 2 * dist_count), jnp.float32),
    )
    (
        (grad_query_exact, grad_reversed),
        (far_grad_keys, far_grad_values),
        (near_grad_keys, near_grad_values),
    ) = sweep(
        grad_step,
        start_grads,
        (blocks_of(back_keys), blocks_of(back_values), prompt_starts),
        (key_low[prompt_rows:], value_low[prompt_rows:], local_start),
    )
    own_grad_keys, own_grad_values = (
        lax.psum_scatter(
            far_grad_keys.reshape(prompt_len, model_width), "ctx", scatter_dimension=0, tiled=True
        ),
        lax.psum_scatter(
            far_grad_values.reshape(prompt_len, model_width), "ctx", scatter_dimension=0, tiled=True
        ),
    )
    grad_key_low = jnp.concatenate([own_grad_keys, near_grad_keys], axis=0).astype(jnp.bfloat16)
    grad_value_low = jnp.concatenate([own_grad_values, near_grad_values], axis=0).astype(
        jnp.bfloat16
    )
    grad_query_low = grad_query_exact.reshape(tok_rows, model_width).astype(jnp.bfloat16)
    grad_query_w = jnp.dot(normed_attn_low.T, grad_query_low, preferred_element_type=jnp.float32)
    grad_key_w = jnp.dot(normed_attn_low.T, grad_key_low, preferred_element_type=jnp.float32)
    grad_value_w = jnp.dot(normed_attn_low.T, grad_value_low, preferred_element_type=jnp.float32)
    grad_normed_attn = jnp.dot(grad_query_low, back_query.T, preferred_element_type=jnp.float32)
    grad_normed_attn = grad_normed_attn + jnp.dot(
        grad_key_low, back_key.T, preferred_element_type=jnp.float32
    )
    grad_normed_attn = grad_normed_attn + jnp.dot(
        grad_value_low, back_value.T, preferred_element_type=jnp.float32
    )
    unused_h, attn_norm_pull = jax.vjp(rms_norm, source, back_gain_attn.astype(jnp.float32))
    grad_source_part, grad_gain_attn_w = attn_norm_pull(grad_normed_attn)
    grad_tokens = (
        (grad_hidden + grad_source_part).astype(jnp.bfloat16).reshape(1, 1, tok_rows, model_width)
    )
    grad_bias_rows = grad_reversed[:, :dist_count][:, ::-1]
    grad_bias_w = jnp.dot(bucket_onehot.T, grad_bias_rows.T, precision=precise)
    small_gain_attn, small_gain_ffn, small_router, small_bias = lax.psum(
        (grad_gain_attn_w, grad_gain_ffn_w, grad_router_w, grad_bias_w), "ctx"
    )
    row_parts = (
        lax.psum_scatter(
            grad_query_w.astype(jnp.bfloat16), "wt", scatter_dimension=0, tiled=True
        ).astype(jnp.float32),
        lax.psum_scatter(
            grad_key_w.astype(jnp.bfloat16), "wt", scatter_dimension=0, tiled=True
        ).astype(jnp.float32),
        lax.psum_scatter(
            grad_value_w.astype(jnp.bfloat16), "wt", scatter_dimension=0, tiled=True
        ).astype(jnp.float32),
        lax.psum_scatter(
            grad_out_w.astype(jnp.bfloat16), "wt", scatter_dimension=0, tiled=True
        ).astype(jnp.float32),
        lax.psum_scatter(
            grad_gate_w.astype(jnp.bfloat16), "wt", scatter_dimension=1, tiled=True
        ).astype(jnp.float32),
        lax.psum_scatter(
            grad_up_w.astype(jnp.bfloat16), "wt", scatter_dimension=1, tiled=True
        ).astype(jnp.float32),
        lax.psum_scatter(
            grad_down_w.astype(jnp.bfloat16), "wt", scatter_dimension=2, tiled=True
        ).astype(jnp.float32),
        lax.psum_scatter(
            small_gain_attn.astype(jnp.bfloat16), "wt", scatter_dimension=0, tiled=True
        ).astype(jnp.float32),
        lax.psum_scatter(
            small_gain_ffn.astype(jnp.bfloat16), "wt", scatter_dimension=0, tiled=True
        ).astype(jnp.float32),
        lax.psum_scatter(
            small_router.astype(jnp.bfloat16), "wt", scatter_dimension=0, tiled=True
        ).astype(jnp.float32),
        lax.psum_scatter(
            small_bias.astype(jnp.bfloat16), "wt", scatter_dimension=1, tiled=True
        ).astype(jnp.float32),
    )
    res_query, res_key, res_value, res_out, res_gate, res_up, res_down = (
        lax.psum_scatter(row_parts[0], "ctx", scatter_dimension=1, tiled=True),
        lax.psum_scatter(row_parts[1], "ctx", scatter_dimension=1, tiled=True),
        lax.psum_scatter(row_parts[2], "ctx", scatter_dimension=1, tiled=True),
        lax.psum_scatter(row_parts[3], "ctx", scatter_dimension=1, tiled=True),
        lax.psum_scatter(row_parts[4], "ctx", scatter_dimension=2, tiled=True),
        lax.psum_scatter(row_parts[5], "ctx", scatter_dimension=2, tiled=True),
        lax.psum_scatter(row_parts[6], "ctx", scatter_dimension=1, tiled=True),
    )
    res_gain_attn, res_gain_ffn, res_router, res_bias = (
        row_parts[7],
        row_parts[8],
        row_parts[9],
        row_parts[10],
    )
    return (
        output,
        grad_tokens,
        res_query,
        res_key,
        res_value,
        res_out,
        res_gain_attn,
        res_gain_ffn,
        res_router,
        res_bias,
        res_gate,
        res_up,
        res_down,
    )


BF = jnp.bfloat16
F32 = jnp.float32
FAST_CTX = 8
FAST_WT = 4
NEG = -1e30

SWAP_Y = [(i, i ^ 1) for i in range(8)]
LINES_Z = [[0, 2, 4, 6], [1, 3, 5, 7]]
PAIR_Z = [(i, i ^ 2) for i in range(8)]
FLIP_Z = [(i, i ^ 6) for i in range(8)]
SWAP_C = [(i, i ^ 1) for i in range(4)]
SWAP_X = [(i, i ^ 2) for i in range(4)]


def move_y(v):
    return lax.ppermute(v, "ctx", SWAP_Y)


def move_x(v):
    return lax.ppermute(v, "wt", SWAP_X)


def move_c(v):
    return lax.ppermute(v, "wt", SWAP_C)


def pair_z(v):
    return lax.ppermute(v, "ctx", PAIR_Z)


def flip_z(v):
    return lax.ppermute(v, "ctx", FLIP_Z)


def phase(*vals):
    return lax.optimization_barrier(vals)


def dot_nt(a, b):
    return lax.dot_general(a, b, (((1,), (1,)), ((), ())), preferred_element_type=F32)


def dot_tn(a, b):
    return lax.dot_general(a, b, (((0,), (0,)), ((), ())), preferred_element_type=F32)


def dot_nn(a, b):
    return jnp.dot(a, b, preferred_element_type=F32)


def params(limit=56 * 2**20):
    return pltpu.CompilerParams(vmem_limit_bytes=limit)


COST_S = pl.CostEstimate(flops=10**6, bytes_accessed=10**6, transcendentals=0)
COST_E = pl.CostEstimate(flops=10**6, bytes_accessed=10**6, transcendentals=0)
ANY = pl.BlockSpec(memory_space=pl.ANY)
SMEM = pl.BlockSpec(memory_space=pltpu.SMEM)


def spread_z(v):
    near, opp = pair_z(v), flip_z(v)
    return {0: v, 1: near, 3: opp, 2: pair_z(opp)}


def attend_kernel(sz, first, x_first, idx, n_ref, w_ref, *refs):
    pieces, refs = refs[:2], refs[2:]
    if not first:
        refs = refs[4:]
    p_ref, o_ref, qkv_ref, wt_ref, bc_ref, bp_ref, qs_ref = refs
    z, y, x, c = idx[0], idx[1], idx[2], idx[3]
    step = pl.program_id(0)
    for ry in range(2):

        @pl.when(step == ry)
        def _(ry=ry):
            for rx in range(2):
                for rc in range(2):
                    row = pl.multiple_of(((x ^ rx) * 2 + (c ^ rc)) * 256, 256)
                    for t in range(3):
                        block = pieces[rc][ry, rx, t] if x_first else pieces[rc][rx, ry, t]
                        wt_ref[0, pl.ds(row, 256), 128 * t : 128 * t + 128] = block

    qkv = dot_nn(n_ref[...], wt_ref[0]).astype(BF)
    qkv_ref[0] = qkv
    k, v = qkv[:, 128:256], qkv[:, 256:]
    qs_ref[...] = qkv[:, :128]
    q_c = qs_ref[512:, :]
    q_p = qs_ref[pl.ds(pl.multiple_of((z * 2 + y) * 64, 64), 64), :]
    lane = lax.broadcasted_iota(jnp.int32, (1, 128), 1)
    outs = []
    for h in range(2):
        base_c, base_p = w_ref[h, 0], w_ref[h, 1]
        for a in range(32):
            bc_ref[8 * a : 8 * a + 8, :] = pltpu.roll(base_c, 1024 - (248 - 8 * a), 1)[:, :768]
        for a in range(8):
            shift = 56 - 8 * a
            bp_ref[8 * a : 8 * a + 8, :] = (pltpu.roll(base_p, 1024 - shift, 1) if shift else base_p)[:, :512]
        mine = (lane < 64) if h == 0 else (lane >= 64)
        head = lambda t: jnp.where(mine, t, jnp.zeros_like(t))
        sc = dot_nt(head(q_c), k) * 0.125 + bc_ref[...]
        sp = dot_nt(head(q_p), k[:512]) * 0.125 + bp_ref[...]

        def soft(t):
            e = jnp.exp(t - jnp.max(t, axis=-1, keepdims=True))
            return (e * (1.0 / jnp.sum(e, axis=-1, keepdims=True))).astype(BF)

        pc, pp = soft(sc), soft(sp)
        p_ref[h, 64:, :] = pc
        p_ref[h, :64, :512] = pp
        p_ref[h, :64, 512:] = jnp.zeros((64, 256), BF)
        outs.append(jnp.concatenate([dot_nn(pp, v[:512]), dot_nn(pc, v)], axis=0))
    o_ref[...] = jnp.where(lane < 64, outs[0], outs[1]).astype(BF)


def attend(sz, x_first, idx, normed, windows, pieces, prev):
    keys, rows = normed.shape[0], 320
    at = lambda i, d: (d[0] ^ sz) * 2 + (d[1] ^ i)
    whole = pl.BlockSpec(memory_space=pltpu.VMEM)
    return pl.pallas_call(
        functools.partial(attend_kernel, sz, prev is None, x_first),
        grid_spec=pltpu.PrefetchScalarGridSpec(
            num_scalar_prefetch=1,
            grid=(2,),
            in_specs=[whole, pl.BlockSpec((2, 2, 8, 1024), lambda i, d: (at(i, d), 0, 0, 0))]
            + [whole] * 2
            + ([] if prev is None else [ANY] * 4),
            out_specs=(
                pl.BlockSpec((2, rows, keys), lambda i, d: (at(i, d), 0, 0)),
                pl.BlockSpec((rows, 128), lambda i, d: (0, at(i, d))),
                pl.BlockSpec((1, keys, 384), lambda i, d: (at(i, d), 0, 0)),
                pl.BlockSpec((1, 1024, 384), lambda i, d: (at(i, d), 0, 0)),
            ),
            scratch_shapes=[pltpu.VMEM((256, 768), F32), pltpu.VMEM((64, 512), F32), pltpu.VMEM((keys, 128), BF)],
        ),
        out_shape=(
            jax.ShapeDtypeStruct((16, rows, keys), BF),
            jax.ShapeDtypeStruct((rows, 1024), BF),
            jax.ShapeDtypeStruct((8, keys, 384), BF),
            jax.ShapeDtypeStruct((8, 1024, 384), BF),
        ),
        input_output_aliases={} if prev is None else {5 + n: n for n in range(4)},
        compiler_params=params(),
        cost_estimate=COST_S,
    )(idx, normed, windows, *pieces, *([] if prev is None else prev))


def attend_back_kernel(first, idx, n_ref, p_ref, qkv_ref, wt_ref, g_ref, m_ref, gl_ref, *refs):
    if not first:
        gn_prev, refs = refs[0], refs[2:]
    keep_ref, send_ref, gn_ref, db_ref, dt_ref, qs_ref = refs
    z, y, x, c = idx[0], idx[1], idx[2], idx[3]
    own = pl.ds(pl.multiple_of((z * 2 + y) * 64, 64), 64)
    qkv = qkv_ref[0]
    k, v = qkv[:, 128:256], qkv[:, 256:]
    qs_ref[...] = qkv[:, :128]
    q = jnp.concatenate([qs_ref[own, :], qs_ref[512:, :]], axis=0)
    g = g_ref[...]
    lane = lax.broadcasted_iota(jnp.int32, (1, 128), 1)
    parts = []
    for h in range(2):
        mine = (lane < 64) if h == 0 else (lane >= 64)
        gh = jnp.where(mine, g, jnp.zeros_like(g))
        p = p_ref[h]
        pf = p.astype(F32)
        dp = dot_nt(gh, v)
        delta = jnp.sum(pf * dp, axis=-1, keepdims=True)
        ds = pf * (dp - delta)
        low = ds.astype(BF)
        acc_c = jnp.zeros((8, 1024), F32)
        for a in range(32):
            part = jnp.concatenate([ds[64 + 8 * a : 72 + 8 * a], jnp.zeros((8, 256), F32)], axis=1)
            acc_c = acc_c + pltpu.roll(part, 248 - 8 * a, 1) if a < 31 else acc_c + part
        acc_p = jnp.zeros((8, 1024), F32)
        for a in range(8):
            part = jnp.concatenate([ds[8 * a : 8 * a + 8, :512], jnp.zeros((8, 512), F32)], axis=1)
            acc_p = acc_p + (pltpu.roll(part, 56 - 8 * a, 1) if a < 7 else part)
        db_ref[h, 0] = acc_c
        db_ref[h, 1] = acc_p
        parts.append((dot_nn(low, k) * 0.125, dot_tn(low, q) * 0.125, dot_tn(p, g)))
    dq, dk, dv = [jnp.where(lane < 64, parts[0][n], parts[1][n]).astype(BF) for n in range(3)]
    dt_ref[:512, :128] = jnp.zeros((512, 128), BF)
    dt_ref[own, :128] = dq[:64]
    dt_ref[512:, :128] = dq[64:]
    dt_ref[:, 128:256] = dk
    dt_ref[:, 256:] = dv
    dt = dt_ref[...]
    dw = jnp.concatenate([dot_tn(n_ref[...], dt).astype(BF), dot_tn(m_ref[...], gl_ref[...]).astype(BF)], axis=1)
    for xx in range(2):
        for cc in range(2):
            block = dw[(xx * 2 + cc) * 256 : (xx * 2 + cc) * 256 + 256]

            @pl.when(c == cc)
            def _():
                keep_ref[x ^ xx, 0] = block

            @pl.when(c != cc)
            def _():
                send_ref[x ^ xx, 0] = block

    gn = dot_nt(dt, wt_ref[0])

    @pl.when(pl.program_id(0) == 0)
    def _():
        gn_ref[...] = gn if first else gn_prev[...] + gn

    @pl.when(pl.program_id(0) != 0)
    def _():
        gn_ref[...] += gn


def attend_back(base, count, idx, normed, p, qkv, wt, g, mixed, g_low, gn_prev, db_prev):
    rows, keys = p.shape[1], p.shape[2]
    at = lambda i, d: (i + base) ^ (d[0] * 2 + d[1])
    whole = pl.BlockSpec((keys, 1024), lambda i, d: (0, 0))
    return pl.pallas_call(
        functools.partial(attend_back_kernel, gn_prev is None),
        grid_spec=pltpu.PrefetchScalarGridSpec(
            num_scalar_prefetch=1,
            grid=(count,),
            in_specs=[
                whole,
                pl.BlockSpec((2, rows, keys), lambda i, d: (at(i, d), 0, 0)),
                pl.BlockSpec((1, keys, 384), lambda i, d: (at(i, d), 0, 0)),
                pl.BlockSpec((1, 1024, 384), lambda i, d: (at(i, d), 0, 0)),
                pl.BlockSpec((rows, 128), lambda i, d: (0, at(i, d))),
                pl.BlockSpec((rows, 1024), lambda i, d: (0, 0)),
                pl.BlockSpec((rows, 128), lambda i, d: (0, at(i, d))),
            ]
            + ([] if gn_prev is None else [whole, ANY]),
            out_specs=(
                pl.BlockSpec((2, 1, 256, 512), lambda i, d: (0, i, 0, 0)),
                pl.BlockSpec((2, 1, 256, 512), lambda i, d: (0, i, 0, 0)),
                whole,
                pl.BlockSpec((2, 2, 8, 1024), lambda i, d: (at(i, d), 0, 0, 0)),
            ),
            scratch_shapes=[pltpu.VMEM((keys, 384), BF), pltpu.VMEM((keys, 128), BF)],
        ),
        out_shape=(
            jax.ShapeDtypeStruct((2, count, 256, 512), BF),
            jax.ShapeDtypeStruct((2, count, 256, 512), BF),
            jax.ShapeDtypeStruct((keys, 1024), F32),
            jax.ShapeDtypeStruct((16, 2, 8, 1024), F32),
        ),
        input_output_aliases={} if gn_prev is None else {9: 3},
        compiler_params=params(),
        cost_estimate=COST_E,
    )(idx, normed, p, qkv, wt, g, mixed, g_low, *([] if gn_prev is None else [gn_prev, db_prev]))


def cut_rows(t):
    return t[:, :, :, :128], t[:, :, :, 128:]


def out_back_kernel(a_ref, b_ref, c_ref, h_ref, gain_ref, cot_ref, w_ref, gh_ref, gl_ref, gm_ref, gg_ref):
    f = lambda t: t.astype(F32)
    dn = f(a_ref[...]) + f(b_ref[...]) + f(c_ref[...])
    hidden, gain = h_ref[...], gain_ref[...]
    scale = lax.rsqrt(jnp.mean(hidden * hidden, axis=-1, keepdims=True) + epsilon)
    unit = hidden * scale
    gg_ref[...] = jnp.broadcast_to(jnp.sum(dn * unit, axis=0, keepdims=True), gg_ref.shape)
    du = dn * gain
    grad = f(cot_ref[...]) + scale * (du - unit * jnp.mean(du * unit, axis=-1, keepdims=True))
    gh_ref[...] = grad
    low = grad.astype(BF)
    gl_ref[...] = low
    gm_ref[...] = dot_nt(low, w_ref[...]).astype(BF)


def out_back(parts, hidden, gain, cot, w_o):
    whole = pl.BlockSpec(memory_space=pltpu.VMEM)
    return pl.pallas_call(
        out_back_kernel,
        in_specs=[whole] * 7,
        out_specs=(whole,) * 4,
        out_shape=(
            jax.ShapeDtypeStruct((320, 1024), F32),
            jax.ShapeDtypeStruct((320, 1024), BF),
            jax.ShapeDtypeStruct((320, 1024), BF),
            jax.ShapeDtypeStruct((8, 1024), F32),
        ),
        compiler_params=params(),
        cost_estimate=COST_S,
    )(*parts, hidden, gain[None], cot, w_o)


def out_kernel(idx, m_ref, s_ref, g_ref, a_ref, b_ref, h_ref, l_ref, w_ref):
    z, y, x, c = idx[0], idx[1], idx[2], idx[3]
    for rx in range(2):
        for ry in range(2):
            for n, sz in enumerate((0, 1, 3, 2)):
                col = pl.multiple_of(((z ^ sz) * 2 + (y ^ ry)) * 128, 128)
                for rc, ref in ((0, a_ref), (1, b_ref)):
                    row = pl.multiple_of(((x ^ rx) * 2 + (c ^ rc)) * 256, 256)
                    w_ref[pl.ds(row, 256), pl.ds(col, 128)] = ref[rx, ry, n]
    hidden = s_ref[...].astype(F32) + dot_nn(m_ref[...], w_ref[...])
    h_ref[...] = hidden
    scale = lax.rsqrt(jnp.mean(hidden * hidden, axis=-1, keepdims=True) + epsilon)
    l_ref[...] = (hidden * scale * g_ref[...]).astype(BF)


def project_out(idx, mixed, rows_own, gain, own, other):
    whole = pl.BlockSpec(memory_space=pltpu.VMEM)
    return pl.pallas_call(
        out_kernel,
        in_specs=[SMEM] + [whole] * 5,
        out_specs=(whole,) * 3,
        out_shape=(
            jax.ShapeDtypeStruct((320, 1024), F32),
            jax.ShapeDtypeStruct((320, 1024), BF),
            jax.ShapeDtypeStruct((1024, 1024), BF),
        ),
        compiler_params=params(),
        cost_estimate=COST_S,
    )(idx, mixed, rows_own, gain[None], own, other)


WIDE = 1920


def window_kernel(idx, t_ref, b_ref, o_ref):
    onehot = jnp.where(lax.broadcasted_iota(jnp.int32, (BUCKETS, WIDE), 0) == t_ref[...], 1.0, 0.0)
    rev = lax.dot_general(b_ref[...], onehot, (((0,), (0,)), ((), ())), precision=precise, preferred_element_type=F32)
    rev = jnp.where(lax.broadcasted_iota(jnp.int32, (16, WIDE), 1) < 768, rev, NEG)
    tail = pltpu.roll(rev, WIDE - 704 + 64 * (idx[0] * 2 + idx[1]), 1)
    for s in range(8):
        o_ref[:, 0, s, :] = (pltpu.roll(rev, WIDE - 7 + s, 1) if s < 7 else rev)[:, :1024]
        o_ref[:, 1, s, :] = (pltpu.roll(tail, WIDE - 7 + s, 1) if s < 7 else tail)[:, :1024]


def bias_windows(idx, table_rev, bias_f):
    whole = pl.BlockSpec(memory_space=pltpu.VMEM)
    return pl.pallas_call(
        window_kernel,
        in_specs=[SMEM, whole, whole],
        out_specs=whole,
        out_shape=jax.ShapeDtypeStruct((16, 2, 8, 1024), F32),
        compiler_params=params(),
    )(idx, table_rev, bias_f)


def pack_kernel(idx, t_ref, db_ref, gn_ref, src_ref, gf_ref, r_ref, small_ref, keep_ref, send_ref):
    z, y = idx[0], idx[1]

    def gather(n):
        total = jnp.zeros((16, WIDE), F32)
        for s in range(8):
            part = jnp.concatenate([db_ref[:, n, s, :], jnp.zeros((16, WIDE - 1024), F32)], axis=1)
            total = total + (pltpu.roll(part, 7 - s, 1) if s < 7 else part)
        return total

    rev = gather(0) + pltpu.roll(gather(1), 704 - 64 * (z * 2 + y), 1)
    onehot = jnp.where(lax.broadcasted_iota(jnp.int32, (BUCKETS, 768), 0) == t_ref[:, :768], 1.0, 0.0)
    bias = lax.dot_general(
        rev[:, :768], onehot, (((1,), (1,)), ((), ())), precision=precise, preferred_element_type=F32
    )
    src = src_ref[...].astype(F32)
    unit = src * lax.rsqrt(jnp.mean(src * src, axis=-1, keepdims=True) + epsilon)
    small_ref[...] = jnp.zeros_like(small_ref)
    small_ref[0:1, :] = jnp.sum(gn_ref[...] * unit, axis=0, keepdims=True)
    small_ref[1:2, :] = gf_ref[0:1, :]
    small_ref[2:5, :] = r_ref[0:3, :]
    small_ref[8:24, 0:BUCKETS] = bias
    for sz in range(4):
        at = lambda yy: pl.ds(pl.multiple_of(((z ^ sz) * 2 + yy) * 64, 64), 64)
        keep_ref[sz] = gn_ref[at(y), :].astype(BF)
        send_ref[sz] = gn_ref[at(y ^ 1), :].astype(BF)


def pack(idx, table_rev, dbias, gn, src, gain_ffn_part, router_part):
    whole = pl.BlockSpec(memory_space=pltpu.VMEM)
    return pl.pallas_call(
        pack_kernel,
        in_specs=[SMEM] + [whole] * 6,
        out_specs=(whole,) * 3,
        out_shape=(
            jax.ShapeDtypeStruct((24, 1024), F32),
            jax.ShapeDtypeStruct((4, 64, 1024), BF),
            jax.ShapeDtypeStruct((4, 64, 1024), BF),
        ),
        compiler_params=params(),
        cost_estimate=COST_S,
    )(idx, table_rev, dbias, gn, src, gain_ffn_part, router_part)


def final_kernel(p_ref, near_ref, opp_ref, gn_ref, src_ref, gain_ref, gh_ref, o_ref):
    f = lambda t: t.astype(F32)
    own = f(p_ref[0]) + f(near_ref[...]) + f(opp_ref[...])
    grad = jnp.concatenate([own, gn_ref[512:, :]], axis=0) * gain_ref[...]
    src = f(src_ref[...])
    scale = lax.rsqrt(jnp.mean(src * src, axis=-1, keepdims=True) + epsilon)
    unit = src * scale
    back = scale * (grad - unit * jnp.mean(grad * unit, axis=-1, keepdims=True))
    o_ref[...] = (gh_ref[...] + back).astype(BF)


def finish(parts, near, opp, gn, src, gain, grad_hidden):
    whole = pl.BlockSpec(memory_space=pltpu.VMEM)
    return pl.pallas_call(
        final_kernel,
        in_specs=[whole] * 7,
        out_specs=whole,
        out_shape=jax.ShapeDtypeStruct((320, 1024), BF),
        compiler_params=params(),
        cost_estimate=COST_S,
    )(parts, near, opp, gn, src, gain[None], grad_hidden)


def add_low(a, b):
    return (a.astype(F32) + b.astype(F32)).astype(BF)


PIECES = [(0, 320), (320, 320), (640, 320), (960, 160), (1120, 160)]


def fetch_pieces(want, x_parts, g_parts, x_scr, g_scr, sem):
    copies = []
    for rc in range(2):
        for n, (row, size) in enumerate(PIECES):
            at = rc * 1280 + row
            tile = at // 640
            if want not in (None, tile):
                continue
            k = rc * 5 + n
            copies.append(pltpu.make_async_copy(x_parts[k], x_scr.at[pl.ds(at, size)], sem.at[k, 0]))
            for h in range(size // 160):
                src = g_parts[k].at[pl.ds(176 * h, 160)]
                dst = g_scr.at[pl.ds(at + 160 * h, 160)]
                copies.append(pltpu.make_async_copy(src, dst, sem.at[k, 1 + h]))
    return copies


def expert_kernel(expert, first, last, *refs):
    refs = list(refs)
    step = pl.program_id(0)
    src, m_ref = refs[:2]
    if first:
        x_parts, g_parts = refs[2:12], refs[12:22]
        at = 22
    else:
        x_ref, g_ref, out_prev, dx_prev = refs[2:6]
        at = 6
    if last:
        s0_ref, s1_ref = refs[at : at + 2]
        at += 2
    if first:
        out_ref, dx_ref, dh_ref, win_ref, s_ref, xo_ref, go_ref, w_scr, sem, x_scr, g_scr, psem = refs[at:]
    elif last:
        out_ref, out_c_ref, dx_ref, dx_c_ref, dh_ref, win_ref, w_scr, sem = refs[at:]
    else:
        out_ref, dx_ref, dh_ref, win_ref, s_ref, w_scr, sem = refs[at:]

    @pl.when(step == 0)
    def _():
        copies = [
            pltpu.make_async_copy(src.at[n], w_scr.at[:, pl.ds(96 * n, 96), :], sem.at[n]) for n in range(4)
        ]
        for copy in copies:
            copy.start()
        if first:
            for copy in fetch_pieces(None, x_parts, g_parts, x_scr, g_scr, psem):
                copy.start()
        for copy in copies:
            copy.wait()

    if first:
        for t in range(4):

            @pl.when(step == t)
            def _(t=t):
                for copy in fetch_pieces(t, x_parts, g_parts, x_scr, g_scr, psem):
                    copy.wait()

        rows = pl.ds(pl.multiple_of(step * 640, 640), 640)
        x, g = x_scr[rows, :], g_scr[rows, :]
        xo_ref[...] = x
        go_ref[...] = g
    else:
        x, g = x_ref[...], g_ref[...]
    w_gu = w_scr[0:2].reshape(768, 1024)
    w_d = w_scr[2]
    gu = dot_nt(x, w_gu)
    gi = dot_nt(g, w_d)
    gate, up = gu[:, :384], gu[:, 384:]
    l = [gate[:, 88 + n : 89 + n] for n in range(3)]
    top = jnp.maximum(jnp.maximum(l[0], l[1]), l[2])
    ex = [jnp.exp(v - top) for v in l]
    inv = 1.0 / (ex[0] + ex[1] + ex[2])
    p = [v * inv for v in ex]
    m = m_ref[...]
    keep = m[:, expert : expert + 1]
    w = p[expert] * keep
    sq = gate * gate
    th = jnp.tanh(0.7978845608028654 * gate * (1.0 + 0.044715 * sq))
    half1 = 0.5 + 0.5 * th
    act = gate * half1
    dact = half1 + (0.5 * gate) * (1.0 - th * th) * (0.7978845608028654 + 0.10703222440890037 * sq)
    inner = (act * up).astype(BF).astype(F32)
    s = jnp.sum(inner * gi, axis=-1, keepdims=True) * keep
    gin = gi * w
    dg = gin * up * dact
    du = gin * act
    if last:
        ss = [s0_ref[...][:, 0:1], s1_ref[...][:, 0:1], s]
        dot = p[0] * ss[0] + p[1] * ss[1] + p[2] * ss[2]
        lane = lax.broadcasted_iota(jnp.int32, (1, 384), 1)
        for n in range(3):
            dg = jnp.where(lane == 88 + n, p[n] * (ss[n] - dot), dg)
    win = (inner * w).astype(BF)
    dh = jnp.concatenate([dg.astype(BF), du.astype(BF)], axis=1)
    dh_ref[...] = dh
    win_ref[...] = win
    if not last:
        s_ref[...] = jnp.broadcast_to(s, s_ref.shape)
    out = dot_nn(win, w_d)
    dx = dot_nn(dh, w_gu)
    if not first:
        out = out + out_prev[...].astype(F32)
        dx = dx + dx_prev[...].astype(F32)
    if last:

        @pl.when(step < 2)
        def _():
            out_c_ref[...] = out.astype(BF)
            dx_c_ref[...] = dx.astype(BF)

        @pl.when(step >= 2)
        def _():
            out_ref[...] = out.astype(BF)
            dx_ref[...] = dx.astype(BF)
    else:
        out_ref[...] = out.astype(BF)
        dx_ref[...] = dx.astype(BF)


def expert_call(expert, x, g, m, src, prev, s_prev, tile=640):
    total = 2560
    first, last = expert == 0, expert == 2
    at = (lambda i: i ^ 2) if last else (lambda i: i)
    row = lambda n: pl.BlockSpec((tile, n), lambda i: (at(i), 0))
    shape = lambda n, t: jax.ShapeDtypeStruct((total, n), t)
    outs = [(1024, BF), (1024, BF), (768, BF), (384, BF), (8, F32)]
    scratch = [pltpu.VMEM((3, 384, 1024), BF), pltpu.SemaphoreType.DMA((4,))]
    if first:
        ins = [src, m, *x, *g]
        specs = [ANY, row(8)] + [ANY] * 20
        outs += [(1024, BF), (1024, BF)]
        scratch += [pltpu.VMEM((total, 1024), BF), pltpu.VMEM((total, 1024), BF), pltpu.SemaphoreType.DMA((10, 3))]
    else:
        ins = [src, m, x, g, *prev]
        specs = [ANY, row(8)] + [row(1024)] * 4
    if last:
        ins += list(s_prev)
        specs += [row(8), row(8)]
        half = jax.ShapeDtypeStruct((total // 2, 1024), BF)
        mine = pl.BlockSpec((tile, 1024), lambda i: (jnp.maximum(i - 2, 0), 0))
        other = pl.BlockSpec((tile, 1024), lambda i: (jnp.minimum(i, 1), 0))
        out_shape = (half, half, half, half, shape(768, BF), shape(384, BF))
        out_specs = (mine, other, mine, other, row(768), row(384))
    else:
        out_shape = tuple(shape(n, t) for n, t in outs)
        out_specs = tuple(row(n) for n, t in outs)
    return pl.pallas_call(
        functools.partial(expert_kernel, expert, first, last),
        grid=(total // tile,),
        out_shape=out_shape,
        in_specs=specs,
        out_specs=out_specs,
        scratch_shapes=scratch,
        compiler_params=params(),
        cost_estimate=COST_E,
    )(*ins)


def line_collect(part_of, z):
    at = lambda n: part_of(z ^ n)
    near = pair_z(at(1))
    opp = flip_z(add_low(at(3), pair_z(at(2))))
    return (at(0).astype(F32) + near.astype(F32) + opp.astype(F32)).astype(BF)


def trade_wt(v):
    return lax.all_to_all(v, "wt", 0, 0, tiled=True)


def sum_all(v):
    v = v + move_c(v)
    v = v + move_x(v)
    v = v + move_y(v)
    v = v + lax.ppermute(v, "ctx", [(i, i ^ 2) for i in range(8)])
    return v + lax.ppermute(v, "ctx", [(i, i ^ 4) for i in range(8)])


def norm_parts(values):
    return values * lax.rsqrt(jnp.mean(values * values, axis=-1, keepdims=True) + epsilon)


def local_fast(
    tokens, cotangent, w_query, w_key, w_value, w_out, gain_attn, gain_ffn, w_router, rel_bias,
    exp_gate, exp_up, exp_down, bucket_table, expert_ids, priority,
):
    ctx_index = lax.axis_index("ctx").astype(jnp.int32)
    wt_index = lax.axis_index("wt").astype(jnp.int32)
    z, y, x, c = ctx_index // 2, ctx_index % 2, wt_index // 2, wt_index % 2
    idx = jnp.stack([z, y, x, c])
    rows_own = tokens[0, 0]

    packed = jnp.concatenate(
        [gain_attn[None], gain_ffn[None], w_router.T, jnp.pad(rel_bias.reshape(1, 128), ((0, 0), (0, 128))),
         jnp.zeros((2, 256), BF)], axis=0
    )
    small = lax.all_gather(packed, "wt", axis=0, tiled=False)
    gain_attn_f = small[:, 0].reshape(1024).astype(F32)
    gain_ffn_f = small[:, 1].reshape(1024).astype(F32)
    bias_f = small[:, 5, :128].reshape(4, 32, 4).transpose(1, 0, 2).reshape(32, 16).astype(F32)

    ids, rank = expert_ids[0, 0], priority[0, 0]
    expert = ids.T.reshape(-1)
    rank_key = (jnp.arange(TOP, dtype=jnp.int32)[:, None] * 320 + rank[None, :]).reshape(-1)
    earlier = (expert[:, None] == expert[None, :]) & (rank_key[None, :] < rank_key[:, None])
    keep = (jnp.sum(earlier.astype(jnp.int32), axis=1) < CAP).reshape(TOP, 320)
    hold = jnp.sum(
        jnp.where((ids.T[:, :, None] == jnp.arange(EXPERTS, dtype=jnp.int32)) & keep[:, :, None], 1.0, 0.0), axis=0
    )
    marks = jnp.pad(hold.reshape(2, 1, 480), ((0, 0), (0, 15), (0, 544))).astype(BF)
    cot = cotangent[0, 0]
    cot_marked = jnp.concatenate([cot[:160], marks[0], cot[160:], marks[1]], axis=0)

    def pieces(v):
        return jnp.pad(v.reshape(3, 4, 88, 256), ((0, 0), (0, 0), (0, 8), (0, 0)))

    gate_t, up_t = exp_gate.transpose(0, 2, 1), exp_up.transpose(0, 2, 1)
    gate_p = pieces(gate_t)
    router_rows = jnp.broadcast_to(
        jnp.pad(w_router.T, ((0, 5), (0, 0)))[None, None], (3, 4, 8, 256)
    )
    gate_p = jnp.concatenate([gate_p[:, :, :88], router_rows], axis=2)
    share = jnp.stack([gate_p, pieces(up_t), pieces(exp_down)], axis=1).transpose(2, 0, 1, 3, 4)
    table_rev = jnp.pad(bucket_table[::-1], (0, WIDE - 768), constant_values=-1)[None]
    windows = bias_windows(idx, table_rev, bias_f)

    qkv_of = lambda u: u[:768].reshape(3, 256, 128)
    prompt_own = rows_own[:64]
    unit = jnp.stack([w_query, w_key, w_value, w_out]).reshape(1024, 128)
    part_0 = qkv_of(unit)
    share, small_first = phase(share, small)
    near, opp, p_near, p_opp, y0 = phase(
        pair_z(unit), flip_z(unit), pair_z(prompt_own), flip_z(prompt_own), move_y(part_0)
    )
    part_1, part_3 = qkv_of(near), qkv_of(opp)
    s0 = jnp.stack([part_0, y0])
    cross, p_cross, x0, x1, y3, share = phase(
        pair_z(opp), pair_z(p_opp), move_x(s0), move_x(part_1), move_y(part_3), trade_wt(share)
    )
    share = share.transpose(1, 2, 3, 0, 4).reshape(3, 3, 96, 1024)
    spread = [lax.all_gather(share[e], "ctx", axis=0, tiled=False, axis_index_groups=LINES_Z) for e in range(3)]
    part_2 = qkv_of(cross)
    t0, s1, s3 = jnp.stack([s0, x0]), jnp.stack([part_1, x1]), jnp.stack([part_3, y3])
    prompt_z = jnp.stack([prompt_own, p_near, p_cross, p_opp])
    prompt_y, c0, y1, x3, x2, windows, cot_marked = phase(
        move_y(prompt_z), move_c(t0), move_y(s1), move_x(s3), move_x(part_2), windows, cot_marked
    )
    prompts = jnp.stack([prompt_z, prompt_y], axis=1).reshape(8, 64, 1024)
    prompts = jnp.take(prompts, jnp.arange(8, dtype=jnp.int32) ^ ctx_index, axis=0).reshape(512, 1024)
    source_all = jnp.concatenate([prompts, rows_own[64:]], axis=0)
    all_low = (norm_parts(source_all.astype(F32)) * gain_attn_f).astype(BF)
    t1, t3, s2 = jnp.stack([s1, y1]), jnp.stack([s3, x3]), jnp.stack([part_2, x2])
    wo_z = jnp.stack([u[768:].reshape(256, 128) for u in (unit, near, opp, cross)])

    state = attend(0, False, idx, all_low, windows, (t0, c0), None)
    *state, c1, c3, y2, wo_y = phase(*state, move_c(t1), move_c(t3), move_y(s2), move_y(wo_z))
    t2, wo_s = jnp.stack([s2, y2]), jnp.stack([wo_z, wo_y])
    cot_marked, mixed_0 = phase(cot_marked, state[1])
    state[1] = mixed_0
    g_x, g_y = move_x(cot_marked), move_y(cot_marked)
    state = attend(1, True, idx, all_low, windows, (t1, c1), state)
    *state, c2, wo_x = phase(*state, move_c(t2), move_x(wo_s))
    wo_t = jnp.stack([wo_s, wo_x])
    state = attend(3, False, idx, all_low, windows, (t3, c3), state)
    *state, wo_c, g_x, g_y = phase(*state, move_c(wo_t), g_x, g_y)
    state = attend(2, True, idx, all_low, windows, (t2, c2), state)
    *state, g_a, g_b, g_cx, g_cy, g_c = phase(
        *state, move_x(g_y[:176]), move_y(g_x[176:]), move_c(g_x), move_c(g_y), move_c(cot_marked)
    )
    probs, mixed, qkv, w_qkv = state
    hidden, normed, w_o = project_out(idx, mixed, rows_own, gain_ffn_f, wo_t, wo_c)

    x_x, x_y, x_c, g_ca, g_cb = phase(move_x(normed), move_y(normed), move_c(normed), move_c(g_a), move_c(g_b))
    x_a, x_b, x_cx, x_cy = phase(move_x(x_y[:160]), move_y(x_x[160:]), move_c(x_x), move_c(x_y))
    x_parts = [normed, x_x, x_y, x_a, x_b, x_c, x_cx, x_cy, move_c(x_a), move_c(x_b)]
    cot_parts = [cot_marked, g_x, g_y, g_a, g_b, g_c, g_cx, g_cy, g_ca, g_cb]
    marks_of = lambda v: [v[n + 160] for n in range(0, v.shape[0], 176)]
    marks_all = jnp.stack(sum([marks_of(v) for v in cot_parts], []))[:, :480].reshape(2560, 3).astype(F32)
    marks_all = jnp.pad(marks_all, ((0, 0), (0, 5)))

    def weight_grads(dh_e, win_e):
        gw = dot_tn(dh_e, x_all).astype(BF).reshape(2, 4, 96, 1024)
        dw = dot_tn(win_e, g_all).astype(BF).reshape(1, 4, 96, 1024)
        return jnp.concatenate([gw, dw], axis=0).transpose(1, 0, 2, 3)

    def along_z(both):
        return lax.psum_scatter(both, "ctx", scatter_dimension=0, axis_index_groups=LINES_Z)

    res = expert_call(0, x_parts, cot_parts, marks_all, spread[0], None, [])
    x_all, g_all = res[5:]
    both_0, s_0 = weight_grads(res[2], res[3]), res[4]
    res = expert_call(1, x_all, g_all, marks_all, spread[1], res[:2], [])
    both_1, s_1 = weight_grads(res[2], res[3]), res[4]
    out, out_c, dx, dx_c, dh_2, win_2 = expert_call(
        2, x_all, g_all, marks_all, spread[2], res[:2], [s_0, s_1]
    )
    bulk = [along_z(both_0), along_z(both_1)]

    got, dh_2, win_2 = phase(move_c(dx_c), dh_2, win_2)
    last, rest = add_low(dx[960:], got[960:]), add_low(dx[:960], got[:960])
    g_w2 = dot_tn(dh_2, x_all).astype(BF)
    d_a, d_b, rest, g_w2, win_2 = phase(move_x(last[:160]), move_y(last[160:]), rest, g_w2, win_2)

    def mix_in(rest, a, b):
        v_x = jnp.concatenate([rest[320:480], add_low(rest[480:640], b)], axis=0)
        v_y = jnp.concatenate([add_low(rest[640:800], a), rest[800:]], axis=0)
        return v_x, v_y

    v_x, v_y = mix_in(rest, d_a, d_b)
    g_d2 = dot_tn(win_2, g_all).astype(BF)
    v_x, v_y, o_got, g_d2 = phase(move_x(v_x), move_y(v_y), move_c(out_c), g_d2)
    both_2 = jnp.concatenate([g_w2.reshape(2, 4, 96, 1024), g_d2.reshape(1, 4, 96, 1024)], axis=0).transpose(1, 0, 2, 3)
    router_part = both_2[0, 0, 88:96].astype(F32)
    grad_hidden, grad_low, grad_mixed, gain_ffn_part = out_back(
        (rest[:320], v_x, v_y), hidden, gain_ffn_f, cot, w_o
    )
    bulk.append(along_z(both_2))
    o_last, o_rest = add_low(out[960:], o_got[960:]), add_low(out[:960], o_got[:960])
    back_of = lambda base, count, *prev: attend_back(
        base, count, idx, all_low, probs, qkv, w_qkv, grad_mixed, mixed, grad_low, *prev
    )
    keep_f, send_f, gn, dbias = back_of(4, 4, None, None)
    o_a, o_b, gn = phase(move_x(o_last[:160]), move_y(o_last[160:]), gn)
    o_x, o_y = mix_in(o_rest, o_a, o_b)
    keep_n, send_n, gn, dbias = back_of(2, 2, gn, dbias)
    o_x, o_y, got, gn = phase(move_x(o_x), move_y(o_y), move_c(send_f), gn)
    combined = o_rest[:320].astype(F32) + o_x.astype(F32) + o_y.astype(F32)
    output = (hidden + combined).astype(BF).reshape(1, 1, 320, 1024)

    fa, fb = cut_rows(add_low(keep_f, got).reshape(2, 2, 2, 256, 512))
    keep_h, send_h, gn_all, dbias = back_of(0, 2, gn, dbias)
    fx, fy, got_n, gn_all = phase(move_x(fa[1]), move_y(fb[:, :, 1]), move_c(send_n), gn_all)
    fa, fb = add_low(fa[0], fx), add_low(fb[:, :, 0], fy)
    packed = pack(idx, table_rev, dbias, gn_all, source_all, gain_ffn_part, router_part)
    got, fy, fx, smalls, gp_keep, gp_send = phase(move_c(send_h), move_y(fa[:, 1]), move_x(fb[1]), *packed)
    far = jnp.concatenate([add_low(fa[:, 0], fy), add_low(fb[0], fx)], axis=1)
    block = lambda t: t.reshape(2, 1, 2, 256, 512)
    h = jnp.concatenate([add_low(block(keep_h), block(got)), add_low(block(keep_n), block(got_n))], axis=1)
    ha, hb = cut_rows(h)
    hx, hy, f_cross, gp_got, sm = phase(
        move_x(ha[1]), move_y(hb[:, :, 1]), pair_z(far[0]), move_y(gp_send), move_c(smalls)
    )
    ha, hb = add_low(ha[0], hx), add_low(hb[:, :, 0], hy)
    gp = add_low(gp_keep, gp_got)
    smalls = smalls + sm
    hy, hx, f_opp, gp_cross, sm = phase(
        move_y(ha[:, 1]), move_x(hb[1]), flip_z(add_low(far[1], f_cross)), pair_z(gp[2]), move_x(smalls)
    )
    here = jnp.concatenate([add_low(ha[:, 0], hy), add_low(hb[0], hx)], axis=1)
    smalls = smalls + sm
    h_near, gp_opp, gp_near, sm = phase(
        pair_z(here[1]), flip_z(add_low(gp[3], gp_cross)), pair_z(gp[1]), move_y(smalls)
    )
    smalls = smalls + sm
    tot = here[0].astype(F32) + h_near.astype(F32) + f_opp.astype(F32)
    grad_tokens = finish(gp, gp_near, gp_opp, gn_all, rows_own, gain_attn_f, grad_hidden).reshape(1, 1, 320, 1024)
    smalls = smalls + pair_z(smalls)
    smalls = smalls + lax.ppermute(smalls, "ctx", [(i, i ^ 4) for i in range(8)])
    mine = lax.dynamic_slice_in_dim(smalls, wt_index * 256, 256, 1)
    res_gain_attn, res_gain_ffn, res_router = mine[0], mine[1], mine[2:5].T
    res_bias = lax.dynamic_slice_in_dim(smalls[8:24, :BUCKETS], wt_index * 4, 4, 0).T

    back = jnp.stack(bulk).reshape(3, 3, 96, 4, 256).transpose(3, 0, 1, 2, 4)
    back = trade_wt(back)[:, :, :, :88].transpose(1, 2, 0, 3, 4).reshape(3, 3, 352, 256).astype(F32)
    res_gate, res_up, res_down = back[:, 0].transpose(0, 2, 1), back[:, 1].transpose(0, 2, 1), back[:, 2]

    return (
        output, grad_tokens, tot[:, :128], tot[:, 128:256], tot[:, 256:384], tot[:, 384:], res_gain_attn, res_gain_ffn, res_router, res_bias,
        res_gate, res_up, res_down,
    )


def solution(mesh):
    fast = mesh.shape["ctx"] == FAST_CTX and mesh.shape["wt"] == FAST_WT
    return jax.shard_map(
        local_fast if fast else local,
        mesh=mesh,
        in_specs=(
            P("wt", "ctx", None, None),
            P("wt", "ctx", None, None),
            P("wt", "ctx"),
            P("wt", "ctx"),
            P("wt", "ctx"),
            P("wt", "ctx"),
            P("wt"),
            P("wt"),
            P("wt", None),
            P(None, "wt"),
            P(None, "wt", "ctx"),
            P(None, "wt", "ctx"),
            P(None, "ctx", "wt"),
            P(),
            P("wt", "ctx", None, None),
            P("wt", "ctx", None),
        ),
        out_specs=(
            P("wt", "ctx", None, None),
            P("wt", "ctx", None, None),
            P("wt", "ctx"),
            P("wt", "ctx"),
            P("wt", "ctx"),
            P("wt", "ctx"),
            P("wt"),
            P("wt"),
            P("wt", None),
            P(None, "wt"),
            P(None, "wt", "ctx"),
            P(None, "wt", "ctx"),
            P(None, "ctx", "wt"),
        ),
        check_vma=False,
    )
```

```python
import functools

import jax
import jax.numpy as jnp
from jax import lax
from jax.experimental import pallas as pl
from jax.experimental.pallas import tpu as pltpu
from jax.sharding import PartitionSpec as P

HEADS = 16
HEAD_DIM = 64
BUCKETS = 32
EXPERTS = 3
TOP = 2
LEN = 256
CAP = 267


epsilon = 1e-06
precise = lax.Precision.HIGHEST


def rms_norm(values, gain_vec):
    return (
        values * lax.rsqrt(jnp.mean(values * values, axis=-1, keepdims=True) + epsilon) * gain_vec
    )


def gelu_product(gate_pre, up_pre):
    return jax.nn.gelu(gate_pre, approximate=True) * up_pre


def routing(expert_ids, priority, capacity, expert_count):
    tok_rows = expert_ids.shape[0]
    top_count = expert_ids.shape[1]
    expert = expert_ids.T.reshape(-1)
    rank_key = (
        jnp.arange(top_count, dtype=jnp.int32)[:, None] * tok_rows + priority[None, :]
    ).reshape(-1)
    earlier = (expert[:, None] == expert[None, :]) & (rank_key[None, :] < rank_key[:, None])
    places = jnp.sum(earlier.astype(jnp.int32), axis=1)
    keep_mask = places < capacity
    slot_ids = expert * capacity + jnp.minimum(places, capacity - 1)
    slot_hits = jnp.where(
        (slot_ids[:, None] == jnp.arange(expert_count * capacity, dtype=jnp.int32)[None, :])
        & keep_mask[:, None],
        1.0,
        0.0,
    )
    dispatch = jnp.sum(slot_hits.reshape(top_count, tok_rows, expert_count * capacity), axis=0).T
    return (keep_mask, slot_ids, slot_hits, dispatch)


def gate_values(logits, expert_ids, keep_mask):
    chances = jax.nn.softmax(logits, axis=-1)
    picked = jnp.take_along_axis(chances, expert_ids, axis=1).T.reshape(-1)
    return jnp.where(keep_mask, picked, 0.0)


def toeplitz(reversed_bias, top_start, row_total, key_total):
    window_len = row_total + key_total
    window = lax.dynamic_slice_in_dim(reversed_bias, top_start, window_len, 1)
    tiled = jnp.tile(window, (1, row_total))[:, : row_total * (window_len - 1)]
    return tiled.reshape(window.shape[0], row_total, window_len - 1)[:, :, row_total - 1 :]


def toeplitz_back(grad_block, row_total, key_total):
    window_len = row_total + key_total
    head_total = grad_block.shape[0]
    placed = jnp.pad(grad_block, ((0, 0), (0, 0), (row_total - 1, 0))).reshape(
        head_total, row_total * (window_len - 1)
    )
    placed = jnp.pad(placed, ((0, 0), (0, row_total)))
    return jnp.sum(placed.reshape(head_total, row_total, window_len), axis=1)


def add_window(table, piece, start):
    current = lax.dynamic_slice_in_dim(table, start, piece.shape[1], 1)
    return lax.dynamic_update_slice_in_dim(table, current + piece, start, 1)


def sweep(step_fn, start_state, prompt_items, local_items):
    state_mid, stacked = lax.scan(step_fn, start_state, prompt_items)
    state_end, last_out = step_fn(state_mid, local_items)
    return (state_end, stacked, last_out)


def local(
    tokens,
    cotangent,
    w_query,
    w_key,
    w_value,
    w_out,
    gain_attn,
    gain_ffn,
    w_router,
    rel_bias,
    exp_gate,
    exp_up,
    exp_down,
    bucket_table,
    expert_ids,
    priority,
):
    tok_rows = tokens.shape[2]
    model_width = tokens.shape[3]
    ctx_count = lax.axis_size("ctx")
    my_block = lax.axis_index("ctx")
    prompt_rows = tok_rows - LEN
    cont_rows = tok_rows - prompt_rows
    prompt_len = prompt_rows * ctx_count
    dist_count = bucket_table.shape[0]
    head_count = HEADS
    head_width = HEAD_DIM
    score_scale = HEAD_DIM ** (-0.5)
    steps_count = max(1, ctx_count // 8)
    block_keys = prompt_len // steps_count
    cols_query, cols_key, cols_value, cols_out, cols_gate, cols_up, cols_down = (
        lax.all_gather(w_query, "ctx", axis=1, tiled=True),
        lax.all_gather(w_key, "ctx", axis=1, tiled=True),
        lax.all_gather(w_value, "ctx", axis=1, tiled=True),
        lax.all_gather(w_out, "ctx", axis=1, tiled=True),
        lax.all_gather(exp_gate, "ctx", axis=2, tiled=True),
        lax.all_gather(exp_up, "ctx", axis=2, tiled=True),
        lax.all_gather(exp_down, "ctx", axis=1, tiled=True),
    )
    gathered = (
        lax.all_gather(cols_query, "wt", axis=0, tiled=True),
        lax.all_gather(cols_key, "wt", axis=0, tiled=True),
        lax.all_gather(cols_value, "wt", axis=0, tiled=True),
        lax.all_gather(cols_out, "wt", axis=0, tiled=True),
        lax.all_gather(cols_gate, "wt", axis=1, tiled=True),
        lax.all_gather(cols_up, "wt", axis=1, tiled=True),
        lax.all_gather(cols_down, "wt", axis=2, tiled=True),
        lax.all_gather(gain_attn, "wt", axis=0, tiled=True),
        lax.all_gather(gain_ffn, "wt", axis=0, tiled=True),
        lax.all_gather(w_router, "wt", axis=0, tiled=True),
        lax.all_gather(rel_bias, "wt", axis=1, tiled=True),
    )
    (
        full_query,
        full_key,
        full_value,
        full_out,
        full_gate,
        full_up,
        full_down,
        full_gain_attn,
        full_gain_ffn,
        full_router,
        full_bias,
    ) = gathered
    gain_attn_f = full_gain_attn.astype(jnp.float32)
    gain_ffn_f = full_gain_ffn.astype(jnp.float32)
    source = tokens[0, 0].astype(jnp.float32)
    normed_attn = rms_norm(source, gain_attn_f)
    normed_attn_low = normed_attn.astype(jnp.bfloat16)
    query_low = jnp.dot(normed_attn_low, full_query, preferred_element_type=jnp.float32).astype(
        jnp.bfloat16
    )
    key_low = jnp.dot(normed_attn_low, full_key, preferred_element_type=jnp.float32).astype(
        jnp.bfloat16
    )
    value_low = jnp.dot(normed_attn_low, full_value, preferred_element_type=jnp.float32).astype(
        jnp.bfloat16
    )
    far_keys, far_values = (
        lax.all_gather(key_low[:prompt_rows], "ctx", axis=0, tiled=True),
        lax.all_gather(value_low[:prompt_rows], "ctx", axis=0, tiled=True),
    )
    row_index = jnp.arange(tok_rows, dtype=jnp.int32)
    query_pos = jnp.where(
        row_index < prompt_rows,
        my_block * prompt_rows + row_index,
        prompt_len + row_index - prompt_rows,
    )
    bucket_onehot = jnp.where(
        bucket_table[:, None] == jnp.arange(BUCKETS, dtype=jnp.int32)[None, :], 1.0, 0.0
    )
    bias_rows = jnp.dot(bucket_onehot, full_bias.astype(jnp.float32), precision=precise).T
    reversed_bias = jnp.concatenate([bias_rows[:, ::-1], jnp.zeros_like(bias_rows)], axis=1)
    prompt_starts = jnp.arange(steps_count, dtype=jnp.int32) * block_keys
    local_start = jnp.asarray(prompt_len, dtype=jnp.int32)
    query_heads = query_low.reshape(tok_rows, head_count, head_width)

    def blocks_of(far_array):
        return far_array.reshape(steps_count, block_keys, model_width)

    def window_starts(key_start):
        prompt_top = dist_count - my_block * prompt_rows + key_start - prompt_rows
        cont_top = dist_count - prompt_len + key_start - cont_rows
        return (prompt_top, cont_top)

    def block_scores(key_block, key_start):
        key_total = key_block.shape[0]
        key_heads = key_block.reshape(key_total, head_count, head_width)
        logit_raw = (
            jnp.einsum("qhd,khd->hqk", query_heads, key_heads, preferred_element_type=jnp.float32)
            * score_scale
        )
        key_pos = key_start + jnp.arange(key_total, dtype=jnp.int32)
        offset = query_pos[:, None] - key_pos[None, :]
        prompt_top, cont_top = window_starts(key_start)
        bias_block = jnp.concatenate(
            [
                toeplitz(reversed_bias, prompt_top, prompt_rows, key_total),
                toeplitz(reversed_bias, cont_top, cont_rows, key_total),
            ],
            axis=1,
        )
        return jnp.where(offset[None] >= 0, logit_raw + bias_block, -1e30)

    def stats_step(state_in, block_item):
        run_max, run_sum = state_in
        scores = block_scores(block_item[0], block_item[1])
        new_max = jnp.maximum(run_max, jnp.max(scores, axis=-1))
        new_sum = run_sum * jnp.exp(run_max - new_max) + jnp.sum(
            jnp.exp(scores - new_max[..., None]), axis=-1
        )
        return ((new_max, new_sum), None)

    start_stats = (
        jnp.full((head_count, tok_rows), -1e30, jnp.float32),
        jnp.zeros((head_count, tok_rows), jnp.float32),
    )
    (row_max, row_sum), unused_a, unused_b = sweep(
        stats_step,
        start_stats,
        (blocks_of(far_keys), prompt_starts),
        (key_low[prompt_rows:], local_start),
    )

    def mix_step(state_in, block_item):
        scores = block_scores(block_item[0], block_item[2])
        weights = (jnp.exp(scores - row_max[..., None]) / row_sum[..., None]).astype(jnp.bfloat16)
        value_heads = block_item[1].reshape(-1, head_count, head_width)
        return (
            state_in
            + jnp.einsum("hqk,khd->qhd", weights, value_heads, preferred_element_type=jnp.float32),
            None,
        )

    mixed_exact, unused_c, unused_d = sweep(
        mix_step,
        jnp.zeros((tok_rows, head_count, head_width), jnp.float32),
        (blocks_of(far_keys), blocks_of(far_values), prompt_starts),
        (key_low[prompt_rows:], value_low[prompt_rows:], local_start),
    )
    mixed_low = mixed_exact.reshape(tok_rows, model_width).astype(jnp.bfloat16)
    hidden = source + jnp.dot(mixed_low, full_out, preferred_element_type=jnp.float32)
    normed_ffn_low = rms_norm(hidden, gain_ffn_f).astype(jnp.bfloat16)
    route_ids = expert_ids[0, 0]
    keep_mask, slot_ids, slot_hits, dispatch = routing(route_ids, priority[0, 0], CAP, EXPERTS)
    inputs = (
        jnp.dot(dispatch.astype(jnp.bfloat16), normed_ffn_low, preferred_element_type=jnp.float32)
        .astype(jnp.bfloat16)
        .reshape(EXPERTS, CAP, model_width)
    )
    gate_pre = jnp.einsum("ecd,edf->ecf", inputs, full_gate, preferred_element_type=jnp.float32)
    up_pre = jnp.einsum("ecd,edf->ecf", inputs, full_up, preferred_element_type=jnp.float32)
    inner_low = gelu_product(gate_pre, up_pre).astype(jnp.bfloat16)
    expert_out = jnp.einsum(
        "ecf,efd->ecd", inner_low, full_down, preferred_element_type=jnp.float32
    ).reshape(EXPERTS * CAP, model_width)
    logits = jnp.dot(normed_ffn_low, full_router, preferred_element_type=jnp.float32)
    weight_pair = gate_values(logits, route_ids, keep_mask)
    picked_rows = jnp.take(expert_out, slot_ids, axis=0)
    combined = jnp.sum(
        (picked_rows * weight_pair[:, None]).reshape(TOP, tok_rows, model_width), axis=0
    )
    output = (hidden + combined).astype(jnp.bfloat16).reshape(1, 1, tok_rows, model_width)
    back_keys, back_values = (far_keys, far_values)
    (
        back_query,
        back_key,
        back_value,
        back_out,
        back_gate,
        back_up,
        back_down,
        back_gain_attn,
        back_gain_ffn,
        back_router,
        back_bias,
    ) = gathered
    grad_final = cotangent[0, 0].astype(jnp.float32)
    grad_pair = jnp.where(
        keep_mask, jnp.sum(jnp.tile(grad_final, (TOP, 1)) * picked_rows, axis=-1), 0.0
    )
    slot_weight = jnp.dot(weight_pair, slot_hits, precision=precise)
    grad_expert_out = (
        (jnp.dot(dispatch, grad_final, precision=precise) * slot_weight[:, None])
        .astype(jnp.bfloat16)
        .reshape(EXPERTS, CAP, model_width)
    )
    grad_inner = jnp.einsum(
        "ecd,efd->ecf", grad_expert_out, back_down, preferred_element_type=jnp.float32
    )
    unused_e, inner_pull = jax.vjp(gelu_product, gate_pre, up_pre)
    grad_gate_pre, grad_up_pre = inner_pull(grad_inner)
    grad_gate_low = grad_gate_pre.astype(jnp.bfloat16)
    grad_up_low = grad_up_pre.astype(jnp.bfloat16)
    grad_gate_w = jnp.einsum(
        "ecd,ecf->edf", inputs, grad_gate_low, preferred_element_type=jnp.float32
    )
    grad_up_w = jnp.einsum("ecd,ecf->edf", inputs, grad_up_low, preferred_element_type=jnp.float32)
    grad_down_w = jnp.einsum(
        "ecf,ecd->efd", inner_low, grad_expert_out, preferred_element_type=jnp.float32
    )
    grad_inputs = jnp.einsum(
        "ecf,edf->ecd", grad_gate_low, back_gate, preferred_element_type=jnp.float32
    ) + jnp.einsum("ecf,edf->ecd", grad_up_low, back_up, preferred_element_type=jnp.float32)

    def gate_of_logits(logit_values):
        return gate_values(logit_values, route_ids, keep_mask)

    unused_f, gate_pull = jax.vjp(gate_of_logits, logits)
    (grad_logits,) = gate_pull(grad_pair)
    grad_router_w = jnp.dot(normed_ffn_low.astype(jnp.float32).T, grad_logits, precision=precise)
    grad_normed_ffn = jnp.dot(grad_logits, back_router.astype(jnp.float32).T, precision=precise)
    grad_normed_ffn = grad_normed_ffn + jnp.dot(
        dispatch.T, grad_inputs.reshape(EXPERTS * CAP, model_width), precision=precise
    )
    unused_g, ffn_norm_pull = jax.vjp(rms_norm, hidden, back_gain_ffn.astype(jnp.float32))
    grad_hidden_part, grad_gain_ffn_w = ffn_norm_pull(grad_normed_ffn)
    grad_hidden = grad_final + grad_hidden_part
    grad_hidden_low = grad_hidden.astype(jnp.bfloat16)
    grad_out_w = jnp.dot(mixed_low.T, grad_hidden_low, preferred_element_type=jnp.float32)
    grad_mixed = jnp.dot(grad_hidden_low, back_out.T, preferred_element_type=jnp.float32).astype(
        jnp.bfloat16
    )
    grad_mixed_heads = grad_mixed.reshape(tok_rows, head_count, head_width)
    row_delta = jnp.sum(grad_mixed_heads.astype(jnp.float32) * mixed_exact, axis=-1).T

    def grad_step(state_in, block_item):
        grad_query_acc, grad_reversed = state_in
        key_block, value_block, key_start = block_item
        key_total = key_block.shape[0]
        scores = block_scores(key_block, key_start)
        chances = jnp.exp(scores - row_max[..., None]) / row_sum[..., None]
        value_heads = value_block.reshape(-1, head_count, head_width)
        key_heads = key_block.reshape(-1, head_count, head_width)
        grad_chance = jnp.einsum(
            "qhd,khd->hqk", grad_mixed_heads, value_heads, preferred_element_type=jnp.float32
        )
        grad_value_block = jnp.einsum(
            "hqk,qhd->khd",
            chances.astype(jnp.bfloat16),
            grad_mixed_heads,
            preferred_element_type=jnp.float32,
        )
        grad_scores = chances * (grad_chance - row_delta[..., None])
        prompt_top, cont_top = window_starts(key_start)
        grad_reversed = add_window(
            grad_reversed,
            toeplitz_back(grad_scores[:, :prompt_rows], prompt_rows, key_total),
            prompt_top,
        )
        grad_reversed = add_window(
            grad_reversed,
            toeplitz_back(grad_scores[:, prompt_rows:], cont_rows, key_total),
            cont_top,
        )
        grad_scores_low = grad_scores.astype(jnp.bfloat16)
        grad_query_acc = grad_query_acc + score_scale * jnp.einsum(
            "hqk,khd->qhd", grad_scores_low, key_heads, preferred_element_type=jnp.float32
        )
        grad_key_block = score_scale * jnp.einsum(
            "hqk,qhd->khd", grad_scores_low, query_heads, preferred_element_type=jnp.float32
        )
        return (
            (grad_query_acc, grad_reversed),
            (grad_key_block.reshape(-1, model_width), grad_value_block.reshape(-1, model_width)),
        )

    start_grads = (
        jnp.zeros((tok_rows, head_count, head_width), jnp.float32),
        jnp.zeros((head_count, 2 * dist_count), jnp.float32),
    )
    (
        (grad_query_exact, grad_reversed),
        (far_grad_keys, far_grad_values),
        (near_grad_keys, near_grad_values),
    ) = sweep(
        grad_step,
        start_grads,
        (blocks_of(back_keys), blocks_of(back_values), prompt_starts),
        (key_low[prompt_rows:], value_low[prompt_rows:], local_start),
    )
    own_grad_keys, own_grad_values = (
        lax.psum_scatter(
            far_grad_keys.reshape(prompt_len, model_width), "ctx", scatter_dimension=0, tiled=True
        ),
        lax.psum_scatter(
            far_grad_values.reshape(prompt_len, model_width), "ctx", scatter_dimension=0, tiled=True
        ),
    )
    grad_key_low = jnp.concatenate([own_grad_keys, near_grad_keys], axis=0).astype(jnp.bfloat16)
    grad_value_low = jnp.concatenate([own_grad_values, near_grad_values], axis=0).astype(
        jnp.bfloat16
    )
    grad_query_low = grad_query_exact.reshape(tok_rows, model_width).astype(jnp.bfloat16)
    grad_query_w = jnp.dot(normed_attn_low.T, grad_query_low, preferred_element_type=jnp.float32)
    grad_key_w = jnp.dot(normed_attn_low.T, grad_key_low, preferred_element_type=jnp.float32)
    grad_value_w = jnp.dot(normed_attn_low.T, grad_value_low, preferred_element_type=jnp.float32)
    grad_normed_attn = jnp.dot(grad_query_low, back_query.T, preferred_element_type=jnp.float32)
    grad_normed_attn = grad_normed_attn + jnp.dot(
        grad_key_low, back_key.T, preferred_element_type=jnp.float32
    )
    grad_normed_attn = grad_normed_attn + jnp.dot(
        grad_value_low, back_value.T, preferred_element_type=jnp.float32
    )
    unused_h, attn_norm_pull = jax.vjp(rms_norm, source, back_gain_attn.astype(jnp.float32))
    grad_source_part, grad_gain_attn_w = attn_norm_pull(grad_normed_attn)
    grad_tokens = (
        (grad_hidden + grad_source_part).astype(jnp.bfloat16).reshape(1, 1, tok_rows, model_width)
    )
    grad_bias_rows = grad_reversed[:, :dist_count][:, ::-1]
    grad_bias_w = jnp.dot(bucket_onehot.T, grad_bias_rows.T, precision=precise)
    small_gain_attn, small_gain_ffn, small_router, small_bias = lax.psum(
        (grad_gain_attn_w, grad_gain_ffn_w, grad_router_w, grad_bias_w), "ctx"
    )
    row_parts = (
        lax.psum_scatter(
            grad_query_w.astype(jnp.bfloat16), "wt", scatter_dimension=0, tiled=True
        ).astype(jnp.float32),
        lax.psum_scatter(
            grad_key_w.astype(jnp.bfloat16), "wt", scatter_dimension=0, tiled=True
        ).astype(jnp.float32),
        lax.psum_scatter(
            grad_value_w.astype(jnp.bfloat16), "wt", scatter_dimension=0, tiled=True
        ).astype(jnp.float32),
        lax.psum_scatter(
            grad_out_w.astype(jnp.bfloat16), "wt", scatter_dimension=0, tiled=True
        ).astype(jnp.float32),
        lax.psum_scatter(
            grad_gate_w.astype(jnp.bfloat16), "wt", scatter_dimension=1, tiled=True
        ).astype(jnp.float32),
        lax.psum_scatter(
            grad_up_w.astype(jnp.bfloat16), "wt", scatter_dimension=1, tiled=True
        ).astype(jnp.float32),
        lax.psum_scatter(
            grad_down_w.astype(jnp.bfloat16), "wt", scatter_dimension=2, tiled=True
        ).astype(jnp.float32),
        lax.psum_scatter(
            small_gain_attn.astype(jnp.bfloat16), "wt", scatter_dimension=0, tiled=True
        ).astype(jnp.float32),
        lax.psum_scatter(
            small_gain_ffn.astype(jnp.bfloat16), "wt", scatter_dimension=0, tiled=True
        ).astype(jnp.float32),
        lax.psum_scatter(
            small_router.astype(jnp.bfloat16), "wt", scatter_dimension=0, tiled=True
        ).astype(jnp.float32),
        lax.psum_scatter(
            small_bias.astype(jnp.bfloat16), "wt", scatter_dimension=1, tiled=True
        ).astype(jnp.float32),
    )
    res_query, res_key, res_value, res_out, res_gate, res_up, res_down = (
        lax.psum_scatter(row_parts[0], "ctx", scatter_dimension=1, tiled=True),
        lax.psum_scatter(row_parts[1], "ctx", scatter_dimension=1, tiled=True),
        lax.psum_scatter(row_parts[2], "ctx", scatter_dimension=1, tiled=True),
        lax.psum_scatter(row_parts[3], "ctx", scatter_dimension=1, tiled=True),
        lax.psum_scatter(row_parts[4], "ctx", scatter_dimension=2, tiled=True),
        lax.psum_scatter(row_parts[5], "ctx", scatter_dimension=2, tiled=True),
        lax.psum_scatter(row_parts[6], "ctx", scatter_dimension=1, tiled=True),
    )
    res_gain_attn, res_gain_ffn, res_router, res_bias = (
        row_parts[7],
        row_parts[8],
        row_parts[9],
        row_parts[10],
    )
    return (
        output,
        grad_tokens,
        res_query,
        res_key,
        res_value,
        res_out,
        res_gain_attn,
        res_gain_ffn,
        res_router,
        res_bias,
        res_gate,
        res_up,
        res_down,
    )


BF = jnp.bfloat16
F32 = jnp.float32
FAST_CTX = 8
FAST_WT = 4
NEG = -1e30

SWAP_Y = [(i, i ^ 1) for i in range(8)]
LINES_Z = [[0, 2, 4, 6], [1, 3, 5, 7]]
PAIR_Z = [(i, i ^ 2) for i in range(8)]
FLIP_Z = [(i, i ^ 6) for i in range(8)]
SWAP_C = [(i, i ^ 1) for i in range(4)]
SWAP_X = [(i, i ^ 2) for i in range(4)]


def move_y(v):
    return lax.ppermute(v, "ctx", SWAP_Y)


def move_x(v):
    return lax.ppermute(v, "wt", SWAP_X)


def move_c(v):
    return lax.ppermute(v, "wt", SWAP_C)


def pair_z(v):
    return lax.ppermute(v, "ctx", PAIR_Z)


def flip_z(v):
    return lax.ppermute(v, "ctx", FLIP_Z)


def phase(*vals):
    return lax.optimization_barrier(vals)


def dot_nt(a, b):
    return lax.dot_general(a, b, (((1,), (1,)), ((), ())), preferred_element_type=F32)


def dot_tn(a, b):
    return lax.dot_general(a, b, (((0,), (0,)), ((), ())), preferred_element_type=F32)


def dot_nn(a, b):
    return jnp.dot(a, b, preferred_element_type=F32)


def params(limit=56 * 2**20):
    return pltpu.CompilerParams(vmem_limit_bytes=limit)


COST_S = pl.CostEstimate(flops=10**10, bytes_accessed=10**6, transcendentals=0)
COST_E = pl.CostEstimate(flops=25 * 10**9, bytes_accessed=10**6, transcendentals=0)
ANY = pl.BlockSpec(memory_space=pl.ANY)
SMEM = pl.BlockSpec(memory_space=pltpu.SMEM)


def spread_z(v):
    near, opp = pair_z(v), flip_z(v)
    return {0: v, 1: near, 3: opp, 2: pair_z(opp)}


def attend_kernel(groups, first, idx, n_ref, w_ref, *refs):
    pieces, refs = refs[: 2 * len(groups)], refs[2 * len(groups) :]
    if not first:
        refs = refs[4:]
    p_ref, o_ref, qkv_ref, wt_ref, bc_ref, bp_ref, qs_ref = refs
    z, y, x, c = idx[0], idx[1], idx[2], idx[3]
    step = pl.program_id(0)
    for n, (sz, x_first) in enumerate(groups):
        for ry in range(2):

            @pl.when(step == 2 * n + ry)
            def _(n=n, ry=ry, x_first=x_first):
                for rx in range(2):
                    for rc in range(2):
                        row = pl.multiple_of(((x ^ rx) * 2 + (c ^ rc)) * 256, 256)
                        src = pieces[2 * n + rc]
                        for t in range(4):
                            rows = slice(256 * t, 256 * t + 256)
                            block = src[ry, rx, rows] if x_first else src[rx, ry, rows]
                            wt_ref[0, pl.ds(row, 256), 128 * t : 128 * t + 128] = block

    qkv = dot_nn(n_ref[...], wt_ref[0, :, :384]).astype(BF)
    qkv_ref[0] = qkv
    k, v = qkv[:, 128:256], qkv[:, 256:]
    qs_ref[...] = qkv[:, :128]
    q_c = qs_ref[512:, :]
    q_p = qs_ref[pl.ds(pl.multiple_of((z * 2 + y) * 64, 64), 64), :]
    lane = lax.broadcasted_iota(jnp.int32, (1, 128), 1)
    outs = []
    for h in range(2):
        base_c, base_p = w_ref[h, 0], w_ref[h, 1]
        for a in range(32):
            bc_ref[8 * a : 8 * a + 8, :] = pltpu.roll(base_c, 1024 - (248 - 8 * a), 1)[:, :768]
        for a in range(8):
            shift = 56 - 8 * a
            bp_ref[8 * a : 8 * a + 8, :] = (pltpu.roll(base_p, 1024 - shift, 1) if shift else base_p)[:, :512]
        mine = (lane < 64) if h == 0 else (lane >= 64)
        head = lambda t: jnp.where(mine, t, jnp.zeros_like(t))
        sc = dot_nt(head(q_c), k) * 0.125 + bc_ref[...]
        sp = dot_nt(head(q_p), k[:512]) * 0.125 + bp_ref[...]

        def soft(t):
            e = jnp.exp(t - jnp.max(t, axis=-1, keepdims=True))
            return (e * (1.0 / jnp.sum(e, axis=-1, keepdims=True))).astype(BF)

        pc, pp = soft(sc), soft(sp)
        p_ref[h, 64:, :] = pc
        p_ref[h, :64, :512] = pp
        p_ref[h, :64, 512:] = jnp.zeros((64, 256), BF)
        outs.append(jnp.concatenate([dot_nn(pp, v[:512]), dot_nn(pc, v)], axis=0))
    o_ref[...] = jnp.where(lane < 64, outs[0], outs[1]).astype(BF)


def norm_kernel(idx, a_ref, b_ref, own_ref, gain_ref, src_ref, low_ref):
    z, y = idx[0], idx[1]
    for sz in range(4):
        at = lambda yy: pl.ds(pl.multiple_of(((z ^ sz) * 2 + yy) * 64, 64), 64)
        src_ref[at(y), :] = a_ref[sz]
        src_ref[at(y ^ 1), :] = b_ref[sz]
    src_ref[512:, :] = own_ref[64:, :]
    values = src_ref[...].astype(F32)
    low_ref[...] = (norm_parts(values) * gain_ref[...]).astype(BF)


def norm_rows(idx, prompt_z, prompt_y, rows_own, gain):
    whole = pl.BlockSpec(memory_space=pltpu.VMEM)
    out = jax.ShapeDtypeStruct((768, 1024), BF)
    return pl.pallas_call(
        norm_kernel,
        in_specs=[SMEM] + [whole] * 4,
        out_specs=(whole, whole),
        out_shape=(out, out),
        compiler_params=params(),
    )(idx, prompt_z, prompt_y, rows_own, gain[None])


def attend(groups, idx, normed, windows, pieces, prev):
    keys, rows = normed.shape[0], 320

    def at(i, d):
        sz = groups[0][0]
        for n, (other, unused) in enumerate(groups):
            sz = jnp.where(i // 2 == n, other, sz)
        return (d[0] ^ sz) * 2 + (d[1] ^ (i % 2))

    whole = pl.BlockSpec(memory_space=pltpu.VMEM)
    return pl.pallas_call(
        functools.partial(attend_kernel, groups, prev is None),
        grid_spec=pltpu.PrefetchScalarGridSpec(
            num_scalar_prefetch=1,
            grid=(2 * len(groups),),
            in_specs=[whole, pl.BlockSpec((2, 2, 8, 1024), lambda i, d: (at(i, d), 0, 0, 0))]
            + [whole] * len(pieces)
            + ([] if prev is None else [ANY] * 4),
            out_specs=(
                pl.BlockSpec((2, rows, keys), lambda i, d: (at(i, d), 0, 0)),
                pl.BlockSpec((rows, 128), lambda i, d: (0, at(i, d))),
                pl.BlockSpec((1, keys, 384), lambda i, d: (at(i, d), 0, 0)),
                pl.BlockSpec((1, 1024, 512), lambda i, d: (at(i, d), 0, 0)),
            ),
            scratch_shapes=[pltpu.VMEM((256, 768), F32), pltpu.VMEM((64, 512), F32), pltpu.VMEM((keys, 128), BF)],
        ),
        out_shape=(
            jax.ShapeDtypeStruct((16, rows, keys), BF),
            jax.ShapeDtypeStruct((rows, 1024), BF),
            jax.ShapeDtypeStruct((8, keys, 384), BF),
            jax.ShapeDtypeStruct((8, 1024, 512), BF),
        ),
        input_output_aliases={} if prev is None else {3 + len(pieces) + n: n for n in range(4)},
        compiler_params=params(),
        cost_estimate=COST_S,
    )(idx, normed, windows, *pieces, *([] if prev is None else prev))


def attend_back_kernel(first, idx, n_ref, p_ref, qkv_ref, wt_ref, g_ref, m_ref, gl_ref, *refs):
    if not first:
        gn_prev, refs = refs[0], refs[2:]
    keep_ref, send_ref, gn_ref, db_ref, dt_ref, qs_ref = refs
    z, y, x, c = idx[0], idx[1], idx[2], idx[3]
    own = pl.ds(pl.multiple_of((z * 2 + y) * 64, 64), 64)
    qkv = qkv_ref[0]
    k, v = qkv[:, 128:256], qkv[:, 256:]
    qs_ref[...] = qkv[:, :128]
    q = jnp.concatenate([qs_ref[own, :], qs_ref[512:, :]], axis=0)
    g = g_ref[...]
    lane = lax.broadcasted_iota(jnp.int32, (1, 128), 1)
    parts = []
    for h in range(2):
        mine = (lane < 64) if h == 0 else (lane >= 64)
        gh = jnp.where(mine, g, jnp.zeros_like(g))
        p = p_ref[h]
        pf = p.astype(F32)
        dp = dot_nt(gh, v)
        delta = jnp.sum(pf * dp, axis=-1, keepdims=True)
        ds = pf * (dp - delta)
        low = ds.astype(BF)
        acc_c = jnp.zeros((8, 1024), F32)
        for a in range(32):
            part = jnp.concatenate([ds[64 + 8 * a : 72 + 8 * a], jnp.zeros((8, 256), F32)], axis=1)
            acc_c = acc_c + pltpu.roll(part, 248 - 8 * a, 1) if a < 31 else acc_c + part
        acc_p = jnp.zeros((8, 1024), F32)
        for a in range(8):
            part = jnp.concatenate([ds[8 * a : 8 * a + 8, :512], jnp.zeros((8, 512), F32)], axis=1)
            acc_p = acc_p + (pltpu.roll(part, 56 - 8 * a, 1) if a < 7 else part)
        db_ref[h, 0] = acc_c
        db_ref[h, 1] = acc_p
        parts.append((dot_nn(low, k) * 0.125, dot_tn(low, q) * 0.125, dot_tn(p, g)))
    dq, dk, dv = [jnp.where(lane < 64, parts[0][n], parts[1][n]).astype(BF) for n in range(3)]
    dt_ref[:512, :128] = jnp.zeros((512, 128), BF)
    dt_ref[own, :128] = dq[:64]
    dt_ref[512:, :128] = dq[64:]
    dt_ref[:, 128:256] = dk
    dt_ref[:, 256:] = dv
    dt = dt_ref[...]
    dw = jnp.concatenate([dot_tn(n_ref[...], dt).astype(BF), dot_tn(m_ref[...], gl_ref[...]).astype(BF)], axis=1)
    for xx in range(2):
        for cc in range(2):
            block = dw[(xx * 2 + cc) * 256 : (xx * 2 + cc) * 256 + 256]

            @pl.when(c == cc)
            def _():
                keep_ref[x ^ xx, 0] = block

            @pl.when(c != cc)
            def _():
                send_ref[x ^ xx, 0] = block

    gn = dot_nt(dt, wt_ref[0, :, :384])

    @pl.when(pl.program_id(0) == 0)
    def _():
        gn_ref[...] = gn if first else gn_prev[...] + gn

    @pl.when(pl.program_id(0) != 0)
    def _():
        gn_ref[...] += gn


def attend_back(base, count, idx, normed, p, qkv, wt, g, mixed, g_low, gn_prev, db_prev):
    rows, keys = p.shape[1], p.shape[2]
    at = lambda i, d: (i + base) ^ (d[0] * 2 + d[1])
    whole = pl.BlockSpec((keys, 1024), lambda i, d: (0, 0))
    return pl.pallas_call(
        functools.partial(attend_back_kernel, gn_prev is None),
        grid_spec=pltpu.PrefetchScalarGridSpec(
            num_scalar_prefetch=1,
            grid=(count,),
            in_specs=[
                whole,
                pl.BlockSpec((2, rows, keys), lambda i, d: (at(i, d), 0, 0)),
                pl.BlockSpec((1, keys, 384), lambda i, d: (at(i, d), 0, 0)),
                pl.BlockSpec((1, 1024, 512), lambda i, d: (at(i, d), 0, 0)),
                pl.BlockSpec((rows, 128), lambda i, d: (0, at(i, d))),
                pl.BlockSpec((rows, 1024), lambda i, d: (0, 0)),
                pl.BlockSpec((rows, 128), lambda i, d: (0, at(i, d))),
            ]
            + ([] if gn_prev is None else [whole, ANY]),
            out_specs=(
                pl.BlockSpec((2, 1, 256, 512), lambda i, d: (0, i, 0, 0)),
                pl.BlockSpec((2, 1, 256, 512), lambda i, d: (0, i, 0, 0)),
                whole,
                pl.BlockSpec((2, 2, 8, 1024), lambda i, d: (at(i, d), 0, 0, 0)),
            ),
            scratch_shapes=[pltpu.VMEM((keys, 384), BF), pltpu.VMEM((keys, 128), BF)],
        ),
        out_shape=(
            jax.ShapeDtypeStruct((2, count, 256, 512), BF),
            jax.ShapeDtypeStruct((2, count, 256, 512), BF),
            jax.ShapeDtypeStruct((keys, 1024), F32),
            jax.ShapeDtypeStruct((16, 2, 8, 1024), F32),
        ),
        input_output_aliases={} if gn_prev is None else {9: 3},
        compiler_params=params(),
        cost_estimate=COST_E,
    )(idx, normed, p, qkv, wt, g, mixed, g_low, *([] if gn_prev is None else [gn_prev, db_prev]))


def cut_rows(t):
    return t[:, :, :, :128], t[:, :, :, 128:]


def out_back_kernel(a_ref, b_ref, c_ref, h_ref, gain_ref, cot_ref, w_ref, gh_ref, gl_ref, gm_ref, gg_ref):
    f = lambda t: t.astype(F32)
    dn = f(a_ref[...]) + f(b_ref[...]) + f(c_ref[...])
    hidden, gain = h_ref[...], gain_ref[...]
    scale = lax.rsqrt(jnp.mean(hidden * hidden, axis=-1, keepdims=True) + epsilon)
    unit = hidden * scale
    gg_ref[...] = jnp.broadcast_to(jnp.sum(dn * unit, axis=0, keepdims=True), gg_ref.shape)
    du = dn * gain
    grad = f(cot_ref[...]) + scale * (du - unit * jnp.mean(du * unit, axis=-1, keepdims=True))
    gh_ref[...] = grad
    low = grad.astype(BF)
    gl_ref[...] = low
    total = dot_nt(low[:, :128], w_ref[0, :, 384:])
    for n in range(1, 8):
        total = total + dot_nt(low[:, 128 * n : 128 * n + 128], w_ref[n, :, 384:])
    gm_ref[...] = total.astype(BF)


def out_back(parts, hidden, gain, cot, w_o):
    whole = pl.BlockSpec(memory_space=pltpu.VMEM)
    return pl.pallas_call(
        out_back_kernel,
        in_specs=[whole] * 7,
        out_specs=(whole,) * 4,
        out_shape=(
            jax.ShapeDtypeStruct((320, 1024), F32),
            jax.ShapeDtypeStruct((320, 1024), BF),
            jax.ShapeDtypeStruct((320, 1024), BF),
            jax.ShapeDtypeStruct((8, 1024), F32),
        ),
        compiler_params=params(),
        cost_estimate=COST_S,
    )(*parts, hidden, gain[None], cot, w_o)


def out_kernel(m_ref, s_ref, g_ref, w_ref, h_ref, l_ref):
    m = m_ref[...]
    for n in range(8):
        cols = slice(128 * n, 128 * n + 128)
        h_ref[:, cols] = s_ref[:, cols].astype(F32) + dot_nn(m, w_ref[n, :, 384:])
    hidden = h_ref[...]
    scale = lax.rsqrt(jnp.mean(hidden * hidden, axis=-1, keepdims=True) + epsilon)
    l_ref[...] = (hidden * scale * g_ref[...]).astype(BF)


def project_out(mixed, rows_own, gain, wt):
    whole = pl.BlockSpec(memory_space=pltpu.VMEM)
    return pl.pallas_call(
        out_kernel,
        in_specs=[whole] * 4,
        out_specs=(whole,) * 2,
        out_shape=(jax.ShapeDtypeStruct((320, 1024), F32), jax.ShapeDtypeStruct((320, 1024), BF)),
        compiler_params=params(),
        cost_estimate=COST_S,
    )(mixed, rows_own, gain[None], wt)


WIDE = 1920


def window_kernel(idx, t_ref, b_ref, o_ref):
    onehot = jnp.where(lax.broadcasted_iota(jnp.int32, (BUCKETS, WIDE), 0) == t_ref[...], 1.0, 0.0)
    rev = lax.dot_general(b_ref[...], onehot, (((0,), (0,)), ((), ())), precision=precise, preferred_element_type=F32)
    rev = jnp.where(lax.broadcasted_iota(jnp.int32, (16, WIDE), 1) < 768, rev, NEG)
    tail = pltpu.roll(rev, WIDE - 704 + 64 * (idx[0] * 2 + idx[1]), 1)
    for s in range(8):
        o_ref[:, 0, s, :] = (pltpu.roll(rev, WIDE - 7 + s, 1) if s < 7 else rev)[:, :1024]
        o_ref[:, 1, s, :] = (pltpu.roll(tail, WIDE - 7 + s, 1) if s < 7 else tail)[:, :1024]


def bias_windows(idx, table_rev, bias_f):
    whole = pl.BlockSpec(memory_space=pltpu.VMEM)
    return pl.pallas_call(
        window_kernel,
        in_specs=[SMEM, whole, whole],
        out_specs=whole,
        out_shape=jax.ShapeDtypeStruct((16, 2, 8, 1024), F32),
        compiler_params=params(),
    )(idx, table_rev, bias_f)


def pack_kernel(idx, t_ref, db_ref, gn_ref, src_ref, gf_ref, r_ref, small_ref, keep_ref, send_ref):
    z, y = idx[0], idx[1]

    def gather(n):
        total = jnp.zeros((16, WIDE), F32)
        for s in range(8):
            part = jnp.concatenate([db_ref[:, n, s, :], jnp.zeros((16, WIDE - 1024), F32)], axis=1)
            total = total + (pltpu.roll(part, 7 - s, 1) if s < 7 else part)
        return total

    rev = gather(0) + pltpu.roll(gather(1), 704 - 64 * (z * 2 + y), 1)
    onehot = jnp.where(lax.broadcasted_iota(jnp.int32, (BUCKETS, 768), 0) == t_ref[:, :768], 1.0, 0.0)
    bias = lax.dot_general(
        rev[:, :768], onehot, (((1,), (1,)), ((), ())), precision=precise, preferred_element_type=F32
    )
    src = src_ref[...].astype(F32)
    unit = src * lax.rsqrt(jnp.mean(src * src, axis=-1, keepdims=True) + epsilon)
    small_ref[...] = jnp.zeros_like(small_ref)
    small_ref[0:1, :] = jnp.sum(gn_ref[...] * unit, axis=0, keepdims=True)
    small_ref[1:2, :] = gf_ref[0:1, :]
    small_ref[2:5, :] = r_ref[0:3, :]
    small_ref[8:24, 0:BUCKETS] = bias
    for sz in range(4):
        at = lambda yy: pl.ds(pl.multiple_of(((z ^ sz) * 2 + yy) * 64, 64), 64)
        keep_ref[sz] = gn_ref[at(y), :].astype(BF)
        send_ref[sz] = gn_ref[at(y ^ 1), :].astype(BF)


def pack(idx, table_rev, dbias, gn, src, gain_ffn_part, router_part):
    whole = pl.BlockSpec(memory_space=pltpu.VMEM)
    return pl.pallas_call(
        pack_kernel,
        in_specs=[SMEM] + [whole] * 6,
        out_specs=(whole,) * 3,
        out_shape=(
            jax.ShapeDtypeStruct((24, 1024), F32),
            jax.ShapeDtypeStruct((4, 64, 1024), BF),
            jax.ShapeDtypeStruct((4, 64, 1024), BF),
        ),
        compiler_params=params(),
        cost_estimate=COST_S,
    )(idx, table_rev, dbias, gn, src, gain_ffn_part, router_part)


def final_kernel(p_ref, near_ref, opp_ref, gn_ref, src_ref, gain_ref, gh_ref, o_ref):
    f = lambda t: t.astype(F32)
    own = f(p_ref[0]) + f(near_ref[...]) + f(opp_ref[...])
    grad = jnp.concatenate([own, gn_ref[512:, :]], axis=0) * gain_ref[...]
    src = f(src_ref[...])
    scale = lax.rsqrt(jnp.mean(src * src, axis=-1, keepdims=True) + epsilon)
    unit = src * scale
    back = scale * (grad - unit * jnp.mean(grad * unit, axis=-1, keepdims=True))
    o_ref[...] = (gh_ref[...] + back).astype(BF)


def finish(parts, near, opp, gn, src, gain, grad_hidden):
    whole = pl.BlockSpec(memory_space=pltpu.VMEM)
    return pl.pallas_call(
        final_kernel,
        in_specs=[whole] * 7,
        out_specs=whole,
        out_shape=jax.ShapeDtypeStruct((320, 1024), BF),
        compiler_params=params(),
        cost_estimate=COST_S,
    )(parts, near, opp, gn, src, gain[None], grad_hidden)


def add_low(a, b):
    return (a.astype(F32) + b.astype(F32)).astype(BF)


PIECES = [(0, 320), (320, 320), (640, 320), (960, 160), (1120, 160)]


def fetch_pieces(want, x_parts, g_parts, x_scr, g_scr, sem):
    copies = []
    for rc in range(2):
        for n, (row, size) in enumerate(PIECES):
            at = rc * 1280 + row
            tile = at // 640
            if want not in (None, tile):
                continue
            k = rc * 5 + n
            copies.append(pltpu.make_async_copy(x_parts[k], x_scr.at[pl.ds(at, size)], sem.at[k, 0]))
            copies.append(pltpu.make_async_copy(g_parts[k], g_scr.at[pl.ds(at, size)], sem.at[k, 1]))
    return copies


def expert_kernel(group, last, *refs):
    refs = list(refs)
    step = pl.program_id(0)
    count = len(group)
    idx, refs = refs[0], refs[1:]
    w_at = idx[2] * 2 + idx[3]
    src, m_ref = refs[:2]
    if not last:
        x_parts, g_parts = refs[2:12], refs[12:22]
        out_ref, dx_ref, dh_ref, win_ref, s_ref, xo_ref, go_ref, w_scr, sem, x_scr, g_scr, psem = refs[22:]
    else:
        x_ref, g_ref, out_prev, dx_prev, s_prev = refs[2:7]
        out_ref, out_c_ref, dx_ref, dx_c_ref, dh_ref, win_ref, w_scr, sem = refs[7:]

    @pl.when(step == 0)
    def _():
        copies = [
            pltpu.make_async_copy(
                src.at[n, r, e],
                w_scr.at[e, :, pl.ds(96 * n, 96), pl.ds(pl.multiple_of((w_at ^ r) * 256, 256), 256)],
                sem.at[n, 4 * e + r],
            )
            for e in range(count)
            for n in range(4)
            for r in range(4)
        ]
        for copy in copies:
            copy.start()
        if not last:
            for copy in fetch_pieces(None, x_parts, g_parts, x_scr, g_scr, psem):
                copy.start()
        for copy in copies:
            copy.wait()

    if not last:
        for t in range(4):

            @pl.when(step == t)
            def _(t=t):
                for copy in fetch_pieces(t, x_parts, g_parts, x_scr, g_scr, psem):
                    copy.wait()

        rows = pl.ds(pl.multiple_of(step * 640, 640), 640)
        x, g = x_scr[rows, :], g_scr[rows, :]
        xo_ref[...] = x
        go_ref[...] = g
    else:
        x, g = x_ref[...], g_ref[...]
    m = m_ref[...]
    lane = lax.broadcasted_iota(jnp.int32, (1, 384), 1)
    scores = []
    for k, expert in enumerate(group):
        w_gu = w_scr[k, 0:2].reshape(768, 1024)
        w_d = w_scr[k, 2]
        gu = dot_nt(x, w_gu)
        gi = dot_nt(g, w_d)
        gate, up = gu[:, :384], gu[:, 384:]
        if k == 0:
            l = [gate[:, 88 + n : 89 + n] for n in range(3)]
            top = jnp.maximum(jnp.maximum(l[0], l[1]), l[2])
            ex = [jnp.exp(v - top) for v in l]
            inv = 1.0 / (ex[0] + ex[1] + ex[2])
            p = [v * inv for v in ex]
        keep = m[:, expert : expert + 1]
        w = p[expert] * keep
        sq = gate * gate
        th = jnp.tanh(0.7978845608028654 * gate * (1.0 + 0.044715 * sq))
        half1 = 0.5 + 0.5 * th
        act = gate * half1
        dact = half1 + (0.5 * gate) * (1.0 - th * th) * (0.7978845608028654 + 0.10703222440890037 * sq)
        inner = (act * up).astype(BF).astype(F32)
        s = jnp.sum(inner * gi, axis=-1, keepdims=True) * keep
        scores.append(s)
        gin = gi * w
        dg = gin * up * dact
        du = gin * act
        if last:
            ss = [s_prev[...][:, 0:1], s_prev[...][:, 1:2], s]
            dot = p[0] * ss[0] + p[1] * ss[1] + p[2] * ss[2]
            for n in range(3):
                dg = jnp.where(lane == 88 + n, p[n] * (ss[n] - dot), dg)
        win = (inner * w).astype(BF)
        dh = jnp.concatenate([dg.astype(BF), du.astype(BF)], axis=1)
        dh_ref[:, 768 * k : 768 * k + 768] = dh
        win_ref[:, 384 * k : 384 * k + 384] = win
        o_k, dx_k = dot_nn(win, w_d), dot_nn(dh, w_gu)
        out, dx = (o_k, dx_k) if k == 0 else (out + o_k, dx + dx_k)
    if last:
        out = (out + out_prev[...].astype(F32)).astype(BF)
        dx = (dx + dx_prev[...].astype(F32)).astype(BF)

        @pl.when(step < 2)
        def _():
            out_c_ref[...] = out
            dx_c_ref[...] = dx

        @pl.when(step >= 2)
        def _():
            out_ref[...] = out
            dx_ref[...] = dx
    else:
        out_ref[...] = out.astype(BF)
        dx_ref[...] = dx.astype(BF)
        s_ref[...] = jnp.where(lane[:, :128] == 0, scores[0], scores[1])


def expert_call(group, idx, x, g, m, src, prev, tile=640):
    total, count = 2560, len(group)
    last = prev is not None
    at = (lambda i: i ^ 2) if last else (lambda i: i)
    row = lambda n: pl.BlockSpec((tile, n), lambda i: (at(i), 0))
    shape = lambda n, t: jax.ShapeDtypeStruct((total, n), t)
    scratch = [pltpu.VMEM((count, 3, 384, 1024), BF), pltpu.SemaphoreType.DMA((4, 4 * count))]
    if not last:
        ins = [idx, src, m, *x, *g]
        specs = [SMEM, ANY, row(128)] + [ANY] * 20
        outs = [(1024, BF), (1024, BF), (768 * count, BF), (384 * count, BF), (128, F32), (1024, BF), (1024, BF)]
        out_shape = tuple(shape(n, t) for n, t in outs)
        out_specs = tuple(row(n) for n, t in outs)
        scratch += [pltpu.VMEM((total, 1024), BF), pltpu.VMEM((total, 1024), BF), pltpu.SemaphoreType.DMA((10, 2))]
    else:
        ins = [idx, src, m, x, g, *prev]
        specs = [SMEM, ANY, row(128)] + [row(1024)] * 4 + [row(128)]
        half = jax.ShapeDtypeStruct((total // 2, 1024), BF)
        mine = pl.BlockSpec((tile, 1024), lambda i: (jnp.maximum(i - 2, 0), 0))
        other = pl.BlockSpec((tile, 1024), lambda i: (jnp.minimum(i, 1), 0))
        out_shape = (half, half, half, half, shape(768 * count, BF), shape(384 * count, BF))
        out_specs = (mine, other, mine, other, row(768 * count), row(384 * count))
    return pl.pallas_call(
        functools.partial(expert_kernel, group, last),
        grid=(total // tile,),
        out_shape=out_shape,
        in_specs=specs,
        out_specs=out_specs,
        scratch_shapes=scratch,
        compiler_params=params(),
        cost_estimate=COST_E,
    )(*ins)


def line_collect(part_of, z):
    at = lambda n: part_of(z ^ n)
    near = pair_z(at(1))
    opp = flip_z(add_low(at(3), pair_z(at(2))))
    return (at(0).astype(F32) + near.astype(F32) + opp.astype(F32)).astype(BF)


def trade_wt(v):
    return lax.all_to_all(v, "wt", 0, 0, tiled=True)


def sum_all(v):
    v = v + move_c(v)
    v = v + move_x(v)
    v = v + move_y(v)
    v = v + lax.ppermute(v, "ctx", [(i, i ^ 2) for i in range(8)])
    return v + lax.ppermute(v, "ctx", [(i, i ^ 4) for i in range(8)])


def norm_parts(values):
    return values * lax.rsqrt(jnp.mean(values * values, axis=-1, keepdims=True) + epsilon)


def local_fast(
    tokens, cotangent, w_query, w_key, w_value, w_out, gain_attn, gain_ffn, w_router, rel_bias,
    exp_gate, exp_up, exp_down, bucket_table, expert_ids, priority,
):
    ctx_index = lax.axis_index("ctx").astype(jnp.int32)
    wt_index = lax.axis_index("wt").astype(jnp.int32)
    z, y, x, c = ctx_index // 2, ctx_index % 2, wt_index // 2, wt_index % 2
    idx = jnp.stack([z, y, x, c])
    rows_own = tokens[0, 0]

    packed = jnp.concatenate(
        [gain_attn[None], gain_ffn[None], w_router.T, jnp.pad(rel_bias.reshape(1, 128), ((0, 0), (0, 128))),
         jnp.zeros((2, 256), BF)], axis=0
    )
    ids, rank = expert_ids[0, 0], priority[0, 0]
    expert = ids.T.reshape(-1)
    rank_key = (jnp.arange(TOP, dtype=jnp.int32)[:, None] * 320 + rank[None, :]).reshape(-1)
    earlier = (expert[:, None] == expert[None, :]) & (rank_key[None, :] < rank_key[:, None])
    keep = (jnp.sum(earlier.astype(jnp.int32), axis=1) < CAP).reshape(TOP, 320)
    hold = jnp.sum(
        jnp.where((ids.T[:, :, None] == jnp.arange(EXPERTS, dtype=jnp.int32)) & keep[:, :, None], 1.0, 0.0), axis=0
    )
    marks = jnp.pad(hold.reshape(960), (0, 1088)).astype(BF).reshape(16, 128)
    cot = cotangent[0, 0]

    def pieces(v):
        return jnp.pad(v.reshape(3, 4, 88, 256), ((0, 0), (0, 0), (0, 8), (0, 0)))

    gate_t, up_t = exp_gate.transpose(0, 2, 1), exp_up.transpose(0, 2, 1)
    gate_p = pieces(gate_t)
    router_rows = jnp.broadcast_to(
        jnp.pad(w_router.T, ((0, 5), (0, 0)))[None, None], (3, 4, 8, 256)
    )
    gate_p = jnp.concatenate([gate_p[:, :, :88], router_rows], axis=2)
    share = jnp.stack([gate_p, pieces(up_t), pieces(exp_down)], axis=1).transpose(2, 0, 1, 3, 4)
    pick = lambda v, n, d: lax.dynamic_index_in_dim(v, n, d, keepdims=False)
    unit = jnp.stack([w_query, w_key, w_value, w_out]).reshape(1024, 128)
    prompt_own = rows_own[:64]
    along = jnp.concatenate([unit, prompt_own.reshape(512, 128)], axis=0)
    weights_in = lambda v: v[:1024]
    rows_in = lambda v: v[1024:].reshape(64, 1024)
    share = share.reshape(2, 2, 3, 3, 96, 256)
    share_x, share_own = pick(share, 1 - x, 0), pick(share, x, 0)
    packed_c, packed_x, packed_xc, along, share_x = phase(
        move_c(packed), move_x(packed), lax.ppermute(packed, "wt", [(i, i ^ 3) for i in range(4)]), along, share_x
    )
    unit_0 = jnp.concatenate([unit, marks], axis=0)
    near, opp, p_cross, y0, share_x, g_y, share_own = phase(
        pair_z(along), flip_z(along), lax.ppermute(prompt_own, "ctx", [(i, i ^ 4) for i in range(8)]),
        move_y(unit_0), move_x(share_x), move_y(cot), share_own
    )
    s0 = jnp.stack([unit_0, y0])
    unit_1, unit_3 = weights_in(near), weights_in(opp)
    prompt_z = jnp.stack([prompt_own, rows_in(near), p_cross, rows_in(opp)])
    share = jnp.stack([share_own, share_x])
    share_own, share_c = pick(share, c, 1), pick(share, 1 - c, 1)
    s0, unit_1, unit_3, prompt_z, share_c, share_own, small = phase(
        s0, unit_1, unit_3, prompt_z, share_c, share_own, jnp.stack([packed, packed_c, packed_x, packed_xc])
    )
    small = jnp.take(small, jnp.arange(4, dtype=jnp.int32) ^ wt_index, axis=0)
    gain_attn_f = small[:, 0].reshape(1024).astype(F32)
    gain_ffn_f = small[:, 1].reshape(1024).astype(F32)
    bias_f = small[:, 5, :128].reshape(4, 32, 4).transpose(1, 0, 2).reshape(32, 16).astype(F32)
    table_rev = jnp.pad(bucket_table[::-1], (0, WIDE - 768), constant_values=-1)[None]
    windows = bias_windows(idx, table_rev, bias_f)
    cross, prompt_y, x0, x1, y3, windows, gain_attn_f = phase(
        pair_z(unit_3), move_y(prompt_z), move_x(s0), move_x(unit_1), move_y(unit_3), windows, gain_attn_f
    )
    t0, s1, s3 = jnp.stack([s0, x0]), jnp.stack([unit_1, x1]), jnp.stack([unit_3, y3])
    t0, s1, s3 = phase(t0, s1, s3)
    c0, share_c, s1, s3 = phase(move_c(t0), move_c(share_c), s1, s3)
    share = jnp.stack([share_own, share_c], axis=1).reshape(4, 3, 3, 96, 256)
    spread = [
        lax.all_gather(t, "ctx", axis=0, tiled=False, axis_index_groups=LINES_Z) for t in (share[:, :2], share[:, 2:])
    ]
    source_all, all_low = norm_rows(idx, prompt_z, prompt_y, rows_own, gain_attn_f)
    state = attend(((0, False),), idx, all_low, windows, (t0, c0), None)
    *state, y1, x3, x2, g_cy = phase(*state, move_y(s1), move_x(s3), move_x(cross), move_c(g_y))
    t1, t3, s2, *state = phase(jnp.stack([s1, y1]), jnp.stack([s3, x3]), jnp.stack([cross, x2]), *state)
    c1, c3, *state = phase(move_c(t1), move_c(t3), *state)
    state = attend(((1, True), (3, False)), idx, all_low, windows, (t1, c1, t3, c3), state)
    *state, y2, g_x, g_c = phase(*state, move_y(s2), move_x(cot), move_c(cot))
    t2, g_ya, g_xb, *state = phase(jnp.stack([s2, y2]), g_y[:160], g_x[160:], *state)
    c2, *state = phase(move_c(t2), *state)
    state = attend(((2, True),), idx, all_low, windows, (t2, c2), state)
    marks_all = jnp.stack([t0[:, :, 1024:], c0[:, :, 1024:]]).reshape(2, 2, 2, 2048)[..., :960]
    marks_all = marks_all.transpose(0, 2, 1, 3).reshape(2560, 3).astype(F32)
    marks_all = jnp.pad(marks_all, ((0, 0), (0, 125)))
    *state, g_a, g_b, g_cx, marks_all = phase(*state, move_x(g_ya), move_y(g_xb), move_c(g_x), marks_all)
    probs, mixed, qkv, w_all = state
    hidden, normed = project_out(mixed, rows_own, gain_ffn_f, w_all)
    hidden, normed, g_ca, g_cb = phase(hidden, normed, move_c(g_a), move_c(g_b))

    x_x, x_y, x_c = phase(move_x(normed), move_y(normed), move_c(normed))
    x_a, x_b, x_cx, x_cy = phase(move_x(x_y[:160]), move_y(x_x[160:]), move_c(x_x), move_c(x_y))
    x_parts = [normed, x_x, x_y, x_a, x_b, x_c, x_cx, x_cy, move_c(x_a), move_c(x_b)]
    cot_parts = [cot, g_x, g_y, g_a, g_b, g_c, g_cx, g_cy, g_ca, g_cb]

    def along_z(gw, dw):
        gw, dw = gw.astype(BF).reshape(-1, 2, 4, 96, 1024), dw.astype(BF).reshape(-1, 1, 4, 96, 1024)
        return jnp.concatenate([gw, dw], axis=1).transpose(2, 0, 1, 3, 4)

    def reduce_z(both):
        flat = both.reshape(4, -1, 1024)
        got = lax.psum_scatter(flat, "ctx", scatter_dimension=0, axis_index_groups=LINES_Z)
        return got.reshape(both.shape[1:])

    out, dx, dh, win, s_01, x_all, g_all = expert_call((0, 1), idx, x_parts, cot_parts, marks_all, spread[0], None)
    both_01 = along_z(dot_tn(dh, x_all), dot_tn(win, g_all))
    both_01, out = phase(both_01, out)
    bulk = [reduce_z(both_01)]
    out, out_c, dx, dx_c, dh_2, win_2 = expert_call(
        (2,), idx, x_all, g_all, marks_all, spread[1], (out, dx, s_01)
    )

    got, g_d2, dh_2 = phase(move_c(dx_c), dot_tn(win_2, g_all), dh_2)
    last, rest = add_low(dx[960:], got[960:]), add_low(dx[:960], got[:960])
    last_a, last_b, dh_2, rest = phase(last[:160], last[160:], dh_2, rest)
    both_2 = along_z(dot_tn(dh_2, x_all), g_d2)
    d_a, d_b, rest, both_2, o_got = phase(move_x(last_a), move_y(last_b), rest, both_2, move_c(out_c))

    def mix_in(rest, a, b):
        v_x = jnp.concatenate([rest[320:480], add_low(rest[480:640], b)], axis=0)
        v_y = jnp.concatenate([add_low(rest[640:800], a), rest[800:]], axis=0)
        return v_x, v_y

    bulk.append(reduce_z(both_2))
    v_x, v_y = mix_in(rest, d_a, d_b)
    v_x, v_y, out, o_got = phase(v_x, v_y, out, o_got)
    o_last, o_rest = add_low(out[960:], o_got[960:]), add_low(out[:960], o_got[:960])
    v_x, v_y, o_la, o_lb, o_rest = phase(move_x(v_x), move_y(v_y), o_last[:160], o_last[160:], o_rest)
    router_part = both_2[0, 0, 0, 88:96].astype(F32)
    grad_hidden, grad_low, grad_mixed, gain_ffn_part = out_back(
        (rest[:320], v_x, v_y), hidden, gain_ffn_f, cot, w_all
    )
    back_of = lambda base, count, *prev: attend_back(
        base, count, idx, all_low, probs, qkv, w_all, grad_mixed, mixed, grad_low, *prev
    )
    keep_f, send_f, gn, dbias = back_of(4, 4, None, None)
    o_a, o_b, gn = phase(move_x(o_la), move_y(o_lb), gn)
    o_x, o_y, gn = phase(*mix_in(o_rest, o_a, o_b), gn)
    o_x, o_y, gn, bulk[0] = phase(o_x, o_y, gn, bulk[0])
    keep_n, send_n, gn, dbias = back_of(2, 2, gn, dbias)
    o_x, o_y, got, gn = phase(move_x(o_x), move_y(o_y), move_c(send_f), gn)
    combined = o_rest[:320].astype(F32) + o_x.astype(F32) + o_y.astype(F32)
    output = (hidden + combined).astype(BF).reshape(1, 1, 320, 1024)

    fa, fb = cut_rows(add_low(keep_f, got).reshape(2, 2, 2, 256, 512))
    fa0, fa1, fb0, fb1, gn = phase(fa[0], fa[1], fb[:, :, 0], fb[:, :, 1], gn)
    keep_h, send_h, gn_all, dbias = back_of(0, 2, gn, dbias)
    fx, fy, got_n, gn_all = phase(move_x(fa1), move_y(fb1), move_c(send_n), gn_all)
    fa, fb = add_low(fa0, fx), add_low(fb0, fy)
    packed = pack(idx, table_rev, dbias, gn_all, source_all, gain_ffn_part, router_part)
    got, fy, fx, smalls, gp_keep, gp_send = phase(move_c(send_h), move_y(fa[:, 1]), move_x(fb[1]), *packed)
    fy, bulk[1] = phase(fy, bulk[1])
    far = jnp.concatenate([add_low(fa[:, 0], fy), add_low(fb[0], fx)], axis=1)
    block = lambda t: t.reshape(2, 1, 2, 256, 512)
    h = jnp.concatenate([add_low(block(keep_h), block(got)), add_low(block(keep_n), block(got_n))], axis=1)
    ha, hb = cut_rows(h)
    hx, hy, f_cross, gp_got, sm = phase(
        move_x(ha[1]), move_y(hb[:, :, 1]), pair_z(far[0]), move_y(gp_send), move_c(smalls)
    )
    ha, hb = add_low(ha[0], hx), add_low(hb[:, :, 0], hy)
    gp = add_low(gp_keep, gp_got)
    smalls = smalls + sm
    hy, hx, f_opp, gp_cross, sm = phase(
        move_y(ha[:, 1]), move_x(hb[1]), flip_z(add_low(far[1], f_cross)), pair_z(gp[2]), move_x(smalls)
    )
    here = jnp.concatenate([add_low(ha[:, 0], hy), add_low(hb[0], hx)], axis=1)
    smalls = smalls + sm
    h_near, gp_opp, gp_near, sm = phase(
        pair_z(here[1]), flip_z(add_low(gp[3], gp_cross)), pair_z(gp[1]), move_y(smalls)
    )
    smalls = smalls + sm
    tot = here[0].astype(F32) + h_near.astype(F32) + f_opp.astype(F32)
    grad_tokens = finish(gp, gp_near, gp_opp, gn_all, rows_own, gain_attn_f, grad_hidden).reshape(1, 1, 320, 1024)
    smalls = smalls + pair_z(smalls)
    smalls = smalls + lax.ppermute(smalls, "ctx", [(i, i ^ 4) for i in range(8)])
    mine = lax.dynamic_slice_in_dim(smalls, wt_index * 256, 256, 1)
    res_gain_attn, res_gain_ffn, res_router = mine[0], mine[1], mine[2:5].T
    res_bias = lax.dynamic_slice_in_dim(smalls[8:24, :BUCKETS], wt_index * 4, 4, 0).T

    back = jnp.concatenate(bulk).reshape(3, 3, 96, 4, 256).transpose(3, 0, 1, 2, 4)
    back = trade_wt(back)[:, :, :, :88].transpose(1, 2, 0, 3, 4).reshape(3, 3, 352, 256).astype(F32)
    res_gate, res_up, res_down = back[:, 0].transpose(0, 2, 1), back[:, 1].transpose(0, 2, 1), back[:, 2]

    return (
        output, grad_tokens, tot[:, :128], tot[:, 128:256], tot[:, 256:384], tot[:, 384:], res_gain_attn, res_gain_ffn, res_router, res_bias,
        res_gate, res_up, res_down,
    )


def solution(mesh):
    fast = mesh.shape["ctx"] == FAST_CTX and mesh.shape["wt"] == FAST_WT
    return jax.shard_map(
        local_fast if fast else local,
        mesh=mesh,
        in_specs=(
            P("wt", "ctx", None, None),
            P("wt", "ctx", None, None),
            P("wt", "ctx"),
            P("wt", "ctx"),
            P("wt", "ctx"),
            P("wt", "ctx"),
            P("wt"),
            P("wt"),
            P("wt", None),
            P(None, "wt"),
            P(None, "wt", "ctx"),
            P(None, "wt", "ctx"),
            P(None, "ctx", "wt"),
            P(),
            P("wt", "ctx", None, None),
            P("wt", "ctx", None),
        ),
        out_specs=(
            P("wt", "ctx", None, None),
            P("wt", "ctx", None, None),
            P("wt", "ctx"),
            P("wt", "ctx"),
            P("wt", "ctx"),
            P("wt", "ctx"),
            P("wt"),
            P("wt"),
            P("wt", None),
            P(None, "wt"),
            P(None, "wt", "ctx"),
            P(None, "wt", "ctx"),
            P(None, "ctx", "wt"),
        ),
        check_vma=False,
    )
```

```python
import functools

import jax
import jax.numpy as jnp
from jax import lax
from jax.experimental import pallas as pl
from jax.experimental.pallas import tpu as pltpu
from jax.sharding import PartitionSpec as P

HEADS = 16
HEAD_DIM = 64
BUCKETS = 32
EXPERTS = 3
TOP = 2
LEN = 256
CAP = 267


epsilon = 1e-06
precise = lax.Precision.HIGHEST


def rms_norm(values, gain_vec):
    return (
        values * lax.rsqrt(jnp.mean(values * values, axis=-1, keepdims=True) + epsilon) * gain_vec
    )


def gelu_product(gate_pre, up_pre):
    return jax.nn.gelu(gate_pre, approximate=True) * up_pre


def routing(expert_ids, priority, capacity, expert_count):
    tok_rows = expert_ids.shape[0]
    top_count = expert_ids.shape[1]
    expert = expert_ids.T.reshape(-1)
    rank_key = (
        jnp.arange(top_count, dtype=jnp.int32)[:, None] * tok_rows + priority[None, :]
    ).reshape(-1)
    earlier = (expert[:, None] == expert[None, :]) & (rank_key[None, :] < rank_key[:, None])
    places = jnp.sum(earlier.astype(jnp.int32), axis=1)
    keep_mask = places < capacity
    slot_ids = expert * capacity + jnp.minimum(places, capacity - 1)
    slot_hits = jnp.where(
        (slot_ids[:, None] == jnp.arange(expert_count * capacity, dtype=jnp.int32)[None, :])
        & keep_mask[:, None],
        1.0,
        0.0,
    )
    dispatch = jnp.sum(slot_hits.reshape(top_count, tok_rows, expert_count * capacity), axis=0).T
    return (keep_mask, slot_ids, slot_hits, dispatch)


def gate_values(logits, expert_ids, keep_mask):
    chances = jax.nn.softmax(logits, axis=-1)
    picked = jnp.take_along_axis(chances, expert_ids, axis=1).T.reshape(-1)
    return jnp.where(keep_mask, picked, 0.0)


def toeplitz(reversed_bias, top_start, row_total, key_total):
    window_len = row_total + key_total
    window = lax.dynamic_slice_in_dim(reversed_bias, top_start, window_len, 1)
    tiled = jnp.tile(window, (1, row_total))[:, : row_total * (window_len - 1)]
    return tiled.reshape(window.shape[0], row_total, window_len - 1)[:, :, row_total - 1 :]


def toeplitz_back(grad_block, row_total, key_total):
    window_len = row_total + key_total
    head_total = grad_block.shape[0]
    placed = jnp.pad(grad_block, ((0, 0), (0, 0), (row_total - 1, 0))).reshape(
        head_total, row_total * (window_len - 1)
    )
    placed = jnp.pad(placed, ((0, 0), (0, row_total)))
    return jnp.sum(placed.reshape(head_total, row_total, window_len), axis=1)


def add_window(table, piece, start):
    current = lax.dynamic_slice_in_dim(table, start, piece.shape[1], 1)
    return lax.dynamic_update_slice_in_dim(table, current + piece, start, 1)


def sweep(step_fn, start_state, prompt_items, local_items):
    state_mid, stacked = lax.scan(step_fn, start_state, prompt_items)
    state_end, last_out = step_fn(state_mid, local_items)
    return (state_end, stacked, last_out)


def local(
    tokens,
    cotangent,
    w_query,
    w_key,
    w_value,
    w_out,
    gain_attn,
    gain_ffn,
    w_router,
    rel_bias,
    exp_gate,
    exp_up,
    exp_down,
    bucket_table,
    expert_ids,
    priority,
):
    tok_rows = tokens.shape[2]
    model_width = tokens.shape[3]
    ctx_count = lax.axis_size("ctx")
    my_block = lax.axis_index("ctx")
    prompt_rows = tok_rows - LEN
    cont_rows = tok_rows - prompt_rows
    prompt_len = prompt_rows * ctx_count
    dist_count = bucket_table.shape[0]
    head_count = HEADS
    head_width = HEAD_DIM
    score_scale = HEAD_DIM ** (-0.5)
    steps_count = max(1, ctx_count // 8)
    block_keys = prompt_len // steps_count
    cols_query, cols_key, cols_value, cols_out, cols_gate, cols_up, cols_down = (
        lax.all_gather(w_query, "ctx", axis=1, tiled=True),
        lax.all_gather(w_key, "ctx", axis=1, tiled=True),
        lax.all_gather(w_value, "ctx", axis=1, tiled=True),
        lax.all_gather(w_out, "ctx", axis=1, tiled=True),
        lax.all_gather(exp_gate, "ctx", axis=2, tiled=True),
        lax.all_gather(exp_up, "ctx", axis=2, tiled=True),
        lax.all_gather(exp_down, "ctx", axis=1, tiled=True),
    )
    gathered = (
        lax.all_gather(cols_query, "wt", axis=0, tiled=True),
        lax.all_gather(cols_key, "wt", axis=0, tiled=True),
        lax.all_gather(cols_value, "wt", axis=0, tiled=True),
        lax.all_gather(cols_out, "wt", axis=0, tiled=True),
        lax.all_gather(cols_gate, "wt", axis=1, tiled=True),
        lax.all_gather(cols_up, "wt", axis=1, tiled=True),
        lax.all_gather(cols_down, "wt", axis=2, tiled=True),
        lax.all_gather(gain_attn, "wt", axis=0, tiled=True),
        lax.all_gather(gain_ffn, "wt", axis=0, tiled=True),
        lax.all_gather(w_router, "wt", axis=0, tiled=True),
        lax.all_gather(rel_bias, "wt", axis=1, tiled=True),
    )
    (
        full_query,
        full_key,
        full_value,
        full_out,
        full_gate,
        full_up,
        full_down,
        full_gain_attn,
        full_gain_ffn,
        full_router,
        full_bias,
    ) = gathered
    gain_attn_f = full_gain_attn.astype(jnp.float32)
    gain_ffn_f = full_gain_ffn.astype(jnp.float32)
    source = tokens[0, 0].astype(jnp.float32)
    normed_attn = rms_norm(source, gain_attn_f)
    normed_attn_low = normed_attn.astype(jnp.bfloat16)
    query_low = jnp.dot(normed_attn_low, full_query, preferred_element_type=jnp.float32).astype(
        jnp.bfloat16
    )
    key_low = jnp.dot(normed_attn_low, full_key, preferred_element_type=jnp.float32).astype(
        jnp.bfloat16
    )
    value_low = jnp.dot(normed_attn_low, full_value, preferred_element_type=jnp.float32).astype(
        jnp.bfloat16
    )
    far_keys, far_values = (
        lax.all_gather(key_low[:prompt_rows], "ctx", axis=0, tiled=True),
        lax.all_gather(value_low[:prompt_rows], "ctx", axis=0, tiled=True),
    )
    row_index = jnp.arange(tok_rows, dtype=jnp.int32)
    query_pos = jnp.where(
        row_index < prompt_rows,
        my_block * prompt_rows + row_index,
        prompt_len + row_index - prompt_rows,
    )
    bucket_onehot = jnp.where(
        bucket_table[:, None] == jnp.arange(BUCKETS, dtype=jnp.int32)[None, :], 1.0, 0.0
    )
    bias_rows = jnp.dot(bucket_onehot, full_bias.astype(jnp.float32), precision=precise).T
    reversed_bias = jnp.concatenate([bias_rows[:, ::-1], jnp.zeros_like(bias_rows)], axis=1)
    prompt_starts = jnp.arange(steps_count, dtype=jnp.int32) * block_keys
    local_start = jnp.asarray(prompt_len, dtype=jnp.int32)
    query_heads = query_low.reshape(tok_rows, head_count, head_width)

    def blocks_of(far_array):
        return far_array.reshape(steps_count, block_keys, model_width)

    def window_starts(key_start):
        prompt_top = dist_count - my_block * prompt_rows + key_start - prompt_rows
        cont_top = dist_count - prompt_len + key_start - cont_rows
        return (prompt_top, cont_top)

    def block_scores(key_block, key_start):
        key_total = key_block.shape[0]
        key_heads = key_block.reshape(key_total, head_count, head_width)
        logit_raw = (
            jnp.einsum("qhd,khd->hqk", query_heads, key_heads, preferred_element_type=jnp.float32)
            * score_scale
        )
        key_pos = key_start + jnp.arange(key_total, dtype=jnp.int32)
        offset = query_pos[:, None] - key_pos[None, :]
        prompt_top, cont_top = window_starts(key_start)
        bias_block = jnp.concatenate(
            [
                toeplitz(reversed_bias, prompt_top, prompt_rows, key_total),
                toeplitz(reversed_bias, cont_top, cont_rows, key_total),
            ],
            axis=1,
        )
        return jnp.where(offset[None] >= 0, logit_raw + bias_block, -1e30)

    def stats_step(state_in, block_item):
        run_max, run_sum = state_in
        scores = block_scores(block_item[0], block_item[1])
        new_max = jnp.maximum(run_max, jnp.max(scores, axis=-1))
        new_sum = run_sum * jnp.exp(run_max - new_max) + jnp.sum(
            jnp.exp(scores - new_max[..., None]), axis=-1
        )
        return ((new_max, new_sum), None)

    start_stats = (
        jnp.full((head_count, tok_rows), -1e30, jnp.float32),
        jnp.zeros((head_count, tok_rows), jnp.float32),
    )
    (row_max, row_sum), unused_a, unused_b = sweep(
        stats_step,
        start_stats,
        (blocks_of(far_keys), prompt_starts),
        (key_low[prompt_rows:], local_start),
    )

    def mix_step(state_in, block_item):
        scores = block_scores(block_item[0], block_item[2])
        weights = (jnp.exp(scores - row_max[..., None]) / row_sum[..., None]).astype(jnp.bfloat16)
        value_heads = block_item[1].reshape(-1, head_count, head_width)
        return (
            state_in
            + jnp.einsum("hqk,khd->qhd", weights, value_heads, preferred_element_type=jnp.float32),
            None,
        )

    mixed_exact, unused_c, unused_d = sweep(
        mix_step,
        jnp.zeros((tok_rows, head_count, head_width), jnp.float32),
        (blocks_of(far_keys), blocks_of(far_values), prompt_starts),
        (key_low[prompt_rows:], value_low[prompt_rows:], local_start),
    )
    mixed_low = mixed_exact.reshape(tok_rows, model_width).astype(jnp.bfloat16)
    hidden = source + jnp.dot(mixed_low, full_out, preferred_element_type=jnp.float32)
    normed_ffn_low = rms_norm(hidden, gain_ffn_f).astype(jnp.bfloat16)
    route_ids = expert_ids[0, 0]
    keep_mask, slot_ids, slot_hits, dispatch = routing(route_ids, priority[0, 0], CAP, EXPERTS)
    inputs = (
        jnp.dot(dispatch.astype(jnp.bfloat16), normed_ffn_low, preferred_element_type=jnp.float32)
        .astype(jnp.bfloat16)
        .reshape(EXPERTS, CAP, model_width)
    )
    gate_pre = jnp.einsum("ecd,edf->ecf", inputs, full_gate, preferred_element_type=jnp.float32)
    up_pre = jnp.einsum("ecd,edf->ecf", inputs, full_up, preferred_element_type=jnp.float32)
    inner_low = gelu_product(gate_pre, up_pre).astype(jnp.bfloat16)
    expert_out = jnp.einsum(
        "ecf,efd->ecd", inner_low, full_down, preferred_element_type=jnp.float32
    ).reshape(EXPERTS * CAP, model_width)
    logits = jnp.dot(normed_ffn_low, full_router, preferred_element_type=jnp.float32)
    weight_pair = gate_values(logits, route_ids, keep_mask)
    picked_rows = jnp.take(expert_out, slot_ids, axis=0)
    combined = jnp.sum(
        (picked_rows * weight_pair[:, None]).reshape(TOP, tok_rows, model_width), axis=0
    )
    output = (hidden + combined).astype(jnp.bfloat16).reshape(1, 1, tok_rows, model_width)
    back_keys, back_values = (far_keys, far_values)
    (
        back_query,
        back_key,
        back_value,
        back_out,
        back_gate,
        back_up,
        back_down,
        back_gain_attn,
        back_gain_ffn,
        back_router,
        back_bias,
    ) = gathered
    grad_final = cotangent[0, 0].astype(jnp.float32)
    grad_pair = jnp.where(
        keep_mask, jnp.sum(jnp.tile(grad_final, (TOP, 1)) * picked_rows, axis=-1), 0.0
    )
    slot_weight = jnp.dot(weight_pair, slot_hits, precision=precise)
    grad_expert_out = (
        (jnp.dot(dispatch, grad_final, precision=precise) * slot_weight[:, None])
        .astype(jnp.bfloat16)
        .reshape(EXPERTS, CAP, model_width)
    )
    grad_inner = jnp.einsum(
        "ecd,efd->ecf", grad_expert_out, back_down, preferred_element_type=jnp.float32
    )
    unused_e, inner_pull = jax.vjp(gelu_product, gate_pre, up_pre)
    grad_gate_pre, grad_up_pre = inner_pull(grad_inner)
    grad_gate_low = grad_gate_pre.astype(jnp.bfloat16)
    grad_up_low = grad_up_pre.astype(jnp.bfloat16)
    grad_gate_w = jnp.einsum(
        "ecd,ecf->edf", inputs, grad_gate_low, preferred_element_type=jnp.float32
    )
    grad_up_w = jnp.einsum("ecd,ecf->edf", inputs, grad_up_low, preferred_element_type=jnp.float32)
    grad_down_w = jnp.einsum(
        "ecf,ecd->efd", inner_low, grad_expert_out, preferred_element_type=jnp.float32
    )
    grad_inputs = jnp.einsum(
        "ecf,edf->ecd", grad_gate_low, back_gate, preferred_element_type=jnp.float32
    ) + jnp.einsum("ecf,edf->ecd", grad_up_low, back_up, preferred_element_type=jnp.float32)

    def gate_of_logits(logit_values):
        return gate_values(logit_values, route_ids, keep_mask)

    unused_f, gate_pull = jax.vjp(gate_of_logits, logits)
    (grad_logits,) = gate_pull(grad_pair)
    grad_router_w = jnp.dot(normed_ffn_low.astype(jnp.float32).T, grad_logits, precision=precise)
    grad_normed_ffn = jnp.dot(grad_logits, back_router.astype(jnp.float32).T, precision=precise)
    grad_normed_ffn = grad_normed_ffn + jnp.dot(
        dispatch.T, grad_inputs.reshape(EXPERTS * CAP, model_width), precision=precise
    )
    unused_g, ffn_norm_pull = jax.vjp(rms_norm, hidden, back_gain_ffn.astype(jnp.float32))
    grad_hidden_part, grad_gain_ffn_w = ffn_norm_pull(grad_normed_ffn)
    grad_hidden = grad_final + grad_hidden_part
    grad_hidden_low = grad_hidden.astype(jnp.bfloat16)
    grad_out_w = jnp.dot(mixed_low.T, grad_hidden_low, preferred_element_type=jnp.float32)
    grad_mixed = jnp.dot(grad_hidden_low, back_out.T, preferred_element_type=jnp.float32).astype(
        jnp.bfloat16
    )
    grad_mixed_heads = grad_mixed.reshape(tok_rows, head_count, head_width)
    row_delta = jnp.sum(grad_mixed_heads.astype(jnp.float32) * mixed_exact, axis=-1).T

    def grad_step(state_in, block_item):
        grad_query_acc, grad_reversed = state_in
        key_block, value_block, key_start = block_item
        key_total = key_block.shape[0]
        scores = block_scores(key_block, key_start)
        chances = jnp.exp(scores - row_max[..., None]) / row_sum[..., None]
        value_heads = value_block.reshape(-1, head_count, head_width)
        key_heads = key_block.reshape(-1, head_count, head_width)
        grad_chance = jnp.einsum(
            "qhd,khd->hqk", grad_mixed_heads, value_heads, preferred_element_type=jnp.float32
        )
        grad_value_block = jnp.einsum(
            "hqk,qhd->khd",
            chances.astype(jnp.bfloat16),
            grad_mixed_heads,
            preferred_element_type=jnp.float32,
        )
        grad_scores = chances * (grad_chance - row_delta[..., None])
        prompt_top, cont_top = window_starts(key_start)
        grad_reversed = add_window(
            grad_reversed,
            toeplitz_back(grad_scores[:, :prompt_rows], prompt_rows, key_total),
            prompt_top,
        )
        grad_reversed = add_window(
            grad_reversed,
            toeplitz_back(grad_scores[:, prompt_rows:], cont_rows, key_total),
            cont_top,
        )
        grad_scores_low = grad_scores.astype(jnp.bfloat16)
        grad_query_acc = grad_query_acc + score_scale * jnp.einsum(
            "hqk,khd->qhd", grad_scores_low, key_heads, preferred_element_type=jnp.float32
        )
        grad_key_block = score_scale * jnp.einsum(
            "hqk,qhd->khd", grad_scores_low, query_heads, preferred_element_type=jnp.float32
        )
        return (
            (grad_query_acc, grad_reversed),
            (grad_key_block.reshape(-1, model_width), grad_value_block.reshape(-1, model_width)),
        )

    start_grads = (
        jnp.zeros((tok_rows, head_count, head_width), jnp.float32),
        jnp.zeros((head_count, 2 * dist_count), jnp.float32),
    )
    (
        (grad_query_exact, grad_reversed),
        (far_grad_keys, far_grad_values),
        (near_grad_keys, near_grad_values),
    ) = sweep(
        grad_step,
        start_grads,
        (blocks_of(back_keys), blocks_of(back_values), prompt_starts),
        (key_low[prompt_rows:], value_low[prompt_rows:], local_start),
    )
    own_grad_keys, own_grad_values = (
        lax.psum_scatter(
            far_grad_keys.reshape(prompt_len, model_width), "ctx", scatter_dimension=0, tiled=True
        ),
        lax.psum_scatter(
            far_grad_values.reshape(prompt_len, model_width), "ctx", scatter_dimension=0, tiled=True
        ),
    )
    grad_key_low = jnp.concatenate([own_grad_keys, near_grad_keys], axis=0).astype(jnp.bfloat16)
    grad_value_low = jnp.concatenate([own_grad_values, near_grad_values], axis=0).astype(
        jnp.bfloat16
    )
    grad_query_low = grad_query_exact.reshape(tok_rows, model_width).astype(jnp.bfloat16)
    grad_query_w = jnp.dot(normed_attn_low.T, grad_query_low, preferred_element_type=jnp.float32)
    grad_key_w = jnp.dot(normed_attn_low.T, grad_key_low, preferred_element_type=jnp.float32)
    grad_value_w = jnp.dot(normed_attn_low.T, grad_value_low, preferred_element_type=jnp.float32)
    grad_normed_attn = jnp.dot(grad_query_low, back_query.T, preferred_element_type=jnp.float32)
    grad_normed_attn = grad_normed_attn + jnp.dot(
        grad_key_low, back_key.T, preferred_element_type=jnp.float32
    )
    grad_normed_attn = grad_normed_attn + jnp.dot(
        grad_value_low, back_value.T, preferred_element_type=jnp.float32
    )
    unused_h, attn_norm_pull = jax.vjp(rms_norm, source, back_gain_attn.astype(jnp.float32))
    grad_source_part, grad_gain_attn_w = attn_norm_pull(grad_normed_attn)
    grad_tokens = (
        (grad_hidden + grad_source_part).astype(jnp.bfloat16).reshape(1, 1, tok_rows, model_width)
    )
    grad_bias_rows = grad_reversed[:, :dist_count][:, ::-1]
    grad_bias_w = jnp.dot(bucket_onehot.T, grad_bias_rows.T, precision=precise)
    small_gain_attn, small_gain_ffn, small_router, small_bias = lax.psum(
        (grad_gain_attn_w, grad_gain_ffn_w, grad_router_w, grad_bias_w), "ctx"
    )
    row_parts = (
        lax.psum_scatter(
            grad_query_w.astype(jnp.bfloat16), "wt", scatter_dimension=0, tiled=True
        ).astype(jnp.float32),
        lax.psum_scatter(
            grad_key_w.astype(jnp.bfloat16), "wt", scatter_dimension=0, tiled=True
        ).astype(jnp.float32),
        lax.psum_scatter(
            grad_value_w.astype(jnp.bfloat16), "wt", scatter_dimension=0, tiled=True
        ).astype(jnp.float32),
        lax.psum_scatter(
            grad_out_w.astype(jnp.bfloat16), "wt", scatter_dimension=0, tiled=True
        ).astype(jnp.float32),
        lax.psum_scatter(
            grad_gate_w.astype(jnp.bfloat16), "wt", scatter_dimension=1, tiled=True
        ).astype(jnp.float32),
        lax.psum_scatter(
            grad_up_w.astype(jnp.bfloat16), "wt", scatter_dimension=1, tiled=True
        ).astype(jnp.float32),
        lax.psum_scatter(
            grad_down_w.astype(jnp.bfloat16), "wt", scatter_dimension=2, tiled=True
        ).astype(jnp.float32),
        lax.psum_scatter(
            small_gain_attn.astype(jnp.bfloat16), "wt", scatter_dimension=0, tiled=True
        ).astype(jnp.float32),
        lax.psum_scatter(
            small_gain_ffn.astype(jnp.bfloat16), "wt", scatter_dimension=0, tiled=True
        ).astype(jnp.float32),
        lax.psum_scatter(
            small_router.astype(jnp.bfloat16), "wt", scatter_dimension=0, tiled=True
        ).astype(jnp.float32),
        lax.psum_scatter(
            small_bias.astype(jnp.bfloat16), "wt", scatter_dimension=1, tiled=True
        ).astype(jnp.float32),
    )
    res_query, res_key, res_value, res_out, res_gate, res_up, res_down = (
        lax.psum_scatter(row_parts[0], "ctx", scatter_dimension=1, tiled=True),
        lax.psum_scatter(row_parts[1], "ctx", scatter_dimension=1, tiled=True),
        lax.psum_scatter(row_parts[2], "ctx", scatter_dimension=1, tiled=True),
        lax.psum_scatter(row_parts[3], "ctx", scatter_dimension=1, tiled=True),
        lax.psum_scatter(row_parts[4], "ctx", scatter_dimension=2, tiled=True),
        lax.psum_scatter(row_parts[5], "ctx", scatter_dimension=2, tiled=True),
        lax.psum_scatter(row_parts[6], "ctx", scatter_dimension=1, tiled=True),
    )
    res_gain_attn, res_gain_ffn, res_router, res_bias = (
        row_parts[7],
        row_parts[8],
        row_parts[9],
        row_parts[10],
    )
    return (
        output,
        grad_tokens,
        res_query,
        res_key,
        res_value,
        res_out,
        res_gain_attn,
        res_gain_ffn,
        res_router,
        res_bias,
        res_gate,
        res_up,
        res_down,
    )


BF = jnp.bfloat16
F32 = jnp.float32
FAST_CTX = 8
FAST_WT = 4
NEG = -1e30

SWAP_Y = [(i, i ^ 1) for i in range(8)]
LINES_Z = [[0, 2, 4, 6], [1, 3, 5, 7]]
PAIR_Z = [(i, i ^ 2) for i in range(8)]
FLIP_Z = [(i, i ^ 6) for i in range(8)]
SWAP_C = [(i, i ^ 1) for i in range(4)]
SWAP_X = [(i, i ^ 2) for i in range(4)]


def move_y(v):
    return lax.ppermute(v, "ctx", SWAP_Y)


def move_x(v):
    return lax.ppermute(v, "wt", SWAP_X)


def move_c(v):
    return lax.ppermute(v, "wt", SWAP_C)


def pair_z(v):
    return lax.ppermute(v, "ctx", PAIR_Z)


def flip_z(v):
    return lax.ppermute(v, "ctx", FLIP_Z)


def phase(*vals):
    return lax.optimization_barrier(vals)


def dot_nt(a, b):
    return lax.dot_general(a, b, (((1,), (1,)), ((), ())), preferred_element_type=F32)


def dot_tn(a, b):
    return lax.dot_general(a, b, (((0,), (0,)), ((), ())), preferred_element_type=F32)


def dot_nn(a, b):
    return jnp.dot(a, b, preferred_element_type=F32)


def params(limit=56 * 2**20):
    return pltpu.CompilerParams(vmem_limit_bytes=limit)


COST_S = pl.CostEstimate(flops=10**10, bytes_accessed=10**6, transcendentals=0)
COST_E = pl.CostEstimate(flops=25 * 10**9, bytes_accessed=10**6, transcendentals=0)
ANY = pl.BlockSpec(memory_space=pl.ANY)
SMEM = pl.BlockSpec(memory_space=pltpu.SMEM)


def spread_z(v):
    near, opp = pair_z(v), flip_z(v)
    return {0: v, 1: near, 3: opp, 2: pair_z(opp)}


def attend_kernel(groups, first, idx, n_ref, w_ref, *refs):
    pieces, refs = refs[: 2 * len(groups)], refs[2 * len(groups) :]
    if not first:
        refs = refs[4:]
    p_ref, o_ref, qkv_ref, wt_ref, bc_ref, bp_ref, qs_ref = refs
    z, y, x, c = idx[0], idx[1], idx[2], idx[3]
    step = pl.program_id(0)
    for n, (sz, x_first) in enumerate(groups):
        for ry in range(2):

            @pl.when(step == 2 * n + ry)
            def _(n=n, ry=ry, x_first=x_first):
                for rx in range(2):
                    for rc in range(2):
                        row = pl.multiple_of(((x ^ rx) * 2 + (c ^ rc)) * 256, 256)
                        src = pieces[2 * n + rc]
                        for t in range(4):
                            rows = slice(256 * t, 256 * t + 256)
                            block = src[ry, rx, rows] if x_first else src[rx, ry, rows]
                            wt_ref[0, pl.ds(row, 256), 128 * t : 128 * t + 128] = block

    qkv = dot_nn(n_ref[...], wt_ref[0, :, :384]).astype(BF)
    qkv_ref[0] = qkv
    k, v = qkv[:, 128:256], qkv[:, 256:]
    qs_ref[...] = qkv[:, :128]
    q_c = qs_ref[512:, :]
    q_p = qs_ref[pl.ds(pl.multiple_of((z * 2 + y) * 64, 64), 64), :]
    lane = lax.broadcasted_iota(jnp.int32, (1, 128), 1)
    outs = []
    for h in range(2):
        base_c, base_p = w_ref[h, 0], w_ref[h, 1]
        for a in range(32):
            bc_ref[8 * a : 8 * a + 8, :] = pltpu.roll(base_c, 1024 - (248 - 8 * a), 1)[:, :768]
        for a in range(8):
            shift = 56 - 8 * a
            bp_ref[8 * a : 8 * a + 8, :] = (pltpu.roll(base_p, 1024 - shift, 1) if shift else base_p)[:, :512]
        mine = (lane < 64) if h == 0 else (lane >= 64)
        head = lambda t: jnp.where(mine, t, jnp.zeros_like(t))
        sc = dot_nt(head(q_c), k) * 0.125 + bc_ref[...]
        sp = dot_nt(head(q_p), k[:512]) * 0.125 + bp_ref[...]

        def soft(t):
            e = jnp.exp(t - jnp.max(t, axis=-1, keepdims=True))
            return (e * (1.0 / jnp.sum(e, axis=-1, keepdims=True))).astype(BF)

        pc, pp = soft(sc), soft(sp)
        p_ref[h, 64:, :] = pc
        p_ref[h, :64, :512] = pp
        p_ref[h, :64, 512:] = jnp.zeros((64, 256), BF)
        outs.append(jnp.concatenate([dot_nn(pp, v[:512]), dot_nn(pc, v)], axis=0))
    o_ref[...] = jnp.where(lane < 64, outs[0], outs[1]).astype(BF)


def norm_kernel(idx, a_ref, b_ref, own_ref, gain_ref, src_ref, low_ref):
    z, y = idx[0], idx[1]
    for sz in range(4):
        at = lambda yy: pl.ds(pl.multiple_of(((z ^ sz) * 2 + yy) * 64, 64), 64)
        src_ref[at(y), :] = a_ref[sz]
        src_ref[at(y ^ 1), :] = b_ref[sz]
    src_ref[512:, :] = own_ref[64:, :]
    values = src_ref[...].astype(F32)
    low_ref[...] = (norm_parts(values) * gain_ref[...]).astype(BF)


def norm_rows(idx, prompt_z, prompt_y, rows_own, gain):
    whole = pl.BlockSpec(memory_space=pltpu.VMEM)
    out = jax.ShapeDtypeStruct((768, 1024), BF)
    return pl.pallas_call(
        norm_kernel,
        in_specs=[SMEM] + [whole] * 4,
        out_specs=(whole, whole),
        out_shape=(out, out),
        compiler_params=params(),
    )(idx, prompt_z, prompt_y, rows_own, gain[None])


def attend(groups, idx, normed, windows, pieces, prev):
    keys, rows = normed.shape[0], 320

    def at(i, d):
        sz = groups[0][0]
        for n, (other, unused) in enumerate(groups):
            sz = jnp.where(i // 2 == n, other, sz)
        return (d[0] ^ sz) * 2 + (d[1] ^ (i % 2))

    whole = pl.BlockSpec(memory_space=pltpu.VMEM)
    return pl.pallas_call(
        functools.partial(attend_kernel, groups, prev is None),
        grid_spec=pltpu.PrefetchScalarGridSpec(
            num_scalar_prefetch=1,
            grid=(2 * len(groups),),
            in_specs=[whole, pl.BlockSpec((2, 2, 8, 1024), lambda i, d: (at(i, d), 0, 0, 0))]
            + [whole] * len(pieces)
            + ([] if prev is None else [ANY] * 4),
            out_specs=(
                pl.BlockSpec((2, rows, keys), lambda i, d: (at(i, d), 0, 0)),
                pl.BlockSpec((rows, 128), lambda i, d: (0, at(i, d))),
                pl.BlockSpec((1, keys, 384), lambda i, d: (at(i, d), 0, 0)),
                pl.BlockSpec((1, 1024, 512), lambda i, d: (at(i, d), 0, 0)),
            ),
            scratch_shapes=[pltpu.VMEM((256, 768), F32), pltpu.VMEM((64, 512), F32), pltpu.VMEM((keys, 128), BF)],
        ),
        out_shape=(
            jax.ShapeDtypeStruct((16, rows, keys), BF),
            jax.ShapeDtypeStruct((rows, 1024), BF),
            jax.ShapeDtypeStruct((8, keys, 384), BF),
            jax.ShapeDtypeStruct((8, 1024, 512), BF),
        ),
        input_output_aliases={} if prev is None else {3 + len(pieces) + n: n for n in range(4)},
        compiler_params=params(),
        cost_estimate=COST_S,
    )(idx, normed, windows, *pieces, *([] if prev is None else prev))


def attend_back_kernel(first, idx, n_ref, p_ref, qkv_ref, wt_ref, g_ref, m_ref, gl_ref, *refs):
    if not first:
        gn_prev, refs = refs[0], refs[2:]
    keep_ref, send_ref, gn_ref, db_ref, dt_ref, qs_ref = refs
    z, y, x, c = idx[0], idx[1], idx[2], idx[3]
    own = pl.ds(pl.multiple_of((z * 2 + y) * 64, 64), 64)
    qkv = qkv_ref[0]
    k, v = qkv[:, 128:256], qkv[:, 256:]
    qs_ref[...] = qkv[:, :128]
    q = jnp.concatenate([qs_ref[own, :], qs_ref[512:, :]], axis=0)
    g = g_ref[...]
    lane = lax.broadcasted_iota(jnp.int32, (1, 128), 1)
    parts = []
    for h in range(2):
        mine = (lane < 64) if h == 0 else (lane >= 64)
        gh = jnp.where(mine, g, jnp.zeros_like(g))
        p = p_ref[h]
        pf = p.astype(F32)
        dp = dot_nt(gh, v)
        delta = jnp.sum(pf * dp, axis=-1, keepdims=True)
        ds = pf * (dp - delta)
        low = ds.astype(BF)
        acc_c = jnp.zeros((8, 1024), F32)
        for a in range(32):
            part = jnp.concatenate([ds[64 + 8 * a : 72 + 8 * a], jnp.zeros((8, 256), F32)], axis=1)
            acc_c = acc_c + pltpu.roll(part, 248 - 8 * a, 1) if a < 31 else acc_c + part
        acc_p = jnp.zeros((8, 1024), F32)
        for a in range(8):
            part = jnp.concatenate([ds[8 * a : 8 * a + 8, :512], jnp.zeros((8, 512), F32)], axis=1)
            acc_p = acc_p + (pltpu.roll(part, 56 - 8 * a, 1) if a < 7 else part)
        db_ref[h, 0] = acc_c
        db_ref[h, 1] = acc_p
        parts.append((dot_nn(low, k) * 0.125, dot_tn(low, q) * 0.125, dot_tn(p, g)))
    dq, dk, dv = [jnp.where(lane < 64, parts[0][n], parts[1][n]).astype(BF) for n in range(3)]
    dt_ref[:512, :128] = jnp.zeros((512, 128), BF)
    dt_ref[own, :128] = dq[:64]
    dt_ref[512:, :128] = dq[64:]
    dt_ref[:, 128:256] = dk
    dt_ref[:, 256:] = dv
    dt = dt_ref[...]
    dw = jnp.concatenate([dot_tn(n_ref[...], dt).astype(BF), dot_tn(m_ref[...], gl_ref[...]).astype(BF)], axis=1)
    for xx in range(2):
        for cc in range(2):
            block = dw[(xx * 2 + cc) * 256 : (xx * 2 + cc) * 256 + 256]

            @pl.when(c == cc)
            def _():
                keep_ref[x ^ xx, 0] = block

            @pl.when(c != cc)
            def _():
                send_ref[x ^ xx, 0] = block

    gn = dot_nt(dt, wt_ref[0, :, :384])

    @pl.when(pl.program_id(0) == 0)
    def _():
        gn_ref[...] = gn if first else gn_prev[...] + gn

    @pl.when(pl.program_id(0) != 0)
    def _():
        gn_ref[...] += gn


def attend_back(base, count, idx, normed, p, qkv, wt, g, mixed, g_low, gn_prev, db_prev):
    rows, keys = p.shape[1], p.shape[2]
    at = lambda i, d: (i + base) ^ (d[0] * 2 + d[1])
    whole = pl.BlockSpec((keys, 1024), lambda i, d: (0, 0))
    return pl.pallas_call(
        functools.partial(attend_back_kernel, gn_prev is None),
        grid_spec=pltpu.PrefetchScalarGridSpec(
            num_scalar_prefetch=1,
            grid=(count,),
            in_specs=[
                whole,
                pl.BlockSpec((2, rows, keys), lambda i, d: (at(i, d), 0, 0)),
                pl.BlockSpec((1, keys, 384), lambda i, d: (at(i, d), 0, 0)),
                pl.BlockSpec((1, 1024, 512), lambda i, d: (at(i, d), 0, 0)),
                pl.BlockSpec((rows, 128), lambda i, d: (0, at(i, d))),
                pl.BlockSpec((rows, 1024), lambda i, d: (0, 0)),
                pl.BlockSpec((rows, 128), lambda i, d: (0, at(i, d))),
            ]
            + ([] if gn_prev is None else [whole, ANY]),
            out_specs=(
                pl.BlockSpec((2, 1, 256, 512), lambda i, d: (0, i, 0, 0)),
                pl.BlockSpec((2, 1, 256, 512), lambda i, d: (0, i, 0, 0)),
                whole,
                pl.BlockSpec((2, 2, 8, 1024), lambda i, d: (at(i, d), 0, 0, 0)),
            ),
            scratch_shapes=[pltpu.VMEM((keys, 384), BF), pltpu.VMEM((keys, 128), BF)],
        ),
        out_shape=(
            jax.ShapeDtypeStruct((2, count, 256, 512), BF),
            jax.ShapeDtypeStruct((2, count, 256, 512), BF),
            jax.ShapeDtypeStruct((keys, 1024), F32),
            jax.ShapeDtypeStruct((16, 2, 8, 1024), F32),
        ),
        input_output_aliases={} if gn_prev is None else {9: 3},
        compiler_params=params(),
        cost_estimate=COST_E,
    )(idx, normed, p, qkv, wt, g, mixed, g_low, *([] if gn_prev is None else [gn_prev, db_prev]))


def cut_rows(t):
    return t[:, :, :, :128], t[:, :, :, 128:]


def out_back_kernel(a_ref, b_ref, c_ref, h_ref, gain_ref, cot_ref, w_ref, gh_ref, gl_ref, gm_ref, gg_ref):
    f = lambda t: t.astype(F32)
    dn = f(a_ref[...]) + f(b_ref[...]) + f(c_ref[...])
    hidden, gain = h_ref[...], gain_ref[...]
    scale = lax.rsqrt(jnp.mean(hidden * hidden, axis=-1, keepdims=True) + epsilon)
    unit = hidden * scale
    gg_ref[...] = jnp.broadcast_to(jnp.sum(dn * unit, axis=0, keepdims=True), gg_ref.shape)
    du = dn * gain
    grad = f(cot_ref[...]) + scale * (du - unit * jnp.mean(du * unit, axis=-1, keepdims=True))
    gh_ref[...] = grad
    low = grad.astype(BF)
    gl_ref[...] = low
    total = dot_nt(low[:, :128], w_ref[0, :, 384:])
    for n in range(1, 8):
        total = total + dot_nt(low[:, 128 * n : 128 * n + 128], w_ref[n, :, 384:])
    gm_ref[...] = total.astype(BF)


def out_back(parts, hidden, gain, cot, w_o):
    whole = pl.BlockSpec(memory_space=pltpu.VMEM)
    return pl.pallas_call(
        out_back_kernel,
        in_specs=[whole] * 7,
        out_specs=(whole,) * 4,
        out_shape=(
            jax.ShapeDtypeStruct((320, 1024), F32),
            jax.ShapeDtypeStruct((320, 1024), BF),
            jax.ShapeDtypeStruct((320, 1024), BF),
            jax.ShapeDtypeStruct((8, 1024), F32),
        ),
        compiler_params=params(),
        cost_estimate=COST_S,
    )(*parts, hidden, gain[None], cot, w_o)


def out_kernel(m_ref, s_ref, g_ref, w_ref, h_ref, l_ref):
    m = m_ref[...]
    for n in range(8):
        cols = slice(128 * n, 128 * n + 128)
        h_ref[:, cols] = s_ref[:, cols].astype(F32) + dot_nn(m, w_ref[n, :, 384:])
    hidden = h_ref[...]
    scale = lax.rsqrt(jnp.mean(hidden * hidden, axis=-1, keepdims=True) + epsilon)
    l_ref[...] = (hidden * scale * g_ref[...]).astype(BF)


def project_out(mixed, rows_own, gain, wt):
    whole = pl.BlockSpec(memory_space=pltpu.VMEM)
    return pl.pallas_call(
        out_kernel,
        in_specs=[whole] * 4,
        out_specs=(whole,) * 2,
        out_shape=(jax.ShapeDtypeStruct((320, 1024), F32), jax.ShapeDtypeStruct((320, 1024), BF)),
        compiler_params=params(),
        cost_estimate=COST_S,
    )(mixed, rows_own, gain[None], wt)


WIDE = 1920


def window_kernel(idx, t_ref, b_ref, o_ref):
    onehot = jnp.where(lax.broadcasted_iota(jnp.int32, (BUCKETS, WIDE), 0) == t_ref[...], 1.0, 0.0)
    rev = lax.dot_general(b_ref[...], onehot, (((0,), (0,)), ((), ())), precision=precise, preferred_element_type=F32)
    rev = jnp.where(lax.broadcasted_iota(jnp.int32, (16, WIDE), 1) < 768, rev, NEG)
    tail = pltpu.roll(rev, WIDE - 704 + 64 * (idx[0] * 2 + idx[1]), 1)
    for s in range(8):
        o_ref[:, 0, s, :] = (pltpu.roll(rev, WIDE - 7 + s, 1) if s < 7 else rev)[:, :1024]
        o_ref[:, 1, s, :] = (pltpu.roll(tail, WIDE - 7 + s, 1) if s < 7 else tail)[:, :1024]


def bias_windows(idx, table_rev, bias_f):
    whole = pl.BlockSpec(memory_space=pltpu.VMEM)
    return pl.pallas_call(
        window_kernel,
        in_specs=[SMEM, whole, whole],
        out_specs=whole,
        out_shape=jax.ShapeDtypeStruct((16, 2, 8, 1024), F32),
        compiler_params=params(),
    )(idx, table_rev, bias_f)


def pack_kernel(idx, t_ref, db_ref, gn_ref, src_ref, gf_ref, r_ref, small_ref, keep_ref, send_ref):
    z, y = idx[0], idx[1]

    def gather(n):
        total = jnp.zeros((16, WIDE), F32)
        for s in range(8):
            part = jnp.concatenate([db_ref[:, n, s, :], jnp.zeros((16, WIDE - 1024), F32)], axis=1)
            total = total + (pltpu.roll(part, 7 - s, 1) if s < 7 else part)
        return total

    rev = gather(0) + pltpu.roll(gather(1), 704 - 64 * (z * 2 + y), 1)
    onehot = jnp.where(lax.broadcasted_iota(jnp.int32, (BUCKETS, 768), 0) == t_ref[:, :768], 1.0, 0.0)
    bias = lax.dot_general(
        rev[:, :768], onehot, (((1,), (1,)), ((), ())), precision=precise, preferred_element_type=F32
    )
    src = src_ref[...].astype(F32)
    unit = src * lax.rsqrt(jnp.mean(src * src, axis=-1, keepdims=True) + epsilon)
    small_ref[...] = jnp.zeros_like(small_ref)
    small_ref[0:1, :] = jnp.sum(gn_ref[...] * unit, axis=0, keepdims=True)
    small_ref[1:2, :] = gf_ref[0:1, :]
    small_ref[2:5, :] = r_ref[0:3, :]
    small_ref[8:24, 0:BUCKETS] = bias
    for sz in range(4):
        at = lambda yy: pl.ds(pl.multiple_of(((z ^ sz) * 2 + yy) * 64, 64), 64)
        keep_ref[sz] = gn_ref[at(y), :].astype(BF)
        send_ref[sz] = gn_ref[at(y ^ 1), :].astype(BF)


def pack(idx, table_rev, dbias, gn, src, gain_ffn_part, router_part):
    whole = pl.BlockSpec(memory_space=pltpu.VMEM)
    return pl.pallas_call(
        pack_kernel,
        in_specs=[SMEM] + [whole] * 6,
        out_specs=(whole,) * 3,
        out_shape=(
            jax.ShapeDtypeStruct((24, 1024), F32),
            jax.ShapeDtypeStruct((4, 64, 1024), BF),
            jax.ShapeDtypeStruct((4, 64, 1024), BF),
        ),
        compiler_params=params(),
        cost_estimate=COST_S,
    )(idx, table_rev, dbias, gn, src, gain_ffn_part, router_part)


def final_kernel(p_ref, near_ref, opp_ref, gn_ref, src_ref, gain_ref, gh_ref, o_ref):
    f = lambda t: t.astype(F32)
    own = f(p_ref[0]) + f(near_ref[...]) + f(opp_ref[...])
    grad = jnp.concatenate([own, gn_ref[512:, :]], axis=0) * gain_ref[...]
    src = f(src_ref[...])
    scale = lax.rsqrt(jnp.mean(src * src, axis=-1, keepdims=True) + epsilon)
    unit = src * scale
    back = scale * (grad - unit * jnp.mean(grad * unit, axis=-1, keepdims=True))
    o_ref[...] = (gh_ref[...] + back).astype(BF)


def finish(parts, near, opp, gn, src, gain, grad_hidden):
    whole = pl.BlockSpec(memory_space=pltpu.VMEM)
    return pl.pallas_call(
        final_kernel,
        in_specs=[whole] * 7,
        out_specs=whole,
        out_shape=jax.ShapeDtypeStruct((320, 1024), BF),
        compiler_params=params(),
        cost_estimate=COST_S,
    )(parts, near, opp, gn, src, gain[None], grad_hidden)


def add_low(a, b):
    return (a.astype(F32) + b.astype(F32)).astype(BF)


PIECES = [(0, 320), (320, 320), (640, 320), (960, 160), (1120, 160)]


def fetch_pieces(want, x_parts, g_parts, x_scr, g_scr, sem):
    copies = []
    for rc in range(2):
        for n, (row, size) in enumerate(PIECES):
            at = rc * 1280 + row
            tile = at // 640
            if want not in (None, tile):
                continue
            k = rc * 5 + n
            copies.append(pltpu.make_async_copy(x_parts[k], x_scr.at[pl.ds(at, size)], sem.at[k, 0]))
            src = g_parts[k].at[pl.ds(160 if n == 4 else 0, size)]
            copies.append(pltpu.make_async_copy(src, g_scr.at[pl.ds(at, size)], sem.at[k, 1]))
    return copies


def expert_kernel(group, last, *refs):
    refs = list(refs)
    step = pl.program_id(0)
    count = len(group)
    idx, refs = refs[0], refs[1:]
    w_at = idx[2] * 2 + idx[3]
    src, m_ref = refs[:2]
    if not last:
        x_parts, g_parts = refs[2:12], refs[12:22]
        out_ref, dx_ref, dh_ref, win_ref, s_ref, xo_ref, go_ref, w_scr, sem, x_scr, g_scr, psem = refs[22:]
    else:
        x_ref, g_ref, out_prev, dx_prev, s_prev = refs[2:7]
        out_ref, out_c_ref, dx_ref, dx_c_ref, dh_ref, win_ref, w_scr, sem = refs[7:]

    @pl.when(step == 0)
    def _():
        copies = [
            pltpu.make_async_copy(
                src.at[n, r, e],
                w_scr.at[e, :, pl.ds(96 * n, 96), pl.ds(pl.multiple_of((w_at ^ r) * 256, 256), 256)],
                sem.at[n, 4 * e + r],
            )
            for e in range(count)
            for n in range(4)
            for r in range(4)
        ]
        for copy in copies:
            copy.start()
        if not last:
            for copy in fetch_pieces(None, x_parts, g_parts, x_scr, g_scr, psem):
                copy.start()
        for copy in copies:
            copy.wait()

    if not last:
        for t in range(4):

            @pl.when(step == t)
            def _(t=t):
                for copy in fetch_pieces(t, x_parts, g_parts, x_scr, g_scr, psem):
                    copy.wait()

        rows = pl.ds(pl.multiple_of(step * 640, 640), 640)
        x, g = x_scr[rows, :], g_scr[rows, :]
        xo_ref[...] = x
        go_ref[...] = g
    else:
        x, g = x_ref[...], g_ref[...]
    m = m_ref[...]
    lane = lax.broadcasted_iota(jnp.int32, (1, 384), 1)
    scores = []
    for k, expert in enumerate(group):
        w_gu = w_scr[k, 0:2].reshape(768, 1024)
        w_d = w_scr[k, 2]
        gu = dot_nt(x, w_gu)
        gi = dot_nt(g, w_d)
        gate, up = gu[:, :384], gu[:, 384:]
        if k == 0:
            l = [gate[:, 88 + n : 89 + n] for n in range(3)]
            top = jnp.maximum(jnp.maximum(l[0], l[1]), l[2])
            ex = [jnp.exp(v - top) for v in l]
            inv = 1.0 / (ex[0] + ex[1] + ex[2])
            p = [v * inv for v in ex]
        keep = m[:, expert : expert + 1]
        w = p[expert] * keep
        sq = gate * gate
        th = jnp.tanh(0.7978845608028654 * gate * (1.0 + 0.044715 * sq))
        half1 = 0.5 + 0.5 * th
        act = gate * half1
        dact = half1 + (0.5 * gate) * (1.0 - th * th) * (0.7978845608028654 + 0.10703222440890037 * sq)
        inner = (act * up).astype(BF).astype(F32)
        s = jnp.sum(inner * gi, axis=-1, keepdims=True) * keep
        scores.append(s)
        gin = gi * w
        dg = gin * up * dact
        du = gin * act
        if last:
            ss = [s_prev[...][:, 0:1], s_prev[...][:, 1:2], s]
            dot = p[0] * ss[0] + p[1] * ss[1] + p[2] * ss[2]
            for n in range(3):
                dg = jnp.where(lane == 88 + n, p[n] * (ss[n] - dot), dg)
        win = (inner * w).astype(BF)
        dh = jnp.concatenate([dg.astype(BF), du.astype(BF)], axis=1)
        dh_ref[:, 768 * k : 768 * k + 768] = dh
        win_ref[:, 384 * k : 384 * k + 384] = win
        o_k, dx_k = dot_nn(win, w_d), dot_nn(dh, w_gu)
        out, dx = (o_k, dx_k) if k == 0 else (out + o_k, dx + dx_k)
    if last:
        out = (out + out_prev[...].astype(F32)).astype(BF)
        dx = (dx + dx_prev[...].astype(F32)).astype(BF)

        @pl.when(step < 2)
        def _():
            out_c_ref[...] = out
            dx_c_ref[...] = dx

        @pl.when(step >= 2)
        def _():
            out_ref[...] = out
            dx_ref[...] = dx
    else:
        out_ref[...] = out.astype(BF)
        dx_ref[...] = dx.astype(BF)
        s_ref[...] = jnp.where(lane[:, :128] == 0, scores[0], scores[1])


def expert_call(group, idx, x, g, m, src, prev, tile=640):
    total, count = 2560, len(group)
    last = prev is not None
    at = (lambda i: i ^ 2) if last else (lambda i: i)
    row = lambda n: pl.BlockSpec((tile, n), lambda i: (at(i), 0))
    shape = lambda n, t: jax.ShapeDtypeStruct((total, n), t)
    scratch = [pltpu.VMEM((count, 3, 384, 1024), BF), pltpu.SemaphoreType.DMA((4, 4 * count))]
    if not last:
        ins = [idx, src, m, *x, *g]
        specs = [SMEM, ANY, row(128)] + [ANY] * 20
        outs = [(1024, BF), (1024, BF), (768 * count, BF), (384 * count, BF), (128, F32), (1024, BF), (1024, BF)]
        out_shape = tuple(shape(n, t) for n, t in outs)
        out_specs = tuple(row(n) for n, t in outs)
        scratch += [pltpu.VMEM((total, 1024), BF), pltpu.VMEM((total, 1024), BF), pltpu.SemaphoreType.DMA((10, 2))]
    else:
        ins = [idx, src, m, x, g, *prev]
        specs = [SMEM, ANY, row(128)] + [row(1024)] * 4 + [row(128)]
        half = jax.ShapeDtypeStruct((total // 2, 1024), BF)
        mine = pl.BlockSpec((tile, 1024), lambda i: (jnp.maximum(i - 2, 0), 0))
        other = pl.BlockSpec((tile, 1024), lambda i: (jnp.minimum(i, 1), 0))
        out_shape = (half, half, half, half, shape(768 * count, BF), shape(384 * count, BF))
        out_specs = (mine, other, mine, other, row(768 * count), row(384 * count))
    return pl.pallas_call(
        functools.partial(expert_kernel, group, last),
        grid=(total // tile,),
        out_shape=out_shape,
        in_specs=specs,
        out_specs=out_specs,
        scratch_shapes=scratch,
        compiler_params=params(),
        cost_estimate=COST_E,
    )(*ins)


def line_collect(part_of, z):
    at = lambda n: part_of(z ^ n)
    near = pair_z(at(1))
    opp = flip_z(add_low(at(3), pair_z(at(2))))
    return (at(0).astype(F32) + near.astype(F32) + opp.astype(F32)).astype(BF)


def trade_wt(v):
    return lax.all_to_all(v, "wt", 0, 0, tiled=True)


def sum_all(v):
    v = v + move_c(v)
    v = v + move_x(v)
    v = v + move_y(v)
    v = v + lax.ppermute(v, "ctx", [(i, i ^ 2) for i in range(8)])
    return v + lax.ppermute(v, "ctx", [(i, i ^ 4) for i in range(8)])


def norm_parts(values):
    return values * lax.rsqrt(jnp.mean(values * values, axis=-1, keepdims=True) + epsilon)


def local_fast(
    tokens, cotangent, w_query, w_key, w_value, w_out, gain_attn, gain_ffn, w_router, rel_bias,
    exp_gate, exp_up, exp_down, bucket_table, expert_ids, priority,
):
    ctx_index = lax.axis_index("ctx").astype(jnp.int32)
    wt_index = lax.axis_index("wt").astype(jnp.int32)
    z, y, x, c = ctx_index // 2, ctx_index % 2, wt_index // 2, wt_index % 2
    idx = jnp.stack([z, y, x, c])
    rows_own = tokens[0, 0]

    packed = jnp.concatenate(
        [gain_attn[None], gain_ffn[None], w_router.T, jnp.pad(rel_bias.reshape(1, 128), ((0, 0), (0, 128))),
         jnp.zeros((2, 256), BF)], axis=0
    )
    ids, rank = expert_ids[0, 0], priority[0, 0]
    expert = ids.T.reshape(-1)
    rank_key = (jnp.arange(TOP, dtype=jnp.int32)[:, None] * 320 + rank[None, :]).reshape(-1)
    earlier = (expert[:, None] == expert[None, :]) & (rank_key[None, :] < rank_key[:, None])
    keep = (jnp.sum(earlier.astype(jnp.int32), axis=1) < CAP).reshape(TOP, 320)
    hold = jnp.sum(
        jnp.where((ids.T[:, :, None] == jnp.arange(EXPERTS, dtype=jnp.int32)) & keep[:, :, None], 1.0, 0.0), axis=0
    )
    marks = jnp.pad(hold.reshape(960), (0, 1088)).astype(BF).reshape(16, 128)
    cot = cotangent[0, 0]

    def pieces(v):
        return jnp.pad(v.reshape(3, 4, 88, 256), ((0, 0), (0, 0), (0, 8), (0, 0)))

    gate_t, up_t = exp_gate.transpose(0, 2, 1), exp_up.transpose(0, 2, 1)
    gate_p = pieces(gate_t)
    router_rows = jnp.broadcast_to(
        jnp.pad(w_router.T, ((0, 5), (0, 0)))[None, None], (3, 4, 8, 256)
    )
    gate_p = jnp.concatenate([gate_p[:, :, :88], router_rows], axis=2)
    share = jnp.stack([gate_p, pieces(up_t), pieces(exp_down)], axis=1).transpose(2, 0, 1, 3, 4)
    pick = lambda v, n, d: lax.dynamic_index_in_dim(v, n, d, keepdims=False)
    unit = jnp.stack([w_query, w_key, w_value, w_out]).reshape(1024, 128)
    prompt_own = rows_own[:64]
    along = jnp.concatenate([unit, prompt_own.reshape(512, 128)], axis=0)
    weights_in = lambda v: v[:1024]
    rows_in = lambda v: v[1024:].reshape(64, 1024)
    share = share.reshape(2, 2, 3, 3, 96, 256)
    share_x, share_own = pick(share, 1 - x, 0), pick(share, x, 0)
    packed_c, packed_x, packed_xc, along, share_x = phase(
        move_c(packed), move_x(packed), lax.ppermute(packed, "wt", [(i, i ^ 3) for i in range(4)]), along, share_x
    )
    unit_0 = jnp.concatenate([unit, marks], axis=0)
    near, opp, p_cross, y0, share_x, g_y, share_own = phase(
        pair_z(along), flip_z(along), lax.ppermute(prompt_own, "ctx", [(i, i ^ 4) for i in range(8)]),
        move_y(unit_0), move_x(share_x), move_y(cot), share_own
    )
    s0 = jnp.stack([unit_0, y0])
    unit_1, unit_3 = weights_in(near), weights_in(opp)
    prompt_z = jnp.stack([prompt_own, rows_in(near), p_cross, rows_in(opp)])
    share = jnp.stack([share_own, share_x])
    share_own, share_c = pick(share, c, 1), pick(share, 1 - c, 1)
    s0, unit_1, unit_3, prompt_z, share_c, share_own, small = phase(
        s0, unit_1, unit_3, prompt_z, share_c, share_own, jnp.stack([packed, packed_c, packed_x, packed_xc])
    )
    small = jnp.take(small, jnp.arange(4, dtype=jnp.int32) ^ wt_index, axis=0)
    gain_attn_f = small[:, 0].reshape(1024).astype(F32)
    gain_ffn_f = small[:, 1].reshape(1024).astype(F32)
    bias_f = small[:, 5, :128].reshape(4, 32, 4).transpose(1, 0, 2).reshape(32, 16).astype(F32)
    table_rev = jnp.pad(bucket_table[::-1], (0, WIDE - 768), constant_values=-1)[None]
    windows = bias_windows(idx, table_rev, bias_f)
    cross, prompt_y, x0, x1, y3, windows, gain_attn_f = phase(
        pair_z(unit_3), move_y(prompt_z), move_x(s0), move_x(unit_1), move_y(unit_3), windows, gain_attn_f
    )
    t0, s1, s3 = jnp.stack([s0, x0]), jnp.stack([unit_1, x1]), jnp.stack([unit_3, y3])
    t0, s1, s3 = phase(t0, s1, s3)
    c0, share_c, s1, s3 = phase(move_c(t0), move_c(share_c), s1, s3)
    share = jnp.stack([share_own, share_c], axis=1).reshape(4, 3, 3, 96, 256)
    spread = [
        lax.all_gather(t, "ctx", axis=0, tiled=False, axis_index_groups=LINES_Z) for t in (share[:, :2], share[:, 2:])
    ]
    source_all, all_low = norm_rows(idx, prompt_z, prompt_y, rows_own, gain_attn_f)
    state = attend(((0, False),), idx, all_low, windows, (t0, c0), None)
    *state, y1, x3, x2, g_cy = phase(*state, move_y(s1), move_x(s3), move_x(cross), move_c(g_y))
    t1, t3, s2, *state = phase(jnp.stack([s1, y1]), jnp.stack([s3, x3]), jnp.stack([cross, x2]), *state)
    c1, c3, *state = phase(move_c(t1), move_c(t3), *state)
    state = attend(((1, True), (3, False)), idx, all_low, windows, (t1, c1, t3, c3), state)
    *state, y2, g_x, g_c = phase(*state, move_y(s2), move_x(cot), move_c(cot))
    t2, *state = phase(jnp.stack([s2, y2]), *state)
    c2, *state = phase(move_c(t2), *state)
    state = attend(((2, True),), idx, all_low, windows, (t2, c2), state)
    marks_all = jnp.stack([t0[:, :, 1024:], c0[:, :, 1024:]]).reshape(2, 2, 2, 2048)[..., :960]
    marks_all = marks_all.transpose(0, 2, 1, 3).reshape(2560, 3).astype(F32)
    marks_all = jnp.pad(marks_all, ((0, 0), (0, 125)))
    *state, g_cx = phase(*state, move_c(g_x))
    probs, mixed, qkv, w_all = state
    hidden, normed = project_out(mixed, rows_own, gain_ffn_f, w_all)
    hidden, normed, g_xy = phase(hidden, normed, move_x(g_y))

    x_x, x_y, x_c, g_cxy, marks_all = phase(move_x(normed), move_y(normed), move_c(normed), move_c(g_xy), marks_all)
    x_a, x_b, x_cx, x_cy = phase(move_x(x_y[:160]), move_y(x_x[160:]), move_c(x_x), move_c(x_y))
    x_parts = [normed, x_x, x_y, x_a, x_b, x_c, x_cx, x_cy, move_c(x_a), move_c(x_b)]
    cot_parts = [cot, g_x, g_y, g_xy, g_xy, g_c, g_cx, g_cy, g_cxy, g_cxy]

    def along_z(gw, dw):
        gw, dw = gw.astype(BF).reshape(-1, 2, 4, 96, 1024), dw.astype(BF).reshape(-1, 1, 4, 96, 1024)
        return jnp.concatenate([gw, dw], axis=1).transpose(2, 0, 1, 3, 4)

    def reduce_z(both):
        flat = both.reshape(4, -1, 1024)
        got = lax.psum_scatter(flat, "ctx", scatter_dimension=0, axis_index_groups=LINES_Z)
        return got.reshape(both.shape[1:])

    out, dx, dh, win, s_01, x_all, g_all = expert_call((0, 1), idx, x_parts, cot_parts, marks_all, spread[0], None)
    both_01 = along_z(dot_tn(dh, x_all), dot_tn(win, g_all))
    both_01, out = phase(both_01, out)
    bulk = [reduce_z(both_01)]
    out, out_c, dx, dx_c, dh_2, win_2 = expert_call(
        (2,), idx, x_all, g_all, marks_all, spread[1], (out, dx, s_01)
    )

    got, g_d2, dh_2 = phase(move_c(dx_c), dot_tn(win_2, g_all), dh_2)
    last, rest = add_low(dx[960:], got[960:]), add_low(dx[:960], got[:960])
    last_a, last_b, dh_2, rest = phase(last[:160], last[160:], dh_2, rest)
    both_2 = along_z(dot_tn(dh_2, x_all), g_d2)
    d_a, d_b, rest, both_2, o_got = phase(move_x(last_a), move_y(last_b), rest, both_2, move_c(out_c))

    def mix_in(rest, a, b):
        v_x = jnp.concatenate([rest[320:480], add_low(rest[480:640], b)], axis=0)
        v_y = jnp.concatenate([add_low(rest[640:800], a), rest[800:]], axis=0)
        return v_x, v_y

    bulk.append(reduce_z(both_2))
    v_x, v_y = mix_in(rest, d_a, d_b)
    v_x, v_y, out, o_got = phase(v_x, v_y, out, o_got)
    o_last, o_rest = add_low(out[960:], o_got[960:]), add_low(out[:960], o_got[:960])
    v_x, v_y, o_la, o_lb, o_rest = phase(move_x(v_x), move_y(v_y), o_last[:160], o_last[160:], o_rest)
    router_part = both_2[0, 0, 0, 88:96].astype(F32)
    grad_hidden, grad_low, grad_mixed, gain_ffn_part = out_back(
        (rest[:320], v_x, v_y), hidden, gain_ffn_f, cot, w_all
    )
    back_of = lambda base, count, *prev: attend_back(
        base, count, idx, all_low, probs, qkv, w_all, grad_mixed, mixed, grad_low, *prev
    )
    keep_f, send_f, gn, dbias = back_of(4, 4, None, None)
    o_a, o_b, gn = phase(move_x(o_la), move_y(o_lb), gn)
    o_x, o_y, gn = phase(*mix_in(o_rest, o_a, o_b), gn)
    o_x, o_y, gn, bulk[0] = phase(o_x, o_y, gn, bulk[0])
    keep_n, send_n, gn, dbias = back_of(2, 2, gn, dbias)
    o_x, o_y, got, gn = phase(move_x(o_x), move_y(o_y), move_c(send_f), gn)
    combined = o_rest[:320].astype(F32) + o_x.astype(F32) + o_y.astype(F32)
    output = (hidden + combined).astype(BF).reshape(1, 1, 320, 1024)

    fa, fb = cut_rows(add_low(keep_f, got).reshape(2, 2, 2, 256, 512))
    fa0, fa1, fb0, fb1, gn = phase(fa[0], fa[1], fb[:, :, 0], fb[:, :, 1], gn)
    keep_h, send_h, gn_all, dbias = back_of(0, 2, gn, dbias)
    fx, fy, got_n, gn_all = phase(move_x(fa1), move_y(fb1), move_c(send_n), gn_all)
    fa, fb = add_low(fa0, fx), add_low(fb0, fy)
    packed = pack(idx, table_rev, dbias, gn_all, source_all, gain_ffn_part, router_part)
    got, fy, fx, smalls, gp_keep, gp_send = phase(move_c(send_h), move_y(fa[:, 1]), move_x(fb[1]), *packed)
    fy, bulk[1] = phase(fy, bulk[1])
    far = jnp.concatenate([add_low(fa[:, 0], fy), add_low(fb[0], fx)], axis=1)
    block = lambda t: t.reshape(2, 1, 2, 256, 512)
    h = jnp.concatenate([add_low(block(keep_h), block(got)), add_low(block(keep_n), block(got_n))], axis=1)
    ha, hb = cut_rows(h)
    hx, hy, f_cross, gp_got, sm = phase(
        move_x(ha[1]), move_y(hb[:, :, 1]), pair_z(far[0]), move_y(gp_send), move_c(smalls)
    )
    ha, hb = add_low(ha[0], hx), add_low(hb[:, :, 0], hy)
    gp = add_low(gp_keep, gp_got)
    smalls = smalls + sm
    hy, hx, f_opp, gp_cross, sm = phase(
        move_y(ha[:, 1]), move_x(hb[1]), flip_z(add_low(far[1], f_cross)), pair_z(gp[2]), move_x(smalls)
    )
    here = jnp.concatenate([add_low(ha[:, 0], hy), add_low(hb[0], hx)], axis=1)
    smalls = smalls + sm
    h_near, gp_opp, gp_near, sm = phase(
        pair_z(here[1]), flip_z(add_low(gp[3], gp_cross)), pair_z(gp[1]), move_y(smalls)
    )
    smalls = smalls + sm
    tot = here[0].astype(F32) + h_near.astype(F32) + f_opp.astype(F32)
    grad_tokens = finish(gp, gp_near, gp_opp, gn_all, rows_own, gain_attn_f, grad_hidden).reshape(1, 1, 320, 1024)
    sm_1, sm_2, sm_3 = [lax.ppermute(smalls, "ctx", [(i, i ^ n) for i in range(8)]) for n in (2, 4, 6)]
    smalls = (smalls + sm_1) + (sm_2 + sm_3)
    mine = lax.dynamic_slice_in_dim(smalls, wt_index * 256, 256, 1)
    res_gain_attn, res_gain_ffn, res_router = mine[0], mine[1], mine[2:5].T
    res_bias = lax.dynamic_slice_in_dim(smalls[8:24, :BUCKETS], wt_index * 4, 4, 0).T

    back = jnp.concatenate(bulk).reshape(3, 3, 96, 4, 256).transpose(3, 0, 1, 2, 4)
    back = trade_wt(back)[:, :, :, :88].transpose(1, 2, 0, 3, 4).reshape(3, 3, 352, 256).astype(F32)
    res_gate, res_up, res_down = back[:, 0].transpose(0, 2, 1), back[:, 1].transpose(0, 2, 1), back[:, 2]

    return (
        output, grad_tokens, tot[:, :128], tot[:, 128:256], tot[:, 256:384], tot[:, 384:], res_gain_attn, res_gain_ffn, res_router, res_bias,
        res_gate, res_up, res_down,
    )


def solution(mesh):
    fast = mesh.shape["ctx"] == FAST_CTX and mesh.shape["wt"] == FAST_WT
    return jax.shard_map(
        local_fast if fast else local,
        mesh=mesh,
        in_specs=(
            P("wt", "ctx", None, None),
            P("wt", "ctx", None, None),
            P("wt", "ctx"),
            P("wt", "ctx"),
            P("wt", "ctx"),
            P("wt", "ctx"),
            P("wt"),
            P("wt"),
            P("wt", None),
            P(None, "wt"),
            P(None, "wt", "ctx"),
            P(None, "wt", "ctx"),
            P(None, "ctx", "wt"),
            P(),
            P("wt", "ctx", None, None),
            P("wt", "ctx", None),
        ),
        out_specs=(
            P("wt", "ctx", None, None),
            P("wt", "ctx", None, None),
            P("wt", "ctx"),
            P("wt", "ctx"),
            P("wt", "ctx"),
            P("wt", "ctx"),
            P("wt"),
            P("wt"),
            P("wt", None),
            P(None, "wt"),
            P(None, "wt", "ctx"),
            P(None, "wt", "ctx"),
            P(None, "ctx", "wt"),
        ),
        check_vma=False,
    )
```

```python
import functools

import jax
import jax.numpy as jnp
from jax import lax
from jax.experimental import pallas as pl
from jax.experimental.pallas import tpu as pltpu
from jax.sharding import PartitionSpec as P

HEADS = 16
HEAD_DIM = 64
BUCKETS = 32
EXPERTS = 3
TOP = 2
LEN = 256
CAP = 267


epsilon = 1e-06
precise = lax.Precision.HIGHEST


def rms_norm(values, gain_vec):
    return (
        values * lax.rsqrt(jnp.mean(values * values, axis=-1, keepdims=True) + epsilon) * gain_vec
    )


def gelu_product(gate_pre, up_pre):
    return jax.nn.gelu(gate_pre, approximate=True) * up_pre


def routing(expert_ids, priority, capacity, expert_count):
    tok_rows = expert_ids.shape[0]
    top_count = expert_ids.shape[1]
    expert = expert_ids.T.reshape(-1)
    rank_key = (
        jnp.arange(top_count, dtype=jnp.int32)[:, None] * tok_rows + priority[None, :]
    ).reshape(-1)
    earlier = (expert[:, None] == expert[None, :]) & (rank_key[None, :] < rank_key[:, None])
    places = jnp.sum(earlier.astype(jnp.int32), axis=1)
    keep_mask = places < capacity
    slot_ids = expert * capacity + jnp.minimum(places, capacity - 1)
    slot_hits = jnp.where(
        (slot_ids[:, None] == jnp.arange(expert_count * capacity, dtype=jnp.int32)[None, :])
        & keep_mask[:, None],
        1.0,
        0.0,
    )
    dispatch = jnp.sum(slot_hits.reshape(top_count, tok_rows, expert_count * capacity), axis=0).T
    return (keep_mask, slot_ids, slot_hits, dispatch)


def gate_values(logits, expert_ids, keep_mask):
    chances = jax.nn.softmax(logits, axis=-1)
    picked = jnp.take_along_axis(chances, expert_ids, axis=1).T.reshape(-1)
    return jnp.where(keep_mask, picked, 0.0)


def toeplitz(reversed_bias, top_start, row_total, key_total):
    window_len = row_total + key_total
    window = lax.dynamic_slice_in_dim(reversed_bias, top_start, window_len, 1)
    tiled = jnp.tile(window, (1, row_total))[:, : row_total * (window_len - 1)]
    return tiled.reshape(window.shape[0], row_total, window_len - 1)[:, :, row_total - 1 :]


def toeplitz_back(grad_block, row_total, key_total):
    window_len = row_total + key_total
    head_total = grad_block.shape[0]
    placed = jnp.pad(grad_block, ((0, 0), (0, 0), (row_total - 1, 0))).reshape(
        head_total, row_total * (window_len - 1)
    )
    placed = jnp.pad(placed, ((0, 0), (0, row_total)))
    return jnp.sum(placed.reshape(head_total, row_total, window_len), axis=1)


def add_window(table, piece, start):
    current = lax.dynamic_slice_in_dim(table, start, piece.shape[1], 1)
    return lax.dynamic_update_slice_in_dim(table, current + piece, start, 1)


def sweep(step_fn, start_state, prompt_items, local_items):
    state_mid, stacked = lax.scan(step_fn, start_state, prompt_items)
    state_end, last_out = step_fn(state_mid, local_items)
    return (state_end, stacked, last_out)


def local(
    tokens,
    cotangent,
    w_query,
    w_key,
    w_value,
    w_out,
    gain_attn,
    gain_ffn,
    w_router,
    rel_bias,
    exp_gate,
    exp_up,
    exp_down,
    bucket_table,
    expert_ids,
    priority,
):
    tok_rows = tokens.shape[2]
    model_width = tokens.shape[3]
    ctx_count = lax.axis_size("ctx")
    my_block = lax.axis_index("ctx")
    prompt_rows = tok_rows - LEN
    cont_rows = tok_rows - prompt_rows
    prompt_len = prompt_rows * ctx_count
    dist_count = bucket_table.shape[0]
    head_count = HEADS
    head_width = HEAD_DIM
    score_scale = HEAD_DIM ** (-0.5)
    steps_count = max(1, ctx_count // 8)
    block_keys = prompt_len // steps_count
    cols_query, cols_key, cols_value, cols_out, cols_gate, cols_up, cols_down = (
        lax.all_gather(w_query, "ctx", axis=1, tiled=True),
        lax.all_gather(w_key, "ctx", axis=1, tiled=True),
        lax.all_gather(w_value, "ctx", axis=1, tiled=True),
        lax.all_gather(w_out, "ctx", axis=1, tiled=True),
        lax.all_gather(exp_gate, "ctx", axis=2, tiled=True),
        lax.all_gather(exp_up, "ctx", axis=2, tiled=True),
        lax.all_gather(exp_down, "ctx", axis=1, tiled=True),
    )
    gathered = (
        lax.all_gather(cols_query, "wt", axis=0, tiled=True),
        lax.all_gather(cols_key, "wt", axis=0, tiled=True),
        lax.all_gather(cols_value, "wt", axis=0, tiled=True),
        lax.all_gather(cols_out, "wt", axis=0, tiled=True),
        lax.all_gather(cols_gate, "wt", axis=1, tiled=True),
        lax.all_gather(cols_up, "wt", axis=1, tiled=True),
        lax.all_gather(cols_down, "wt", axis=2, tiled=True),
        lax.all_gather(gain_attn, "wt", axis=0, tiled=True),
        lax.all_gather(gain_ffn, "wt", axis=0, tiled=True),
        lax.all_gather(w_router, "wt", axis=0, tiled=True),
        lax.all_gather(rel_bias, "wt", axis=1, tiled=True),
    )
    (
        full_query,
        full_key,
        full_value,
        full_out,
        full_gate,
        full_up,
        full_down,
        full_gain_attn,
        full_gain_ffn,
        full_router,
        full_bias,
    ) = gathered
    gain_attn_f = full_gain_attn.astype(jnp.float32)
    gain_ffn_f = full_gain_ffn.astype(jnp.float32)
    source = tokens[0, 0].astype(jnp.float32)
    normed_attn = rms_norm(source, gain_attn_f)
    normed_attn_low = normed_attn.astype(jnp.bfloat16)
    query_low = jnp.dot(normed_attn_low, full_query, preferred_element_type=jnp.float32).astype(
        jnp.bfloat16
    )
    key_low = jnp.dot(normed_attn_low, full_key, preferred_element_type=jnp.float32).astype(
        jnp.bfloat16
    )
    value_low = jnp.dot(normed_attn_low, full_value, preferred_element_type=jnp.float32).astype(
        jnp.bfloat16
    )
    far_keys, far_values = (
        lax.all_gather(key_low[:prompt_rows], "ctx", axis=0, tiled=True),
        lax.all_gather(value_low[:prompt_rows], "ctx", axis=0, tiled=True),
    )
    row_index = jnp.arange(tok_rows, dtype=jnp.int32)
    query_pos = jnp.where(
        row_index < prompt_rows,
        my_block * prompt_rows + row_index,
        prompt_len + row_index - prompt_rows,
    )
    bucket_onehot = jnp.where(
        bucket_table[:, None] == jnp.arange(BUCKETS, dtype=jnp.int32)[None, :], 1.0, 0.0
    )
    bias_rows = jnp.dot(bucket_onehot, full_bias.astype(jnp.float32), precision=precise).T
    reversed_bias = jnp.concatenate([bias_rows[:, ::-1], jnp.zeros_like(bias_rows)], axis=1)
    prompt_starts = jnp.arange(steps_count, dtype=jnp.int32) * block_keys
    local_start = jnp.asarray(prompt_len, dtype=jnp.int32)
    query_heads = query_low.reshape(tok_rows, head_count, head_width)

    def blocks_of(far_array):
        return far_array.reshape(steps_count, block_keys, model_width)

    def window_starts(key_start):
        prompt_top = dist_count - my_block * prompt_rows + key_start - prompt_rows
        cont_top = dist_count - prompt_len + key_start - cont_rows
        return (prompt_top, cont_top)

    def block_scores(key_block, key_start):
        key_total = key_block.shape[0]
        key_heads = key_block.reshape(key_total, head_count, head_width)
        logit_raw = (
            jnp.einsum("qhd,khd->hqk", query_heads, key_heads, preferred_element_type=jnp.float32)
            * score_scale
        )
        key_pos = key_start + jnp.arange(key_total, dtype=jnp.int32)
        offset = query_pos[:, None] - key_pos[None, :]
        prompt_top, cont_top = window_starts(key_start)
        bias_block = jnp.concatenate(
            [
                toeplitz(reversed_bias, prompt_top, prompt_rows, key_total),
                toeplitz(reversed_bias, cont_top, cont_rows, key_total),
            ],
            axis=1,
        )
        return jnp.where(offset[None] >= 0, logit_raw + bias_block, -1e30)

    def stats_step(state_in, block_item):
        run_max, run_sum = state_in
        scores = block_scores(block_item[0], block_item[1])
        new_max = jnp.maximum(run_max, jnp.max(scores, axis=-1))
        new_sum = run_sum * jnp.exp(run_max - new_max) + jnp.sum(
            jnp.exp(scores - new_max[..., None]), axis=-1
        )
        return ((new_max, new_sum), None)

    start_stats = (
        jnp.full((head_count, tok_rows), -1e30, jnp.float32),
        jnp.zeros((head_count, tok_rows), jnp.float32),
    )
    (row_max, row_sum), unused_a, unused_b = sweep(
        stats_step,
        start_stats,
        (blocks_of(far_keys), prompt_starts),
        (key_low[prompt_rows:], local_start),
    )

    def mix_step(state_in, block_item):
        scores = block_scores(block_item[0], block_item[2])
        weights = (jnp.exp(scores - row_max[..., None]) / row_sum[..., None]).astype(jnp.bfloat16)
        value_heads = block_item[1].reshape(-1, head_count, head_width)
        return (
            state_in
            + jnp.einsum("hqk,khd->qhd", weights, value_heads, preferred_element_type=jnp.float32),
            None,
        )

    mixed_exact, unused_c, unused_d = sweep(
        mix_step,
        jnp.zeros((tok_rows, head_count, head_width), jnp.float32),
        (blocks_of(far_keys), blocks_of(far_values), prompt_starts),
        (key_low[prompt_rows:], value_low[prompt_rows:], local_start),
    )
    mixed_low = mixed_exact.reshape(tok_rows, model_width).astype(jnp.bfloat16)
    hidden = source + jnp.dot(mixed_low, full_out, preferred_element_type=jnp.float32)
    normed_ffn_low = rms_norm(hidden, gain_ffn_f).astype(jnp.bfloat16)
    route_ids = expert_ids[0, 0]
    keep_mask, slot_ids, slot_hits, dispatch = routing(route_ids, priority[0, 0], CAP, EXPERTS)
    inputs = (
        jnp.dot(dispatch.astype(jnp.bfloat16), normed_ffn_low, preferred_element_type=jnp.float32)
        .astype(jnp.bfloat16)
        .reshape(EXPERTS, CAP, model_width)
    )
    gate_pre = jnp.einsum("ecd,edf->ecf", inputs, full_gate, preferred_element_type=jnp.float32)
    up_pre = jnp.einsum("ecd,edf->ecf", inputs, full_up, preferred_element_type=jnp.float32)
    inner_low = gelu_product(gate_pre, up_pre).astype(jnp.bfloat16)
    expert_out = jnp.einsum(
        "ecf,efd->ecd", inner_low, full_down, preferred_element_type=jnp.float32
    ).reshape(EXPERTS * CAP, model_width)
    logits = jnp.dot(normed_ffn_low, full_router, preferred_element_type=jnp.float32)
    weight_pair = gate_values(logits, route_ids, keep_mask)
    picked_rows = jnp.take(expert_out, slot_ids, axis=0)
    combined = jnp.sum(
        (picked_rows * weight_pair[:, None]).reshape(TOP, tok_rows, model_width), axis=0
    )
    output = (hidden + combined).astype(jnp.bfloat16).reshape(1, 1, tok_rows, model_width)
    back_keys, back_values = (far_keys, far_values)
    (
        back_query,
        back_key,
        back_value,
        back_out,
        back_gate,
        back_up,
        back_down,
        back_gain_attn,
        back_gain_ffn,
        back_router,
        back_bias,
    ) = gathered
    grad_final = cotangent[0, 0].astype(jnp.float32)
    grad_pair = jnp.where(
        keep_mask, jnp.sum(jnp.tile(grad_final, (TOP, 1)) * picked_rows, axis=-1), 0.0
    )
    slot_weight = jnp.dot(weight_pair, slot_hits, precision=precise)
    grad_expert_out = (
        (jnp.dot(dispatch, grad_final, precision=precise) * slot_weight[:, None])
        .astype(jnp.bfloat16)
        .reshape(EXPERTS, CAP, model_width)
    )
    grad_inner = jnp.einsum(
        "ecd,efd->ecf", grad_expert_out, back_down, preferred_element_type=jnp.float32
    )
    unused_e, inner_pull = jax.vjp(gelu_product, gate_pre, up_pre)
    grad_gate_pre, grad_up_pre = inner_pull(grad_inner)
    grad_gate_low = grad_gate_pre.astype(jnp.bfloat16)
    grad_up_low = grad_up_pre.astype(jnp.bfloat16)
    grad_gate_w = jnp.einsum(
        "ecd,ecf->edf", inputs, grad_gate_low, preferred_element_type=jnp.float32
    )
    grad_up_w = jnp.einsum("ecd,ecf->edf", inputs, grad_up_low, preferred_element_type=jnp.float32)
    grad_down_w = jnp.einsum(
        "ecf,ecd->efd", inner_low, grad_expert_out, preferred_element_type=jnp.float32
    )
    grad_inputs = jnp.einsum(
        "ecf,edf->ecd", grad_gate_low, back_gate, preferred_element_type=jnp.float32
    ) + jnp.einsum("ecf,edf->ecd", grad_up_low, back_up, preferred_element_type=jnp.float32)

    def gate_of_logits(logit_values):
        return gate_values(logit_values, route_ids, keep_mask)

    unused_f, gate_pull = jax.vjp(gate_of_logits, logits)
    (grad_logits,) = gate_pull(grad_pair)
    grad_router_w = jnp.dot(normed_ffn_low.astype(jnp.float32).T, grad_logits, precision=precise)
    grad_normed_ffn = jnp.dot(grad_logits, back_router.astype(jnp.float32).T, precision=precise)
    grad_normed_ffn = grad_normed_ffn + jnp.dot(
        dispatch.T, grad_inputs.reshape(EXPERTS * CAP, model_width), precision=precise
    )
    unused_g, ffn_norm_pull = jax.vjp(rms_norm, hidden, back_gain_ffn.astype(jnp.float32))
    grad_hidden_part, grad_gain_ffn_w = ffn_norm_pull(grad_normed_ffn)
    grad_hidden = grad_final + grad_hidden_part
    grad_hidden_low = grad_hidden.astype(jnp.bfloat16)
    grad_out_w = jnp.dot(mixed_low.T, grad_hidden_low, preferred_element_type=jnp.float32)
    grad_mixed = jnp.dot(grad_hidden_low, back_out.T, preferred_element_type=jnp.float32).astype(
        jnp.bfloat16
    )
    grad_mixed_heads = grad_mixed.reshape(tok_rows, head_count, head_width)
    row_delta = jnp.sum(grad_mixed_heads.astype(jnp.float32) * mixed_exact, axis=-1).T

    def grad_step(state_in, block_item):
        grad_query_acc, grad_reversed = state_in
        key_block, value_block, key_start = block_item
        key_total = key_block.shape[0]
        scores = block_scores(key_block, key_start)
        chances = jnp.exp(scores - row_max[..., None]) / row_sum[..., None]
        value_heads = value_block.reshape(-1, head_count, head_width)
        key_heads = key_block.reshape(-1, head_count, head_width)
        grad_chance = jnp.einsum(
            "qhd,khd->hqk", grad_mixed_heads, value_heads, preferred_element_type=jnp.float32
        )
        grad_value_block = jnp.einsum(
            "hqk,qhd->khd",
            chances.astype(jnp.bfloat16),
            grad_mixed_heads,
            preferred_element_type=jnp.float32,
        )
        grad_scores = chances * (grad_chance - row_delta[..., None])
        prompt_top, cont_top = window_starts(key_start)
        grad_reversed = add_window(
            grad_reversed,
            toeplitz_back(grad_scores[:, :prompt_rows], prompt_rows, key_total),
            prompt_top,
        )
        grad_reversed = add_window(
            grad_reversed,
            toeplitz_back(grad_scores[:, prompt_rows:], cont_rows, key_total),
            cont_top,
        )
        grad_scores_low = grad_scores.astype(jnp.bfloat16)
        grad_query_acc = grad_query_acc + score_scale * jnp.einsum(
            "hqk,khd->qhd", grad_scores_low, key_heads, preferred_element_type=jnp.float32
        )
        grad_key_block = score_scale * jnp.einsum(
            "hqk,qhd->khd", grad_scores_low, query_heads, preferred_element_type=jnp.float32
        )
        return (
            (grad_query_acc, grad_reversed),
            (grad_key_block.reshape(-1, model_width), grad_value_block.reshape(-1, model_width)),
        )

    start_grads = (
        jnp.zeros((tok_rows, head_count, head_width), jnp.float32),
        jnp.zeros((head_count, 2 * dist_count), jnp.float32),
    )
    (
        (grad_query_exact, grad_reversed),
        (far_grad_keys, far_grad_values),
        (near_grad_keys, near_grad_values),
    ) = sweep(
        grad_step,
        start_grads,
        (blocks_of(back_keys), blocks_of(back_values), prompt_starts),
        (key_low[prompt_rows:], value_low[prompt_rows:], local_start),
    )
    own_grad_keys, own_grad_values = (
        lax.psum_scatter(
            far_grad_keys.reshape(prompt_len, model_width), "ctx", scatter_dimension=0, tiled=True
        ),
        lax.psum_scatter(
            far_grad_values.reshape(prompt_len, model_width), "ctx", scatter_dimension=0, tiled=True
        ),
    )
    grad_key_low = jnp.concatenate([own_grad_keys, near_grad_keys], axis=0).astype(jnp.bfloat16)
    grad_value_low = jnp.concatenate([own_grad_values, near_grad_values], axis=0).astype(
        jnp.bfloat16
    )
    grad_query_low = grad_query_exact.reshape(tok_rows, model_width).astype(jnp.bfloat16)
    grad_query_w = jnp.dot(normed_attn_low.T, grad_query_low, preferred_element_type=jnp.float32)
    grad_key_w = jnp.dot(normed_attn_low.T, grad_key_low, preferred_element_type=jnp.float32)
    grad_value_w = jnp.dot(normed_attn_low.T, grad_value_low, preferred_element_type=jnp.float32)
    grad_normed_attn = jnp.dot(grad_query_low, back_query.T, preferred_element_type=jnp.float32)
    grad_normed_attn = grad_normed_attn + jnp.dot(
        grad_key_low, back_key.T, preferred_element_type=jnp.float32
    )
    grad_normed_attn = grad_normed_attn + jnp.dot(
        grad_value_low, back_value.T, preferred_element_type=jnp.float32
    )
    unused_h, attn_norm_pull = jax.vjp(rms_norm, source, back_gain_attn.astype(jnp.float32))
    grad_source_part, grad_gain_attn_w = attn_norm_pull(grad_normed_attn)
    grad_tokens = (
        (grad_hidden + grad_source_part).astype(jnp.bfloat16).reshape(1, 1, tok_rows, model_width)
    )
    grad_bias_rows = grad_reversed[:, :dist_count][:, ::-1]
    grad_bias_w = jnp.dot(bucket_onehot.T, grad_bias_rows.T, precision=precise)
    small_gain_attn, small_gain_ffn, small_router, small_bias = lax.psum(
        (grad_gain_attn_w, grad_gain_ffn_w, grad_router_w, grad_bias_w), "ctx"
    )
    row_parts = (
        lax.psum_scatter(
            grad_query_w.astype(jnp.bfloat16), "wt", scatter_dimension=0, tiled=True
        ).astype(jnp.float32),
        lax.psum_scatter(
            grad_key_w.astype(jnp.bfloat16), "wt", scatter_dimension=0, tiled=True
        ).astype(jnp.float32),
        lax.psum_scatter(
            grad_value_w.astype(jnp.bfloat16), "wt", scatter_dimension=0, tiled=True
        ).astype(jnp.float32),
        lax.psum_scatter(
            grad_out_w.astype(jnp.bfloat16), "wt", scatter_dimension=0, tiled=True
        ).astype(jnp.float32),
        lax.psum_scatter(
            grad_gate_w.astype(jnp.bfloat16), "wt", scatter_dimension=1, tiled=True
        ).astype(jnp.float32),
        lax.psum_scatter(
            grad_up_w.astype(jnp.bfloat16), "wt", scatter_dimension=1, tiled=True
        ).astype(jnp.float32),
        lax.psum_scatter(
            grad_down_w.astype(jnp.bfloat16), "wt", scatter_dimension=2, tiled=True
        ).astype(jnp.float32),
        lax.psum_scatter(
            small_gain_attn.astype(jnp.bfloat16), "wt", scatter_dimension=0, tiled=True
        ).astype(jnp.float32),
        lax.psum_scatter(
            small_gain_ffn.astype(jnp.bfloat16), "wt", scatter_dimension=0, tiled=True
        ).astype(jnp.float32),
        lax.psum_scatter(
            small_router.astype(jnp.bfloat16), "wt", scatter_dimension=0, tiled=True
        ).astype(jnp.float32),
        lax.psum_scatter(
            small_bias.astype(jnp.bfloat16), "wt", scatter_dimension=1, tiled=True
        ).astype(jnp.float32),
    )
    res_query, res_key, res_value, res_out, res_gate, res_up, res_down = (
        lax.psum_scatter(row_parts[0], "ctx", scatter_dimension=1, tiled=True),
        lax.psum_scatter(row_parts[1], "ctx", scatter_dimension=1, tiled=True),
        lax.psum_scatter(row_parts[2], "ctx", scatter_dimension=1, tiled=True),
        lax.psum_scatter(row_parts[3], "ctx", scatter_dimension=1, tiled=True),
        lax.psum_scatter(row_parts[4], "ctx", scatter_dimension=2, tiled=True),
        lax.psum_scatter(row_parts[5], "ctx", scatter_dimension=2, tiled=True),
        lax.psum_scatter(row_parts[6], "ctx", scatter_dimension=1, tiled=True),
    )
    res_gain_attn, res_gain_ffn, res_router, res_bias = (
        row_parts[7],
        row_parts[8],
        row_parts[9],
        row_parts[10],
    )
    return (
        output,
        grad_tokens,
        res_query,
        res_key,
        res_value,
        res_out,
        res_gain_attn,
        res_gain_ffn,
        res_router,
        res_bias,
        res_gate,
        res_up,
        res_down,
    )


BF = jnp.bfloat16
F32 = jnp.float32
FAST_CTX = 8
FAST_WT = 4
NEG = -1e30

SWAP_Y = [(i, i ^ 1) for i in range(8)]
LINES_Z = [[0, 2, 4, 6], [1, 3, 5, 7]]
PAIR_Z = [(i, i ^ 2) for i in range(8)]
FLIP_Z = [(i, i ^ 6) for i in range(8)]
SWAP_C = [(i, i ^ 1) for i in range(4)]
SWAP_X = [(i, i ^ 2) for i in range(4)]


def move_y(v):
    return lax.ppermute(v, "ctx", SWAP_Y)


def move_x(v):
    return lax.ppermute(v, "wt", SWAP_X)


def move_c(v):
    return lax.ppermute(v, "wt", SWAP_C)


def pair_z(v):
    return lax.ppermute(v, "ctx", PAIR_Z)


def flip_z(v):
    return lax.ppermute(v, "ctx", FLIP_Z)


def phase(*vals):
    return lax.optimization_barrier(vals)


def dot_nt(a, b):
    return lax.dot_general(a, b, (((1,), (1,)), ((), ())), preferred_element_type=F32)


def dot_tn(a, b):
    return lax.dot_general(a, b, (((0,), (0,)), ((), ())), preferred_element_type=F32)


def dot_nn(a, b):
    return jnp.dot(a, b, preferred_element_type=F32)


def params(limit=56 * 2**20):
    return pltpu.CompilerParams(vmem_limit_bytes=limit)


COST_S = pl.CostEstimate(flops=10**10, bytes_accessed=10**6, transcendentals=0)
COST_E = pl.CostEstimate(flops=25 * 10**9, bytes_accessed=10**6, transcendentals=0)
ANY = pl.BlockSpec(memory_space=pl.ANY)
SMEM = pl.BlockSpec(memory_space=pltpu.SMEM)


def spread_z(v):
    near, opp = pair_z(v), flip_z(v)
    return {0: v, 1: near, 3: opp, 2: pair_z(opp)}


def attend_kernel(groups, first, idx, n_ref, w_ref, *refs):
    pieces, refs = refs[: 2 * len(groups)], refs[2 * len(groups) :]
    if not first:
        refs = refs[4:]
    p_ref, o_ref, qkv_ref, wt_ref, bc_ref, bp_ref, qs_ref = refs
    z, y, x, c = idx[0], idx[1], idx[2], idx[3]
    step = pl.program_id(0)
    for n, (sz, x_first) in enumerate(groups):
        for ry in range(2):

            @pl.when(step == 2 * n + ry)
            def _(n=n, ry=ry, x_first=x_first):
                for rx in range(2):
                    for rc in range(2):
                        row = pl.multiple_of(((x ^ rx) * 2 + (c ^ rc)) * 256, 256)
                        src = pieces[2 * n + rc]
                        for t in range(4):
                            rows = slice(256 * t, 256 * t + 256)
                            block = src[ry, rx, rows] if x_first else src[rx, ry, rows]
                            wt_ref[0, pl.ds(row, 256), 128 * t : 128 * t + 128] = block

    qkv = dot_nn(n_ref[...], wt_ref[0, :, :384]).astype(BF)
    qkv_ref[0] = qkv
    k, v = qkv[:, 128:256], qkv[:, 256:]
    qs_ref[...] = qkv[:, :128]
    q_c = qs_ref[512:, :]
    q_p = qs_ref[pl.ds(pl.multiple_of((z * 2 + y) * 64, 64), 64), :]
    lane = lax.broadcasted_iota(jnp.int32, (1, 128), 1)
    outs = []
    for h in range(2):
        base_c, base_p = w_ref[h, 0], w_ref[h, 1]
        for a in range(32):
            bc_ref[8 * a : 8 * a + 8, :] = pltpu.roll(base_c, 1024 - (248 - 8 * a), 1)[:, :768]
        for a in range(8):
            shift = 56 - 8 * a
            bp_ref[8 * a : 8 * a + 8, :] = (pltpu.roll(base_p, 1024 - shift, 1) if shift else base_p)[:, :512]
        mine = (lane < 64) if h == 0 else (lane >= 64)
        head = lambda t: jnp.where(mine, t, jnp.zeros_like(t))
        sc = dot_nt(head(q_c), k) * 0.125 + bc_ref[...]
        sp = dot_nt(head(q_p), k[:512]) * 0.125 + bp_ref[...]

        def soft(t):
            e = jnp.exp(t - jnp.max(t, axis=-1, keepdims=True))
            return (e * (1.0 / jnp.sum(e, axis=-1, keepdims=True))).astype(BF)

        pc, pp = soft(sc), soft(sp)
        p_ref[h, 64:, :] = pc
        p_ref[h, :64, :512] = pp
        p_ref[h, :64, 512:] = jnp.zeros((64, 256), BF)
        outs.append(jnp.concatenate([dot_nn(pp, v[:512]), dot_nn(pc, v)], axis=0))
    o_ref[...] = jnp.where(lane < 64, outs[0], outs[1]).astype(BF)


def norm_kernel(idx, a_ref, b_ref, own_ref, gain_ref, src_ref, low_ref):
    z, y = idx[0], idx[1]
    for sz in range(4):
        at = lambda yy: pl.ds(pl.multiple_of(((z ^ sz) * 2 + yy) * 64, 64), 64)
        src_ref[at(y), :] = a_ref[sz]
        src_ref[at(y ^ 1), :] = b_ref[sz]
    src_ref[512:, :] = own_ref[64:, :]
    values = src_ref[...].astype(F32)
    low_ref[...] = (norm_parts(values) * gain_ref[...]).astype(BF)


def norm_rows(idx, prompt_z, prompt_y, rows_own, gain):
    whole = pl.BlockSpec(memory_space=pltpu.VMEM)
    out = jax.ShapeDtypeStruct((768, 1024), BF)
    return pl.pallas_call(
        norm_kernel,
        in_specs=[SMEM] + [whole] * 4,
        out_specs=(whole, whole),
        out_shape=(out, out),
        compiler_params=params(),
    )(idx, prompt_z, prompt_y, rows_own, gain[None])


def attend(groups, idx, normed, windows, pieces, prev):
    keys, rows = normed.shape[0], 320

    def at(i, d):
        sz = groups[0][0]
        for n, (other, unused) in enumerate(groups):
            sz = jnp.where(i // 2 == n, other, sz)
        return (d[0] ^ sz) * 2 + (d[1] ^ (i % 2))

    whole = pl.BlockSpec(memory_space=pltpu.VMEM)
    return pl.pallas_call(
        functools.partial(attend_kernel, groups, prev is None),
        grid_spec=pltpu.PrefetchScalarGridSpec(
            num_scalar_prefetch=1,
            grid=(2 * len(groups),),
            in_specs=[whole, pl.BlockSpec((2, 2, 8, 1024), lambda i, d: (at(i, d), 0, 0, 0))]
            + [whole] * len(pieces)
            + ([] if prev is None else [ANY] * 4),
            out_specs=(
                pl.BlockSpec((2, rows, keys), lambda i, d: (at(i, d), 0, 0)),
                pl.BlockSpec((rows, 128), lambda i, d: (0, at(i, d))),
                pl.BlockSpec((1, keys, 384), lambda i, d: (at(i, d), 0, 0)),
                pl.BlockSpec((1, 1024, 512), lambda i, d: (at(i, d), 0, 0)),
            ),
            scratch_shapes=[pltpu.VMEM((256, 768), F32), pltpu.VMEM((64, 512), F32), pltpu.VMEM((keys, 128), BF)],
        ),
        out_shape=(
            jax.ShapeDtypeStruct((16, rows, keys), BF),
            jax.ShapeDtypeStruct((rows, 1024), BF),
            jax.ShapeDtypeStruct((8, keys, 384), BF),
            jax.ShapeDtypeStruct((8, 1024, 512), BF),
        ),
        input_output_aliases={} if prev is None else {3 + len(pieces) + n: n for n in range(4)},
        compiler_params=params(),
        cost_estimate=COST_S,
    )(idx, normed, windows, *pieces, *([] if prev is None else prev))


def attend_back_kernel(first, final, idx, n_ref, p_ref, qkv_ref, wt_ref, g_ref, m_ref, gl_ref, *refs):
    if not first:
        gn_prev, refs = refs[0], refs[2:]
    if final:
        gp_ref, refs = refs[4], refs[:4] + refs[5:]
    keep_ref, send_ref, gn_ref, db_ref, dt_ref, qs_ref = refs
    z, y, x, c = idx[0], idx[1], idx[2], idx[3]
    own = pl.ds(pl.multiple_of((z * 2 + y) * 64, 64), 64)
    qkv = qkv_ref[0]
    k, v = qkv[:, 128:256], qkv[:, 256:]
    qs_ref[...] = qkv[:, :128]
    q = jnp.concatenate([qs_ref[own, :], qs_ref[512:, :]], axis=0)
    g = g_ref[...]
    lane = lax.broadcasted_iota(jnp.int32, (1, 128), 1)
    parts = []
    for h in range(2):
        mine = (lane < 64) if h == 0 else (lane >= 64)
        gh = jnp.where(mine, g, jnp.zeros_like(g))
        p = p_ref[h]
        pf = p.astype(F32)
        dp = dot_nt(gh, v)
        delta = jnp.sum(pf * dp, axis=-1, keepdims=True)
        ds = pf * (dp - delta)
        low = ds.astype(BF)
        acc_c = jnp.zeros((8, 1024), F32)
        for a in range(32):
            part = jnp.concatenate([ds[64 + 8 * a : 72 + 8 * a], jnp.zeros((8, 256), F32)], axis=1)
            acc_c = acc_c + pltpu.roll(part, 248 - 8 * a, 1) if a < 31 else acc_c + part
        acc_p = jnp.zeros((8, 1024), F32)
        for a in range(8):
            part = jnp.concatenate([ds[8 * a : 8 * a + 8, :512], jnp.zeros((8, 512), F32)], axis=1)
            acc_p = acc_p + (pltpu.roll(part, 56 - 8 * a, 1) if a < 7 else part)
        db_ref[h, 0] = acc_c
        db_ref[h, 1] = acc_p
        parts.append((dot_nn(low, k) * 0.125, dot_tn(low, q) * 0.125, dot_tn(p, g)))
    dq, dk, dv = [jnp.where(lane < 64, parts[0][n], parts[1][n]).astype(BF) for n in range(3)]
    dt_ref[:512, :128] = jnp.zeros((512, 128), BF)
    dt_ref[own, :128] = dq[:64]
    dt_ref[512:, :128] = dq[64:]
    dt_ref[:, 128:256] = dk
    dt_ref[:, 256:] = dv
    dt = dt_ref[...]
    dw = jnp.concatenate([dot_tn(n_ref[...], dt).astype(BF), dot_tn(m_ref[...], gl_ref[...]).astype(BF)], axis=1)
    for xx in range(2):
        for cc in range(2):
            block = dw[(xx * 2 + cc) * 256 : (xx * 2 + cc) * 256 + 256]

            @pl.when(c == cc)
            def _():
                keep_ref[x ^ xx, 0] = block

            @pl.when(c != cc)
            def _():
                send_ref[x ^ xx, 0] = block

    gn = dot_nt(dt, wt_ref[0, :, :384])

    @pl.when(pl.program_id(0) == 0)
    def _():
        gn_ref[...] = gn if first else gn_prev[...] + gn

    @pl.when(pl.program_id(0) != 0)
    def _():
        gn_ref[...] += gn

    if final:

        @pl.when(pl.program_id(0) == pl.num_programs(0) - 1)
        def _():
            for sz in range(4):
                for ry in range(2):
                    rows = pl.ds(pl.multiple_of(((z ^ sz) * 2 + (y ^ ry)) * 64, 64), 64)
                    gp_ref[sz, ry] = gn_ref[rows, :].astype(BF)


def attend_back(base, count, idx, normed, p, qkv, wt, g, mixed, g_low, gn_prev, db_prev):
    rows, keys = p.shape[1], p.shape[2]
    final = base == 0
    at = lambda i, d: (i + base) ^ (d[0] * 2 + d[1])
    whole = pl.BlockSpec((keys, 1024), lambda i, d: (0, 0))
    return pl.pallas_call(
        functools.partial(attend_back_kernel, gn_prev is None, final),
        grid_spec=pltpu.PrefetchScalarGridSpec(
            num_scalar_prefetch=1,
            grid=(count,),
            in_specs=[
                whole,
                pl.BlockSpec((2, rows, keys), lambda i, d: (at(i, d), 0, 0)),
                pl.BlockSpec((1, keys, 384), lambda i, d: (at(i, d), 0, 0)),
                pl.BlockSpec((1, 1024, 512), lambda i, d: (at(i, d), 0, 0)),
                pl.BlockSpec((rows, 128), lambda i, d: (0, at(i, d))),
                pl.BlockSpec((rows, 1024), lambda i, d: (0, 0)),
                pl.BlockSpec((rows, 128), lambda i, d: (0, at(i, d))),
            ]
            + ([] if gn_prev is None else [whole, ANY]),
            out_specs=(
                pl.BlockSpec((2, 1, 256, 512), lambda i, d: (0, i, 0, 0)),
                pl.BlockSpec((2, 1, 256, 512), lambda i, d: (0, i, 0, 0)),
                whole,
                pl.BlockSpec((2, 2, 8, 1024), lambda i, d: (at(i, d), 0, 0, 0)),
            )
            + ((pl.BlockSpec((4, 2, 64, 1024), lambda i, d: (0, 0, 0, 0)),) if final else ()),
            scratch_shapes=[pltpu.VMEM((keys, 384), BF), pltpu.VMEM((keys, 128), BF)],
        ),
        out_shape=(
            jax.ShapeDtypeStruct((2, count, 256, 512), BF),
            jax.ShapeDtypeStruct((2, count, 256, 512), BF),
            jax.ShapeDtypeStruct((keys, 1024), F32),
            jax.ShapeDtypeStruct((16, 2, 8, 1024), F32),
        )
        + ((jax.ShapeDtypeStruct((4, 2, 64, 1024), BF),) if final else ()),
        input_output_aliases={} if gn_prev is None else {9: 3},
        compiler_params=params(),
        cost_estimate=COST_E,
    )(idx, normed, p, qkv, wt, g, mixed, g_low, *([] if gn_prev is None else [gn_prev, db_prev]))


def cut_rows(t):
    return t[:, :, :, :128], t[:, :, :, 128:]


def out_back_kernel(a_ref, b_ref, c_ref, h_ref, gain_ref, cot_ref, w_ref, gh_ref, gl_ref, gm_ref, gg_ref):
    f = lambda t: t.astype(F32)
    dn = f(a_ref[...]) + f(b_ref[...]) + f(c_ref[...])
    hidden, gain = h_ref[...], gain_ref[...]
    scale = lax.rsqrt(jnp.mean(hidden * hidden, axis=-1, keepdims=True) + epsilon)
    unit = hidden * scale
    gg_ref[...] = jnp.broadcast_to(jnp.sum(dn * unit, axis=0, keepdims=True), gg_ref.shape)
    du = dn * gain
    grad = f(cot_ref[...]) + scale * (du - unit * jnp.mean(du * unit, axis=-1, keepdims=True))
    gh_ref[...] = grad
    low = grad.astype(BF)
    gl_ref[...] = low
    total = dot_nt(low[:, :128], w_ref[0, :, 384:])
    for n in range(1, 8):
        total = total + dot_nt(low[:, 128 * n : 128 * n + 128], w_ref[n, :, 384:])
    gm_ref[...] = total.astype(BF)


def out_back(parts, hidden, gain, cot, w_o):
    whole = pl.BlockSpec(memory_space=pltpu.VMEM)
    return pl.pallas_call(
        out_back_kernel,
        in_specs=[whole] * 7,
        out_specs=(whole,) * 4,
        out_shape=(
            jax.ShapeDtypeStruct((320, 1024), F32),
            jax.ShapeDtypeStruct((320, 1024), BF),
            jax.ShapeDtypeStruct((320, 1024), BF),
            jax.ShapeDtypeStruct((8, 1024), F32),
        ),
        compiler_params=params(),
        cost_estimate=COST_S,
    )(*parts, hidden, gain[None], cot, w_o)


def out_kernel(m_ref, s_ref, g_ref, w_ref, h_ref, l_ref):
    m = m_ref[...]
    for n in range(8):
        cols = slice(128 * n, 128 * n + 128)
        h_ref[:, cols] = s_ref[:, cols].astype(F32) + dot_nn(m, w_ref[n, :, 384:])
    hidden = h_ref[...]
    scale = lax.rsqrt(jnp.mean(hidden * hidden, axis=-1, keepdims=True) + epsilon)
    l_ref[...] = (hidden * scale * g_ref[...]).astype(BF)


def project_out(mixed, rows_own, gain, wt):
    whole = pl.BlockSpec(memory_space=pltpu.VMEM)
    return pl.pallas_call(
        out_kernel,
        in_specs=[whole] * 4,
        out_specs=(whole,) * 2,
        out_shape=(jax.ShapeDtypeStruct((320, 1024), F32), jax.ShapeDtypeStruct((320, 1024), BF)),
        compiler_params=params(),
        cost_estimate=COST_S,
    )(mixed, rows_own, gain[None], wt)


WIDE = 1920


def window_kernel(idx, t_ref, b_ref, o_ref):
    onehot = jnp.where(lax.broadcasted_iota(jnp.int32, (BUCKETS, WIDE), 0) == t_ref[...], 1.0, 0.0)
    rev = lax.dot_general(b_ref[...], onehot, (((0,), (0,)), ((), ())), precision=precise, preferred_element_type=F32)
    rev = jnp.where(lax.broadcasted_iota(jnp.int32, (16, WIDE), 1) < 768, rev, NEG)
    tail = pltpu.roll(rev, WIDE - 704 + 64 * (idx[0] * 2 + idx[1]), 1)
    for s in range(8):
        o_ref[:, 0, s, :] = (pltpu.roll(rev, WIDE - 7 + s, 1) if s < 7 else rev)[:, :1024]
        o_ref[:, 1, s, :] = (pltpu.roll(tail, WIDE - 7 + s, 1) if s < 7 else tail)[:, :1024]


def bias_windows(idx, table_rev, bias_f):
    whole = pl.BlockSpec(memory_space=pltpu.VMEM)
    return pl.pallas_call(
        window_kernel,
        in_specs=[SMEM, whole, whole],
        out_specs=whole,
        out_shape=jax.ShapeDtypeStruct((16, 2, 8, 1024), F32),
        compiler_params=params(),
    )(idx, table_rev, bias_f)


def pack_kernel(idx, t_ref, db_ref, gn_ref, src_ref, gf_ref, r_ref, small_ref):
    z, y = idx[0], idx[1]

    def gather(n):
        total = jnp.zeros((16, WIDE), F32)
        for s in range(8):
            part = jnp.concatenate([db_ref[:, n, s, :], jnp.zeros((16, WIDE - 1024), F32)], axis=1)
            total = total + (pltpu.roll(part, 7 - s, 1) if s < 7 else part)
        return total

    rev = gather(0) + pltpu.roll(gather(1), 704 - 64 * (z * 2 + y), 1)
    onehot = jnp.where(lax.broadcasted_iota(jnp.int32, (BUCKETS, 768), 0) == t_ref[:, :768], 1.0, 0.0)
    bias = lax.dot_general(
        rev[:, :768], onehot, (((1,), (1,)), ((), ())), precision=precise, preferred_element_type=F32
    )
    src = src_ref[...].astype(F32)
    unit = src * lax.rsqrt(jnp.mean(src * src, axis=-1, keepdims=True) + epsilon)
    small_ref[...] = jnp.zeros_like(small_ref)
    small_ref[0:1, :] = jnp.sum(gn_ref[...] * unit, axis=0, keepdims=True)
    small_ref[1:2, :] = gf_ref[0:1, :]
    small_ref[2:5, :] = r_ref[0:3, :]
    small_ref[8:24, 0:BUCKETS] = bias


def pack(idx, table_rev, dbias, gn, src, gain_ffn_part, router_part):
    whole = pl.BlockSpec(memory_space=pltpu.VMEM)
    return pl.pallas_call(
        pack_kernel,
        in_specs=[SMEM] + [whole] * 6,
        out_specs=whole,
        out_shape=jax.ShapeDtypeStruct((24, 1024), F32),
        compiler_params=params(),
        cost_estimate=COST_S,
    )(idx, table_rev, dbias, gn, src, gain_ffn_part, router_part)


def final_kernel(p_ref, q_ref, gn_ref, src_ref, gain_ref, gh_ref, o_ref):
    f = lambda t: t.astype(F32)
    own = f(p_ref[...]) + f(q_ref[...])
    grad = jnp.concatenate([own, gn_ref[512:, :]], axis=0) * gain_ref[...]
    src = f(src_ref[...])
    scale = lax.rsqrt(jnp.mean(src * src, axis=-1, keepdims=True) + epsilon)
    unit = src * scale
    back = scale * (grad - unit * jnp.mean(grad * unit, axis=-1, keepdims=True))
    o_ref[...] = (gh_ref[...] + back).astype(BF)


def finish(own, other, gn, src, gain, grad_hidden):
    whole = pl.BlockSpec(memory_space=pltpu.VMEM)
    return pl.pallas_call(
        final_kernel,
        in_specs=[whole] * 6,
        out_specs=whole,
        out_shape=jax.ShapeDtypeStruct((320, 1024), BF),
        compiler_params=params(),
        cost_estimate=COST_S,
    )(own, other, gn, src, gain[None], grad_hidden)


def add_low(a, b):
    return (a.astype(F32) + b.astype(F32)).astype(BF)


PIECES = [(0, 320), (320, 320), (640, 320), (960, 160), (1120, 160)]


def fetch_pieces(want, x_parts, g_parts, x_scr, g_scr, sem):
    copies = []
    for rc in range(2):
        for n, (row, size) in enumerate(PIECES):
            at = rc * 1280 + row
            tile = at // 640
            if want not in (None, tile):
                continue
            k = rc * 5 + n
            copies.append(pltpu.make_async_copy(x_parts[k], x_scr.at[pl.ds(at, size)], sem.at[k, 0]))
            src = g_parts[k].at[pl.ds(160 if n == 4 else 0, size)]
            copies.append(pltpu.make_async_copy(src, g_scr.at[pl.ds(at, size)], sem.at[k, 1]))
    return copies


def expert_kernel(group, last, *refs):
    refs = list(refs)
    step = pl.program_id(0)
    count = len(group)
    idx, refs = refs[0], refs[1:]
    w_at = idx[2] * 2 + idx[3]
    src, m_ref = refs[:2]
    if not last:
        x_parts, g_parts = refs[2:12], refs[12:22]
        out_ref, dx_ref, dh_ref, win_ref, s_ref, xo_ref, go_ref, w_scr, sem, x_scr, g_scr, psem = refs[22:]
    else:
        x_ref, g_ref, out_prev, dx_prev, s_prev = refs[2:7]
        out_ref, out_c_ref, dx_ref, dx_c_ref, dh_ref, win_ref, w_scr, sem = refs[7:]

    @pl.when(step == 0)
    def _():
        copies = [
            pltpu.make_async_copy(
                src.at[n, r, e],
                w_scr.at[e, :, pl.ds(96 * n, 96), pl.ds(pl.multiple_of((w_at ^ r) * 256, 256), 256)],
                sem.at[n, 4 * e + r],
            )
            for e in range(count)
            for n in range(4)
            for r in range(4)
        ]
        for copy in copies:
            copy.start()
        if not last:
            for copy in fetch_pieces(None, x_parts, g_parts, x_scr, g_scr, psem):
                copy.start()
        for copy in copies:
            copy.wait()

    if not last:
        for t in range(4):

            @pl.when(step == t)
            def _(t=t):
                for copy in fetch_pieces(t, x_parts, g_parts, x_scr, g_scr, psem):
                    copy.wait()

        rows = pl.ds(pl.multiple_of(step * 640, 640), 640)
        x, g = x_scr[rows, :], g_scr[rows, :]
        xo_ref[...] = x
        go_ref[...] = g
    else:
        x, g = x_ref[...], g_ref[...]
    m = m_ref[...]
    lane = lax.broadcasted_iota(jnp.int32, (1, 384), 1)
    scores = []
    for k, expert in enumerate(group):
        w_gu = w_scr[k, 0:2].reshape(768, 1024)
        w_d = w_scr[k, 2]
        gu = dot_nt(x, w_gu)
        gi = dot_nt(g, w_d)
        gate, up = gu[:, :384], gu[:, 384:]
        if k == 0:
            l = [gate[:, 88 + n : 89 + n] for n in range(3)]
            top = jnp.maximum(jnp.maximum(l[0], l[1]), l[2])
            ex = [jnp.exp(v - top) for v in l]
            inv = 1.0 / (ex[0] + ex[1] + ex[2])
            p = [v * inv for v in ex]
        keep = m[:, expert : expert + 1]
        w = p[expert] * keep
        sq = gate * gate
        th = jnp.tanh(0.7978845608028654 * gate * (1.0 + 0.044715 * sq))
        half1 = 0.5 + 0.5 * th
        act = gate * half1
        dact = half1 + (0.5 * gate) * (1.0 - th * th) * (0.7978845608028654 + 0.10703222440890037 * sq)
        inner = (act * up).astype(BF).astype(F32)
        s = jnp.sum(inner * gi, axis=-1, keepdims=True) * keep
        scores.append(s)
        gin = gi * w
        dg = gin * up * dact
        du = gin * act
        if last:
            ss = [s_prev[...][:, 0:1], s_prev[...][:, 1:2], s]
            dot = p[0] * ss[0] + p[1] * ss[1] + p[2] * ss[2]
            for n in range(3):
                dg = jnp.where(lane == 88 + n, p[n] * (ss[n] - dot), dg)
        win = (inner * w).astype(BF)
        dh = jnp.concatenate([dg.astype(BF), du.astype(BF)], axis=1)
        dh_ref[:, 768 * k : 768 * k + 768] = dh
        win_ref[:, 384 * k : 384 * k + 384] = win
        o_k, dx_k = dot_nn(win, w_d), dot_nn(dh, w_gu)
        out, dx = (o_k, dx_k) if k == 0 else (out + o_k, dx + dx_k)
    if last:
        out = (out + out_prev[...].astype(F32)).astype(BF)
        dx = (dx + dx_prev[...].astype(F32)).astype(BF)

        @pl.when(step < 2)
        def _():
            out_c_ref[...] = out
            dx_c_ref[...] = dx

        @pl.when(step >= 2)
        def _():
            out_ref[...] = out
            dx_ref[...] = dx
    else:
        out_ref[...] = out.astype(BF)
        dx_ref[...] = dx.astype(BF)
        s_ref[...] = jnp.where(lane[:, :128] == 0, scores[0], scores[1])


def expert_call(group, idx, x, g, m, src, prev, tile=640):
    total, count = 2560, len(group)
    last = prev is not None
    at = (lambda i: i ^ 2) if last else (lambda i: i)
    row = lambda n: pl.BlockSpec((tile, n), lambda i: (at(i), 0))
    shape = lambda n, t: jax.ShapeDtypeStruct((total, n), t)
    scratch = [pltpu.VMEM((count, 3, 384, 1024), BF), pltpu.SemaphoreType.DMA((4, 4 * count))]
    if not last:
        ins = [idx, src, m, *x, *g]
        specs = [SMEM, ANY, row(128)] + [ANY] * 20
        outs = [(1024, BF), (1024, BF), (768 * count, BF), (384 * count, BF), (128, F32), (1024, BF), (1024, BF)]
        out_shape = tuple(shape(n, t) for n, t in outs)
        out_specs = tuple(row(n) for n, t in outs)
        scratch += [pltpu.VMEM((total, 1024), BF), pltpu.VMEM((total, 1024), BF), pltpu.SemaphoreType.DMA((10, 2))]
    else:
        ins = [idx, src, m, x, g, *prev]
        specs = [SMEM, ANY, row(128)] + [row(1024)] * 4 + [row(128)]
        half = jax.ShapeDtypeStruct((total // 2, 1024), BF)
        mine = pl.BlockSpec((tile, 1024), lambda i: (jnp.maximum(i - 2, 0), 0))
        other = pl.BlockSpec((tile, 1024), lambda i: (jnp.minimum(i, 1), 0))
        out_shape = (half, half, half, half, shape(768 * count, BF), shape(384 * count, BF))
        out_specs = (mine, other, mine, other, row(768 * count), row(384 * count))
    return pl.pallas_call(
        functools.partial(expert_kernel, group, last),
        grid=(total // tile,),
        out_shape=out_shape,
        in_specs=specs,
        out_specs=out_specs,
        scratch_shapes=scratch,
        compiler_params=params(),
        cost_estimate=COST_E,
    )(*ins)


def line_collect(part_of, z):
    at = lambda n: part_of(z ^ n)
    near = pair_z(at(1))
    opp = flip_z(add_low(at(3), pair_z(at(2))))
    return (at(0).astype(F32) + near.astype(F32) + opp.astype(F32)).astype(BF)


def trade_wt(v):
    return lax.all_to_all(v, "wt", 0, 0, tiled=True)


def sum_all(v):
    v = v + move_c(v)
    v = v + move_x(v)
    v = v + move_y(v)
    v = v + lax.ppermute(v, "ctx", [(i, i ^ 2) for i in range(8)])
    return v + lax.ppermute(v, "ctx", [(i, i ^ 4) for i in range(8)])


def norm_parts(values):
    return values * lax.rsqrt(jnp.mean(values * values, axis=-1, keepdims=True) + epsilon)


def local_fast(
    tokens, cotangent, w_query, w_key, w_value, w_out, gain_attn, gain_ffn, w_router, rel_bias,
    exp_gate, exp_up, exp_down, bucket_table, expert_ids, priority,
):
    ctx_index = lax.axis_index("ctx").astype(jnp.int32)
    wt_index = lax.axis_index("wt").astype(jnp.int32)
    z, y, x, c = ctx_index // 2, ctx_index % 2, wt_index // 2, wt_index % 2
    idx = jnp.stack([z, y, x, c])
    rows_own = tokens[0, 0]

    packed = jnp.concatenate(
        [gain_attn[None], gain_ffn[None], w_router.T, jnp.pad(rel_bias.reshape(1, 128), ((0, 0), (0, 128))),
         jnp.zeros((2, 256), BF)], axis=0
    )
    ids, rank = expert_ids[0, 0], priority[0, 0]
    expert = ids.T.reshape(-1)
    rank_key = (jnp.arange(TOP, dtype=jnp.int32)[:, None] * 320 + rank[None, :]).reshape(-1)
    earlier = (expert[:, None] == expert[None, :]) & (rank_key[None, :] < rank_key[:, None])
    keep = (jnp.sum(earlier.astype(jnp.int32), axis=1) < CAP).reshape(TOP, 320)
    hold = jnp.sum(
        jnp.where((ids.T[:, :, None] == jnp.arange(EXPERTS, dtype=jnp.int32)) & keep[:, :, None], 1.0, 0.0), axis=0
    )
    marks = jnp.pad(hold.reshape(960), (0, 1088)).astype(BF).reshape(16, 128)
    cot = cotangent[0, 0]

    def pieces(v):
        return jnp.pad(v.reshape(3, 4, 88, 256), ((0, 0), (0, 0), (0, 8), (0, 0)))

    gate_t, up_t = exp_gate.transpose(0, 2, 1), exp_up.transpose(0, 2, 1)
    gate_p = pieces(gate_t)
    router_rows = jnp.broadcast_to(
        jnp.pad(w_router.T, ((0, 5), (0, 0)))[None, None], (3, 4, 8, 256)
    )
    gate_p = jnp.concatenate([gate_p[:, :, :88], router_rows], axis=2)
    share = jnp.stack([gate_p, pieces(up_t), pieces(exp_down)], axis=1).transpose(2, 0, 1, 3, 4)
    pick = lambda v, n, d: lax.dynamic_index_in_dim(v, n, d, keepdims=False)
    unit = jnp.stack([w_query, w_key, w_value, w_out]).reshape(1024, 128)
    prompt_own = rows_own[:64]
    along = jnp.concatenate([unit, prompt_own.reshape(512, 128)], axis=0)
    weights_in = lambda v: v[:1024]
    rows_in = lambda v: v[1024:].reshape(64, 1024)
    share = share.reshape(2, 2, 3, 3, 96, 256)
    share_x, share_own = pick(share, 1 - x, 0), pick(share, x, 0)
    packed_c, packed_x, packed_xc, along, share_x = phase(
        move_c(packed), move_x(packed), lax.ppermute(packed, "wt", [(i, i ^ 3) for i in range(4)]), along, share_x
    )
    unit_0 = jnp.concatenate([unit, marks], axis=0)
    near, opp, p_cross, y0, share_x, g_y, share_own = phase(
        pair_z(along), flip_z(along), lax.ppermute(prompt_own, "ctx", [(i, i ^ 4) for i in range(8)]),
        move_y(unit_0), move_x(share_x), move_y(cot), share_own
    )
    s0 = jnp.stack([unit_0, y0])
    unit_1, unit_3 = weights_in(near), weights_in(opp)
    prompt_z = jnp.stack([prompt_own, rows_in(near), p_cross, rows_in(opp)])
    share = jnp.stack([share_own, share_x])
    share_own, share_c = pick(share, c, 1), pick(share, 1 - c, 1)
    s0, unit_1, unit_3, prompt_z, share_c, share_own, small = phase(
        s0, unit_1, unit_3, prompt_z, share_c, share_own, jnp.stack([packed, packed_c, packed_x, packed_xc])
    )
    small = jnp.take(small, jnp.arange(4, dtype=jnp.int32) ^ wt_index, axis=0)
    gain_attn_f = small[:, 0].reshape(1024).astype(F32)
    gain_ffn_f = small[:, 1].reshape(1024).astype(F32)
    bias_f = small[:, 5, :128].reshape(4, 32, 4).transpose(1, 0, 2).reshape(32, 16).astype(F32)
    table_rev = jnp.pad(bucket_table[::-1], (0, WIDE - 768), constant_values=-1)[None]
    windows = bias_windows(idx, table_rev, bias_f)
    cross, prompt_y, x0, x1, y3, windows, gain_attn_f = phase(
        pair_z(unit_3), move_y(prompt_z), move_x(s0), move_x(unit_1), move_y(unit_3), windows, gain_attn_f
    )
    t0, s1, s3 = jnp.stack([s0, x0]), jnp.stack([unit_1, x1]), jnp.stack([unit_3, y3])
    t0, s1, s3 = phase(t0, s1, s3)
    c0, share_c, s1, s3 = phase(move_c(t0), move_c(share_c), s1, s3)
    share = jnp.stack([share_own, share_c], axis=1).reshape(4, 3, 3, 96, 256)
    spread = [
        lax.all_gather(t, "ctx", axis=0, tiled=False, axis_index_groups=LINES_Z) for t in (share[:, :2], share[:, 2:])
    ]
    source_all, all_low = norm_rows(idx, prompt_z, prompt_y, rows_own, gain_attn_f)
    state = attend(((0, False),), idx, all_low, windows, (t0, c0), None)
    *state, y1, x3, x2, g_cy = phase(*state, move_y(s1), move_x(s3), move_x(cross), move_c(g_y))
    t1, t3, s2, *state = phase(jnp.stack([s1, y1]), jnp.stack([s3, x3]), jnp.stack([cross, x2]), *state)
    c1, c3, *state = phase(move_c(t1), move_c(t3), *state)
    state = attend(((1, True), (3, False)), idx, all_low, windows, (t1, c1, t3, c3), state)
    *state, y2, g_x, g_c = phase(*state, move_y(s2), move_x(cot), move_c(cot))
    t2, *state = phase(jnp.stack([s2, y2]), *state)
    c2, *state = phase(move_c(t2), *state)
    state = attend(((2, True),), idx, all_low, windows, (t2, c2), state)
    marks_all = jnp.stack([t0[:, :, 1024:], c0[:, :, 1024:]]).reshape(2, 2, 2, 2048)[..., :960]
    marks_all = marks_all.transpose(0, 2, 1, 3).reshape(2560, 3).astype(F32)
    marks_all = jnp.pad(marks_all, ((0, 0), (0, 125)))
    *state, g_cx = phase(*state, move_c(g_x))
    probs, mixed, qkv, w_all = state
    hidden, normed = project_out(mixed, rows_own, gain_ffn_f, w_all)
    hidden, normed, g_xy = phase(hidden, normed, move_x(g_y))

    x_x, x_y, x_c, g_cxy, marks_all = phase(move_x(normed), move_y(normed), move_c(normed), move_c(g_xy), marks_all)
    x_a, x_b, x_cx, x_cy = phase(move_x(x_y[:160]), move_y(x_x[160:]), move_c(x_x), move_c(x_y))
    x_parts = [normed, x_x, x_y, x_a, x_b, x_c, x_cx, x_cy, move_c(x_a), move_c(x_b)]
    cot_parts = [cot, g_x, g_y, g_xy, g_xy, g_c, g_cx, g_cy, g_cxy, g_cxy]

    def along_z(gw, dw):
        gw, dw = gw.astype(BF).reshape(-1, 2, 4, 96, 1024), dw.astype(BF).reshape(-1, 1, 4, 96, 1024)
        return jnp.concatenate([gw, dw], axis=1).transpose(2, 0, 1, 3, 4)

    def reduce_z(both):
        flat = both.reshape(4, -1, 1024)
        got = lax.psum_scatter(flat, "ctx", scatter_dimension=0, axis_index_groups=LINES_Z)
        return got.reshape(both.shape[1:])

    out, dx, dh, win, s_01, x_all, g_all = expert_call((0, 1), idx, x_parts, cot_parts, marks_all, spread[0], None)
    both_01 = along_z(dot_tn(dh, x_all), dot_tn(win, g_all))
    both_01, out = phase(both_01, out)
    bulk = [reduce_z(both_01)]
    out, out_c, dx, dx_c, dh_2, win_2 = expert_call(
        (2,), idx, x_all, g_all, marks_all, spread[1], (out, dx, s_01)
    )

    got, g_d2, dh_2 = phase(move_c(dx_c), dot_tn(win_2, g_all), dh_2)
    last, rest = add_low(dx[960:], got[960:]), add_low(dx[:960], got[:960])
    last_a, last_b, dh_2, rest = phase(last[:160], last[160:], dh_2, rest)
    both_2 = along_z(dot_tn(dh_2, x_all), g_d2)
    d_a, d_b, rest, both_2, o_got = phase(move_x(last_a), move_y(last_b), rest, both_2, move_c(out_c))

    def mix_in(rest, a, b):
        v_x = jnp.concatenate([rest[320:480], add_low(rest[480:640], b)], axis=0)
        v_y = jnp.concatenate([add_low(rest[640:800], a), rest[800:]], axis=0)
        return v_x, v_y

    bulk.append(reduce_z(both_2))
    v_x, v_y = mix_in(rest, d_a, d_b)
    v_x, v_y, out, o_got = phase(v_x, v_y, out, o_got)
    o_last, o_rest = add_low(out[960:], o_got[960:]), add_low(out[:960], o_got[:960])
    v_x, v_y, o_la, o_lb, o_rest = phase(move_x(v_x), move_y(v_y), o_last[:160], o_last[160:], o_rest)
    router_part = both_2[0, 0, 0, 88:96].astype(F32)
    grad_hidden, grad_low, grad_mixed, gain_ffn_part = out_back(
        (rest[:320], v_x, v_y), hidden, gain_ffn_f, cot, w_all
    )
    back_of = lambda base, count, *prev: attend_back(
        base, count, idx, all_low, probs, qkv, w_all, grad_mixed, mixed, grad_low, *prev
    )
    keep_f, send_f, gn, dbias = back_of(4, 4, None, None)
    o_a, o_b, gn = phase(move_x(o_la), move_y(o_lb), gn)
    o_x, o_y, gn = phase(*mix_in(o_rest, o_a, o_b), gn)
    o_x, o_y, gn, bulk[0] = phase(o_x, o_y, gn, bulk[0])
    keep_n, send_n, gn, dbias = back_of(2, 2, gn, dbias)
    o_x, o_y, got, gn = phase(move_x(o_x), move_y(o_y), move_c(send_f), gn)
    combined = o_rest[:320].astype(F32) + o_x.astype(F32) + o_y.astype(F32)
    output = (hidden + combined).astype(BF).reshape(1, 1, 320, 1024)

    fa, fb = cut_rows(add_low(keep_f, got).reshape(2, 2, 2, 256, 512))
    fa0, fa1, fb0, fb1, gn = phase(fa[0], fa[1], fb[:, :, 0], fb[:, :, 1], gn)
    keep_h, send_h, gn_all, dbias, gp = back_of(0, 2, gn, dbias)
    fx, fy, got_n, gn_all, gp = phase(move_x(fa1), move_y(fb1), move_c(send_n), gn_all, gp)
    fa, fb = add_low(fa0, fx), add_low(fb0, fy)
    smalls = pack(idx, table_rev, dbias, gn_all, source_all, gain_ffn_part, router_part)
    got, fy, fx, gp_cross, smalls = phase(
        move_c(send_h), move_y(fa[:, 1]), move_x(fb[1]), pair_z(gp[2]), smalls
    )
    fy, bulk[1] = phase(fy, bulk[1])
    far = jnp.concatenate([add_low(fa[:, 0], fy), add_low(fb[0], fx)], axis=1)
    block = lambda t: t.reshape(2, 1, 2, 256, 512)
    h = jnp.concatenate([add_low(block(keep_h), block(got)), add_low(block(keep_n), block(got_n))], axis=1)
    ha, hb = cut_rows(h)
    hx, hy, f_cross, gp_opp, gp_near, sm = phase(
        move_x(ha[1]), move_y(hb[:, :, 1]), pair_z(far[0]), flip_z(add_low(gp[3], gp_cross)), pair_z(gp[1]),
        move_c(smalls),
    )
    ha, hb = add_low(ha[0], hx), add_low(hb[:, :, 0], hy)
    gp = (gp[0].astype(F32) + gp_near.astype(F32) + gp_opp.astype(F32)).astype(BF)
    smalls = smalls + sm
    hy, hx, f_opp, gp_y, sm = phase(
        move_y(ha[:, 1]), move_x(hb[1]), flip_z(add_low(far[1], f_cross)), move_y(gp[1]), move_x(smalls)
    )
    here = jnp.concatenate([add_low(ha[:, 0], hy), add_low(hb[0], hx)], axis=1)
    smalls = smalls + sm
    h_near, sm = phase(pair_z(here[1]), move_y(smalls))
    smalls = smalls + sm
    tot = here[0].astype(F32) + h_near.astype(F32) + f_opp.astype(F32)
    grad_tokens = finish(gp[0], gp_y, gn_all, rows_own, gain_attn_f, grad_hidden).reshape(1, 1, 320, 1024)
    sm_1, sm_2, sm_3 = [lax.ppermute(smalls, "ctx", [(i, i ^ n) for i in range(8)]) for n in (2, 4, 6)]
    smalls = (smalls + sm_1) + (sm_2 + sm_3)
    mine = lax.dynamic_slice_in_dim(smalls, wt_index * 256, 256, 1)
    res_gain_attn, res_gain_ffn, res_router = mine[0], mine[1], mine[2:5].T
    res_bias = lax.dynamic_slice_in_dim(smalls[8:24, :BUCKETS], wt_index * 4, 4, 0).T

    back = jnp.concatenate(bulk).reshape(3, 3, 96, 4, 256).transpose(3, 0, 1, 2, 4)
    back = trade_wt(back)[:, :, :, :88].transpose(1, 2, 0, 3, 4).reshape(3, 3, 352, 256).astype(F32)
    res_gate, res_up, res_down = back[:, 0].transpose(0, 2, 1), back[:, 1].transpose(0, 2, 1), back[:, 2]

    return (
        output, grad_tokens, tot[:, :128], tot[:, 128:256], tot[:, 256:384], tot[:, 384:], res_gain_attn, res_gain_ffn, res_router, res_bias,
        res_gate, res_up, res_down,
    )


def solution(mesh):
    fast = mesh.shape["ctx"] == FAST_CTX and mesh.shape["wt"] == FAST_WT
    return jax.shard_map(
        local_fast if fast else local,
        mesh=mesh,
        in_specs=(
            P("wt", "ctx", None, None),
            P("wt", "ctx", None, None),
            P("wt", "ctx"),
            P("wt", "ctx"),
            P("wt", "ctx"),
            P("wt", "ctx"),
            P("wt"),
            P("wt"),
            P("wt", None),
            P(None, "wt"),
            P(None, "wt", "ctx"),
            P(None, "wt", "ctx"),
            P(None, "ctx", "wt"),
            P(),
            P("wt", "ctx", None, None),
            P("wt", "ctx", None),
        ),
        out_specs=(
            P("wt", "ctx", None, None),
            P("wt", "ctx", None, None),
            P("wt", "ctx"),
            P("wt", "ctx"),
            P("wt", "ctx"),
            P("wt", "ctx"),
            P("wt"),
            P("wt"),
            P("wt", None),
            P(None, "wt"),
            P(None, "wt", "ctx"),
            P(None, "wt", "ctx"),
            P(None, "ctx", "wt"),
        ),
        check_vma=False,
    )
```

```python
import functools

import jax
import jax.numpy as jnp
from jax import lax
from jax.experimental import pallas as pl
from jax.experimental.pallas import tpu as pltpu
from jax.sharding import PartitionSpec as P

HEADS = 16
HEAD_DIM = 64
BUCKETS = 32
EXPERTS = 3
TOP = 2
LEN = 256
CAP = 267


epsilon = 1e-06
precise = lax.Precision.HIGHEST


def rms_norm(values, gain_vec):
    return (
        values * lax.rsqrt(jnp.mean(values * values, axis=-1, keepdims=True) + epsilon) * gain_vec
    )


def gelu_product(gate_pre, up_pre):
    return jax.nn.gelu(gate_pre, approximate=True) * up_pre


def routing(expert_ids, priority, capacity, expert_count):
    tok_rows = expert_ids.shape[0]
    top_count = expert_ids.shape[1]
    expert = expert_ids.T.reshape(-1)
    rank_key = (
        jnp.arange(top_count, dtype=jnp.int32)[:, None] * tok_rows + priority[None, :]
    ).reshape(-1)
    earlier = (expert[:, None] == expert[None, :]) & (rank_key[None, :] < rank_key[:, None])
    places = jnp.sum(earlier.astype(jnp.int32), axis=1)
    keep_mask = places < capacity
    slot_ids = expert * capacity + jnp.minimum(places, capacity - 1)
    slot_hits = jnp.where(
        (slot_ids[:, None] == jnp.arange(expert_count * capacity, dtype=jnp.int32)[None, :])
        & keep_mask[:, None],
        1.0,
        0.0,
    )
    dispatch = jnp.sum(slot_hits.reshape(top_count, tok_rows, expert_count * capacity), axis=0).T
    return (keep_mask, slot_ids, slot_hits, dispatch)


def gate_values(logits, expert_ids, keep_mask):
    chances = jax.nn.softmax(logits, axis=-1)
    picked = jnp.take_along_axis(chances, expert_ids, axis=1).T.reshape(-1)
    return jnp.where(keep_mask, picked, 0.0)


def toeplitz(reversed_bias, top_start, row_total, key_total):
    window_len = row_total + key_total
    window = lax.dynamic_slice_in_dim(reversed_bias, top_start, window_len, 1)
    tiled = jnp.tile(window, (1, row_total))[:, : row_total * (window_len - 1)]
    return tiled.reshape(window.shape[0], row_total, window_len - 1)[:, :, row_total - 1 :]


def toeplitz_back(grad_block, row_total, key_total):
    window_len = row_total + key_total
    head_total = grad_block.shape[0]
    placed = jnp.pad(grad_block, ((0, 0), (0, 0), (row_total - 1, 0))).reshape(
        head_total, row_total * (window_len - 1)
    )
    placed = jnp.pad(placed, ((0, 0), (0, row_total)))
    return jnp.sum(placed.reshape(head_total, row_total, window_len), axis=1)


def add_window(table, piece, start):
    current = lax.dynamic_slice_in_dim(table, start, piece.shape[1], 1)
    return lax.dynamic_update_slice_in_dim(table, current + piece, start, 1)


def sweep(step_fn, start_state, prompt_items, local_items):
    state_mid, stacked = lax.scan(step_fn, start_state, prompt_items)
    state_end, last_out = step_fn(state_mid, local_items)
    return (state_end, stacked, last_out)


def local(
    tokens,
    cotangent,
    w_query,
    w_key,
    w_value,
    w_out,
    gain_attn,
    gain_ffn,
    w_router,
    rel_bias,
    exp_gate,
    exp_up,
    exp_down,
    bucket_table,
    expert_ids,
    priority,
):
    tok_rows = tokens.shape[2]
    model_width = tokens.shape[3]
    ctx_count = lax.axis_size("ctx")
    my_block = lax.axis_index("ctx")
    prompt_rows = tok_rows - LEN
    cont_rows = tok_rows - prompt_rows
    prompt_len = prompt_rows * ctx_count
    dist_count = bucket_table.shape[0]
    head_count = HEADS
    head_width = HEAD_DIM
    score_scale = HEAD_DIM ** (-0.5)
    steps_count = max(1, ctx_count // 8)
    block_keys = prompt_len // steps_count
    cols_query, cols_key, cols_value, cols_out, cols_gate, cols_up, cols_down = (
        lax.all_gather(w_query, "ctx", axis=1, tiled=True),
        lax.all_gather(w_key, "ctx", axis=1, tiled=True),
        lax.all_gather(w_value, "ctx", axis=1, tiled=True),
        lax.all_gather(w_out, "ctx", axis=1, tiled=True),
        lax.all_gather(exp_gate, "ctx", axis=2, tiled=True),
        lax.all_gather(exp_up, "ctx", axis=2, tiled=True),
        lax.all_gather(exp_down, "ctx", axis=1, tiled=True),
    )
    gathered = (
        lax.all_gather(cols_query, "wt", axis=0, tiled=True),
        lax.all_gather(cols_key, "wt", axis=0, tiled=True),
        lax.all_gather(cols_value, "wt", axis=0, tiled=True),
        lax.all_gather(cols_out, "wt", axis=0, tiled=True),
        lax.all_gather(cols_gate, "wt", axis=1, tiled=True),
        lax.all_gather(cols_up, "wt", axis=1, tiled=True),
        lax.all_gather(cols_down, "wt", axis=2, tiled=True),
        lax.all_gather(gain_attn, "wt", axis=0, tiled=True),
        lax.all_gather(gain_ffn, "wt", axis=0, tiled=True),
        lax.all_gather(w_router, "wt", axis=0, tiled=True),
        lax.all_gather(rel_bias, "wt", axis=1, tiled=True),
    )
    (
        full_query,
        full_key,
        full_value,
        full_out,
        full_gate,
        full_up,
        full_down,
        full_gain_attn,
        full_gain_ffn,
        full_router,
        full_bias,
    ) = gathered
    gain_attn_f = full_gain_attn.astype(jnp.float32)
    gain_ffn_f = full_gain_ffn.astype(jnp.float32)
    source = tokens[0, 0].astype(jnp.float32)
    normed_attn = rms_norm(source, gain_attn_f)
    normed_attn_low = normed_attn.astype(jnp.bfloat16)
    query_low = jnp.dot(normed_attn_low, full_query, preferred_element_type=jnp.float32).astype(
        jnp.bfloat16
    )
    key_low = jnp.dot(normed_attn_low, full_key, preferred_element_type=jnp.float32).astype(
        jnp.bfloat16
    )
    value_low = jnp.dot(normed_attn_low, full_value, preferred_element_type=jnp.float32).astype(
        jnp.bfloat16
    )
    far_keys, far_values = (
        lax.all_gather(key_low[:prompt_rows], "ctx", axis=0, tiled=True),
        lax.all_gather(value_low[:prompt_rows], "ctx", axis=0, tiled=True),
    )
    row_index = jnp.arange(tok_rows, dtype=jnp.int32)
    query_pos = jnp.where(
        row_index < prompt_rows,
        my_block * prompt_rows + row_index,
        prompt_len + row_index - prompt_rows,
    )
    bucket_onehot = jnp.where(
        bucket_table[:, None] == jnp.arange(BUCKETS, dtype=jnp.int32)[None, :], 1.0, 0.0
    )
    bias_rows = jnp.dot(bucket_onehot, full_bias.astype(jnp.float32), precision=precise).T
    reversed_bias = jnp.concatenate([bias_rows[:, ::-1], jnp.zeros_like(bias_rows)], axis=1)
    prompt_starts = jnp.arange(steps_count, dtype=jnp.int32) * block_keys
    local_start = jnp.asarray(prompt_len, dtype=jnp.int32)
    query_heads = query_low.reshape(tok_rows, head_count, head_width)

    def blocks_of(far_array):
        return far_array.reshape(steps_count, block_keys, model_width)

    def window_starts(key_start):
        prompt_top = dist_count - my_block * prompt_rows + key_start - prompt_rows
        cont_top = dist_count - prompt_len + key_start - cont_rows
        return (prompt_top, cont_top)

    def block_scores(key_block, key_start):
        key_total = key_block.shape[0]
        key_heads = key_block.reshape(key_total, head_count, head_width)
        logit_raw = (
            jnp.einsum("qhd,khd->hqk", query_heads, key_heads, preferred_element_type=jnp.float32)
            * score_scale
        )
        key_pos = key_start + jnp.arange(key_total, dtype=jnp.int32)
        offset = query_pos[:, None] - key_pos[None, :]
        prompt_top, cont_top = window_starts(key_start)
        bias_block = jnp.concatenate(
            [
                toeplitz(reversed_bias, prompt_top, prompt_rows, key_total),
                toeplitz(reversed_bias, cont_top, cont_rows, key_total),
            ],
            axis=1,
        )
        return jnp.where(offset[None] >= 0, logit_raw + bias_block, -1e30)

    def stats_step(state_in, block_item):
        run_max, run_sum = state_in
        scores = block_scores(block_item[0], block_item[1])
        new_max = jnp.maximum(run_max, jnp.max(scores, axis=-1))
        new_sum = run_sum * jnp.exp(run_max - new_max) + jnp.sum(
            jnp.exp(scores - new_max[..., None]), axis=-1
        )
        return ((new_max, new_sum), None)

    start_stats = (
        jnp.full((head_count, tok_rows), -1e30, jnp.float32),
        jnp.zeros((head_count, tok_rows), jnp.float32),
    )
    (row_max, row_sum), unused_a, unused_b = sweep(
        stats_step,
        start_stats,
        (blocks_of(far_keys), prompt_starts),
        (key_low[prompt_rows:], local_start),
    )

    def mix_step(state_in, block_item):
        scores = block_scores(block_item[0], block_item[2])
        weights = (jnp.exp(scores - row_max[..., None]) / row_sum[..., None]).astype(jnp.bfloat16)
        value_heads = block_item[1].reshape(-1, head_count, head_width)
        return (
            state_in
            + jnp.einsum("hqk,khd->qhd", weights, value_heads, preferred_element_type=jnp.float32),
            None,
        )

    mixed_exact, unused_c, unused_d = sweep(
        mix_step,
        jnp.zeros((tok_rows, head_count, head_width), jnp.float32),
        (blocks_of(far_keys), blocks_of(far_values), prompt_starts),
        (key_low[prompt_rows:], value_low[prompt_rows:], local_start),
    )
    mixed_low = mixed_exact.reshape(tok_rows, model_width).astype(jnp.bfloat16)
    hidden = source + jnp.dot(mixed_low, full_out, preferred_element_type=jnp.float32)
    normed_ffn_low = rms_norm(hidden, gain_ffn_f).astype(jnp.bfloat16)
    route_ids = expert_ids[0, 0]
    keep_mask, slot_ids, slot_hits, dispatch = routing(route_ids, priority[0, 0], CAP, EXPERTS)
    inputs = (
        jnp.dot(dispatch.astype(jnp.bfloat16), normed_ffn_low, preferred_element_type=jnp.float32)
        .astype(jnp.bfloat16)
        .reshape(EXPERTS, CAP, model_width)
    )
    gate_pre = jnp.einsum("ecd,edf->ecf", inputs, full_gate, preferred_element_type=jnp.float32)
    up_pre = jnp.einsum("ecd,edf->ecf", inputs, full_up, preferred_element_type=jnp.float32)
    inner_low = gelu_product(gate_pre, up_pre).astype(jnp.bfloat16)
    expert_out = jnp.einsum(
        "ecf,efd->ecd", inner_low, full_down, preferred_element_type=jnp.float32
    ).reshape(EXPERTS * CAP, model_width)
    logits = jnp.dot(normed_ffn_low, full_router, preferred_element_type=jnp.float32)
    weight_pair = gate_values(logits, route_ids, keep_mask)
    picked_rows = jnp.take(expert_out, slot_ids, axis=0)
    combined = jnp.sum(
        (picked_rows * weight_pair[:, None]).reshape(TOP, tok_rows, model_width), axis=0
    )
    output = (hidden + combined).astype(jnp.bfloat16).reshape(1, 1, tok_rows, model_width)
    back_keys, back_values = (far_keys, far_values)
    (
        back_query,
        back_key,
        back_value,
        back_out,
        back_gate,
        back_up,
        back_down,
        back_gain_attn,
        back_gain_ffn,
        back_router,
        back_bias,
    ) = gathered
    grad_final = cotangent[0, 0].astype(jnp.float32)
    grad_pair = jnp.where(
        keep_mask, jnp.sum(jnp.tile(grad_final, (TOP, 1)) * picked_rows, axis=-1), 0.0
    )
    slot_weight = jnp.dot(weight_pair, slot_hits, precision=precise)
    grad_expert_out = (
        (jnp.dot(dispatch, grad_final, precision=precise) * slot_weight[:, None])
        .astype(jnp.bfloat16)
        .reshape(EXPERTS, CAP, model_width)
    )
    grad_inner = jnp.einsum(
        "ecd,efd->ecf", grad_expert_out, back_down, preferred_element_type=jnp.float32
    )
    unused_e, inner_pull = jax.vjp(gelu_product, gate_pre, up_pre)
    grad_gate_pre, grad_up_pre = inner_pull(grad_inner)
    grad_gate_low = grad_gate_pre.astype(jnp.bfloat16)
    grad_up_low = grad_up_pre.astype(jnp.bfloat16)
    grad_gate_w = jnp.einsum(
        "ecd,ecf->edf", inputs, grad_gate_low, preferred_element_type=jnp.float32
    )
    grad_up_w = jnp.einsum("ecd,ecf->edf", inputs, grad_up_low, preferred_element_type=jnp.float32)
    grad_down_w = jnp.einsum(
        "ecf,ecd->efd", inner_low, grad_expert_out, preferred_element_type=jnp.float32
    )
    grad_inputs = jnp.einsum(
        "ecf,edf->ecd", grad_gate_low, back_gate, preferred_element_type=jnp.float32
    ) + jnp.einsum("ecf,edf->ecd", grad_up_low, back_up, preferred_element_type=jnp.float32)

    def gate_of_logits(logit_values):
        return gate_values(logit_values, route_ids, keep_mask)

    unused_f, gate_pull = jax.vjp(gate_of_logits, logits)
    (grad_logits,) = gate_pull(grad_pair)
    grad_router_w = jnp.dot(normed_ffn_low.astype(jnp.float32).T, grad_logits, precision=precise)
    grad_normed_ffn = jnp.dot(grad_logits, back_router.astype(jnp.float32).T, precision=precise)
    grad_normed_ffn = grad_normed_ffn + jnp.dot(
        dispatch.T, grad_inputs.reshape(EXPERTS * CAP, model_width), precision=precise
    )
    unused_g, ffn_norm_pull = jax.vjp(rms_norm, hidden, back_gain_ffn.astype(jnp.float32))
    grad_hidden_part, grad_gain_ffn_w = ffn_norm_pull(grad_normed_ffn)
    grad_hidden = grad_final + grad_hidden_part
    grad_hidden_low = grad_hidden.astype(jnp.bfloat16)
    grad_out_w = jnp.dot(mixed_low.T, grad_hidden_low, preferred_element_type=jnp.float32)
    grad_mixed = jnp.dot(grad_hidden_low, back_out.T, preferred_element_type=jnp.float32).astype(
        jnp.bfloat16
    )
    grad_mixed_heads = grad_mixed.reshape(tok_rows, head_count, head_width)
    row_delta = jnp.sum(grad_mixed_heads.astype(jnp.float32) * mixed_exact, axis=-1).T

    def grad_step(state_in, block_item):
        grad_query_acc, grad_reversed = state_in
        key_block, value_block, key_start = block_item
        key_total = key_block.shape[0]
        scores = block_scores(key_block, key_start)
        chances = jnp.exp(scores - row_max[..., None]) / row_sum[..., None]
        value_heads = value_block.reshape(-1, head_count, head_width)
        key_heads = key_block.reshape(-1, head_count, head_width)
        grad_chance = jnp.einsum(
            "qhd,khd->hqk", grad_mixed_heads, value_heads, preferred_element_type=jnp.float32
        )
        grad_value_block = jnp.einsum(
            "hqk,qhd->khd",
            chances.astype(jnp.bfloat16),
            grad_mixed_heads,
            preferred_element_type=jnp.float32,
        )
        grad_scores = chances * (grad_chance - row_delta[..., None])
        prompt_top, cont_top = window_starts(key_start)
        grad_reversed = add_window(
            grad_reversed,
            toeplitz_back(grad_scores[:, :prompt_rows], prompt_rows, key_total),
            prompt_top,
        )
        grad_reversed = add_window(
            grad_reversed,
            toeplitz_back(grad_scores[:, prompt_rows:], cont_rows, key_total),
            cont_top,
        )
        grad_scores_low = grad_scores.astype(jnp.bfloat16)
        grad_query_acc = grad_query_acc + score_scale * jnp.einsum(
            "hqk,khd->qhd", grad_scores_low, key_heads, preferred_element_type=jnp.float32
        )
        grad_key_block = score_scale * jnp.einsum(
            "hqk,qhd->khd", grad_scores_low, query_heads, preferred_element_type=jnp.float32
        )
        return (
            (grad_query_acc, grad_reversed),
            (grad_key_block.reshape(-1, model_width), grad_value_block.reshape(-1, model_width)),
        )

    start_grads = (
        jnp.zeros((tok_rows, head_count, head_width), jnp.float32),
        jnp.zeros((head_count, 2 * dist_count), jnp.float32),
    )
    (
        (grad_query_exact, grad_reversed),
        (far_grad_keys, far_grad_values),
        (near_grad_keys, near_grad_values),
    ) = sweep(
        grad_step,
        start_grads,
        (blocks_of(back_keys), blocks_of(back_values), prompt_starts),
        (key_low[prompt_rows:], value_low[prompt_rows:], local_start),
    )
    own_grad_keys, own_grad_values = (
        lax.psum_scatter(
            far_grad_keys.reshape(prompt_len, model_width), "ctx", scatter_dimension=0, tiled=True
        ),
        lax.psum_scatter(
            far_grad_values.reshape(prompt_len, model_width), "ctx", scatter_dimension=0, tiled=True
        ),
    )
    grad_key_low = jnp.concatenate([own_grad_keys, near_grad_keys], axis=0).astype(jnp.bfloat16)
    grad_value_low = jnp.concatenate([own_grad_values, near_grad_values], axis=0).astype(
        jnp.bfloat16
    )
    grad_query_low = grad_query_exact.reshape(tok_rows, model_width).astype(jnp.bfloat16)
    grad_query_w = jnp.dot(normed_attn_low.T, grad_query_low, preferred_element_type=jnp.float32)
    grad_key_w = jnp.dot(normed_attn_low.T, grad_key_low, preferred_element_type=jnp.float32)
    grad_value_w = jnp.dot(normed_attn_low.T, grad_value_low, preferred_element_type=jnp.float32)
    grad_normed_attn = jnp.dot(grad_query_low, back_query.T, preferred_element_type=jnp.float32)
    grad_normed_attn = grad_normed_attn + jnp.dot(
        grad_key_low, back_key.T, preferred_element_type=jnp.float32
    )
    grad_normed_attn = grad_normed_attn + jnp.dot(
        grad_value_low, back_value.T, preferred_element_type=jnp.float32
    )
    unused_h, attn_norm_pull = jax.vjp(rms_norm, source, back_gain_attn.astype(jnp.float32))
    grad_source_part, grad_gain_attn_w = attn_norm_pull(grad_normed_attn)
    grad_tokens = (
        (grad_hidden + grad_source_part).astype(jnp.bfloat16).reshape(1, 1, tok_rows, model_width)
    )
    grad_bias_rows = grad_reversed[:, :dist_count][:, ::-1]
    grad_bias_w = jnp.dot(bucket_onehot.T, grad_bias_rows.T, precision=precise)
    small_gain_attn, small_gain_ffn, small_router, small_bias = lax.psum(
        (grad_gain_attn_w, grad_gain_ffn_w, grad_router_w, grad_bias_w), "ctx"
    )
    row_parts = (
        lax.psum_scatter(
            grad_query_w.astype(jnp.bfloat16), "wt", scatter_dimension=0, tiled=True
        ).astype(jnp.float32),
        lax.psum_scatter(
            grad_key_w.astype(jnp.bfloat16), "wt", scatter_dimension=0, tiled=True
        ).astype(jnp.float32),
        lax.psum_scatter(
            grad_value_w.astype(jnp.bfloat16), "wt", scatter_dimension=0, tiled=True
        ).astype(jnp.float32),
        lax.psum_scatter(
            grad_out_w.astype(jnp.bfloat16), "wt", scatter_dimension=0, tiled=True
        ).astype(jnp.float32),
        lax.psum_scatter(
            grad_gate_w.astype(jnp.bfloat16), "wt", scatter_dimension=1, tiled=True
        ).astype(jnp.float32),
        lax.psum_scatter(
            grad_up_w.astype(jnp.bfloat16), "wt", scatter_dimension=1, tiled=True
        ).astype(jnp.float32),
        lax.psum_scatter(
            grad_down_w.astype(jnp.bfloat16), "wt", scatter_dimension=2, tiled=True
        ).astype(jnp.float32),
        lax.psum_scatter(
            small_gain_attn.astype(jnp.bfloat16), "wt", scatter_dimension=0, tiled=True
        ).astype(jnp.float32),
        lax.psum_scatter(
            small_gain_ffn.astype(jnp.bfloat16), "wt", scatter_dimension=0, tiled=True
        ).astype(jnp.float32),
        lax.psum_scatter(
            small_router.astype(jnp.bfloat16), "wt", scatter_dimension=0, tiled=True
        ).astype(jnp.float32),
        lax.psum_scatter(
            small_bias.astype(jnp.bfloat16), "wt", scatter_dimension=1, tiled=True
        ).astype(jnp.float32),
    )
    res_query, res_key, res_value, res_out, res_gate, res_up, res_down = (
        lax.psum_scatter(row_parts[0], "ctx", scatter_dimension=1, tiled=True),
        lax.psum_scatter(row_parts[1], "ctx", scatter_dimension=1, tiled=True),
        lax.psum_scatter(row_parts[2], "ctx", scatter_dimension=1, tiled=True),
        lax.psum_scatter(row_parts[3], "ctx", scatter_dimension=1, tiled=True),
        lax.psum_scatter(row_parts[4], "ctx", scatter_dimension=2, tiled=True),
        lax.psum_scatter(row_parts[5], "ctx", scatter_dimension=2, tiled=True),
        lax.psum_scatter(row_parts[6], "ctx", scatter_dimension=1, tiled=True),
    )
    res_gain_attn, res_gain_ffn, res_router, res_bias = (
        row_parts[7],
        row_parts[8],
        row_parts[9],
        row_parts[10],
    )
    return (
        output,
        grad_tokens,
        res_query,
        res_key,
        res_value,
        res_out,
        res_gain_attn,
        res_gain_ffn,
        res_router,
        res_bias,
        res_gate,
        res_up,
        res_down,
    )


BF = jnp.bfloat16
F32 = jnp.float32
FAST_CTX = 8
FAST_WT = 4
NEG = -1e30

SWAP_Y = [(i, i ^ 1) for i in range(8)]
LINES_Z = [[0, 2, 4, 6], [1, 3, 5, 7]]
PAIR_Z = [(i, i ^ 2) for i in range(8)]
FLIP_Z = [(i, i ^ 6) for i in range(8)]
SWAP_C = [(i, i ^ 1) for i in range(4)]
SWAP_X = [(i, i ^ 2) for i in range(4)]


def move_y(v):
    return lax.ppermute(v, "ctx", SWAP_Y)


def move_x(v):
    return lax.ppermute(v, "wt", SWAP_X)


def move_c(v):
    return lax.ppermute(v, "wt", SWAP_C)


def pair_z(v):
    return lax.ppermute(v, "ctx", PAIR_Z)


def flip_z(v):
    return lax.ppermute(v, "ctx", FLIP_Z)


def phase(*vals):
    return lax.optimization_barrier(vals)


def dot_nt(a, b):
    return lax.dot_general(a, b, (((1,), (1,)), ((), ())), preferred_element_type=F32)


def dot_tn(a, b):
    return lax.dot_general(a, b, (((0,), (0,)), ((), ())), preferred_element_type=F32)


def dot_nn(a, b):
    return jnp.dot(a, b, preferred_element_type=F32)


def params(limit=56 * 2**20):
    return pltpu.CompilerParams(vmem_limit_bytes=limit)


COST_S = pl.CostEstimate(flops=10**10, bytes_accessed=10**6, transcendentals=0)
COST_E = pl.CostEstimate(flops=25 * 10**9, bytes_accessed=10**6, transcendentals=0)
ANY = pl.BlockSpec(memory_space=pl.ANY)
SMEM = pl.BlockSpec(memory_space=pltpu.SMEM)


def spread_z(v):
    near, opp = pair_z(v), flip_z(v)
    return {0: v, 1: near, 3: opp, 2: pair_z(opp)}


def attend_kernel(groups, first, idx, n_ref, w_ref, *refs):
    pieces, refs = refs[: 2 * len(groups)], refs[2 * len(groups) :]
    if not first:
        refs = refs[4:]
    p_ref, o_ref, qkv_ref, wt_ref, bc_ref, bp_ref, qs_ref = refs
    z, y, x, c = idx[0], idx[1], idx[2], idx[3]
    step = pl.program_id(0)
    for n, (sz, x_first) in enumerate(groups):
        for ry in range(2):

            @pl.when(step == 2 * n + ry)
            def _(n=n, ry=ry, x_first=x_first):
                for rx in range(2):
                    for rc in range(2):
                        row = pl.multiple_of(((x ^ rx) * 2 + (c ^ rc)) * 256, 256)
                        src = pieces[2 * n + rc]
                        for t in range(4):
                            rows = slice(256 * t, 256 * t + 256)
                            block = src[ry, rx, rows] if x_first else src[rx, ry, rows]
                            wt_ref[0, pl.ds(row, 256), 128 * t : 128 * t + 128] = block

    qkv = dot_nn(n_ref[...], wt_ref[0, :, :384]).astype(BF)
    qkv_ref[0] = qkv
    k, v = qkv[:, 128:256], qkv[:, 256:]
    qs_ref[...] = qkv[:, :128]
    q_c = qs_ref[512:, :]
    q_p = qs_ref[pl.ds(pl.multiple_of((z * 2 + y) * 64, 64), 64), :]
    lane = lax.broadcasted_iota(jnp.int32, (1, 128), 1)
    outs = []
    for h in range(2):
        base_c, base_p = w_ref[h, 0], w_ref[h, 1]
        for a in range(32):
            bc_ref[8 * a : 8 * a + 8, :] = pltpu.roll(base_c, 1024 - (248 - 8 * a), 1)[:, :768]
        for a in range(8):
            shift = 56 - 8 * a
            bp_ref[8 * a : 8 * a + 8, :] = (pltpu.roll(base_p, 1024 - shift, 1) if shift else base_p)[:, :512]
        mine = (lane < 64) if h == 0 else (lane >= 64)
        head = lambda t: jnp.where(mine, t, jnp.zeros_like(t))
        sc = dot_nt(head(q_c), k) * 0.125 + bc_ref[...]
        sp = dot_nt(head(q_p), k[:512]) * 0.125 + bp_ref[...]

        def soft(t):
            e = jnp.exp(t - jnp.max(t, axis=-1, keepdims=True))
            return (e * (1.0 / jnp.sum(e, axis=-1, keepdims=True))).astype(BF)

        pc, pp = soft(sc), soft(sp)
        p_ref[h, 64:, :] = pc
        p_ref[h, :64, :512] = pp
        p_ref[h, :64, 512:] = jnp.zeros((64, 256), BF)
        outs.append(jnp.concatenate([dot_nn(pp, v[:512]), dot_nn(pc, v)], axis=0))
    o_ref[...] = jnp.where(lane < 64, outs[0], outs[1]).astype(BF)


def norm_kernel(idx, a_ref, b_ref, own_ref, gain_ref, src_ref, low_ref):
    z, y = idx[0], idx[1]
    for sz in range(4):
        at = lambda yy: pl.ds(pl.multiple_of(((z ^ sz) * 2 + yy) * 64, 64), 64)
        src_ref[at(y), :] = a_ref[sz]
        src_ref[at(y ^ 1), :] = b_ref[sz]
    src_ref[512:, :] = own_ref[64:, :]
    values = src_ref[...].astype(F32)
    low_ref[...] = (norm_parts(values) * gain_ref[...]).astype(BF)


def norm_rows(idx, prompt_z, prompt_y, rows_own, gain):
    whole = pl.BlockSpec(memory_space=pltpu.VMEM)
    out = jax.ShapeDtypeStruct((768, 1024), BF)
    return pl.pallas_call(
        norm_kernel,
        in_specs=[SMEM] + [whole] * 4,
        out_specs=(whole, whole),
        out_shape=(out, out),
        compiler_params=params(),
    )(idx, prompt_z, prompt_y, rows_own, gain[None])


def attend(groups, idx, normed, windows, pieces, prev):
    keys, rows = normed.shape[0], 320

    def at(i, d):
        sz = groups[0][0]
        for n, (other, unused) in enumerate(groups):
            sz = jnp.where(i // 2 == n, other, sz)
        return (d[0] ^ sz) * 2 + (d[1] ^ (i % 2))

    whole = pl.BlockSpec(memory_space=pltpu.VMEM)
    return pl.pallas_call(
        functools.partial(attend_kernel, groups, prev is None),
        grid_spec=pltpu.PrefetchScalarGridSpec(
            num_scalar_prefetch=1,
            grid=(2 * len(groups),),
            in_specs=[whole, pl.BlockSpec((2, 2, 8, 1024), lambda i, d: (at(i, d), 0, 0, 0))]
            + [whole] * len(pieces)
            + ([] if prev is None else [ANY] * 4),
            out_specs=(
                pl.BlockSpec((2, rows, keys), lambda i, d: (at(i, d), 0, 0)),
                pl.BlockSpec((rows, 128), lambda i, d: (0, at(i, d))),
                pl.BlockSpec((1, keys, 384), lambda i, d: (at(i, d), 0, 0)),
                pl.BlockSpec((1, 1024, 512), lambda i, d: (at(i, d), 0, 0)),
            ),
            scratch_shapes=[pltpu.VMEM((256, 768), F32), pltpu.VMEM((64, 512), F32), pltpu.VMEM((keys, 128), BF)],
        ),
        out_shape=(
            jax.ShapeDtypeStruct((16, rows, keys), BF),
            jax.ShapeDtypeStruct((rows, 1024), BF),
            jax.ShapeDtypeStruct((8, keys, 384), BF),
            jax.ShapeDtypeStruct((8, 1024, 512), BF),
        ),
        input_output_aliases={} if prev is None else {3 + len(pieces) + n: n for n in range(4)},
        compiler_params=params(),
        cost_estimate=COST_S,
    )(idx, normed, windows, *pieces, *([] if prev is None else prev))


def attend_back_kernel(first, final, idx, n_ref, p_ref, qkv_ref, wt_ref, g_ref, m_ref, gl_ref, *refs):
    if not first:
        gn_prev, refs = refs[0], refs[2:]
    if final:
        gp_ref, refs = refs[4], refs[:4] + refs[5:]
    keep_ref, send_ref, gn_ref, db_ref, dt_ref, qs_ref = refs
    z, y, x, c = idx[0], idx[1], idx[2], idx[3]
    own = pl.ds(pl.multiple_of((z * 2 + y) * 64, 64), 64)
    qkv = qkv_ref[0]
    k, v = qkv[:, 128:256], qkv[:, 256:]
    qs_ref[...] = qkv[:, :128]
    q = jnp.concatenate([qs_ref[own, :], qs_ref[512:, :]], axis=0)
    g = g_ref[...]
    lane = lax.broadcasted_iota(jnp.int32, (1, 128), 1)
    parts = []
    for h in range(2):
        mine = (lane < 64) if h == 0 else (lane >= 64)
        gh = jnp.where(mine, g, jnp.zeros_like(g))
        p = p_ref[h]
        pf = p.astype(F32)
        dp = dot_nt(gh, v)
        delta = jnp.sum(pf * dp, axis=-1, keepdims=True)
        ds = pf * (dp - delta)
        low = ds.astype(BF)
        acc_c = jnp.zeros((8, 1024), F32)
        for a in range(32):
            part = jnp.concatenate([ds[64 + 8 * a : 72 + 8 * a], jnp.zeros((8, 256), F32)], axis=1)
            acc_c = acc_c + pltpu.roll(part, 248 - 8 * a, 1) if a < 31 else acc_c + part
        acc_p = jnp.zeros((8, 1024), F32)
        for a in range(8):
            part = jnp.concatenate([ds[8 * a : 8 * a + 8, :512], jnp.zeros((8, 512), F32)], axis=1)
            acc_p = acc_p + (pltpu.roll(part, 56 - 8 * a, 1) if a < 7 else part)
        db_ref[h, 0] = acc_c
        db_ref[h, 1] = acc_p
        parts.append((dot_nn(low, k) * 0.125, dot_tn(low, q) * 0.125, dot_tn(p, g)))
    dq, dk, dv = [jnp.where(lane < 64, parts[0][n], parts[1][n]).astype(BF) for n in range(3)]
    dt_ref[:512, :128] = jnp.zeros((512, 128), BF)
    dt_ref[own, :128] = dq[:64]
    dt_ref[512:, :128] = dq[64:]
    dt_ref[:, 128:256] = dk
    dt_ref[:, 256:] = dv
    dt = dt_ref[...]
    dw = jnp.concatenate([dot_tn(n_ref[...], dt).astype(BF), dot_tn(m_ref[...], gl_ref[...]).astype(BF)], axis=1)
    for xx in range(2):
        for cc in range(2):
            block = dw[(xx * 2 + cc) * 256 : (xx * 2 + cc) * 256 + 256]

            @pl.when(c == cc)
            def _():
                keep_ref[x ^ xx, 0] = block

            @pl.when(c != cc)
            def _():
                send_ref[x ^ xx, 0] = block

    gn = dot_nt(dt, wt_ref[0, :, :384])

    @pl.when(pl.program_id(0) == 0)
    def _():
        gn_ref[...] = gn if first else gn_prev[...] + gn

    @pl.when(pl.program_id(0) != 0)
    def _():
        gn_ref[...] += gn

    if final:

        @pl.when(pl.program_id(0) == pl.num_programs(0) - 1)
        def _():
            for sz in range(4):
                for ry in range(2):
                    rows = pl.ds(pl.multiple_of(((z ^ sz) * 2 + (y ^ ry)) * 64, 64), 64)
                    gp_ref[sz, ry] = gn_ref[rows, :].astype(BF)


def attend_back(base, count, idx, normed, p, qkv, wt, g, mixed, g_low, gn_prev, db_prev):
    rows, keys = p.shape[1], p.shape[2]
    final = base == 0
    at = lambda i, d: (i + base) ^ (d[0] * 2 + d[1])
    whole = pl.BlockSpec((keys, 1024), lambda i, d: (0, 0))
    return pl.pallas_call(
        functools.partial(attend_back_kernel, gn_prev is None, final),
        grid_spec=pltpu.PrefetchScalarGridSpec(
            num_scalar_prefetch=1,
            grid=(count,),
            in_specs=[
                whole,
                pl.BlockSpec((2, rows, keys), lambda i, d: (at(i, d), 0, 0)),
                pl.BlockSpec((1, keys, 384), lambda i, d: (at(i, d), 0, 0)),
                pl.BlockSpec((1, 1024, 512), lambda i, d: (at(i, d), 0, 0)),
                pl.BlockSpec((rows, 128), lambda i, d: (0, at(i, d))),
                pl.BlockSpec((rows, 1024), lambda i, d: (0, 0)),
                pl.BlockSpec((rows, 128), lambda i, d: (0, at(i, d))),
            ]
            + ([] if gn_prev is None else [whole, ANY]),
            out_specs=(
                pl.BlockSpec((2, 1, 256, 512), lambda i, d: (0, i, 0, 0)),
                pl.BlockSpec((2, 1, 256, 512), lambda i, d: (0, i, 0, 0)),
                whole,
                pl.BlockSpec((2, 2, 8, 1024), lambda i, d: (at(i, d), 0, 0, 0)),
            )
            + ((pl.BlockSpec((4, 2, 64, 1024), lambda i, d: (0, 0, 0, 0)),) if final else ()),
            scratch_shapes=[pltpu.VMEM((keys, 384), BF), pltpu.VMEM((keys, 128), BF)],
        ),
        out_shape=(
            jax.ShapeDtypeStruct((2, count, 256, 512), BF),
            jax.ShapeDtypeStruct((2, count, 256, 512), BF),
            jax.ShapeDtypeStruct((keys, 1024), F32),
            jax.ShapeDtypeStruct((16, 2, 8, 1024), F32),
        )
        + ((jax.ShapeDtypeStruct((4, 2, 64, 1024), BF),) if final else ()),
        input_output_aliases={} if gn_prev is None else {9: 3},
        compiler_params=params(),
        cost_estimate=COST_E,
    )(idx, normed, p, qkv, wt, g, mixed, g_low, *([] if gn_prev is None else [gn_prev, db_prev]))


def cut_rows(t):
    return t[:, :, :, :128], t[:, :, :, 128:]


def out_back_kernel(a_ref, b_ref, c_ref, h_ref, gain_ref, cot_ref, w_ref, gh_ref, gl_ref, gm_ref, gg_ref):
    f = lambda t: t.astype(F32)
    dn = f(a_ref[...]) + f(b_ref[...]) + f(c_ref[...])
    hidden, gain = h_ref[...], gain_ref[...]
    scale = lax.rsqrt(jnp.mean(hidden * hidden, axis=-1, keepdims=True) + epsilon)
    unit = hidden * scale
    gg_ref[...] = jnp.broadcast_to(jnp.sum(dn * unit, axis=0, keepdims=True), gg_ref.shape)
    du = dn * gain
    grad = f(cot_ref[...]) + scale * (du - unit * jnp.mean(du * unit, axis=-1, keepdims=True))
    gh_ref[...] = grad
    low = grad.astype(BF)
    gl_ref[...] = low
    total = dot_nt(low[:, :128], w_ref[0, :, 384:])
    for n in range(1, 8):
        total = total + dot_nt(low[:, 128 * n : 128 * n + 128], w_ref[n, :, 384:])
    gm_ref[...] = total.astype(BF)


def out_back(parts, hidden, gain, cot, w_o):
    whole = pl.BlockSpec(memory_space=pltpu.VMEM)
    return pl.pallas_call(
        out_back_kernel,
        in_specs=[whole] * 7,
        out_specs=(whole,) * 4,
        out_shape=(
            jax.ShapeDtypeStruct((320, 1024), F32),
            jax.ShapeDtypeStruct((320, 1024), BF),
            jax.ShapeDtypeStruct((320, 1024), BF),
            jax.ShapeDtypeStruct((8, 1024), F32),
        ),
        compiler_params=params(),
        cost_estimate=COST_S,
    )(*parts, hidden, gain[None], cot, w_o)


def out_kernel(m_ref, s_ref, g_ref, w_ref, h_ref, l_ref):
    m = m_ref[...]
    for n in range(8):
        cols = slice(128 * n, 128 * n + 128)
        h_ref[:, cols] = s_ref[:, cols].astype(F32) + dot_nn(m, w_ref[n, :, 384:])
    hidden = h_ref[...]
    scale = lax.rsqrt(jnp.mean(hidden * hidden, axis=-1, keepdims=True) + epsilon)
    l_ref[...] = (hidden * scale * g_ref[...]).astype(BF)


def project_out(mixed, rows_own, gain, wt):
    whole = pl.BlockSpec(memory_space=pltpu.VMEM)
    return pl.pallas_call(
        out_kernel,
        in_specs=[whole] * 4,
        out_specs=(whole,) * 2,
        out_shape=(jax.ShapeDtypeStruct((320, 1024), F32), jax.ShapeDtypeStruct((320, 1024), BF)),
        compiler_params=params(),
        cost_estimate=COST_S,
    )(mixed, rows_own, gain[None], wt)


WIDE = 1920


def window_kernel(idx, t_ref, b_ref, o_ref):
    onehot = jnp.where(lax.broadcasted_iota(jnp.int32, (BUCKETS, WIDE), 0) == t_ref[...], 1.0, 0.0)
    rev = lax.dot_general(b_ref[...], onehot, (((0,), (0,)), ((), ())), precision=precise, preferred_element_type=F32)
    rev = jnp.where(lax.broadcasted_iota(jnp.int32, (16, WIDE), 1) < 768, rev, NEG)
    tail = pltpu.roll(rev, WIDE - 704 + 64 * (idx[0] * 2 + idx[1]), 1)
    for s in range(8):
        o_ref[:, 0, s, :] = (pltpu.roll(rev, WIDE - 7 + s, 1) if s < 7 else rev)[:, :1024]
        o_ref[:, 1, s, :] = (pltpu.roll(tail, WIDE - 7 + s, 1) if s < 7 else tail)[:, :1024]


def bias_windows(idx, table_rev, bias_f):
    whole = pl.BlockSpec(memory_space=pltpu.VMEM)
    return pl.pallas_call(
        window_kernel,
        in_specs=[SMEM, whole, whole],
        out_specs=whole,
        out_shape=jax.ShapeDtypeStruct((16, 2, 8, 1024), F32),
        compiler_params=params(),
    )(idx, table_rev, bias_f)


def pack_kernel(idx, t_ref, db_ref, gn_ref, src_ref, gf_ref, r_ref, small_ref):
    z, y = idx[0], idx[1]

    def gather(n):
        total = jnp.zeros((16, WIDE), F32)
        for s in range(8):
            part = jnp.concatenate([db_ref[:, n, s, :], jnp.zeros((16, WIDE - 1024), F32)], axis=1)
            total = total + (pltpu.roll(part, 7 - s, 1) if s < 7 else part)
        return total

    rev = gather(0) + pltpu.roll(gather(1), 704 - 64 * (z * 2 + y), 1)
    onehot = jnp.where(lax.broadcasted_iota(jnp.int32, (BUCKETS, 768), 0) == t_ref[:, :768], 1.0, 0.0)
    bias = lax.dot_general(
        rev[:, :768], onehot, (((1,), (1,)), ((), ())), precision=precise, preferred_element_type=F32
    )
    src = src_ref[...].astype(F32)
    unit = src * lax.rsqrt(jnp.mean(src * src, axis=-1, keepdims=True) + epsilon)
    small_ref[...] = jnp.zeros_like(small_ref)
    small_ref[0:1, :] = jnp.sum(gn_ref[...] * unit, axis=0, keepdims=True)
    small_ref[1:2, :] = gf_ref[0:1, :]
    small_ref[2:5, :] = r_ref[0:3, :]
    small_ref[8:24, 0:BUCKETS] = bias


def pack(idx, table_rev, dbias, gn, src, gain_ffn_part, router_part):
    whole = pl.BlockSpec(memory_space=pltpu.VMEM)
    return pl.pallas_call(
        pack_kernel,
        in_specs=[SMEM] + [whole] * 6,
        out_specs=whole,
        out_shape=jax.ShapeDtypeStruct((24, 1024), F32),
        compiler_params=params(),
        cost_estimate=COST_S,
    )(idx, table_rev, dbias, gn, src, gain_ffn_part, router_part)


def final_kernel(p_ref, q_ref, gn_ref, src_ref, gain_ref, gh_ref, o_ref):
    f = lambda t: t.astype(F32)
    own = f(p_ref[...]) + f(q_ref[...])
    grad = jnp.concatenate([own, gn_ref[512:, :]], axis=0) * gain_ref[...]
    src = f(src_ref[...])
    scale = lax.rsqrt(jnp.mean(src * src, axis=-1, keepdims=True) + epsilon)
    unit = src * scale
    back = scale * (grad - unit * jnp.mean(grad * unit, axis=-1, keepdims=True))
    o_ref[...] = (gh_ref[...] + back).astype(BF)


def finish(own, other, gn, src, gain, grad_hidden):
    whole = pl.BlockSpec(memory_space=pltpu.VMEM)
    return pl.pallas_call(
        final_kernel,
        in_specs=[whole] * 6,
        out_specs=whole,
        out_shape=jax.ShapeDtypeStruct((320, 1024), BF),
        compiler_params=params(),
        cost_estimate=COST_S,
    )(own, other, gn, src, gain[None], grad_hidden)


def add_low(a, b):
    return (a.astype(F32) + b.astype(F32)).astype(BF)


PIECES = [(0, 320), (320, 320), (640, 320), (960, 160), (1120, 160)]


def fetch_pieces(want, x_parts, g_parts, x_scr, g_scr, sem):
    copies = []
    for rc in range(2):
        for n, (row, size) in enumerate(PIECES):
            at = rc * 1280 + row
            tile = at // 640
            if want not in (None, tile):
                continue
            k = rc * 5 + n
            copies.append(pltpu.make_async_copy(x_parts[k], x_scr.at[pl.ds(at, size)], sem.at[k, 0]))
            src = g_parts[k].at[pl.ds(160 if n == 4 else 0, size)]
            copies.append(pltpu.make_async_copy(src, g_scr.at[pl.ds(at, size)], sem.at[k, 1]))
    return copies


def expert_kernel(group, last, *refs):
    refs = list(refs)
    step = pl.program_id(0)
    count = len(group)
    idx, refs = refs[0], refs[1:]
    w_at = idx[2] * 2 + idx[3]
    src, m_ref = refs[:2]
    if not last:
        x_parts, g_parts = refs[2:12], refs[12:22]
        out_ref, dx_ref, dh_ref, win_ref, s_ref, xo_ref, go_ref, w_scr, sem, x_scr, g_scr, psem = refs[22:]
    else:
        x_ref, g_ref, out_prev, dx_prev, s_prev = refs[2:7]
        out_ref, out_c_ref, dx_ref, dx_c_ref, dh_ref, win_ref, w_scr, sem = refs[7:]

    @pl.when(step == 0)
    def _():
        copies = [
            pltpu.make_async_copy(
                src.at[n, r, e],
                w_scr.at[e, :, pl.ds(96 * n, 96), pl.ds(pl.multiple_of((w_at ^ r) * 256, 256), 256)],
                sem.at[n, 4 * e + r],
            )
            for e in range(count)
            for n in range(4)
            for r in range(4)
        ]
        for copy in copies:
            copy.start()
        if not last:
            for copy in fetch_pieces(None, x_parts, g_parts, x_scr, g_scr, psem):
                copy.start()
        for copy in copies:
            copy.wait()

    if not last:
        for t in range(4):

            @pl.when(step == t)
            def _(t=t):
                for copy in fetch_pieces(t, x_parts, g_parts, x_scr, g_scr, psem):
                    copy.wait()

        rows = pl.ds(pl.multiple_of(step * 640, 640), 640)
        x, g = x_scr[rows, :], g_scr[rows, :]
        xo_ref[...] = x
        go_ref[...] = g
    else:
        x, g = x_ref[...], g_ref[...]
    m = m_ref[...]
    lane = lax.broadcasted_iota(jnp.int32, (1, 384), 1)
    scores = []
    for k, expert in enumerate(group):
        w_gu = w_scr[k, 0:2].reshape(768, 1024)
        w_d = w_scr[k, 2]
        gu = dot_nt(x, w_gu)
        gi = dot_nt(g, w_d)
        gate, up = gu[:, :384], gu[:, 384:]
        if k == 0:
            l = [gate[:, 88 + n : 89 + n] for n in range(3)]
            top = jnp.maximum(jnp.maximum(l[0], l[1]), l[2])
            ex = [jnp.exp(v - top) for v in l]
            inv = 1.0 / (ex[0] + ex[1] + ex[2])
            p = [v * inv for v in ex]
        keep = m[:, expert : expert + 1]
        w = p[expert] * keep
        sq = gate * gate
        th = jnp.tanh(0.7978845608028654 * gate * (1.0 + 0.044715 * sq))
        half1 = 0.5 + 0.5 * th
        act = gate * half1
        dact = half1 + (0.5 * gate) * (1.0 - th * th) * (0.7978845608028654 + 0.10703222440890037 * sq)
        inner = (act * up).astype(BF).astype(F32)
        s = jnp.sum(inner * gi, axis=-1, keepdims=True) * keep
        scores.append(s)
        gin = gi * w
        dg = gin * up * dact
        du = gin * act
        if last:
            ss = [s_prev[...][:, 0:1], s_prev[...][:, 1:2], s]
            dot = p[0] * ss[0] + p[1] * ss[1] + p[2] * ss[2]
            edge = dg[:, :128]
            for n in range(3):
                edge = jnp.where(lane[:, :128] == 88 + n, p[n] * (ss[n] - dot), edge)
            dg = jnp.concatenate([edge, dg[:, 128:]], axis=1)
        win = (inner * w).astype(BF)
        dh = jnp.concatenate([dg.astype(BF), du.astype(BF)], axis=1)
        dh_ref[:, 768 * k : 768 * k + 768] = dh
        win_ref[:, 384 * k : 384 * k + 384] = win
        o_k, dx_k = dot_nn(win, w_d), dot_nn(dh, w_gu)
        out, dx = (o_k, dx_k) if k == 0 else (out + o_k, dx + dx_k)
    if last:
        out = (out + out_prev[...].astype(F32)).astype(BF)
        dx = (dx + dx_prev[...].astype(F32)).astype(BF)

        @pl.when(step < 2)
        def _():
            out_c_ref[...] = out
            dx_c_ref[...] = dx

        @pl.when(step >= 2)
        def _():
            out_ref[...] = out
            dx_ref[...] = dx
    else:
        out_ref[...] = out.astype(BF)
        dx_ref[...] = dx.astype(BF)
        s_ref[...] = jnp.where(lane[:, :128] == 0, scores[0], scores[1])


def expert_call(group, idx, x, g, m, src, prev, tile=640):
    total, count = 2560, len(group)
    last = prev is not None
    at = (lambda i: i ^ 2) if last else (lambda i: i)
    row = lambda n: pl.BlockSpec((tile, n), lambda i: (at(i), 0))
    shape = lambda n, t: jax.ShapeDtypeStruct((total, n), t)
    scratch = [pltpu.VMEM((count, 3, 384, 1024), BF), pltpu.SemaphoreType.DMA((4, 4 * count))]
    if not last:
        ins = [idx, src, m, *x, *g]
        specs = [SMEM, ANY, row(128)] + [ANY] * 20
        outs = [(1024, BF), (1024, BF), (768 * count, BF), (384 * count, BF), (128, F32), (1024, BF), (1024, BF)]
        out_shape = tuple(shape(n, t) for n, t in outs)
        out_specs = tuple(row(n) for n, t in outs)
        scratch += [pltpu.VMEM((total, 1024), BF), pltpu.VMEM((total, 1024), BF), pltpu.SemaphoreType.DMA((10, 2))]
    else:
        ins = [idx, src, m, x, g, *prev]
        specs = [SMEM, ANY, row(128)] + [row(1024)] * 4 + [row(128)]
        half = jax.ShapeDtypeStruct((total // 2, 1024), BF)
        mine = pl.BlockSpec((tile, 1024), lambda i: (jnp.maximum(i - 2, 0), 0))
        other = pl.BlockSpec((tile, 1024), lambda i: (jnp.minimum(i, 1), 0))
        out_shape = (half, half, half, half, shape(768 * count, BF), shape(384 * count, BF))
        out_specs = (mine, other, mine, other, row(768 * count), row(384 * count))
    return pl.pallas_call(
        functools.partial(expert_kernel, group, last),
        grid=(total // tile,),
        out_shape=out_shape,
        in_specs=specs,
        out_specs=out_specs,
        scratch_shapes=scratch,
        compiler_params=params(),
        cost_estimate=COST_E,
    )(*ins)


def line_collect(part_of, z):
    at = lambda n: part_of(z ^ n)
    near = pair_z(at(1))
    opp = flip_z(add_low(at(3), pair_z(at(2))))
    return (at(0).astype(F32) + near.astype(F32) + opp.astype(F32)).astype(BF)


def trade_wt(v):
    return lax.all_to_all(v, "wt", 0, 0, tiled=True)


def sum_all(v):
    v = v + move_c(v)
    v = v + move_x(v)
    v = v + move_y(v)
    v = v + lax.ppermute(v, "ctx", [(i, i ^ 2) for i in range(8)])
    return v + lax.ppermute(v, "ctx", [(i, i ^ 4) for i in range(8)])


def norm_parts(values):
    return values * lax.rsqrt(jnp.mean(values * values, axis=-1, keepdims=True) + epsilon)


def local_fast(
    tokens, cotangent, w_query, w_key, w_value, w_out, gain_attn, gain_ffn, w_router, rel_bias,
    exp_gate, exp_up, exp_down, bucket_table, expert_ids, priority,
):
    ctx_index = lax.axis_index("ctx").astype(jnp.int32)
    wt_index = lax.axis_index("wt").astype(jnp.int32)
    z, y, x, c = ctx_index // 2, ctx_index % 2, wt_index // 2, wt_index % 2
    idx = jnp.stack([z, y, x, c])
    rows_own = tokens[0, 0]

    packed = jnp.concatenate(
        [gain_attn[None], gain_ffn[None], w_router.T, jnp.pad(rel_bias.reshape(1, 128), ((0, 0), (0, 128))),
         jnp.zeros((2, 256), BF)], axis=0
    )
    ids, rank = expert_ids[0, 0], priority[0, 0]
    expert = ids.T.reshape(-1)
    rank_key = (jnp.arange(TOP, dtype=jnp.int32)[:, None] * 320 + rank[None, :]).reshape(-1)
    earlier = (expert[:, None] == expert[None, :]) & (rank_key[None, :] < rank_key[:, None])
    keep = (jnp.sum(earlier.astype(jnp.int32), axis=1) < CAP).reshape(TOP, 320)
    hold = jnp.sum(
        jnp.where((ids.T[:, :, None] == jnp.arange(EXPERTS, dtype=jnp.int32)) & keep[:, :, None], 1.0, 0.0), axis=0
    )
    marks = jnp.pad(hold.reshape(960), (0, 1088)).astype(BF).reshape(16, 128)
    cot = cotangent[0, 0]

    def pieces(v):
        return jnp.pad(v.reshape(3, 4, 88, 256), ((0, 0), (0, 0), (0, 8), (0, 0)))

    gate_t, up_t = exp_gate.transpose(0, 2, 1), exp_up.transpose(0, 2, 1)
    gate_p = pieces(gate_t)
    router_rows = jnp.broadcast_to(
        jnp.pad(w_router.T, ((0, 5), (0, 0)))[None, None], (3, 4, 8, 256)
    )
    gate_p = jnp.concatenate([gate_p[:, :, :88], router_rows], axis=2)
    share = jnp.stack([gate_p, pieces(up_t), pieces(exp_down)], axis=1).transpose(2, 0, 1, 3, 4)
    pick = lambda v, n, d: lax.dynamic_index_in_dim(v, n, d, keepdims=False)
    unit = jnp.stack([w_query, w_key, w_value, w_out]).reshape(1024, 128)
    prompt_own = rows_own[:64]
    along = jnp.concatenate([unit, prompt_own.reshape(512, 128)], axis=0)
    weights_in = lambda v: v[:1024]
    rows_in = lambda v: v[1024:].reshape(64, 1024)
    share = share.reshape(2, 2, 3, 3, 96, 256)
    share_x, share_own = pick(share, 1 - x, 0), pick(share, x, 0)
    packed_c, packed_x, packed_xc, along, share_x = phase(
        move_c(packed), move_x(packed), lax.ppermute(packed, "wt", [(i, i ^ 3) for i in range(4)]), along, share_x
    )
    unit_0 = jnp.concatenate([unit, marks], axis=0)
    near, opp, p_cross, y0, share_x, g_y, share_own = phase(
        pair_z(along), flip_z(along), lax.ppermute(prompt_own, "ctx", [(i, i ^ 4) for i in range(8)]),
        move_y(unit_0), move_x(share_x), move_y(cot), share_own
    )
    s0 = jnp.stack([unit_0, y0])
    unit_1, unit_3 = weights_in(near), weights_in(opp)
    prompt_z = jnp.stack([prompt_own, rows_in(near), p_cross, rows_in(opp)])
    share = jnp.stack([share_own, share_x])
    share_own, share_c = pick(share, c, 1), pick(share, 1 - c, 1)
    s0, unit_1, unit_3, prompt_z, share_c, share_own, small = phase(
        s0, unit_1, unit_3, prompt_z, share_c, share_own, jnp.stack([packed, packed_c, packed_x, packed_xc])
    )
    small = jnp.take(small, jnp.arange(4, dtype=jnp.int32) ^ wt_index, axis=0)
    gain_attn_f = small[:, 0].reshape(1024).astype(F32)
    gain_ffn_f = small[:, 1].reshape(1024).astype(F32)
    bias_f = small[:, 5, :128].reshape(4, 32, 4).transpose(1, 0, 2).reshape(32, 16).astype(F32)
    table_rev = jnp.pad(bucket_table[::-1], (0, WIDE - 768), constant_values=-1)[None]
    windows = bias_windows(idx, table_rev, bias_f)
    cross, prompt_y, x0, x1, y3, windows, gain_attn_f = phase(
        pair_z(unit_3), move_y(prompt_z), move_x(s0), move_x(unit_1), move_y(unit_3), windows, gain_attn_f
    )
    t0, s1, s3 = jnp.stack([s0, x0]), jnp.stack([unit_1, x1]), jnp.stack([unit_3, y3])
    t0, s1, s3 = phase(t0, s1, s3)
    c0, share_c, s1, s3 = phase(move_c(t0), move_c(share_c), s1, s3)
    share = jnp.stack([share_own, share_c], axis=1).reshape(4, 3, 3, 96, 256)
    spread = [
        lax.all_gather(t, "ctx", axis=0, tiled=False, axis_index_groups=LINES_Z) for t in (share[:, :2], share[:, 2:])
    ]
    source_all, all_low = norm_rows(idx, prompt_z, prompt_y, rows_own, gain_attn_f)
    state = attend(((0, False),), idx, all_low, windows, (t0, c0), None)
    *state, y1, x3, x2, g_cy = phase(*state, move_y(s1), move_x(s3), move_x(cross), move_c(g_y))
    t1, t3, s2, *state = phase(jnp.stack([s1, y1]), jnp.stack([s3, x3]), jnp.stack([cross, x2]), *state)
    c1, c3, *state = phase(move_c(t1), move_c(t3), *state)
    state = attend(((1, True), (3, False)), idx, all_low, windows, (t1, c1, t3, c3), state)
    *state, y2, g_x, g_c = phase(*state, move_y(s2), move_x(cot), move_c(cot))
    t2, *state = phase(jnp.stack([s2, y2]), *state)
    c2, *state = phase(move_c(t2), *state)
    state = attend(((2, True),), idx, all_low, windows, (t2, c2), state)
    marks_all = jnp.stack([t0[:, :, 1024:], c0[:, :, 1024:]]).reshape(2, 2, 2, 2048)[..., :960]
    marks_all = marks_all.transpose(0, 2, 1, 3).reshape(2560, 3).astype(F32)
    marks_all = jnp.pad(marks_all, ((0, 0), (0, 125)))
    *state, g_cx = phase(*state, move_c(g_x))
    probs, mixed, qkv, w_all = state
    hidden, normed = project_out(mixed, rows_own, gain_ffn_f, w_all)
    hidden, normed, g_xy = phase(hidden, normed, move_x(g_y))

    x_x, x_y, x_c, g_cxy, marks_all = phase(move_x(normed), move_y(normed), move_c(normed), move_c(g_xy), marks_all)
    x_a, x_b, x_cx, x_cy = phase(move_x(x_y[:160]), move_y(x_x[160:]), move_c(x_x), move_c(x_y))
    x_parts = [normed, x_x, x_y, x_a, x_b, x_c, x_cx, x_cy, move_c(x_a), move_c(x_b)]
    cot_parts = [cot, g_x, g_y, g_xy, g_xy, g_c, g_cx, g_cy, g_cxy, g_cxy]

    def along_z(gw, dw):
        gw, dw = gw.astype(BF).reshape(-1, 2, 4, 96, 1024), dw.astype(BF).reshape(-1, 1, 4, 96, 1024)
        return jnp.concatenate([gw, dw], axis=1).transpose(2, 0, 1, 3, 4)

    def reduce_z(both):
        flat = both.reshape(4, -1, 1024)
        got = lax.psum_scatter(flat, "ctx", scatter_dimension=0, axis_index_groups=LINES_Z)
        return got.reshape(both.shape[1:])

    out, dx, dh, win, s_01, x_all, g_all = expert_call((0, 1), idx, x_parts, cot_parts, marks_all, spread[0], None)
    both_01 = along_z(dot_tn(dh, x_all), dot_tn(win, g_all))
    both_01, out = phase(both_01, out)
    bulk = [reduce_z(both_01)]
    out, out_c, dx, dx_c, dh_2, win_2 = expert_call(
        (2,), idx, x_all, g_all, marks_all, spread[1], (out, dx, s_01)
    )

    got, g_d2, dh_2 = phase(move_c(dx_c), dot_tn(win_2, g_all), dh_2)
    last, rest = add_low(dx[960:], got[960:]), add_low(dx[:960], got[:960])
    last_a, last_b, dh_2, rest = phase(last[:160], last[160:], dh_2, rest)
    both_2 = along_z(dot_tn(dh_2, x_all), g_d2)
    d_a, d_b, rest, both_2, o_got = phase(move_x(last_a), move_y(last_b), rest, both_2, move_c(out_c))

    def mix_in(rest, a, b):
        v_x = jnp.concatenate([rest[320:480], add_low(rest[480:640], b)], axis=0)
        v_y = jnp.concatenate([add_low(rest[640:800], a), rest[800:]], axis=0)
        return v_x, v_y

    bulk.append(reduce_z(both_2))
    v_x, v_y = mix_in(rest, d_a, d_b)
    v_x, v_y, out, o_got = phase(v_x, v_y, out, o_got)
    o_last, o_rest = add_low(out[960:], o_got[960:]), add_low(out[:960], o_got[:960])
    v_x, v_y, o_la, o_lb, o_rest = phase(move_x(v_x), move_y(v_y), o_last[:160], o_last[160:], o_rest)
    router_part = both_2[0, 0, 0, 88:96].astype(F32)
    grad_hidden, grad_low, grad_mixed, gain_ffn_part = out_back(
        (rest[:320], v_x, v_y), hidden, gain_ffn_f, cot, w_all
    )
    back_of = lambda base, count, *prev: attend_back(
        base, count, idx, all_low, probs, qkv, w_all, grad_mixed, mixed, grad_low, *prev
    )
    keep_f, send_f, gn, dbias = back_of(4, 4, None, None)
    o_a, o_b, gn = phase(move_x(o_la), move_y(o_lb), gn)
    o_x, o_y, gn = phase(*mix_in(o_rest, o_a, o_b), gn)
    o_x, o_y, gn, bulk[0] = phase(o_x, o_y, gn, bulk[0])
    keep_n, send_n, gn, dbias = back_of(2, 2, gn, dbias)
    o_x, o_y, got, gn = phase(move_x(o_x), move_y(o_y), move_c(send_f), gn)
    combined = o_rest[:320].astype(F32) + o_x.astype(F32) + o_y.astype(F32)
    output = (hidden + combined).astype(BF).reshape(1, 1, 320, 1024)

    fa, fb = cut_rows(add_low(keep_f, got).reshape(2, 2, 2, 256, 512))
    fa0, fa1, fb0, fb1, gn = phase(fa[0], fa[1], fb[:, :, 0], fb[:, :, 1], gn)
    keep_h, send_h, gn_all, dbias, gp = back_of(0, 2, gn, dbias)
    fx, fy, got_n, gn_all, gp = phase(move_x(fa1), move_y(fb1), move_c(send_n), gn_all, gp)
    fa, fb = add_low(fa0, fx), add_low(fb0, fy)
    smalls = pack(idx, table_rev, dbias, gn_all, source_all, gain_ffn_part, router_part)
    got, fy, fx, gp_cross, smalls = phase(
        move_c(send_h), move_y(fa[:, 1]), move_x(fb[1]), pair_z(gp[2]), smalls
    )
    fy, bulk[1] = phase(fy, bulk[1])
    far = jnp.concatenate([add_low(fa[:, 0], fy), add_low(fb[0], fx)], axis=1)
    block = lambda t: t.reshape(2, 1, 2, 256, 512)
    h = jnp.concatenate([add_low(block(keep_h), block(got)), add_low(block(keep_n), block(got_n))], axis=1)
    ha, hb = cut_rows(h)
    hx, hy, f_cross, gp_opp, gp_near, sm = phase(
        move_x(ha[1]), move_y(hb[:, :, 1]), pair_z(far[0]), flip_z(add_low(gp[3], gp_cross)), pair_z(gp[1]),
        move_c(smalls),
    )
    ha, hb = add_low(ha[0], hx), add_low(hb[:, :, 0], hy)
    gp = (gp[0].astype(F32) + gp_near.astype(F32) + gp_opp.astype(F32)).astype(BF)
    smalls = smalls + sm
    hy, hx, f_opp, gp_y, sm = phase(
        move_y(ha[:, 1]), move_x(hb[1]), flip_z(add_low(far[1], f_cross)), move_y(gp[1]), move_x(smalls)
    )
    here = jnp.concatenate([add_low(ha[:, 0], hy), add_low(hb[0], hx)], axis=1)
    smalls = smalls + sm
    h_near, sm = phase(pair_z(here[1]), move_y(smalls))
    smalls = smalls + sm
    tot = here[0].astype(F32) + h_near.astype(F32) + f_opp.astype(F32)
    grad_tokens = finish(gp[0], gp_y, gn_all, rows_own, gain_attn_f, grad_hidden).reshape(1, 1, 320, 1024)
    sm_1, sm_2, sm_3 = [lax.ppermute(smalls, "ctx", [(i, i ^ n) for i in range(8)]) for n in (2, 4, 6)]
    smalls = (smalls + sm_1) + (sm_2 + sm_3)
    mine = lax.dynamic_slice_in_dim(smalls, wt_index * 256, 256, 1)
    res_gain_attn, res_gain_ffn, res_router = mine[0], mine[1], mine[2:5].T
    res_bias = lax.dynamic_slice_in_dim(smalls[8:24, :BUCKETS], wt_index * 4, 4, 0).T

    back = jnp.concatenate(bulk).reshape(3, 3, 96, 4, 256).transpose(3, 0, 1, 2, 4)
    back = trade_wt(back)[:, :, :, :88].transpose(1, 2, 0, 3, 4).reshape(3, 3, 352, 256).astype(F32)
    res_gate, res_up, res_down = back[:, 0].transpose(0, 2, 1), back[:, 1].transpose(0, 2, 1), back[:, 2]

    return (
        output, grad_tokens, tot[:, :128], tot[:, 128:256], tot[:, 256:384], tot[:, 384:], res_gain_attn, res_gain_ffn, res_router, res_bias,
        res_gate, res_up, res_down,
    )


def solution(mesh):
    fast = mesh.shape["ctx"] == FAST_CTX and mesh.shape["wt"] == FAST_WT
    return jax.shard_map(
        local_fast if fast else local,
        mesh=mesh,
        in_specs=(
            P("wt", "ctx", None, None),
            P("wt", "ctx", None, None),
            P("wt", "ctx"),
            P("wt", "ctx"),
            P("wt", "ctx"),
            P("wt", "ctx"),
            P("wt"),
            P("wt"),
            P("wt", None),
            P(None, "wt"),
            P(None, "wt", "ctx"),
            P(None, "wt", "ctx"),
            P(None, "ctx", "wt"),
            P(),
            P("wt", "ctx", None, None),
            P("wt", "ctx", None),
        ),
        out_specs=(
            P("wt", "ctx", None, None),
            P("wt", "ctx", None, None),
            P("wt", "ctx"),
            P("wt", "ctx"),
            P("wt", "ctx"),
            P("wt", "ctx"),
            P("wt"),
            P("wt"),
            P("wt", None),
            P(None, "wt"),
            P(None, "wt", "ctx"),
            P(None, "wt", "ctx"),
            P(None, "ctx", "wt"),
        ),
        check_vma=False,
    )
```
